32 devices in a mesh: fsdp: 4 (over z), tensor: 8 (over y, x, core).
Axes of the slice: x: 2, y: 2, z: 4, core: 2. Of those that a mesh axis runs over, the one named last changes fastest.
Arguments:
- momentum: float32 [4, 1152, 7168], P(None, 'fsdp', 'tensor'), may hold values from -600 to 600
- gradient: float32 [4, 1152, 7168], P(None, 'fsdp', 'tensor'), may hold values from -600 to 600
- live_ranks: int32 [4], replicated, may hold values from 0 to 1, as said below
- owner_group: int32 [4], replicated, may hold values from 0 to 3, each once
- row_counts: int32 [4, 4], replicated, may hold values from 1 to 288, as said below
- row_offsets: int32 [4, 4], replicated, may hold values from 0 to 575, as said below
Outputs:
- new_momentum: float32 [4, 1152, 7168], P(None, 'fsdp', 'tensor')
- update_shards: float32 [4, 1152, 7168], P(None, 'fsdp', 'tensor')
- owned_update: float32 [4, 576, 7168], P('fsdp', None, 'tensor')
The draws below stay inside these ranges and needn't reach their ends.
Inputs may be any that keep to these rules, and one draw needn't show every extreme that they name: `live_ranks`: exactly one rank is dead. For every matrix the live ranks' segments [row_offsets, row_offsets + row_counts) are disjoint and cover all 576 rows, and one live rank holds exactly 288 rows. The dead rank's entries are stale and describe no rows. `row_offsets`: see row_counts.
All inputs are finite; a program needn't handle non-finite values.
Results may differ from the reference program's by a relative error of at most 0.0003.
Values sent between devices are 32-bit elements; how exact they have to be, the bound alone decides.
No kernel may reach another device: no remote copies, remote signals or barrier semaphores. Data moves between devices by JAX's collectives and lax.ppermute only.
A program may use at most 64 MiB of HBM per device.

```python
import math
import jax
import jax.numpy as jnp
from jax import lax

WIDTH = 7168
INNER = 576
ITERS = 2
MATS = 4
CAP = 288
SLOTS = 1152
N_FSDP = 4


def scaled_field(key, salt):
    key_main = jax.random.fold_in(key, salt)
    key_entries, key_rows, key_columns = jax.random.split(key_main, 3)
    entries = jax.random.truncated_normal(key_entries, -5.0, 5.0, (MATS, SLOTS, WIDTH), jnp.float32)
    spread = math.log(10.0)
    row_scale = jnp.exp(jax.random.uniform(key_rows, (MATS, SLOTS, 1), jnp.float32, 0.0, spread))
    column_scale = jnp.exp(jax.random.uniform(key_columns, (MATS, 1, WIDTH), jnp.float32, 0.0, spread))
    return entries * row_scale * column_scale


def rank_order(sub_key):
    return jax.random.permutation(sub_key, N_FSDP).astype(jnp.int32)


def layout_tables(key):
    key_main = jax.random.fold_in(key, 9173)
    key_dead, key_order, key_shift, key_stale, key_start = jax.random.split(key_main, 5)
    rank_ids = jnp.arange(N_FSDP, dtype=jnp.int32)
    first_matrix = (jnp.arange(MATS, dtype=jnp.int32) == 0)[:, None]
    dead_rank = jax.random.randint(key_dead, (), 0, N_FSDP, dtype=jnp.int32)
    alive_flags = (rank_ids != dead_rank).astype(jnp.int32)
    orders = jax.vmap(rank_order)(jax.random.split(key_order, MATS))
    matches = (orders[:, :, None] == rank_ids[None, None, :]).astype(jnp.int32)
    placing = jnp.sum(matches * rank_ids[None, :, None], axis=1)
    is_dead = (rank_ids == dead_rank)[None, :]
    dead_place = jnp.sum(placing * is_dead.astype(jnp.int32), axis=1, keepdims=True)
    live_index = placing - (placing > dead_place).astype(jnp.int32)
    others = N_FSDP - 2
    share_rows = (INNER - CAP) // others
    extra_rows = INNER - CAP - share_rows * others
    rest_index = live_index - 1
    shifts = jax.random.randint(key_shift, (MATS, N_FSDP), 0, share_rows, dtype=jnp.int32)
    pair_shift = jnp.take_along_axis(shifts, jnp.clip(rest_index // 2, 0, N_FSDP - 1), axis=1)
    partnered = rest_index // 2 * 2 + 1 < others
    signed = jnp.where(rest_index % 2 == 0, -pair_shift, pair_shift)
    counts = share_rows + jnp.where(partnered, signed, 0) + (rest_index < extra_rows).astype(jnp.int32)
    counts = jnp.where(live_index == 0, CAP, counts)
    stale_count = jax.random.randint(key_stale, (MATS, N_FSDP), 1, CAP + 1, dtype=jnp.int32)
    stale_count = jnp.where(first_matrix, 1, stale_count).astype(jnp.int32)
    counts = jnp.where(is_dead, stale_count, counts).astype(jnp.int32)
    live_counts = counts * alive_flags[None, :]
    before = (placing[:, :, None] < placing[:, None, :]).astype(jnp.int32)
    offsets = jnp.sum(live_counts[:, :, None] * before, axis=1)
    stale_start = jax.random.randint(key_start, (MATS, N_FSDP), 0, INNER - stale_count + 1, dtype=jnp.int32)
    stale_start = jnp.where(first_matrix, INNER - 1, stale_start).astype(jnp.int32)
    offsets = jnp.where(is_dead, stale_start, offsets).astype(jnp.int32)
    return (alive_flags, counts, offsets)


def draw_momentum(key, part):
    return scaled_field(key, 11)


def draw_gradient(key, part):
    return scaled_field(key, 23)


def draw_live_ranks(key, part):
    return layout_tables(key)[0]


def draw_row_counts(key, part):
    return layout_tables(key)[1]


def draw_row_offsets(key, part):
    return layout_tables(key)[2]


def setup_inputs(seed: int = 0) -> dict:
    splits = jax.random.split(jax.random.key(seed), 7)
    momentum = draw_momentum(jax.random.fold_in(splits[6], 71), 0)
    gradient = draw_gradient(jax.random.fold_in(splits[6], 71), 0)
    live_ranks = draw_live_ranks(jax.random.fold_in(splits[6], 71), 0)
    owner_group = jax.random.permutation(splits[3], N_FSDP).astype(jnp.int32)
    row_counts = draw_row_counts(jax.random.fold_in(splits[6], 71), 0)
    row_offsets = draw_row_offsets(jax.random.fold_in(splits[6], 71), 0)
    return {"momentum": momentum, "gradient": gradient, "live_ranks": live_ranks, "owner_group": owner_group, "row_counts": row_counts, "row_offsets": row_offsets}


MOMENTUM_RATE = 0.95
QUINTIC_FIRST = 3.4445
QUINTIC_SECOND = -4.775
QUINTIC_THIRD = 2.0315
EPSILON = 1e-07
HIGHEST = lax.Precision.HIGHEST

def matmul(left_side, right_side):
    return jnp.dot(left_side, right_side, precision=HIGHEST, preferred_element_type=jnp.float32)

def orthogonalize(matrix):
    square_total = jnp.sum(matrix * matrix)
    iterate = matrix / (jnp.sqrt(square_total) + EPSILON)
    for repeat in range(ITERS):
        gram_now = lax.dot_general(iterate, iterate, (((1,), (1,)), ((), ())), precision=HIGHEST, preferred_element_type=jnp.float32)
        combined = QUINTIC_SECOND * gram_now + QUINTIC_THIRD * matmul(gram_now, gram_now)
        iterate = QUINTIC_FIRST * iterate + matmul(combined, iterate)
    return iterate * (0.2 * math.sqrt(max(INNER, WIDTH)))

def reference(momentum, gradient, live_ranks, owner_group, row_counts, row_offsets):
    position = jnp.arange(CAP, dtype=jnp.int32)

    def one_matrix(matrix_id):
        counts_now = row_counts[matrix_id] * live_ranks
        offsets_now = row_offsets[matrix_id]
        keep_grid = position[None, :] < counts_now[:, None]
        target = jnp.where(keep_grid, offsets_now[:, None] + position[None, :], INNER).reshape(-1).astype(jnp.int32)
        keep_slot = keep_grid.reshape(-1)[:, None]
        old_state = momentum[matrix_id]
        grad_now = gradient[matrix_id]
        fresh_slots = jnp.where(keep_slot, MOMENTUM_RATE * old_state + grad_now, 0.0)
        blended = grad_now + MOMENTUM_RATE * fresh_slots
        assembled = jnp.zeros((INNER, WIDTH), jnp.float32).at[target].add(blended, mode='drop')
        result = orthogonalize(assembled)
        picked = jnp.take(result, jnp.minimum(target, INNER - 1).astype(jnp.int32), axis=0)
        sent_back = jnp.where(keep_slot, picked, 0.0)
        return (fresh_slots, sent_back, result)
    fresh_all, back_all, results = lax.map(one_matrix, jnp.arange(MATS, dtype=jnp.int32))
    owned_rows = jnp.zeros_like(results).at[owner_group].set(results)
    return (fresh_all, back_all, owned_rows)
```

```python
import functools
import math

import jax
import jax.numpy as jnp
from jax import lax
from jax.experimental import pallas as pl
from jax.experimental.pallas import tpu as pltpu
from jax.sharding import PartitionSpec as P

WIDTH = 7168
INNER = 576
PANELS = 3
SUBLANES = 8
PANEL = INNER // PANELS

MOMENTUM_RATE = 0.95
QUINTIC_FIRST = 3.4445
QUINTIC_SECOND = -4.775
QUINTIC_THIRD = 2.0315
EPSILON = 1e-07
OUT_SCALE = 0.2 * math.sqrt(max(INNER, WIDTH))
VMEM_LIMIT = 48 * 1024 * 1024


def halves(value):
    high = value.astype(jnp.bfloat16)
    low = (value - high.astype(jnp.float32)).astype(jnp.bfloat16)
    return high, low


def dot(left, right, contract):
    return lax.dot_general(left, right, (contract, ((), ())), preferred_element_type=jnp.float32)


def dot_halves(left, right, contract=((1,), (0,))):
    (left_high, left_low), (right_high, right_low) = left, right
    return (
        dot(left_high, right_low, contract) + dot(left_low, right_high, contract)
    ) + dot(left_high, right_high, contract)


def aligned(start, slots):
    shift = start % SUBLANES
    return pl.ds(pl.multiple_of(start - shift, SUBLANES), slots + SUBLANES), shift


def gram_kernel(starts, *refs):
    *blocks, iterate, gram, padded = refs
    slots = blocks[0].shape[0]
    padded[...] = jnp.zeros_like(padded)
    tail = jnp.zeros((SUBLANES, blocks[0].shape[1]), jnp.float32)
    for place, block in enumerate(blocks):
        rows, shift = aligned(starts[place], slots)
        moved = pltpu.roll(jnp.concatenate([block[...], tail], axis=0), shift, 0)
        padded[rows, :] = padded[rows, :] + moved
    whole = padded[:INNER, :]
    iterate[...] = whole
    high, low = halves(whole)
    for panel in range(PANELS):
        here = slice(panel * PANEL, (panel + 1) * PANEL)
        after = (panel + 1) % PANELS
        there = slice(after * PANEL, (after + 1) * PANEL)
        gram[here, :PANEL] = dot_halves((high[here], low[here]), (high[here], low[here]), ((1,), (1,)))
        gram[here, PANEL:] = dot_halves((high[here], low[here]), (high[there], low[there]), ((1,), (1,)))


def update_kernel(starts, counts, packed, iterate, result, *refs):
    *blocks, gram, padded = refs
    slots, columns = blocks[0].shape
    for panel in range(PANELS):
        here = slice(panel * PANEL, (panel + 1) * PANEL)
        after = (panel + 1) % PANELS
        there = slice(after * PANEL, (after + 1) * PANEL)
        gram[here, here] = packed[here, :PANEL]
        side = packed[here, PANEL:]
        gram[here, there] = side
        gram[there, here] = side.T
    raw = gram[...]
    diagonal = lax.broadcasted_iota(jnp.int32, raw.shape, 0) == lax.broadcasted_iota(jnp.int32, raw.shape, 1)
    square_total = jnp.sum(jnp.where(diagonal, raw, 0.0))
    norm = jnp.sqrt(jnp.full((1, 1), square_total, jnp.float32)) + EPSILON
    inverse = 1.0 / norm
    first = (raw * inverse) * inverse
    first_halves = halves(first)
    second = dot_halves(first_halves, first_halves)
    inner = QUINTIC_SECOND * first + QUINTIC_THIRD * second + jnp.where(diagonal, QUINTIC_FIRST, 0.0)
    inner_halves = halves(inner)
    next_gram = dot_halves(inner_halves, halves(dot_halves(inner_halves, first_halves)))
    next_halves = halves(next_gram)
    outer = (
        QUINTIC_SECOND * next_gram
        + QUINTIC_THIRD * dot_halves(next_halves, next_halves)
        + jnp.where(diagonal, QUINTIC_FIRST, 0.0)
    )
    total = dot_halves(halves(outer), inner_halves) * (inverse * OUT_SCALE)
    update = dot_halves(halves(total), halves(iterate[...]))
    result[...] = update
    padded[:INNER, :] = update
    position = lax.broadcasted_iota(jnp.int32, (slots, columns), 0)
    for place, block in enumerate(blocks):
        rows, shift = aligned(starts[place], slots)
        back = jnp.where(shift == 0, 0, slots + SUBLANES - shift)
        moved = pltpu.roll(padded[rows, :], back, 0)[:slots]
        block[...] = jnp.where(position < counts[place], moved, 0.0)


def in_vmem(count):
    return [pl.BlockSpec(memory_space=pltpu.VMEM)] * count


def in_smem(count):
    return [pl.BlockSpec(memory_space=pltpu.SMEM)] * count


def assemble_and_gram(starts, blocks):
    slots, columns = blocks[0].shape
    flops = 2 * 3 * INNER * 2 * PANEL * columns
    return pl.pallas_call(
        gram_kernel,
        out_shape=[
            jax.ShapeDtypeStruct((INNER, columns), jnp.float32),
            jax.ShapeDtypeStruct((INNER, 2 * PANEL), jnp.float32),
        ],
        in_specs=in_smem(1) + in_vmem(len(blocks)),
        out_specs=in_vmem(2),
        scratch_shapes=[pltpu.VMEM((INNER + slots + SUBLANES, columns), jnp.float32)],
        compiler_params=pltpu.CompilerParams(vmem_limit_bytes=VMEM_LIMIT),
        cost_estimate=pl.CostEstimate(flops=flops, bytes_accessed=8 * INNER * columns, transcendentals=0),
        name="assemble_and_gram",
    )(starts, *blocks)


def apply_update(starts, counts, packed, iterate, slots):
    columns = iterate.shape[1]
    ranks = starts.shape[0]
    flops = 2 * 3 * INNER * INNER * (5 * INNER + columns)
    return pl.pallas_call(
        update_kernel,
        out_shape=[jax.ShapeDtypeStruct((INNER, columns), jnp.float32)]
        + [jax.ShapeDtypeStruct((slots, columns), jnp.float32)] * ranks,
        in_specs=in_smem(2) + in_vmem(2),
        out_specs=in_vmem(1 + ranks),
        scratch_shapes=[
            pltpu.VMEM((INNER, INNER), jnp.float32),
            pltpu.VMEM((INNER + slots + SUBLANES, columns), jnp.float32),
        ],
        compiler_params=pltpu.CompilerParams(vmem_limit_bytes=VMEM_LIMIT),
        cost_estimate=pl.CostEstimate(flops=flops, bytes_accessed=16 * INNER * columns, transcendentals=0),
        name="apply_update",
    )(starts, counts, packed, iterate)


def group_stages(size):
    stages, shift = [], 0
    while (1 << shift) < size:
        wide = 1 if shift == 0 or (2 << shift) >= size else 2
        stages.append((shift, 1 << wide))
        shift += wide
    return stages


def sum_over(block, axis):
    size = lax.axis_size(axis)
    if size & (size - 1) or block.shape[0] % size:
        return lax.psum(block, axis)
    index = lax.axis_index(axis)

    def exchange(piece, step):
        return lax.ppermute(piece, axis, [(i, i ^ step) for i in range(size)])

    stages = group_stages(size)
    for shift, group in stages:
        digit = (index >> shift) & (group - 1)
        part = block.shape[0] // group
        pieces = [
            lax.dynamic_slice_in_dim(block, (digit ^ step) * part, part, 0) for step in range(group)
        ]
        arrived = [exchange(pieces[step], step << shift) for step in range(1, group)]
        block = functools.reduce(jnp.add, arrived, pieces[0])
    for shift, group in reversed(stages):
        digit = (index >> shift) & (group - 1)
        part = block.shape[0]
        pieces = [block] + [exchange(block, step << shift) for step in range(1, group)]
        block = jnp.zeros((part * group, block.shape[1]), block.dtype)
        for step, piece in enumerate(pieces):
            block = lax.dynamic_update_slice_in_dim(block, piece, (digit ^ step) * part, 0)
    return block


def on_device(momentum, gradient, live_ranks, owner_group, row_counts, row_offsets):
    ranks = lax.axis_size("fsdp")
    my_rank = lax.axis_index("fsdp")
    matrices, slots, columns = momentum.shape
    matrix_ids = jnp.arange(matrices, dtype=jnp.int32)
    rank_ids = jnp.arange(ranks, dtype=jnp.int32)
    position = jnp.arange(slots, dtype=jnp.int32)
    owned_by = jnp.sum(
        matrix_ids[None, :] * (owner_group[None, :] == rank_ids[:, None]).astype(jnp.int32), axis=1
    )
    live_counts = row_counts * live_ranks[None, :]
    own_counts = lax.dynamic_index_in_dim(live_counts, my_rank, 1, keepdims=False)
    owned_matrix = owned_by[my_rank]

    def shifted(step):
        return lax.rem(my_rank + step + ranks, ranks)

    def passes(step):
        return [(i, (i + step) % ranks) for i in range(ranks)]

    def blended(matrix):
        old_state = lax.dynamic_index_in_dim(momentum, matrix, 0, keepdims=False)
        grad_now = lax.dynamic_index_in_dim(gradient, matrix, 0, keepdims=False)
        fresh = MOMENTUM_RATE * old_state + grad_now
        keep = (position < own_counts[matrix])[:, None]
        return jnp.where(keep, grad_now + MOMENTUM_RATE * fresh, 0.0)

    steps = sorted(range(1, ranks), key=lambda step: -min(step, ranks - step))
    blocks = {step: lax.ppermute(blended(owned_by[shifted(step)]), "fsdp", passes(step)) for step in steps}
    blocks[0] = blended(owned_matrix)
    keep_home = (position[None, :] < own_counts[:, None])[:, :, None]
    new_momentum = jnp.where(keep_home, MOMENTUM_RATE * momentum + gradient, 0.0)

    offsets_here = lax.dynamic_index_in_dim(row_offsets, owned_matrix, 0, keepdims=False)
    counts_here = lax.dynamic_index_in_dim(live_counts, owned_matrix, 0, keepdims=False)
    came_from = lax.rem(my_rank - rank_ids + ranks, ranks)
    goes_to = lax.rem(my_rank + rank_ids, ranks)
    iterate, gram_part = assemble_and_gram(offsets_here[came_from], [blocks[step] for step in range(ranks)])
    packed = sum_over(gram_part, "tensor")
    result, *home = apply_update(offsets_here[goes_to], counts_here[goes_to], packed, iterate, slots)

    update_shards = jnp.zeros_like(momentum)
    update_shards = lax.dynamic_update_index_in_dim(update_shards, home[0], owned_matrix, 0)
    returned = {step: lax.ppermute(home[step], "fsdp", passes(step)) for step in steps}
    for step in reversed(steps):
        update_shards = lax.dynamic_update_index_in_dim(
            update_shards, returned[step], owned_by[shifted(-step)], 0
        )
    return (new_momentum, update_shards, result[None])


def solution(mesh):
    placed = (P(None, "fsdp", "tensor"), P(None, "fsdp", "tensor"), P(), P(), P(), P())
    return jax.shard_map(
        on_device,
        mesh=mesh,
        in_specs=placed,
        out_specs=(P(None, "fsdp", "tensor"), P(None, "fsdp", "tensor"), P("fsdp", None, "tensor")),
        check_vma=False,
    )
```

```python
import functools
import math

import jax
import jax.numpy as jnp
from jax import lax
from jax.experimental import pallas as pl
from jax.experimental.pallas import tpu as pltpu
from jax.sharding import PartitionSpec as P

WIDTH = 7168
INNER = 576
PANELS = 3
PANEL = INNER // PANELS
TILE = 256
SUBLANES = 8

MOMENTUM_RATE = 0.95
QUINTIC_FIRST = 3.4445
QUINTIC_SECOND = -4.775
QUINTIC_THIRD = 2.0315
EPSILON = 1e-07
OUT_SCALE = 0.2 * math.sqrt(max(INNER, WIDTH))
VMEM_LIMIT = 48 * 1024 * 1024


def halves(value):
    high = value.astype(jnp.bfloat16)
    low = (value - high.astype(jnp.float32)).astype(jnp.bfloat16)
    return high, low


def dot(left, right, contract):
    return lax.dot_general(left, right, (contract, ((), ())), preferred_element_type=jnp.float32)


def dot_halves(left, right, contract=((1,), (0,))):
    (left_high, left_low), (right_high, right_low) = left, right
    return (
        dot(left_high, right_low, contract) + dot(left_low, right_high, contract)
    ) + dot(left_high, right_high, contract)


def aligned(start, slots):
    shift = start % SUBLANES
    return pl.ds(pl.multiple_of(start - shift, SUBLANES), slots + SUBLANES), shift


def matrix_of(owner_group, rank):
    found = jnp.int32(0)
    for matrix in range(owner_group.shape[0]):
        found = jnp.where(owner_group[matrix] == rank, matrix, found)
    return found


def blend_kernel(step, chunks, owner_group, live_ranks, row_counts, momentum, gradient, out, olds, grads, mixed, arrive, leave):
    ranks = live_ranks.shape[0]
    rank = lax.axis_index("fsdp")
    matrix = matrix_of(owner_group, lax.rem(rank + step, ranks))
    count = row_counts[matrix, rank] * live_ranks[rank]
    slots, columns = mixed.shape
    size = slots // chunks

    def part(chunk):
        return pl.ds(chunk * size, size)

    incoming = [
        [
            pltpu.make_async_copy(source.at[matrix, part(chunk)], held.at[part(chunk)], arrive.at[chunk, side])
            for side, (source, held) in enumerate(((momentum, olds), (gradient, grads)))
        ]
        for chunk in range(chunks)
    ]
    outgoing = [
        pltpu.make_async_copy(mixed.at[part(chunk)], out.at[part(chunk)], leave.at[chunk]) for chunk in range(chunks)
    ]
    for pair in incoming:
        for copy in pair:
            copy.start()
    for chunk in range(chunks):
        for copy in incoming[chunk]:
            copy.wait()
        rows = slice(chunk * size, (chunk + 1) * size)
        grad_now = grads[rows, :]
        fresh = MOMENTUM_RATE * olds[rows, :] + grad_now
        position = lax.broadcasted_iota(jnp.int32, (size, columns), 0) + chunk * size
        mixed[rows, :] = jnp.where(position < count, grad_now + MOMENTUM_RATE * fresh, 0.0)
        outgoing[chunk].start()
    for copy in outgoing:
        copy.wait()


def gram_kernel(owner_group, row_offsets, *refs):
    *blocks, high_out, low_out, gram, padded = refs
    slots, columns = blocks[0].shape
    ranks = len(blocks)
    rank = lax.axis_index("fsdp")
    matrix = matrix_of(owner_group, rank)
    padded[...] = jnp.zeros_like(padded)
    tail = jnp.zeros((SUBLANES, columns), jnp.float32)
    for step, block in enumerate(blocks):
        source = lax.rem(rank + ranks - step, ranks)
        rows, shift = aligned(row_offsets[matrix, source], slots)
        moved = pltpu.roll(jnp.concatenate([block[...], tail], axis=0), shift, 0)
        padded[rows, :] = padded[rows, :] + moved
    high, low = halves(padded[:INNER, :])
    high_out[...] = high
    low_out[...] = low
    for panel in range(PANELS):
        here = slice(panel * PANEL, (panel + 1) * PANEL)
        after = (panel + 1) % PANELS
        there = slice(after * PANEL, (after + 1) * PANEL)
        gram[here, :PANEL] = dot_halves((high[here], low[here]), (high[here], low[here]), ((1,), (1,)))
        gram[here, PANEL:] = dot_halves((high[here], low[here]), (high[there], low[there]), ((1,), (1,)))


def symmetric_product(left, right, out):
    for begin in range(0, INNER, TILE):
        end = min(begin + TILE, INNER)
        part = dot_halves(
            tuple(half[begin:] for half in left), tuple(half[:, begin:end] for half in right)
        )
        out[begin:, begin:end] = part
        if end < INNER:
            out[begin:end, end:] = part[end - begin :].T
    return out[...]


def update_kernel(owner_group, live_ranks, row_counts, row_offsets, packed, high, low, result, shards, *refs):
    *sends, gram, padded, held, leave = refs
    ranks, slots, columns = held.shape
    rank = lax.axis_index("fsdp")
    matrix = matrix_of(owner_group, rank)
    for panel in range(PANELS):
        here = slice(panel * PANEL, (panel + 1) * PANEL)
        after = (panel + 1) % PANELS
        there = slice(after * PANEL, (after + 1) * PANEL)
        gram[here, here] = packed[here, :PANEL]
        side = packed[here, PANEL:]
        gram[here, there] = side
        gram[there, here] = side.T
    raw = gram[...]
    diagonal = lax.broadcasted_iota(jnp.int32, raw.shape, 0) == lax.broadcasted_iota(jnp.int32, raw.shape, 1)
    square_total = jnp.sum(jnp.where(diagonal, raw, 0.0))
    norm = jnp.sqrt(jnp.full((1, 1), square_total, jnp.float32)) + EPSILON
    inverse = 1.0 / norm
    first = (raw * inverse) * inverse
    first_halves = halves(first)
    second = symmetric_product(first_halves, first_halves, gram)
    inner = QUINTIC_SECOND * first + QUINTIC_THIRD * second + jnp.where(diagonal, QUINTIC_FIRST, 0.0)
    inner_halves = halves(inner)
    third_halves = halves(symmetric_product(inner_halves, first_halves, gram))
    next_gram = symmetric_product(inner_halves, third_halves, gram)
    next_halves = halves(next_gram)
    outer = (
        QUINTIC_SECOND * next_gram
        + QUINTIC_THIRD * symmetric_product(next_halves, next_halves, gram)
        + jnp.where(diagonal, QUINTIC_FIRST, 0.0)
    )
    total = symmetric_product(halves(outer), inner_halves, gram) * (inverse * OUT_SCALE)
    padded[:INNER, :] = dot_halves(halves(total), (high[...], low[...]))
    copies = [pltpu.make_async_copy(padded.at[pl.ds(0, INNER)], result, leave.at[ranks])]
    copies[0].start()
    position = lax.broadcasted_iota(jnp.int32, (slots, columns), 0)
    for step in [*range(1, ranks), 0]:
        target = lax.rem(rank + step, ranks)
        count = row_counts[matrix, target] * live_ranks[target]
        rows, shift = aligned(row_offsets[matrix, target], slots)
        back = jnp.where(shift == 0, 0, slots + SUBLANES - shift)
        moved = pltpu.roll(padded[rows, :], back, 0)[:slots]
        held[step] = jnp.where(position < count, moved, 0.0)
        place = sends[step - 1] if step else shards.at[matrix]
        copies.append(pltpu.make_async_copy(held.at[step], place, leave.at[step]))
        copies[-1].start()
    for copy in copies:
        copy.wait()


def in_vmem(count):
    return [pl.BlockSpec(memory_space=pltpu.VMEM)] * count


def in_smem(count):
    return [pl.BlockSpec(memory_space=pltpu.SMEM)] * count


def anywhere(count):
    return [pl.BlockSpec(memory_space=pl.ANY)] * count


PARAMS = pltpu.CompilerParams(vmem_limit_bytes=VMEM_LIMIT)


def blend(step, owner_group, live_ranks, row_counts, momentum, gradient):
    _, slots, columns = momentum.shape
    chunks = 4 if slots % (4 * SUBLANES) == 0 else 1
    block = (slots, columns)
    return pl.pallas_call(
        functools.partial(blend_kernel, step, chunks),
        out_shape=jax.ShapeDtypeStruct(block, jnp.float32),
        in_specs=in_smem(3) + anywhere(2),
        out_specs=pl.BlockSpec(memory_space=pl.ANY),
        scratch_shapes=[pltpu.VMEM(block, jnp.float32)] * 3
        + [pltpu.SemaphoreType.DMA((chunks, 2)), pltpu.SemaphoreType.DMA((chunks,))],
        compiler_params=PARAMS,
        cost_estimate=pl.CostEstimate(flops=4 * slots * columns, bytes_accessed=12 * slots * columns, transcendentals=0),
        name="blend",
    )(owner_group, live_ranks, row_counts, momentum, gradient)


def assemble_and_gram(owner_group, row_offsets, blocks):
    slots, columns = blocks[0].shape
    flops = 2 * 3 * INNER * 2 * PANEL * columns
    return pl.pallas_call(
        gram_kernel,
        out_shape=[jax.ShapeDtypeStruct((INNER, columns), jnp.bfloat16)] * 2
        + [jax.ShapeDtypeStruct((INNER, 2 * PANEL), jnp.float32)],
        in_specs=in_smem(2) + in_vmem(len(blocks)),
        out_specs=in_vmem(3),
        scratch_shapes=[pltpu.VMEM((INNER + slots + SUBLANES, columns), jnp.float32)],
        compiler_params=PARAMS,
        cost_estimate=pl.CostEstimate(flops=flops, bytes_accessed=16 * INNER * columns, transcendentals=0),
        name="assemble_and_gram",
    )(owner_group, row_offsets, *blocks)


def apply_update(owner_group, live_ranks, row_counts, row_offsets, packed, high, low, shape):
    ranks, (matrices, slots, columns) = live_ranks.shape[0], shape
    flops = 2 * 3 * INNER * INNER * (5 * INNER + columns)
    return pl.pallas_call(
        update_kernel,
        out_shape=[jax.ShapeDtypeStruct((INNER, columns), jnp.float32), jax.ShapeDtypeStruct(shape, jnp.float32)]
        + [jax.ShapeDtypeStruct((slots, columns), jnp.float32)] * (ranks - 1),
        in_specs=in_smem(4) + in_vmem(3),
        out_specs=anywhere(1 + ranks),
        scratch_shapes=[
            pltpu.VMEM((INNER, INNER), jnp.float32),
            pltpu.VMEM((INNER + slots + SUBLANES, columns), jnp.float32),
            pltpu.VMEM((ranks, slots, columns), jnp.float32),
            pltpu.SemaphoreType.DMA((ranks + 1,)),
        ],
        compiler_params=PARAMS,
        cost_estimate=pl.CostEstimate(flops=flops, bytes_accessed=16 * INNER * columns, transcendentals=0),
        name="apply_update",
    )(owner_group, live_ranks, row_counts, row_offsets, packed, high, low)


def group_stages(size):
    stages, shift = [], 0
    while (1 << shift) < size:
        wide = 1 if shift == 0 or (2 << shift) >= size else 2
        stages.append((shift, 1 << wide))
        shift += wide
    return stages


def sum_over(block, axis):
    size = lax.axis_size(axis)
    if size & (size - 1) or block.shape[0] % size:
        return lax.psum(block, axis)
    index = lax.axis_index(axis)

    def exchange(piece, step):
        return lax.ppermute(piece, axis, [(i, i ^ step) for i in range(size)])

    stages = group_stages(size)
    for shift, group in stages:
        digit = (index >> shift) & (group - 1)
        part = block.shape[0] // group
        pieces = [
            lax.dynamic_slice_in_dim(block, (digit ^ step) * part, part, 0) for step in range(group)
        ]
        arrived = [exchange(pieces[step], step << shift) for step in range(1, group)]
        block = functools.reduce(jnp.add, arrived, pieces[0])
    for shift, group in reversed(stages):
        digit = (index >> shift) & (group - 1)
        part = block.shape[0]
        pieces = [block] + [exchange(block, step << shift) for step in range(1, group)]
        block = jnp.zeros((part * group, block.shape[1]), block.dtype)
        for step, piece in enumerate(pieces):
            block = lax.dynamic_update_slice_in_dim(block, piece, (digit ^ step) * part, 0)
    return block


def on_device(momentum, gradient, live_ranks, owner_group, row_counts, row_offsets):
    ranks = lax.axis_size("fsdp")
    my_rank = lax.axis_index("fsdp")
    slots = momentum.shape[1]
    rank_ids = jnp.arange(ranks, dtype=jnp.int32)

    def passes(step):
        return [(i, (i + step) % ranks) for i in range(ranks)]

    steps = sorted(range(1, ranks), key=lambda step: -min(step, ranks - step))
    blocks = {}
    for step in [*steps, 0]:
        block = blend(step, owner_group, live_ranks, row_counts, momentum, gradient)
        blocks[step] = lax.ppermute(block, "fsdp", passes(step)) if step else block
    own = (rank_ids == my_rank).astype(jnp.int32)
    own_counts = jnp.sum(row_counts * (live_ranks * own)[None, :], axis=1)
    keep_home = (jnp.arange(slots, dtype=jnp.int32)[None, :] < own_counts[:, None])[:, :, None]
    new_momentum = jnp.where(keep_home, MOMENTUM_RATE * momentum + gradient, 0.0)

    high, low, gram_part = assemble_and_gram(owner_group, row_offsets, [blocks[step] for step in range(ranks)])
    packed = sum_over(gram_part, "tensor")
    result, update_shards, *home = apply_update(
        owner_group, live_ranks, row_counts, row_offsets, packed, high, low, momentum.shape
    )
    returned = {step: lax.ppermute(home[step - 1], "fsdp", passes(step)) for step in steps}
    for step in reversed(steps):
        source = lax.rem(my_rank + ranks - step, ranks)
        owned = jnp.sum(jnp.where(owner_group == source, jnp.arange(owner_group.shape[0], dtype=jnp.int32), 0))
        update_shards = lax.dynamic_update_index_in_dim(update_shards, returned[step], owned, 0)
    return (new_momentum, update_shards, result[None])


def solution(mesh):
    placed = (P(None, "fsdp", "tensor"), P(None, "fsdp", "tensor"), P(), P(), P(), P())
    return jax.shard_map(
        on_device,
        mesh=mesh,
        in_specs=placed,
        out_specs=(P(None, "fsdp", "tensor"), P(None, "fsdp", "tensor"), P("fsdp", None, "tensor")),
        check_vma=False,
    )
```

```python
import functools
import math

import jax
import jax.numpy as jnp
from jax import lax
from jax.experimental import pallas as pl
from jax.experimental.pallas import tpu as pltpu
from jax.sharding import PartitionSpec as P

WIDTH = 7168
INNER = 576
PANEL = INNER // 3
TILE = 256
SUBLANES = 8

MOMENTUM_RATE = 0.95
QUINTIC_FIRST = 3.4445
QUINTIC_SECOND = -4.775
QUINTIC_THIRD = 2.0315
EPSILON = 1e-07
OUT_SCALE = 0.2 * math.sqrt(max(INNER, WIDTH))
FULL = pltpu.CompilerParams(vmem_limit_bytes=60 * 1024 * 1024)
PARAMS = pltpu.CompilerParams(vmem_limit_bytes=48 * 1024 * 1024)
HBM = pl.BlockSpec(memory_space=pltpu.HBM)
ANY = pl.BlockSpec(memory_space=pl.ANY)
VMEM = pl.BlockSpec(memory_space=pltpu.VMEM)


def halves(value):
    high = value.astype(jnp.bfloat16)
    low = (value - high.astype(jnp.float32)).astype(jnp.bfloat16)
    return high, low


def dot(left, right, contract):
    return lax.dot_general(left, right, (contract, ((), ())), preferred_element_type=jnp.float32)


def dot_halves(left, right, contract=((1,), (0,))):
    (left_high, left_low), (right_high, right_low) = left, right
    return (
        dot(left_high, right_low, contract) + dot(left_low, right_high, contract)
    ) + dot(left_high, right_high, contract)


def in_phase(rank, ranks, inner):
    low = ranks // 4
    return ((rank >= low) & (rank < ranks - low)) == inner


def table_scratch(matrices, ranks):
    return [
        pltpu.SMEM((matrices,), jnp.int32),
        pltpu.SMEM((ranks,), jnp.int32),
        pltpu.SMEM((matrices, ranks), jnp.int32),
        pltpu.SMEM((matrices, ranks), jnp.int32),
        pltpu.SemaphoreType.DMA((4,)),
    ]


def fetch_tables(tables, held):
    *places, arrive = held
    copies = [
        pltpu.make_async_copy(table, place, arrive.at[index])
        for index, (table, place) in enumerate(zip(tables, places))
    ]
    for copy in copies:
        copy.start()
    for copy in copies:
        copy.wait()
    return places


def matrix_of(owner_group, rank):
    found = jnp.int32(0)
    for matrix in range(owner_group.shape[0]):
        found = jnp.where(owner_group[matrix] == rank, matrix, found)
    return found


def send_step(place, ranks, inner):
    return (place + ranks - 3) % (ranks - 1) + 1 if inner else place


def blend_kernel(places, chunks, *refs):
    tables, (momentum, gradient) = refs[:4], refs[4:6]
    *outs, token, olds, grads, arrive = refs[-len(places) - 9 : -5]
    owner_group, live_ranks, row_counts, _ = fetch_tables(tables, refs[-5:])
    rank, ranks = lax.axis_index("fsdp"), live_ranks.shape[0]
    slots, columns = outs[0].shape
    size = slots // chunks
    incoming, counts = [], []
    for index, place in enumerate(places):
        early, late = (send_step(place, ranks, inner) for inner in (True, False))
        matrix = matrix_of(owner_group, rank ^ jnp.where(in_phase(rank, ranks, True), early, late))
        counts.append(row_counts[matrix, rank] * live_ranks[rank])
        for chunk in range(chunks):
            part = pl.ds(chunk * size, size)
            for side, (source, kept) in enumerate(((momentum, olds), (gradient, grads))):
                flag = arrive.at[index * chunks + chunk, side]
                incoming.append(pltpu.make_async_copy(source.at[matrix, part], kept.at[index, part], flag))
                incoming[-1].start()
    token[...] = jnp.zeros_like(token)
    for index, out in enumerate(outs):
        for chunk in range(chunks):
            first = 2 * (index * chunks + chunk)
            for copy in incoming[first : first + 2]:
                copy.wait()
            rows = slice(chunk * size, (chunk + 1) * size)
            grad_now = grads[index, rows, :]
            fresh = MOMENTUM_RATE * olds[index, rows, :] + grad_now
            position = lax.broadcasted_iota(jnp.int32, (size, columns), 0) + chunk * size
            out[rows, :] = jnp.where(position < counts[index], grad_now + MOMENTUM_RATE * fresh, 0.0)


def home_kernel(owner_group, live_ranks, row_counts, momentum, gradient, fresh_out, own):
    rank, matrix = lax.axis_index("fsdp"), pl.program_id(0)
    grad_now = gradient[...]
    position = lax.broadcasted_iota(jnp.int32, grad_now.shape, 0)
    keep = position < row_counts[matrix, rank] * live_ranks[rank]
    fresh = jnp.where(keep, MOMENTUM_RATE * momentum[...] + grad_now, 0.0)
    fresh_out[...] = fresh

    @pl.when(owner_group[matrix] == rank)
    def _():
        own[...] = jnp.where(keep, grad_now + MOMENTUM_RATE * fresh, 0.0)


def gram_kernel(ranks, *refs):
    tables, blocks, refs = refs[:4], refs[4 : 4 + ranks], refs[4 + ranks :]
    high_out, low_out, gram, landed, padded, arrive = refs[:6]
    held = refs[6:]
    rank = lax.axis_index("fsdp")
    slots, columns = blocks[0].shape
    copies = []
    for step in range(ranks):
        copies.append(pltpu.make_async_copy(blocks[step], landed.at[step], arrive.at[step]))
        copies[-1].start()
    owner_group, _, _, row_offsets = fetch_tables(tables, held)
    matrix = matrix_of(owner_group, rank)
    padded[...] = jnp.zeros_like(padded)
    sublane = lax.broadcasted_iota(jnp.int32, (SUBLANES, columns), 0)
    for step in range(ranks):
        start = row_offsets[matrix, rank ^ step]
        shift = start % SUBLANES
        base = start - shift
        copies[step].wait()

        def tile(index, before, base=base, shift=shift, step=step):
            moved = pltpu.roll(landed[step, pl.ds(pl.multiple_of(index * SUBLANES, SUBLANES), SUBLANES), :], shift, 0)
            rows = pl.ds(pl.multiple_of(base + index * SUBLANES, SUBLANES), SUBLANES)
            padded[rows, :] = padded[rows, :] + jnp.where(sublane < shift, before, moved)
            return moved

        after = lax.fori_loop(0, slots // SUBLANES, tile, jnp.zeros((SUBLANES, columns), jnp.float32))
        rows = pl.ds(pl.multiple_of(base + slots, SUBLANES), SUBLANES)
        padded[rows, :] = padded[rows, :] + jnp.where(sublane < shift, after, 0.0)
    high, low = halves(padded[:INNER, :])
    high_out[...] = high
    low_out[...] = low
    for panel in range(3):
        here = slice(panel * PANEL, (panel + 1) * PANEL)
        part = dot_halves((high[panel * PANEL :], low[panel * PANEL :]), (high[here], low[here]), ((1,), (1,)))
        if panel == 0:
            gram[:, :PANEL] = part
        elif panel == 1:
            gram[: 2 * PANEL, PANEL:] = part
        else:
            gram[2 * PANEL :, PANEL:] = part


def symmetric_product(left, right, out):
    for begin in range(0, INNER, TILE):
        end = min(begin + TILE, INNER)
        part = dot_halves(tuple(half[begin:] for half in left), tuple(half[:, begin:end] for half in right))
        out[begin:, begin:end] = part
        if end < INNER:
            out[begin:end, end:] = part[end - begin :].T
    return out[...]


def update_kernel(ranks, *refs):
    tables, (packed, high, low, result), refs = refs[:4], refs[4:8], refs[8:]
    homes, refs = refs[:ranks], refs[ranks:]
    gram, padded, staged, leave = refs[:4]
    held = refs[4:]
    _, slots, columns = staged.shape
    rank = lax.axis_index("fsdp")
    owner_group, live_ranks, row_counts, row_offsets = fetch_tables(tables, held)
    matrix = matrix_of(owner_group, rank)
    gram[:, :PANEL] = packed[:, :PANEL]
    gram[PANEL:, PANEL : 2 * PANEL] = packed[: 2 * PANEL, PANEL:]
    gram[2 * PANEL :, 2 * PANEL :] = packed[2 * PANEL :, PANEL:]
    gram[:PANEL, PANEL:] = packed[PANEL:, :PANEL].T
    gram[PANEL : 2 * PANEL, 2 * PANEL :] = packed[PANEL : 2 * PANEL, PANEL:].T
    raw = gram[...]
    diagonal = lax.broadcasted_iota(jnp.int32, raw.shape, 0) == lax.broadcasted_iota(jnp.int32, raw.shape, 1)
    square_total = jnp.sum(jnp.where(diagonal, raw, 0.0))
    norm = jnp.sqrt(jnp.full((1, 1), square_total, jnp.float32)) + EPSILON
    inverse = 1.0 / norm
    first = (raw * inverse) * inverse
    first_halves = halves(first)
    second = symmetric_product(first_halves, first_halves, gram)
    base = QUINTIC_SECOND * first + QUINTIC_THIRD * second + jnp.where(diagonal, QUINTIC_FIRST, 0.0)
    base_halves = halves(base)
    third_halves = halves(symmetric_product(base_halves, first_halves, gram))
    next_gram = symmetric_product(base_halves, third_halves, gram)
    next_halves = halves(next_gram)
    outer = (
        QUINTIC_SECOND * next_gram
        + QUINTIC_THIRD * symmetric_product(next_halves, next_halves, gram)
        + jnp.where(diagonal, QUINTIC_FIRST, 0.0)
    )
    total = symmetric_product(halves(outer), base_halves, gram) * (inverse * OUT_SCALE)
    padded[:INNER, :] = dot_halves(halves(total), (high[...], low[...]))
    copies = [pltpu.make_async_copy(padded.at[pl.ds(0, INNER)], result, leave.at[ranks])]
    copies[0].start()
    sublane = lax.broadcasted_iota(jnp.int32, (SUBLANES, columns), 0)
    for step in [*range(ranks - 1, 0, -1), 0]:
        target = rank ^ step
        count = row_counts[matrix, target] * live_ranks[target]
        start = row_offsets[matrix, target]
        shift = start % SUBLANES
        first_row = start - shift
        back = jnp.where(shift == 0, 0, SUBLANES - shift)

        def window(index, first_row=first_row, back=back):
            rows = pl.ds(pl.multiple_of(first_row + index * SUBLANES, SUBLANES), SUBLANES)
            return pltpu.roll(padded[rows, :], back, 0)

        def tile(index, here, step=step, count=count, shift=shift, window=window):
            after = window(index + 1)
            moved = jnp.where(sublane < SUBLANES - shift, here, after)
            rows = pl.ds(pl.multiple_of(index * SUBLANES, SUBLANES), SUBLANES)
            staged[step, rows, :] = jnp.where(sublane < count - index * SUBLANES, moved, 0.0)
            return after

        lax.fori_loop(0, slots // SUBLANES, tile, window(0))
        copies.append(pltpu.make_async_copy(staged.at[step], homes[step], leave.at[step]))
        copies[-1].start()
    for copy in copies:
        copy.wait()


def each_copy(copies, action):
    for condition, source, place, flag in copies:

        @pl.when(condition)
        def _(source=source, place=place, flag=flag):
            getattr(pltpu.make_async_copy(source, place, flag), action)()


def first_place_kernel(ranks, table, inner_result, outer_result, inner_own, outer_own, result, shards, *refs):
    owner_group, arrive, leave = refs
    rank = lax.axis_index("fsdp")
    fetch = pltpu.make_async_copy(table, owner_group, arrive)
    fetch.start()
    fetch.wait()
    matrix = matrix_of(owner_group, rank)
    copies = []
    for inner, update, own in ((True, inner_result, inner_own), (False, outer_result, outer_own)):
        mine = in_phase(rank, ranks, inner)
        copies += [(mine, update, result, leave.at[0]), (mine, own, shards.at[matrix], leave.at[1])]
    each_copy(copies, "start")
    each_copy(copies, "wait")


def place_kernel(inner, ranks, steps, *refs):
    table, blocks, shards = refs[0], refs[1 : 1 + len(steps)], refs[2 + len(steps)]
    owner_group, arrive, leave = refs[3 + len(steps) :]
    rank = lax.axis_index("fsdp")
    fetch = pltpu.make_async_copy(table, owner_group, arrive)
    fetch.start()
    fetch.wait()
    copies = [
        (
            in_phase(rank ^ step, ranks, inner),
            blocks[order],
            shards.at[matrix_of(owner_group, rank ^ step)],
            leave.at[order],
        )
        for order, step in enumerate(steps)
    ]
    each_copy(copies, "start")
    each_copy(copies, "wait")


def idle_kernel(*refs):
    pass


def blend(places, tables, momentum, gradient, before):
    _, slots, columns = momentum.shape
    chunks = 4 if slots % (4 * SUBLANES) == 0 else 1
    held = (len(places), slots, columns)
    return pl.pallas_call(
        functools.partial(blend_kernel, places, chunks),
        out_shape=[jax.ShapeDtypeStruct((slots, columns), jnp.float32)] * len(places)
        + [jax.ShapeDtypeStruct((SUBLANES, 128), jnp.float32)],
        in_specs=[HBM] * 6 + [ANY] * len(before),
        out_specs=[VMEM] * (len(places) + 1),
        scratch_shapes=[pltpu.VMEM(held, jnp.float32)] * 2
        + [pltpu.SemaphoreType.DMA((len(places) * chunks, 2))]
        + table_scratch(*tables[2].shape),
        compiler_params=FULL,
        cost_estimate=pl.CostEstimate(flops=0, bytes_accessed=0, transcendentals=0),
        name="blend",
    )(*tables, momentum, gradient, *before)


def home(tables, momentum, gradient, before):
    matrices, slots, columns = momentum.shape
    block = pl.BlockSpec((None, slots, columns), lambda matrix: (matrix, 0, 0))

    def body(*refs):
        home_kernel(*refs[:5], *refs[-2:])

    return pl.pallas_call(
        body,
        grid=(matrices,),
        out_shape=[
            jax.ShapeDtypeStruct(momentum.shape, jnp.float32),
            jax.ShapeDtypeStruct((slots, columns), jnp.float32),
        ],
        in_specs=[pl.BlockSpec(memory_space=pltpu.SMEM)] * 3 + [block] * 2 + [ANY],
        out_specs=[block, pl.BlockSpec((slots, columns), lambda matrix: (0, 0))],
        compiler_params=FULL,
        cost_estimate=pl.CostEstimate(flops=0, bytes_accessed=0, transcendentals=0),
        name="home",
    )(*tables[:3], momentum, gradient, before)


def assemble_and_gram(tables, blocks):
    slots, columns = blocks[0].shape
    ranks = len(blocks)
    flops = 2 * 3 * INNER * 2 * PANEL * columns
    return pl.pallas_call(
        functools.partial(gram_kernel, ranks),
        out_shape=[jax.ShapeDtypeStruct((INNER, columns), jnp.bfloat16)] * 2
        + [jax.ShapeDtypeStruct((INNER, 2 * PANEL), jnp.float32)],
        in_specs=[HBM] * 4 + [ANY] * ranks,
        out_specs=[VMEM] * 3,
        scratch_shapes=[
            pltpu.VMEM((ranks, slots, columns), jnp.float32),
            pltpu.VMEM((INNER + slots + SUBLANES, columns), jnp.float32),
            pltpu.SemaphoreType.DMA((ranks,)),
        ]
        + table_scratch(*tables[2].shape),
        compiler_params=PARAMS,
        cost_estimate=pl.CostEstimate(flops=flops, bytes_accessed=16 * INNER * columns, transcendentals=0),
        name="assemble_and_gram",
    )(*tables, *blocks)


def update_shapes(ranks, slots, columns):
    return [jax.ShapeDtypeStruct((INNER, columns), jnp.float32)] + [
        jax.ShapeDtypeStruct((slots, columns), jnp.float32)
    ] * ranks


def apply_update(tables, packed, high, low, slots):
    ranks, columns = tables[1].shape[0], high.shape[1]
    flops = 2 * 3 * INNER * INNER * (5 * INNER + columns)
    return pl.pallas_call(
        functools.partial(update_kernel, ranks),
        out_shape=update_shapes(ranks, slots, columns),
        in_specs=[HBM] * 4 + [VMEM] * 3,
        out_specs=[ANY] * (1 + ranks),
        scratch_shapes=[
            pltpu.VMEM((INNER, INNER), jnp.float32),
            pltpu.VMEM((INNER + slots + 2 * SUBLANES, columns), jnp.float32),
            pltpu.VMEM((ranks, slots, columns), jnp.float32),
            pltpu.SemaphoreType.DMA((ranks + 1,)),
        ]
        + table_scratch(*tables[2].shape),
        compiler_params=PARAMS,
        cost_estimate=pl.CostEstimate(flops=flops, bytes_accessed=16 * INNER * columns, transcendentals=0),
        name="apply_update",
    )(*tables, packed, high, low)


def nothing(ranks, slots, columns):
    return pl.pallas_call(
        idle_kernel,
        out_shape=update_shapes(ranks, slots, columns),
        out_specs=[ANY] * (1 + ranks),
        name="nothing",
    )()


def first_place(owner_group, results, owns, shape, ranks):
    return pl.pallas_call(
        functools.partial(first_place_kernel, ranks),
        out_shape=[
            jax.ShapeDtypeStruct(results[0].shape, jnp.float32),
            jax.ShapeDtypeStruct(shape, jnp.float32),
        ],
        in_specs=[HBM] + [ANY] * 4,
        out_specs=[HBM] * 2,
        scratch_shapes=[
            pltpu.SMEM(owner_group.shape, jnp.int32),
            pltpu.SemaphoreType.DMA(()),
            pltpu.SemaphoreType.DMA((2,)),
        ],
        compiler_params=PARAMS,
        cost_estimate=pl.CostEstimate(flops=0, bytes_accessed=8 * results[0].size, transcendentals=0),
        name="first_place",
    )(owner_group, *results, *owns)


def place_blocks(inner, owner_group, steps, blocks, shards, ranks):
    return pl.pallas_call(
        functools.partial(place_kernel, inner, ranks, steps),
        out_shape=jax.ShapeDtypeStruct(shards.shape, shards.dtype),
        in_specs=[HBM] + [ANY] * len(blocks) + [HBM],
        out_specs=HBM,
        scratch_shapes=[
            pltpu.SMEM(owner_group.shape, jnp.int32),
            pltpu.SemaphoreType.DMA(()),
            pltpu.SemaphoreType.DMA((len(steps),)),
        ],
        input_output_aliases={1 + len(blocks): 0},
        compiler_params=PARAMS,
        cost_estimate=pl.CostEstimate(flops=0, bytes_accessed=8 * blocks[0].size, transcendentals=0),
        name="place_blocks",
    )(owner_group, *blocks, shards)


def group_stages(size):
    stages, shift = [], 0
    while (1 << shift) < size:
        wide = 1 if shift == 0 or (2 << shift) >= size else 2
        stages.append((shift, 1 << wide))
        shift += wide
    return stages


def sum_over(block, axis):
    size = lax.axis_size(axis)
    if size & (size - 1) or block.shape[0] % size:
        return lax.psum(block, axis)
    index = lax.axis_index(axis)

    def exchange(piece, step):
        return lax.ppermute(piece, axis, [(i, i ^ step) for i in range(size)])

    stages = group_stages(size)
    for shift, group in stages:
        digit = (index >> shift) & (group - 1)
        part = block.shape[0] // group
        pieces = [lax.dynamic_slice_in_dim(block, (digit ^ step) * part, part, 0) for step in range(group)]
        arrived = [exchange(pieces[step], step << shift) for step in range(1, group)]
        block = functools.reduce(jnp.add, arrived, pieces[0])
    for shift, group in reversed(stages):
        digit = (index >> shift) & (group - 1)
        part = block.shape[0]
        pieces = [block] + [exchange(block, step << shift) for step in range(1, group)]
        block = jnp.zeros((part * group, block.shape[1]), block.dtype)
        for step, piece in enumerate(pieces):
            block = lax.dynamic_update_slice_in_dim(block, piece, (digit ^ step) * part, 0)
    return block


def on_device(momentum, gradient, live_ranks, owner_group, row_counts, row_offsets):
    ranks = lax.axis_size("fsdp")
    my_rank = lax.axis_index("fsdp")
    slots = momentum.shape[1]
    tables = (owner_group, live_ranks, row_counts, row_offsets)
    steps = list(range(1, ranks))

    def inside(rank, inner):
        return bool(in_phase(rank, ranks, inner))

    *blends, token = blend(steps[:-1], tables, momentum, gradient, [])
    last, token = blend(steps[-1:], tables, momentum, gradient, [token])
    blends.append(last)

    sent = {}
    for place in steps:
        for kind in (False, True, "cross"):
            pairs = []
            for i in range(ranks):
                target = i ^ send_step(place, ranks, inside(i, True))
                same = inside(i, True) == inside(target, True)
                if (kind == "cross" and not same) or (same and inside(i, True) == kind):
                    pairs.append((i, target))
            if pairs:
                sent[place, kind] = lax.ppermute(blends[place - 1], "fsdp", pairs)

    def received(step, inner):
        whole = None
        for source in (False, True):
            if any(inside(i, inner) and inside(i ^ step, source) for i in range(ranks)):
                place = next(place for place in steps if send_step(place, ranks, source) == step)
                part = sent[place, inner if source == inner else "cross"]
                pick = in_phase(my_rank ^ step, ranks, source)
                whole = part if whole is None else jnp.where(pick, part, whole)
        return whole

    def to_home(block, step, inner):
        return lax.ppermute(block, "fsdp", [(i, i ^ step) for i in range(ranks) if inside(i, inner)])

    new_momentum, own_block = home(tables, momentum, gradient, token)
    owner_blocks = {inner: [own_block] + [received(step, inner) for step in steps] for inner in (True, False)}

    def compute(blocks):
        high, low, gram_part = assemble_and_gram(tables, blocks)
        return apply_update(tables, sum_over(gram_part, "tensor"), high, low, slots)

    def skip(blocks):
        return nothing(ranks, *blocks[0].shape)

    results, owns, returned = [], [], {}
    for inner in (True, False):
        result, *homes = lax.cond(in_phase(my_rank, ranks, inner), compute, skip, owner_blocks[inner])
        results.append(result)
        owns.append(homes[0])
        returned[inner] = {step: to_home(homes[step], step, inner) for step in steps}
    result, shards = first_place(owner_group, results, owns, momentum.shape, ranks)
    shards = place_blocks(True, owner_group, steps, [returned[True][step] for step in steps], shards, ranks)
    for step in steps:
        shards = place_blocks(False, owner_group, [step], [returned[False][step]], shards, ranks)
    return (new_momentum, shards, result[None])


def solution(mesh):
    placed = (P(None, "fsdp", "tensor"), P(None, "fsdp", "tensor"), P(), P(), P(), P())
    return jax.shard_map(
        on_device,
        mesh=mesh,
        in_specs=placed,
        out_specs=(P(None, "fsdp", "tensor"), P(None, "fsdp", "tensor"), P("fsdp", None, "tensor")),
        check_vma=False,
    )
```

```python
import functools
import math

import jax
import jax.numpy as jnp
from jax import lax
from jax.experimental import pallas as pl
from jax.experimental.pallas import tpu as pltpu
from jax.sharding import PartitionSpec as P

WIDTH = 7168
INNER = 576
PANEL = INNER // 3
TILE = 256
SUBLANES = 8

MOMENTUM_RATE = 0.95
QUINTIC_FIRST = 3.4445
QUINTIC_SECOND = -4.775
QUINTIC_THIRD = 2.0315
EPSILON = 1e-07
OUT_SCALE = 0.2 * math.sqrt(max(INNER, WIDTH))
FULL = pltpu.CompilerParams(vmem_limit_bytes=60 * 1024 * 1024)
PARAMS = pltpu.CompilerParams(vmem_limit_bytes=48 * 1024 * 1024)
HBM = pl.BlockSpec(memory_space=pltpu.HBM)
ANY = pl.BlockSpec(memory_space=pl.ANY)
VMEM = pl.BlockSpec(memory_space=pltpu.VMEM)


def halves(value):
    high = value.astype(jnp.bfloat16)
    low = (value - high.astype(jnp.float32)).astype(jnp.bfloat16)
    return high, low


def dot(left, right, contract):
    return lax.dot_general(left, right, (contract, ((), ())), preferred_element_type=jnp.float32)


def dot_halves(left, right, contract=((1,), (0,))):
    (left_high, left_low), (right_high, right_low) = left, right
    return (
        dot(left_high, right_low, contract) + dot(left_low, right_high, contract)
    ) + dot(left_high, right_high, contract)


def in_phase(rank, ranks, inner):
    low = ranks // 4
    return ((rank >= low) & (rank < ranks - low)) == inner


def table_scratch(matrices, ranks):
    return [
        pltpu.SMEM((matrices,), jnp.int32),
        pltpu.SMEM((ranks,), jnp.int32),
        pltpu.SMEM((matrices, ranks), jnp.int32),
        pltpu.SMEM((matrices, ranks), jnp.int32),
        pltpu.SemaphoreType.DMA((4,)),
    ]


def fetch_tables(tables, held):
    *places, arrive = held
    copies = [
        pltpu.make_async_copy(table, place, arrive.at[index])
        for index, (table, place) in enumerate(zip(tables, places))
    ]
    for copy in copies:
        copy.start()
    for copy in copies:
        copy.wait()
    return places


def matrix_of(owner_group, rank):
    found = jnp.int32(0)
    for matrix in range(owner_group.shape[0]):
        found = jnp.where(owner_group[matrix] == rank, matrix, found)
    return found


def send_step(place, ranks, inner):
    return (place + ranks - 3) % (ranks - 1) + 1 if inner else place


def blend_kernel(places, chunks, *refs):
    tables, (momentum, gradient) = refs[:4], refs[4:6]
    *outs, token, olds, grads, arrive = refs[-len(places) - 9 : -5]
    owner_group, live_ranks, row_counts, _ = fetch_tables(tables, refs[-5:])
    rank, ranks = lax.axis_index("fsdp"), live_ranks.shape[0]
    slots, columns = outs[0].shape
    size = slots // chunks
    incoming, counts = [], []
    for index, place in enumerate(places):
        early, late = (send_step(place, ranks, inner) for inner in (True, False))
        matrix = matrix_of(owner_group, rank ^ jnp.where(in_phase(rank, ranks, True), early, late))
        counts.append(row_counts[matrix, rank] * live_ranks[rank])
        for chunk in range(chunks):
            part = pl.ds(chunk * size, size)
            for side, (source, kept) in enumerate(((momentum, olds), (gradient, grads))):
                flag = arrive.at[index * chunks + chunk, side]
                incoming.append(pltpu.make_async_copy(source.at[matrix, part], kept.at[index, part], flag))
                incoming[-1].start()
    token[...] = jnp.zeros_like(token)
    for index, out in enumerate(outs):
        for chunk in range(chunks):
            first = 2 * (index * chunks + chunk)
            for copy in incoming[first : first + 2]:
                copy.wait()
            rows = slice(chunk * size, (chunk + 1) * size)
            grad_now = grads[index, rows, :]
            fresh = MOMENTUM_RATE * olds[index, rows, :] + grad_now
            position = lax.broadcasted_iota(jnp.int32, (size, columns), 0) + chunk * size
            out[rows, :] = jnp.where(position < counts[index], grad_now + MOMENTUM_RATE * fresh, 0.0)


def home_kernel(owner_group, live_ranks, row_counts, momentum, gradient, fresh_out, own):
    rank, matrix = lax.axis_index("fsdp"), pl.program_id(0)
    grad_now = gradient[...]
    position = lax.broadcasted_iota(jnp.int32, grad_now.shape, 0)
    keep = position < row_counts[matrix, rank] * live_ranks[rank]
    fresh = jnp.where(keep, MOMENTUM_RATE * momentum[...] + grad_now, 0.0)
    fresh_out[...] = fresh

    @pl.when(owner_group[matrix] == rank)
    def _():
        own[...] = jnp.where(keep, grad_now + MOMENTUM_RATE * fresh, 0.0)


def gram_kernel(ranks, *refs):
    tables, blocks, refs = refs[:4], refs[4 : 4 + ranks], refs[4 + ranks :]
    high_out, low_out, gram, landed, padded, arrive = refs[:6]
    held = refs[6:]
    rank = lax.axis_index("fsdp")
    slots, columns = blocks[0].shape
    copies = []
    for step in range(ranks):
        copies.append(pltpu.make_async_copy(blocks[step], landed.at[step], arrive.at[step]))
        copies[-1].start()
    owner_group, _, _, row_offsets = fetch_tables(tables, held)
    matrix = matrix_of(owner_group, rank)
    padded[...] = jnp.zeros_like(padded)
    sublane = lax.broadcasted_iota(jnp.int32, (SUBLANES, columns), 0)
    for step in range(ranks):
        start = row_offsets[matrix, rank ^ step]
        shift = start % SUBLANES
        base = start - shift
        copies[step].wait()

        def tile(index, before, base=base, shift=shift, step=step):
            moved = pltpu.roll(landed[step, pl.ds(pl.multiple_of(index * SUBLANES, SUBLANES), SUBLANES), :], shift, 0)
            rows = pl.ds(pl.multiple_of(base + index * SUBLANES, SUBLANES), SUBLANES)
            padded[rows, :] = padded[rows, :] + jnp.where(sublane < shift, before, moved)
            return moved

        after = lax.fori_loop(0, slots // SUBLANES, tile, jnp.zeros((SUBLANES, columns), jnp.float32))
        rows = pl.ds(pl.multiple_of(base + slots, SUBLANES), SUBLANES)
        padded[rows, :] = padded[rows, :] + jnp.where(sublane < shift, after, 0.0)
    high, low = halves(padded[:INNER, :])
    high_out[...] = high
    low_out[...] = low
    for panel in range(3):
        here = slice(panel * PANEL, (panel + 1) * PANEL)
        part = dot_halves((high[panel * PANEL :], low[panel * PANEL :]), (high[here], low[here]), ((1,), (1,)))
        if panel == 0:
            gram[:, :PANEL] = part
        elif panel == 1:
            gram[: 2 * PANEL, PANEL:] = part
        else:
            gram[2 * PANEL :, PANEL:] = part


def symmetric_product(left, right, out):
    for begin in range(0, INNER, TILE):
        end = min(begin + TILE, INNER)
        part = dot_halves(tuple(half[begin:] for half in left), tuple(half[:, begin:end] for half in right))
        out[begin:, begin:end] = part
        if end < INNER:
            out[begin:end, end:] = part[end - begin :].T
    return out[...]


def update_kernel(ranks, *refs):
    tables, (packed, high, low, result), refs = refs[:4], refs[4:8], refs[8:]
    homes, refs = refs[:ranks], refs[ranks:]
    gram, padded, staged, leave = refs[:4]
    held = refs[4:]
    _, slots, columns = staged.shape
    rank = lax.axis_index("fsdp")
    owner_group, live_ranks, row_counts, row_offsets = fetch_tables(tables, held)
    matrix = matrix_of(owner_group, rank)
    gram[:, :PANEL] = packed[:, :PANEL]
    gram[PANEL:, PANEL : 2 * PANEL] = packed[: 2 * PANEL, PANEL:]
    gram[2 * PANEL :, 2 * PANEL :] = packed[2 * PANEL :, PANEL:]
    gram[:PANEL, PANEL:] = packed[PANEL:, :PANEL].T
    gram[PANEL : 2 * PANEL, 2 * PANEL :] = packed[PANEL : 2 * PANEL, PANEL:].T
    raw = gram[...]
    diagonal = lax.broadcasted_iota(jnp.int32, raw.shape, 0) == lax.broadcasted_iota(jnp.int32, raw.shape, 1)
    square_total = jnp.sum(jnp.where(diagonal, raw, 0.0))
    norm = jnp.sqrt(jnp.full((1, 1), square_total, jnp.float32)) + EPSILON
    inverse = 1.0 / norm
    first = (raw * inverse) * inverse
    first_halves = halves(first)
    second = symmetric_product(first_halves, first_halves, gram)
    base = QUINTIC_SECOND * first + QUINTIC_THIRD * second + jnp.where(diagonal, QUINTIC_FIRST, 0.0)
    base_halves = halves(base)
    third_halves = halves(symmetric_product(base_halves, first_halves, gram))
    next_gram = symmetric_product(base_halves, third_halves, gram)
    next_halves = halves(next_gram)
    outer = (
        QUINTIC_SECOND * next_gram
        + QUINTIC_THIRD * symmetric_product(next_halves, next_halves, gram)
        + jnp.where(diagonal, QUINTIC_FIRST, 0.0)
    )
    total = symmetric_product(halves(outer), base_halves, gram) * (inverse * OUT_SCALE)
    padded[:INNER, :] = dot_halves(halves(total), (high[...], low[...]))
    copies = [pltpu.make_async_copy(padded.at[pl.ds(0, INNER)], result, leave.at[ranks])]
    copies[0].start()
    sublane = lax.broadcasted_iota(jnp.int32, (SUBLANES, columns), 0)
    for step in [*range(ranks - 1, 0, -1), 0]:
        target = rank ^ step
        count = row_counts[matrix, target] * live_ranks[target]
        start = row_offsets[matrix, target]
        shift = start % SUBLANES
        first_row = start - shift
        back = jnp.where(shift == 0, 0, SUBLANES - shift)

        def window(index, first_row=first_row, back=back):
            rows = pl.ds(pl.multiple_of(first_row + index * SUBLANES, SUBLANES), SUBLANES)
            return pltpu.roll(padded[rows, :], back, 0)

        def tile(index, here, step=step, count=count, shift=shift, window=window):
            after = window(index + 1)
            moved = jnp.where(sublane < SUBLANES - shift, here, after)
            rows = pl.ds(pl.multiple_of(index * SUBLANES, SUBLANES), SUBLANES)
            staged[step, rows, :] = jnp.where(sublane < count - index * SUBLANES, moved, 0.0)
            return after

        lax.fori_loop(0, slots // SUBLANES, tile, window(0))
        copies.append(pltpu.make_async_copy(staged.at[step], homes[step], leave.at[step]))
        copies[-1].start()
    for copy in copies:
        copy.wait()


def each_copy(copies, action):
    for condition, source, place, flag in copies:

        @pl.when(condition)
        def _(source=source, place=place, flag=flag):
            getattr(pltpu.make_async_copy(source, place, flag), action)()


def first_place_kernel(ranks, table, inner_result, outer_result, inner_own, outer_own, result, shards, *refs):
    owner_group, arrive, leave = refs
    rank = lax.axis_index("fsdp")
    fetch = pltpu.make_async_copy(table, owner_group, arrive)
    fetch.start()
    fetch.wait()
    matrix = matrix_of(owner_group, rank)
    copies = []
    for inner, update, own in ((True, inner_result, inner_own), (False, outer_result, outer_own)):
        mine = in_phase(rank, ranks, inner)
        copies += [(mine, update, result, leave.at[0]), (mine, own, shards.at[matrix], leave.at[1])]
    each_copy(copies, "start")
    each_copy(copies, "wait")


def place_kernel(inner, ranks, steps, *refs):
    table, blocks, shards = refs[0], refs[1 : 1 + len(steps)], refs[2 + len(steps)]
    owner_group, arrive, leave = refs[3 + len(steps) :]
    rank = lax.axis_index("fsdp")
    fetch = pltpu.make_async_copy(table, owner_group, arrive)
    fetch.start()
    fetch.wait()
    copies = [
        (
            in_phase(rank ^ step, ranks, inner),
            blocks[order],
            shards.at[matrix_of(owner_group, rank ^ step)],
            leave.at[order],
        )
        for order, step in enumerate(steps)
    ]
    each_copy(copies, "start")
    each_copy(copies, "wait")


def idle_kernel(*refs):
    pass


def blend(places, tables, momentum, gradient, before):
    _, slots, columns = momentum.shape
    chunks = 4 if slots % (4 * SUBLANES) == 0 else 1
    held = (len(places), slots, columns)
    return pl.pallas_call(
        functools.partial(blend_kernel, places, chunks),
        out_shape=[jax.ShapeDtypeStruct((slots, columns), jnp.float32)] * len(places)
        + [jax.ShapeDtypeStruct((SUBLANES, 128), jnp.float32)],
        in_specs=[HBM] * 6 + [ANY] * len(before),
        out_specs=[VMEM] * (len(places) + 1),
        scratch_shapes=[pltpu.VMEM(held, jnp.float32)] * 2
        + [pltpu.SemaphoreType.DMA((len(places) * chunks, 2))]
        + table_scratch(*tables[2].shape),
        compiler_params=FULL,
        cost_estimate=pl.CostEstimate(flops=0, bytes_accessed=0, transcendentals=0),
        name="blend",
    )(*tables, momentum, gradient, *before)


def home(tables, momentum, gradient, before):
    matrices, slots, columns = momentum.shape
    block = pl.BlockSpec((None, slots, columns), lambda matrix: (matrix, 0, 0))

    def body(*refs):
        home_kernel(*refs[:5], *refs[-2:])

    return pl.pallas_call(
        body,
        grid=(matrices,),
        out_shape=[
            jax.ShapeDtypeStruct(momentum.shape, jnp.float32),
            jax.ShapeDtypeStruct((slots, columns), jnp.float32),
        ],
        in_specs=[pl.BlockSpec(memory_space=pltpu.SMEM)] * 3 + [block] * 2 + [ANY],
        out_specs=[block, pl.BlockSpec((slots, columns), lambda matrix: (0, 0))],
        compiler_params=FULL,
        cost_estimate=pl.CostEstimate(flops=0, bytes_accessed=0, transcendentals=0),
        name="home",
    )(*tables[:3], momentum, gradient, before)


def assemble_and_gram(tables, blocks):
    slots, columns = blocks[0].shape
    ranks = len(blocks)
    flops = 2 * 3 * INNER * 2 * PANEL * columns
    return pl.pallas_call(
        functools.partial(gram_kernel, ranks),
        out_shape=[jax.ShapeDtypeStruct((INNER, columns), jnp.bfloat16)] * 2
        + [jax.ShapeDtypeStruct((INNER, 2 * PANEL), jnp.float32)],
        in_specs=[HBM] * 4 + [ANY] * ranks,
        out_specs=[VMEM] * 3,
        scratch_shapes=[
            pltpu.VMEM((ranks, slots, columns), jnp.float32),
            pltpu.VMEM((INNER + slots + SUBLANES, columns), jnp.float32),
            pltpu.SemaphoreType.DMA((ranks,)),
        ]
        + table_scratch(*tables[2].shape),
        compiler_params=PARAMS,
        cost_estimate=pl.CostEstimate(flops=flops, bytes_accessed=16 * INNER * columns, transcendentals=0),
        name="assemble_and_gram",
    )(*tables, *blocks)


def update_shapes(ranks, slots, columns):
    return [jax.ShapeDtypeStruct((INNER, columns), jnp.float32)] + [
        jax.ShapeDtypeStruct((slots, columns), jnp.float32)
    ] * ranks


def apply_update(tables, packed, high, low, slots):
    ranks, columns = tables[1].shape[0], high.shape[1]
    flops = 2 * 3 * INNER * INNER * (5 * INNER + columns)
    return pl.pallas_call(
        functools.partial(update_kernel, ranks),
        out_shape=update_shapes(ranks, slots, columns),
        in_specs=[HBM] * 4 + [VMEM] * 3,
        out_specs=[ANY] * (1 + ranks),
        scratch_shapes=[
            pltpu.VMEM((INNER, INNER), jnp.float32),
            pltpu.VMEM((INNER + slots + 2 * SUBLANES, columns), jnp.float32),
            pltpu.VMEM((ranks, slots, columns), jnp.float32),
            pltpu.SemaphoreType.DMA((ranks + 1,)),
        ]
        + table_scratch(*tables[2].shape),
        compiler_params=PARAMS,
        cost_estimate=pl.CostEstimate(flops=flops, bytes_accessed=16 * INNER * columns, transcendentals=0),
        name="apply_update",
    )(*tables, packed, high, low)


def nothing(ranks, slots, columns):
    return pl.pallas_call(
        idle_kernel,
        out_shape=update_shapes(ranks, slots, columns),
        out_specs=[ANY] * (1 + ranks),
        name="nothing",
    )()


def first_place(owner_group, results, owns, shape, ranks):
    return pl.pallas_call(
        functools.partial(first_place_kernel, ranks),
        out_shape=[
            jax.ShapeDtypeStruct(results[0].shape, jnp.float32),
            jax.ShapeDtypeStruct(shape, jnp.float32),
        ],
        in_specs=[HBM] + [VMEM] * 4,
        out_specs=[HBM] * 2,
        scratch_shapes=[
            pltpu.SMEM(owner_group.shape, jnp.int32),
            pltpu.SemaphoreType.DMA(()),
            pltpu.SemaphoreType.DMA((2,)),
        ],
        compiler_params=PARAMS,
        cost_estimate=pl.CostEstimate(flops=0, bytes_accessed=8 * results[0].size, transcendentals=0),
        name="first_place",
    )(owner_group, *results, *owns)


def place_blocks(inner, owner_group, steps, blocks, shards, ranks):
    return pl.pallas_call(
        functools.partial(place_kernel, inner, ranks, steps),
        out_shape=jax.ShapeDtypeStruct(shards.shape, shards.dtype),
        in_specs=[HBM] + [VMEM] * len(blocks) + [HBM],
        out_specs=HBM,
        scratch_shapes=[
            pltpu.SMEM(owner_group.shape, jnp.int32),
            pltpu.SemaphoreType.DMA(()),
            pltpu.SemaphoreType.DMA((len(steps),)),
        ],
        input_output_aliases={1 + len(blocks): 0},
        compiler_params=PARAMS,
        cost_estimate=pl.CostEstimate(flops=0, bytes_accessed=8 * blocks[0].size, transcendentals=0),
        name="place_blocks",
    )(owner_group, *blocks, shards)


def group_stages(size):
    stages, shift = [], 0
    while (1 << shift) < size:
        wide = 1 if shift == 0 or (2 << shift) >= size else 2
        stages.append((shift, 1 << wide))
        shift += wide
    return stages


def sum_over(block, axis):
    size = lax.axis_size(axis)
    if size & (size - 1) or block.shape[0] % size:
        return lax.psum(block, axis)
    index = lax.axis_index(axis)

    def exchange(piece, step):
        return lax.ppermute(piece, axis, [(i, i ^ step) for i in range(size)])

    stages = group_stages(size)
    for shift, group in stages:
        digit = (index >> shift) & (group - 1)
        part = block.shape[0] // group
        pieces = [lax.dynamic_slice_in_dim(block, (digit ^ step) * part, part, 0) for step in range(group)]
        arrived = [exchange(pieces[step], step << shift) for step in range(1, group)]
        block = functools.reduce(jnp.add, arrived, pieces[0])
    for shift, group in reversed(stages):
        digit = (index >> shift) & (group - 1)
        part = block.shape[0]
        pieces = [block] + [exchange(block, step << shift) for step in range(1, group)]
        block = jnp.zeros((part * group, block.shape[1]), block.dtype)
        for step, piece in enumerate(pieces):
            block = lax.dynamic_update_slice_in_dim(block, piece, (digit ^ step) * part, 0)
    return block


def on_device(momentum, gradient, live_ranks, owner_group, row_counts, row_offsets):
    ranks = lax.axis_size("fsdp")
    my_rank = lax.axis_index("fsdp")
    slots = momentum.shape[1]
    tables = (owner_group, live_ranks, row_counts, row_offsets)
    steps = list(range(1, ranks))

    def inside(rank, inner):
        return bool(in_phase(rank, ranks, inner))

    *blends, token = blend(steps[:-1], tables, momentum, gradient, [])
    last, token = blend(steps[-1:], tables, momentum, gradient, [token])
    blends.append(last)

    sent = {}
    for place in steps:
        for kind in (False, True, "cross"):
            pairs = []
            for i in range(ranks):
                target = i ^ send_step(place, ranks, inside(i, True))
                same = inside(i, True) == inside(target, True)
                if (kind == "cross" and not same) or (same and inside(i, True) == kind):
                    pairs.append((i, target))
            if pairs:
                sent[place, kind] = lax.ppermute(blends[place - 1], "fsdp", pairs)

    def received(step, inner):
        whole = None
        for source in (False, True):
            if any(inside(i, inner) and inside(i ^ step, source) for i in range(ranks)):
                place = next(place for place in steps if send_step(place, ranks, source) == step)
                part = sent[place, inner if source == inner else "cross"]
                pick = in_phase(my_rank ^ step, ranks, source)
                whole = part if whole is None else jnp.where(pick, part, whole)
        return whole

    def to_home(block, step, inner):
        return lax.ppermute(block, "fsdp", [(i, i ^ step) for i in range(ranks) if inside(i, inner)])

    new_momentum, own_block = home(tables, momentum, gradient, token)
    owner_blocks = {inner: [own_block] + [received(step, inner) for step in steps] for inner in (True, False)}

    def compute(blocks):
        high, low, gram_part = assemble_and_gram(tables, blocks)
        return apply_update(tables, sum_over(gram_part, "tensor"), high, low, slots)

    def skip(blocks):
        return nothing(ranks, *blocks[0].shape)

    results, owns, returned = [], [], {}
    for inner in (True, False):
        result, *homes = lax.cond(in_phase(my_rank, ranks, inner), compute, skip, owner_blocks[inner])
        results.append(result)
        owns.append(homes[0])
        returned[inner] = {step: to_home(homes[step], step, inner) for step in steps}
    result, shards = first_place(owner_group, results, owns, momentum.shape, ranks)
    shards = place_blocks(True, owner_group, steps, [returned[True][step] for step in steps], shards, ranks)
    for step in steps:
        shards = place_blocks(False, owner_group, [step], [returned[False][step]], shards, ranks)
    return (new_momentum, shards, result[None])


def solution(mesh):
    placed = (P(None, "fsdp", "tensor"), P(None, "fsdp", "tensor"), P(), P(), P(), P())
    return jax.shard_map(
        on_device,
        mesh=mesh,
        in_specs=placed,
        out_specs=(P(None, "fsdp", "tensor"), P(None, "fsdp", "tensor"), P("fsdp", None, "tensor")),
        check_vma=False,
    )
```

```python
import functools
import math

import jax
import jax.numpy as jnp
from jax import lax
from jax.experimental import pallas as pl
from jax.experimental.pallas import tpu as pltpu
from jax.sharding import PartitionSpec as P

WIDTH = 7168
INNER = 576
PANEL = INNER // 3
TILE = 256
SUBLANES = 8

MOMENTUM_RATE = 0.95
QUINTIC_FIRST = 3.4445
QUINTIC_SECOND = -4.775
QUINTIC_THIRD = 2.0315
EPSILON = 1e-07
OUT_SCALE = 0.2 * math.sqrt(max(INNER, WIDTH))
FULL = pltpu.CompilerParams(vmem_limit_bytes=60 * 1024 * 1024)
PARAMS = pltpu.CompilerParams(vmem_limit_bytes=48 * 1024 * 1024)
HBM = pl.BlockSpec(memory_space=pltpu.HBM)
ANY = pl.BlockSpec(memory_space=pl.ANY)
VMEM = pl.BlockSpec(memory_space=pltpu.VMEM)


def halves(value):
    high = value.astype(jnp.bfloat16)
    low = (value - high.astype(jnp.float32)).astype(jnp.bfloat16)
    return high, low


def dot(left, right, contract):
    return lax.dot_general(left, right, (contract, ((), ())), preferred_element_type=jnp.float32)


def dot_halves(left, right, contract=((1,), (0,))):
    (left_high, left_low), (right_high, right_low) = left, right
    return (
        dot(left_high, right_low, contract) + dot(left_low, right_high, contract)
    ) + dot(left_high, right_high, contract)


def is_inner(rank, ranks):
    low = ranks // 4
    return (rank >= low) & (rank < ranks - low)


def mate(ranks):
    return ranks // 4


def table_scratch(matrices, ranks):
    return [
        pltpu.SMEM((matrices,), jnp.int32),
        pltpu.SMEM((ranks,), jnp.int32),
        pltpu.SMEM((matrices, ranks), jnp.int32),
        pltpu.SMEM((matrices, ranks), jnp.int32),
        pltpu.SemaphoreType.DMA((4,)),
    ]


def fetch_tables(tables, held):
    *places, arrive = held
    copies = [
        pltpu.make_async_copy(table, place, arrive.at[index])
        for index, (table, place) in enumerate(zip(tables, places))
    ]
    for copy in copies:
        copy.start()
    for copy in copies:
        copy.wait()
    return places


def matrix_of(owner_group, rank):
    found = jnp.int32(0)
    for matrix in range(owner_group.shape[0]):
        found = jnp.where(owner_group[matrix] == rank, matrix, found)
    return found


def each_copy(copies, action):
    for condition, source, place, flag in copies:

        @pl.when(condition)
        def _(source=source, place=place, flag=flag):
            getattr(pltpu.make_async_copy(source, place, flag), action)()


def blend_kernel(first, chunks, *refs):
    tables, (momentum, gradient) = refs[:4], refs[4:6]
    ranks = tables[1].shape[0]
    *outs, token, olds, grads, arrive, leave = refs[-ranks - 10 : -5]
    owner_group, live_ranks, row_counts, _ = fetch_tables(tables, refs[-5:])
    rank = lax.axis_index("fsdp")
    slots, columns = outs[0].shape
    size = slots // chunks
    jobs = []
    for step in [*range(1, ranks), 0]:
        target = rank ^ step
        matrix = matrix_of(owner_group, target ^ mate(ranks) if first else target)
        count = row_counts[matrix, rank] * live_ranks[rank]
        for chunk in range(chunks):
            part = pl.ds(chunk * size, size)
            flags = arrive.at[step, chunk, 0], arrive.at[step, chunk, 1]
            incoming = (
                (is_inner(target, ranks), momentum.at[matrix, part], olds.at[step, part], flags[0]),
                (is_inner(target, ranks), gradient.at[matrix, part], grads.at[step, part], flags[1]),
            )
            outgoing = (is_inner(target, ranks), olds.at[step, part], outs[step].at[part], leave.at[step, chunk])
            jobs.append((step, chunk, count, incoming, outgoing))
            each_copy(incoming, "start")
    token[...] = jnp.zeros_like(token)
    for step, chunk, count, incoming, outgoing in jobs:

        @pl.when(incoming[0][0])
        def _(step=step, chunk=chunk, count=count, incoming=incoming, outgoing=outgoing):
            for _, source, place, flag in incoming:
                pltpu.make_async_copy(source, place, flag).wait()
            rows = slice(chunk * size, (chunk + 1) * size)
            grad_now = grads[step, rows, :]
            fresh = MOMENTUM_RATE * olds[step, rows, :] + grad_now
            position = lax.broadcasted_iota(jnp.int32, (size, columns), 0) + chunk * size
            olds[step, rows, :] = jnp.where(position < count, grad_now + MOMENTUM_RATE * fresh, 0.0)
            pltpu.make_async_copy(*outgoing[1:]).start()

    each_copy([job[-1] for job in jobs], "wait")


def fresh_kernel(live_ranks, row_counts, momentum, gradient, _, out):
    rank, matrix = lax.axis_index("fsdp"), pl.program_id(0)
    position = lax.broadcasted_iota(jnp.int32, out.shape, 0)
    keep = position < row_counts[matrix, rank] * live_ranks[rank]
    out[...] = jnp.where(keep, MOMENTUM_RATE * momentum[...] + gradient[...], 0.0)


def gram_kernel(first, ranks, *refs):
    tables, blocks, refs = refs[:4], refs[4 : 4 + ranks], refs[5 + ranks :]
    high_out, low_out, gram = refs[:3]
    landed, padded, high_held, low_held, arrive, leave = refs[-11:-5]
    slots, columns = blocks[0].shape
    rank = lax.axis_index("fsdp")

    @pl.when(is_inner(rank, ranks))
    def _():
        copies = []
        for step in range(ranks):
            copies.append(pltpu.make_async_copy(blocks[step], landed.at[step], arrive.at[step]))
            copies[-1].start()
        owner_group, _, _, row_offsets = fetch_tables(tables, refs[-5:])
        matrix = matrix_of(owner_group, rank ^ mate(ranks) if first else rank)
        padded[...] = jnp.zeros_like(padded)
        sublane = lax.broadcasted_iota(jnp.int32, (SUBLANES, columns), 0)
        for step in range(ranks):
            start = row_offsets[matrix, rank ^ step]
            shift = start % SUBLANES
            base = start - shift
            copies[step].wait()

            def tile(index, before, base=base, shift=shift, step=step):
                moved = pltpu.roll(landed[step, pl.ds(pl.multiple_of(index * SUBLANES, SUBLANES), SUBLANES), :], shift, 0)
                rows = pl.ds(pl.multiple_of(base + index * SUBLANES, SUBLANES), SUBLANES)
                padded[rows, :] = padded[rows, :] + jnp.where(sublane < shift, before, moved)
                return moved

            after = lax.fori_loop(0, slots // SUBLANES, tile, jnp.zeros((SUBLANES, columns), jnp.float32))
            rows = pl.ds(pl.multiple_of(base + slots, SUBLANES), SUBLANES)
            padded[rows, :] = padded[rows, :] + jnp.where(sublane < shift, after, 0.0)
        high, low = halves(padded[:INNER, :])
        high_held[...] = high
        low_held[...] = low
        outgoing = [
            pltpu.make_async_copy(high_held, high_out, leave.at[0]),
            pltpu.make_async_copy(low_held, low_out, leave.at[1]),
        ]
        if first:
            outgoing.append(pltpu.make_async_copy(padded.at[pl.ds(0, INNER)], refs[3], leave.at[2]))
        for copy in outgoing:
            copy.start()
        for panel in range(3):
            here = slice(panel * PANEL, (panel + 1) * PANEL)
            part = dot_halves((high[panel * PANEL :], low[panel * PANEL :]), (high[here], low[here]), ((1,), (1,)))
            store_panel(gram, panel, part)
        for copy in outgoing:
            copy.wait()


def store_panel(packed, panel, part):
    if panel == 0:
        packed[:, :PANEL] = part
    elif panel == 1:
        packed[: 2 * PANEL, PANEL:] = part
    else:
        packed[2 * PANEL :, PANEL:] = part


def unpack(packed, gram):
    gram[:, :PANEL] = packed[:, :PANEL]
    gram[PANEL:, PANEL : 2 * PANEL] = packed[: 2 * PANEL, PANEL:]
    gram[2 * PANEL :, 2 * PANEL :] = packed[2 * PANEL :, PANEL:]
    gram[:PANEL, PANEL:] = packed[PANEL:, :PANEL].T
    gram[PANEL : 2 * PANEL, 2 * PANEL :] = packed[PANEL : 2 * PANEL, PANEL:].T
    return gram[...]


def symmetric_product(left, right, out):
    for begin in range(0, INNER, TILE):
        end = min(begin + TILE, INNER)
        part = dot_halves(tuple(half[begin:] for half in left), tuple(half[:, begin:end] for half in right))
        out[begin:, begin:end] = part
        if end < INNER:
            out[begin:end, end:] = part[end - begin :].T
    return out[...]


def polynomial(raw, gram):
    diagonal = lax.broadcasted_iota(jnp.int32, raw.shape, 0) == lax.broadcasted_iota(jnp.int32, raw.shape, 1)
    square_total = jnp.sum(jnp.where(diagonal, raw, 0.0))
    norm = jnp.sqrt(jnp.full((1, 1), square_total, jnp.float32)) + EPSILON
    inverse = 1.0 / norm
    first = (raw * inverse) * inverse
    first_halves = halves(first)
    second = symmetric_product(first_halves, first_halves, gram)
    base = QUINTIC_SECOND * first + QUINTIC_THIRD * second + jnp.where(diagonal, QUINTIC_FIRST, 0.0)
    base_halves = halves(base)
    third_halves = halves(symmetric_product(base_halves, first_halves, gram))
    next_gram = symmetric_product(base_halves, third_halves, gram)
    next_halves = halves(next_gram)
    outer = (
        QUINTIC_SECOND * next_gram
        + QUINTIC_THIRD * symmetric_product(next_halves, next_halves, gram)
        + jnp.where(diagonal, QUINTIC_FIRST, 0.0)
    )
    return symmetric_product(halves(outer), base_halves, gram) * (inverse * OUT_SCALE)


def extract(padded, start, count, staged, step):
    _, slots, columns = staged.shape
    sublane = lax.broadcasted_iota(jnp.int32, (SUBLANES, columns), 0)
    shift = start % SUBLANES
    base = start - shift
    back = jnp.where(shift == 0, 0, SUBLANES - shift)

    def window(index):
        rows = pl.ds(pl.multiple_of(base + index * SUBLANES, SUBLANES), SUBLANES)
        return pltpu.roll(padded[rows, :], back, 0)

    def tile(index, here):
        after = window(index + 1)
        moved = jnp.where(sublane < SUBLANES - shift, here, after)
        rows = pl.ds(pl.multiple_of(index * SUBLANES, SUBLANES), SUBLANES)
        staged[step, rows, :] = jnp.where(sublane < count - index * SUBLANES, moved, 0.0)
        return after

    lax.fori_loop(0, slots // SUBLANES, tile, window(0))


def update_kernel(first, steps, *refs):
    tables, (packed, high, low, whole), refs = refs[:4], refs[4:8], refs[8:]
    homes, refs = refs[: len(steps)], refs[len(steps) :]
    gram, padded, staged, high_held, low_held, held, arrive, leave = refs[:8]
    ranks = tables[1].shape[0]
    rank = lax.axis_index("fsdp")
    incoming = [
        pltpu.make_async_copy(high, high_held, arrive.at[0]),
        pltpu.make_async_copy(low, low_held, arrive.at[1]),
    ]
    for copy in incoming:
        copy.start()
    owner_group, live_ranks, row_counts, row_offsets = fetch_tables(tables, refs[8:])
    matrix = matrix_of(owner_group, rank ^ mate(ranks) if first else rank)
    total = polynomial(unpack(packed, gram), gram)
    if first:
        for panel in range(3):
            store_panel(held, panel, total[panel * PANEL :, panel * PANEL : (panel + 1) * PANEL])
        copies = [pltpu.make_async_copy(held, whole, leave.at[len(steps)])]
        copies[0].start()
    for copy in incoming:
        copy.wait()
    padded[:INNER, :] = dot_halves(halves(total), (high_held[...], low_held[...]))
    if not first:
        copies = [pltpu.make_async_copy(padded.at[pl.ds(0, INNER)], whole, leave.at[len(steps)])]
        copies[0].start()
    for index, step in enumerate(steps):
        target = rank ^ step
        extract(padded, row_offsets[matrix, target], row_counts[matrix, target] * live_ranks[target], staged, index)
        copies.append(pltpu.make_async_copy(staged.at[index], homes[index], leave.at[index]))
        copies[-1].start()
    for copy in copies:
        copy.wait()


def finish_kernel(ranks, *refs):
    tables, (packed, iterate, inner_result, own_first, own_last, result, shards), refs = refs[:4], refs[4:11], refs[11:]
    gram, padded, staged, whole, held, arrive, leave = refs[:7]
    rank = lax.axis_index("fsdp")
    owner_group, live_ranks, row_counts, row_offsets = fetch_tables(tables, refs[7:])
    matrix = matrix_of(owner_group, rank)

    def run(jobs):
        copies = [pltpu.make_async_copy(*job) for job in jobs]
        for copy in copies:
            copy.start()
        for copy in copies:
            copy.wait()

    @pl.when(is_inner(rank, ranks))
    def _():
        run(
            [
                (inner_result, whole, arrive.at[0]),
                (own_first, staged.at[0], arrive.at[1]),
                (own_last, staged.at[1], arrive.at[2]),
            ]
        )
        other = matrix_of(owner_group, rank ^ mate(ranks))
        run(
            [
                (whole, result, leave.at[0]),
                (staged.at[0], shards.at[other], leave.at[1]),
                (staged.at[1], shards.at[matrix], leave.at[2]),
            ]
        )

    @pl.when(jnp.logical_not(is_inner(rank, ranks)))
    def _():
        run([(iterate, whole, arrive.at[0]), (packed, held, arrive.at[1])])
        padded[:INNER, :] = dot_halves(halves(unpack(held, gram)), halves(whole[...]))
        extract(padded, row_offsets[matrix, rank], row_counts[matrix, rank] * live_ranks[rank], staged, 0)
        run(
            [
                (padded.at[pl.ds(0, INNER)], result, leave.at[0]),
                (staged.at[0], shards.at[matrix], leave.at[1]),
            ]
        )


def place_kernel(first, ranks, steps, *refs):
    table, blocks, shards = refs[0], refs[1 : 1 + len(steps)], refs[2 + len(steps)]
    owner_group, arrive, leave = refs[3 + len(steps) :]
    rank = lax.axis_index("fsdp")
    fetch = pltpu.make_async_copy(table, owner_group, arrive)
    fetch.start()
    fetch.wait()
    copies = []
    for index, step in enumerate(steps):
        source = rank ^ step
        matrix = matrix_of(owner_group, source ^ mate(ranks) if first else source)
        copies.append((is_inner(source, ranks), blocks[index], shards.at[matrix], leave.at[index]))
    each_copy(copies, "start")
    each_copy(copies, "wait")


def idle_kernel(*refs):
    pass


def floats(*shape):
    return jax.ShapeDtypeStruct(shape, jnp.float32)


def vmem(*shape, dtype=jnp.float32):
    return pltpu.VMEM(shape, dtype)


def flags(*shape):
    return pltpu.SemaphoreType.DMA(shape)


FREE = pl.CostEstimate(flops=0, bytes_accessed=0, transcendentals=0)


def blend(first, tables, momentum, gradient, before):
    _, slots, columns = momentum.shape
    ranks = tables[1].shape[0]
    chunks = 4 if slots % (4 * SUBLANES) == 0 else 1
    return pl.pallas_call(
        functools.partial(blend_kernel, first, chunks),
        out_shape=[floats(slots, columns)] * ranks + [floats(SUBLANES, 128)],
        in_specs=[HBM] * 6 + [ANY] * len(before),
        out_specs=[ANY] * ranks + [VMEM],
        scratch_shapes=[vmem(ranks, slots, columns)] * 2
        + [flags(ranks, chunks, 2), flags(ranks, chunks)]
        + table_scratch(*tables[2].shape),
        compiler_params=FULL,
        cost_estimate=FREE,
        name="blend",
    )(*tables, momentum, gradient, *before)


def fresh_momentum(tables, momentum, gradient, before):
    matrices, slots, columns = momentum.shape
    block = pl.BlockSpec((None, slots, columns), lambda matrix: (matrix, 0, 0))
    return pl.pallas_call(
        fresh_kernel,
        grid=(matrices,),
        out_shape=floats(*momentum.shape),
        in_specs=[pl.BlockSpec(memory_space=pltpu.SMEM)] * 2 + [block] * 2 + [ANY],
        out_specs=block,
        compiler_params=FULL,
        cost_estimate=FREE,
        name="fresh_momentum",
    )(*tables[1:3], momentum, gradient, before)


def assemble_and_gram(first, tables, blocks, after):
    slots, columns = blocks[0].shape
    ranks = len(blocks)
    half = jax.ShapeDtypeStruct((INNER, columns), jnp.bfloat16)
    return pl.pallas_call(
        functools.partial(gram_kernel, first, ranks),
        out_shape=[half, half, floats(INNER, 2 * PANEL)] + [floats(INNER, columns)] * first,
        in_specs=[HBM] * 4 + [ANY] * (ranks + 1),
        out_specs=[ANY, ANY, VMEM] + [ANY] * first,
        scratch_shapes=[
            vmem(ranks, slots, columns),
            vmem(INNER + slots + SUBLANES, columns),
            vmem(INNER, columns, dtype=jnp.bfloat16),
            vmem(INNER, columns, dtype=jnp.bfloat16),
            flags(ranks),
            flags(3),
        ]
        + table_scratch(*tables[2].shape),
        compiler_params=PARAMS,
        cost_estimate=FREE,
        name="assemble_and_gram",
    )(*tables, *blocks, after)


def update_shapes(first, steps, slots, columns):
    whole = floats(INNER, 2 * PANEL if first else columns)
    return [whole] + [floats(slots, columns)] * len(steps)


def apply_update(first, steps, tables, packed, high, low, slots):
    columns = high.shape[1]
    return pl.pallas_call(
        functools.partial(update_kernel, first, steps),
        out_shape=update_shapes(first, steps, slots, columns),
        in_specs=[HBM] * 4 + [VMEM] + [ANY] * 2,
        out_specs=[ANY] * (1 + len(steps)),
        scratch_shapes=[
            vmem(INNER, INNER),
            vmem(INNER + slots + 2 * SUBLANES, columns),
            vmem(len(steps), slots, columns),
            vmem(INNER, columns, dtype=jnp.bfloat16),
            vmem(INNER, columns, dtype=jnp.bfloat16),
            vmem(INNER, 2 * PANEL),
            flags(2),
            flags(len(steps) + 1),
        ]
        + table_scratch(*tables[2].shape),
        compiler_params=PARAMS,
        cost_estimate=FREE,
        name="apply_update",
    )(*tables, packed, high, low)


def nothing(shapes):
    return pl.pallas_call(idle_kernel, out_shape=shapes, out_specs=[ANY] * len(shapes), name="nothing")()


def finish(tables, packed, iterate, inner_result, own_first, own_last, shape):
    slots, columns = own_first.shape
    return pl.pallas_call(
        functools.partial(finish_kernel, tables[1].shape[0]),
        out_shape=[floats(INNER, columns), floats(*shape)],
        in_specs=[HBM] * 4 + [ANY] * 5,
        out_specs=[HBM] * 2,
        scratch_shapes=[
            vmem(INNER, INNER),
            vmem(INNER + slots + 2 * SUBLANES, columns),
            vmem(2, slots, columns),
            vmem(INNER, columns),
            vmem(INNER, 2 * PANEL),
            flags(3),
            flags(3),
        ]
        + table_scratch(*tables[2].shape),
        compiler_params=PARAMS,
        cost_estimate=FREE,
        name="finish",
    )(*tables, packed, iterate, inner_result, own_first, own_last)


def place_blocks(first, owner_group, steps, blocks, shards, ranks):
    return pl.pallas_call(
        functools.partial(place_kernel, first, ranks, steps),
        out_shape=floats(*shards.shape),
        in_specs=[HBM] + [VMEM] * len(blocks) + [HBM],
        out_specs=HBM,
        scratch_shapes=[pltpu.SMEM(owner_group.shape, jnp.int32), flags(), flags(len(steps))],
        input_output_aliases={1 + len(blocks): 0},
        compiler_params=PARAMS,
        cost_estimate=FREE,
        name="place_blocks",
    )(owner_group, *blocks, shards)


def group_stages(size):
    stages, shift = [], 0
    while (1 << shift) < size:
        wide = 1 if shift == 0 or (2 << shift) >= size else 2
        stages.append((shift, 1 << wide))
        shift += wide
    return stages


def sum_over(block, axis):
    size = lax.axis_size(axis)
    if size & (size - 1) or block.shape[0] % size:
        return lax.psum(block, axis)
    index = lax.axis_index(axis)

    def exchange(piece, step):
        return lax.ppermute(piece, axis, [(i, i ^ step) for i in range(size)])

    stages = group_stages(size)
    for shift, group in stages:
        digit = (index >> shift) & (group - 1)
        part = block.shape[0] // group
        pieces = [lax.dynamic_slice_in_dim(block, (digit ^ step) * part, part, 0) for step in range(group)]
        arrived = [exchange(pieces[step], step << shift) for step in range(1, group)]
        block = functools.reduce(jnp.add, arrived, pieces[0])
    for shift, group in reversed(stages):
        digit = (index >> shift) & (group - 1)
        part = block.shape[0]
        pieces = [block] + [exchange(block, step << shift) for step in range(1, group)]
        block = jnp.zeros((part * group, block.shape[1]), block.dtype)
        for step, piece in enumerate(pieces):
            block = lax.dynamic_update_slice_in_dim(block, piece, (digit ^ step) * part, 0)
    return block


def on_device(momentum, gradient, live_ranks, owner_group, row_counts, row_offsets):
    ranks = lax.axis_size("fsdp")
    my_rank = lax.axis_index("fsdp")
    _, slots, columns = momentum.shape
    tables = (owner_group, live_ranks, row_counts, row_offsets)
    inner = is_inner(my_rank, ranks)
    last = [2, 1, *range(3, ranks)]
    early = [step for step in last if step != mate(ranks)]

    def pairs(step, inward):
        return [(i, i ^ step) for i in range(ranks) if is_inner(i ^ step if inward else i, ranks)]

    def to_inner(block, step):
        return lax.ppermute(block, "fsdp", pairs(step, True))

    def from_inner(block, step):
        return lax.ppermute(block, "fsdp", pairs(step, False))

    *blends, token = blend(True, tables, momentum, gradient, [])
    first_blocks = [blends[0]] + [to_inner(blends[step], step) for step in range(1, ranks)]
    *blends, token = blend(False, tables, momentum, gradient, [token])
    last_blocks = [blends[0]] + [to_inner(blends[step], step) for step in range(1, ranks)]
    new_momentum = fresh_momentum(tables, momentum, gradient, token)

    high, low, gram_part, iterate = assemble_and_gram(True, tables, first_blocks, new_momentum)
    iterate = from_inner(iterate, mate(ranks))

    def first_update(high, low, gram_part):
        return apply_update(True, [0, *early], tables, sum_over(gram_part, "tensor"), high, low, slots)

    def first_skip(high, low, gram_part):
        return nothing(update_shapes(True, [0, *early], slots, columns))

    packed, own_first, *homes = lax.cond(inner, first_update, first_skip, high, low, gram_part)
    packed_there = from_inner(packed, mate(ranks))
    first_home = [from_inner(block, step) for step, block in zip(early, homes)]

    def last_update(after, *blocks):
        high, low, gram_part = assemble_and_gram(False, tables, blocks, after)
        return apply_update(False, [0, *last], tables, sum_over(gram_part, "tensor"), high, low, slots)

    def last_skip(after, *blocks):
        return nothing(update_shapes(False, [0, *last], slots, columns))

    result, own_last, *homes = lax.cond(inner, last_update, last_skip, packed, *last_blocks)
    last_home = [from_inner(block, step) for step, block in zip(last, homes)]

    result, shards = finish(tables, packed_there, iterate, result, own_first, own_last, momentum.shape)
    shards = place_blocks(True, owner_group, early, first_home, shards, ranks)
    for step, block in zip(last, last_home):
        shards = place_blocks(False, owner_group, [step], [block], shards, ranks)
    return (new_momentum, shards, result[None])


def solution(mesh):
    placed = (P(None, "fsdp", "tensor"), P(None, "fsdp", "tensor"), P(), P(), P(), P())
    return jax.shard_map(
        on_device,
        mesh=mesh,
        in_specs=placed,
        out_specs=(P(None, "fsdp", "tensor"), P(None, "fsdp", "tensor"), P("fsdp", None, "tensor")),
        check_vma=False,
    )
```

```python
import functools
import math

import jax
import jax.numpy as jnp
from jax import lax
from jax.experimental import pallas as pl
from jax.experimental.pallas import tpu as pltpu
from jax.sharding import PartitionSpec as P

WIDTH = 7168
INNER = 576
PANEL = INNER // 3
TILE = 256
SUBLANES = 8

MOMENTUM_RATE = 0.95
QUINTIC_FIRST = 3.4445
QUINTIC_SECOND = -4.775
QUINTIC_THIRD = 2.0315
EPSILON = 1e-07
OUT_SCALE = 0.2 * math.sqrt(max(INNER, WIDTH))
FULL = pltpu.CompilerParams(vmem_limit_bytes=60 * 1024 * 1024)
PARAMS = pltpu.CompilerParams(vmem_limit_bytes=48 * 1024 * 1024)
HBM = pl.BlockSpec(memory_space=pltpu.HBM)
ANY = pl.BlockSpec(memory_space=pl.ANY)
VMEM = pl.BlockSpec(memory_space=pltpu.VMEM)


def halves(value):
    high = value.astype(jnp.bfloat16)
    low = (value - high.astype(jnp.float32)).astype(jnp.bfloat16)
    return high, low


def dot(left, right, contract):
    return lax.dot_general(left, right, (contract, ((), ())), preferred_element_type=jnp.float32)


def dot_halves(left, right, contract=((1,), (0,))):
    (left_high, left_low), (right_high, right_low) = left, right
    return (
        dot(left_high, right_low, contract) + dot(left_low, right_high, contract)
    ) + dot(left_high, right_high, contract)


def is_inner(rank, ranks):
    low = ranks // 4
    return (rank >= low) & (rank < ranks - low)


def mate(ranks):
    return ranks // 4


def table_scratch(matrices, ranks):
    return [
        pltpu.SMEM((matrices,), jnp.int32),
        pltpu.SMEM((ranks,), jnp.int32),
        pltpu.SMEM((matrices, ranks), jnp.int32),
        pltpu.SMEM((matrices, ranks), jnp.int32),
        pltpu.SemaphoreType.DMA((4,)),
    ]


def fetch_tables(tables, held):
    *places, arrive = held
    copies = [
        pltpu.make_async_copy(table, place, arrive.at[index])
        for index, (table, place) in enumerate(zip(tables, places))
    ]
    for copy in copies:
        copy.start()
    for copy in copies:
        copy.wait()
    return places


def matrix_of(owner_group, rank):
    found = jnp.int32(0)
    for matrix in range(owner_group.shape[0]):
        found = jnp.where(owner_group[matrix] == rank, matrix, found)
    return found


def each_copy(copies, action):
    for condition, source, place, flag in copies:

        @pl.when(condition)
        def _(source=source, place=place, flag=flag):
            getattr(pltpu.make_async_copy(source, place, flag), action)()


def blend_kernel(first, chunks, *refs):
    tables, (momentum, gradient) = refs[:4], refs[4:6]
    ranks = tables[1].shape[0]
    *outs, token, olds, grads, arrive, leave = refs[-ranks - 10 : -5]
    owner_group, live_ranks, row_counts, _ = fetch_tables(tables, refs[-5:])
    rank = lax.axis_index("fsdp")
    slots, columns = outs[0].shape
    size = slots // chunks
    jobs = []
    for step in [*range(1, ranks), 0]:
        target = rank ^ step
        matrix = matrix_of(owner_group, target ^ mate(ranks) if first else target)
        count = row_counts[matrix, rank] * live_ranks[rank]
        for chunk in range(chunks):
            part = pl.ds(chunk * size, size)
            flags = arrive.at[step, chunk, 0], arrive.at[step, chunk, 1]
            incoming = (
                (is_inner(target, ranks), momentum.at[matrix, part], olds.at[step, part], flags[0]),
                (is_inner(target, ranks), gradient.at[matrix, part], grads.at[step, part], flags[1]),
            )
            outgoing = (is_inner(target, ranks), olds.at[step, part], outs[step].at[part], leave.at[step, chunk])
            jobs.append((step, chunk, count, incoming, outgoing))
            each_copy(incoming, "start")
    token[...] = jnp.zeros_like(token)
    for step, chunk, count, incoming, outgoing in jobs:

        @pl.when(incoming[0][0])
        def _(step=step, chunk=chunk, count=count, incoming=incoming, outgoing=outgoing):
            for _, source, place, flag in incoming:
                pltpu.make_async_copy(source, place, flag).wait()
            rows = slice(chunk * size, (chunk + 1) * size)
            grad_now = grads[step, rows, :]
            fresh = MOMENTUM_RATE * olds[step, rows, :] + grad_now
            position = lax.broadcasted_iota(jnp.int32, (size, columns), 0) + chunk * size
            olds[step, rows, :] = jnp.where(position < count, grad_now + MOMENTUM_RATE * fresh, 0.0)
            pltpu.make_async_copy(*outgoing[1:]).start()

    each_copy([job[-1] for job in jobs], "wait")


def fresh_kernel(live_ranks, row_counts, momentum, gradient, _, out):
    rank, matrix = lax.axis_index("fsdp"), pl.program_id(0)
    position = lax.broadcasted_iota(jnp.int32, out.shape, 0)
    keep = position < row_counts[matrix, rank] * live_ranks[rank]
    out[...] = jnp.where(keep, MOMENTUM_RATE * momentum[...] + gradient[...], 0.0)


def gram_kernel(first, ranks, *refs):
    tables, blocks, refs = refs[:4], refs[4 : 4 + ranks], refs[5 + ranks :]
    high_out, low_out, gram = refs[:3]
    landed, padded, high_held, low_held, arrive, leave = refs[-11:-5]
    slots, columns = blocks[0].shape
    rank = lax.axis_index("fsdp")

    @pl.when(is_inner(rank, ranks))
    def _():
        copies = []
        for step in range(ranks):
            copies.append(pltpu.make_async_copy(blocks[step], landed.at[step], arrive.at[step]))
            copies[-1].start()
        owner_group, _, _, row_offsets = fetch_tables(tables, refs[-5:])
        matrix = matrix_of(owner_group, rank ^ mate(ranks) if first else rank)
        padded[...] = jnp.zeros_like(padded)
        sublane = lax.broadcasted_iota(jnp.int32, (SUBLANES, columns), 0)
        for step in range(ranks):
            start = row_offsets[matrix, rank ^ step]
            shift = start % SUBLANES
            base = start - shift
            copies[step].wait()

            def tile(index, before, base=base, shift=shift, step=step):
                moved = pltpu.roll(landed[step, pl.ds(pl.multiple_of(index * SUBLANES, SUBLANES), SUBLANES), :], shift, 0)
                rows = pl.ds(pl.multiple_of(base + index * SUBLANES, SUBLANES), SUBLANES)
                padded[rows, :] = padded[rows, :] + jnp.where(sublane < shift, before, moved)
                return moved

            after = lax.fori_loop(0, slots // SUBLANES, tile, jnp.zeros((SUBLANES, columns), jnp.float32))
            rows = pl.ds(pl.multiple_of(base + slots, SUBLANES), SUBLANES)
            padded[rows, :] = padded[rows, :] + jnp.where(sublane < shift, after, 0.0)
        high, low = halves(padded[:INNER, :])
        high_held[...] = high
        low_held[...] = low
        outgoing = [
            pltpu.make_async_copy(high_held, high_out, leave.at[0]),
            pltpu.make_async_copy(low_held, low_out, leave.at[1]),
        ]
        if first:
            outgoing.append(pltpu.make_async_copy(padded.at[pl.ds(0, INNER)], refs[3], leave.at[2]))
        for copy in outgoing:
            copy.start()
        for panel in range(3):
            here = slice(panel * PANEL, (panel + 1) * PANEL)
            part = dot_halves((high[panel * PANEL :], low[panel * PANEL :]), (high[here], low[here]), ((1,), (1,)))
            store_panel(gram, panel, part)
        for copy in outgoing:
            copy.wait()


def store_panel(packed, panel, part):
    if panel == 0:
        packed[:, :PANEL] = part
    elif panel == 1:
        packed[: 2 * PANEL, PANEL:] = part
    else:
        packed[2 * PANEL :, PANEL:] = part


def unpack(packed, gram):
    gram[:, :PANEL] = packed[:, :PANEL]
    gram[PANEL:, PANEL : 2 * PANEL] = packed[: 2 * PANEL, PANEL:]
    gram[2 * PANEL :, 2 * PANEL :] = packed[2 * PANEL :, PANEL:]
    gram[:PANEL, PANEL:] = packed[PANEL:, :PANEL].T
    gram[PANEL : 2 * PANEL, 2 * PANEL :] = packed[PANEL : 2 * PANEL, PANEL:].T
    return gram[...]


def symmetric_product(left, right, out):
    for begin in range(0, INNER, TILE):
        end = min(begin + TILE, INNER)
        part = dot_halves(tuple(half[begin:] for half in left), tuple(half[:, begin:end] for half in right))
        out[begin:, begin:end] = part
        if end < INNER:
            out[begin:end, end:] = part[end - begin :].T
    return out[...]


def polynomial(raw, gram):
    diagonal = lax.broadcasted_iota(jnp.int32, raw.shape, 0) == lax.broadcasted_iota(jnp.int32, raw.shape, 1)
    square_total = jnp.sum(jnp.where(diagonal, raw, 0.0))
    norm = jnp.sqrt(jnp.full((1, 1), square_total, jnp.float32)) + EPSILON
    inverse = 1.0 / norm
    first = (raw * inverse) * inverse
    first_halves = halves(first)
    second = symmetric_product(first_halves, first_halves, gram)
    base = QUINTIC_SECOND * first + QUINTIC_THIRD * second + jnp.where(diagonal, QUINTIC_FIRST, 0.0)
    base_halves = halves(base)
    third_halves = halves(symmetric_product(base_halves, first_halves, gram))
    next_gram = symmetric_product(base_halves, third_halves, gram)
    next_halves = halves(next_gram)
    outer = (
        QUINTIC_SECOND * next_gram
        + QUINTIC_THIRD * symmetric_product(next_halves, next_halves, gram)
        + jnp.where(diagonal, QUINTIC_FIRST, 0.0)
    )
    return symmetric_product(halves(outer), base_halves, gram) * (inverse * OUT_SCALE)


def extract(padded, start, count, staged, step):
    _, slots, columns = staged.shape
    sublane = lax.broadcasted_iota(jnp.int32, (SUBLANES, columns), 0)
    shift = start % SUBLANES
    base = start - shift
    back = jnp.where(shift == 0, 0, SUBLANES - shift)

    def window(index):
        rows = pl.ds(pl.multiple_of(base + index * SUBLANES, SUBLANES), SUBLANES)
        return pltpu.roll(padded[rows, :], back, 0)

    def tile(index, here):
        after = window(index + 1)
        moved = jnp.where(sublane < SUBLANES - shift, here, after)
        rows = pl.ds(pl.multiple_of(index * SUBLANES, SUBLANES), SUBLANES)
        staged[step, rows, :] = jnp.where(sublane < count - index * SUBLANES, moved, 0.0)
        return after

    lax.fori_loop(0, slots // SUBLANES, tile, window(0))


def update_kernel(first, steps, *refs):
    tables, (packed, high, low), refs = refs[:4], refs[4:7], refs[8 if first else 7 :]
    whole, refs = refs[0], refs[1:]
    homes, refs = refs[: len(steps)], refs[len(steps) :]
    gram, padded, staged, high_held, low_held, held, arrive, leave = refs[:8]
    ranks = tables[1].shape[0]
    rank = lax.axis_index("fsdp")
    incoming = [
        pltpu.make_async_copy(high, high_held, arrive.at[0]),
        pltpu.make_async_copy(low, low_held, arrive.at[1]),
    ]
    for copy in incoming:
        copy.start()
    owner_group, live_ranks, row_counts, row_offsets = fetch_tables(tables, refs[8:])
    matrix = matrix_of(owner_group, rank ^ mate(ranks) if first else rank)
    total = polynomial(unpack(packed, gram), gram)
    if first:
        for panel in range(3):
            store_panel(held, panel, total[panel * PANEL :, panel * PANEL : (panel + 1) * PANEL])
        copies = [pltpu.make_async_copy(held, whole, leave.at[len(steps)])]
        copies[0].start()
    for copy in incoming:
        copy.wait()
    padded[:INNER, :] = dot_halves(halves(total), (high_held[...], low_held[...]))
    if not first:
        copies = [pltpu.make_async_copy(padded.at[pl.ds(0, INNER)], whole, leave.at[len(steps)])]
        copies[0].start()
    for index, step in enumerate(steps):
        target = rank ^ step
        extract(padded, row_offsets[matrix, target], row_counts[matrix, target] * live_ranks[target], staged, index)
        copies.append(pltpu.make_async_copy(staged.at[index], homes[index], leave.at[index]))
        copies[-1].start()
    for copy in copies:
        copy.wait()


def finish_kernel(ranks, *refs):
    tables, (packed, iterate, inner_result, own_first, own_last, result, shards), refs = refs[:4], refs[4:11], refs[11:]
    gram, padded, staged, whole, held, arrive, leave = refs[:7]
    rank = lax.axis_index("fsdp")
    owner_group, live_ranks, row_counts, row_offsets = fetch_tables(tables, refs[7:])
    matrix = matrix_of(owner_group, rank)

    def run(jobs):
        copies = [pltpu.make_async_copy(*job) for job in jobs]
        for copy in copies:
            copy.start()
        for copy in copies:
            copy.wait()

    @pl.when(is_inner(rank, ranks))
    def _():
        run(
            [
                (inner_result, whole, arrive.at[0]),
                (own_first, staged.at[0], arrive.at[1]),
                (own_last, staged.at[1], arrive.at[2]),
            ]
        )
        other = matrix_of(owner_group, rank ^ mate(ranks))
        run(
            [
                (whole, result, leave.at[0]),
                (staged.at[0], shards.at[other], leave.at[1]),
                (staged.at[1], shards.at[matrix], leave.at[2]),
            ]
        )

    @pl.when(jnp.logical_not(is_inner(rank, ranks)))
    def _():
        run([(iterate, whole, arrive.at[0]), (packed, held, arrive.at[1])])
        padded[:INNER, :] = dot_halves(halves(unpack(held, gram)), halves(whole[...]))
        extract(padded, row_offsets[matrix, rank], row_counts[matrix, rank] * live_ranks[rank], staged, 0)
        run(
            [
                (padded.at[pl.ds(0, INNER)], result, leave.at[0]),
                (staged.at[0], shards.at[matrix], leave.at[1]),
            ]
        )


def place_kernel(first, ranks, steps, *refs):
    table, blocks, shards = refs[0], refs[1 : 1 + len(steps)], refs[2 + len(steps)]
    owner_group, arrive, leave = refs[3 + len(steps) :]
    rank = lax.axis_index("fsdp")
    fetch = pltpu.make_async_copy(table, owner_group, arrive)
    fetch.start()
    fetch.wait()
    copies = []
    for index, step in enumerate(steps):
        source = rank ^ step
        matrix = matrix_of(owner_group, source ^ mate(ranks) if first else source)
        copies.append((is_inner(source, ranks), blocks[index], shards.at[matrix], leave.at[index]))
    each_copy(copies, "start")
    each_copy(copies, "wait")


def idle_kernel(*refs):
    pass


def floats(*shape):
    return jax.ShapeDtypeStruct(shape, jnp.float32)


def vmem(*shape, dtype=jnp.float32):
    return pltpu.VMEM(shape, dtype)


def flags(*shape):
    return pltpu.SemaphoreType.DMA(shape)


FREE = pl.CostEstimate(flops=0, bytes_accessed=0, transcendentals=0)


def blend(first, tables, momentum, gradient, before):
    _, slots, columns = momentum.shape
    ranks = tables[1].shape[0]
    chunks = 4 if slots % (4 * SUBLANES) == 0 else 1
    return pl.pallas_call(
        functools.partial(blend_kernel, first, chunks),
        out_shape=[floats(slots, columns)] * ranks + [floats(SUBLANES, 128)],
        in_specs=[HBM] * 6 + [ANY] * len(before),
        out_specs=[HBM] * ranks + [VMEM],
        scratch_shapes=[vmem(ranks, slots, columns)] * 2
        + [flags(ranks, chunks, 2), flags(ranks, chunks)]
        + table_scratch(*tables[2].shape),
        compiler_params=FULL,
        cost_estimate=FREE,
        name="blend",
    )(*tables, momentum, gradient, *before)


def fresh_momentum(tables, momentum, gradient, before):
    matrices, slots, columns = momentum.shape
    block = pl.BlockSpec((None, slots, columns), lambda matrix: (matrix, 0, 0))
    return pl.pallas_call(
        fresh_kernel,
        grid=(matrices,),
        out_shape=floats(*momentum.shape),
        in_specs=[pl.BlockSpec(memory_space=pltpu.SMEM)] * 2 + [block] * 2 + [ANY],
        out_specs=block,
        compiler_params=FULL,
        cost_estimate=FREE,
        name="fresh_momentum",
    )(*tables[1:3], momentum, gradient, before)


def assemble_and_gram(first, tables, blocks, after):
    slots, columns = blocks[0].shape
    ranks = len(blocks)
    half = jax.ShapeDtypeStruct((INNER, columns), jnp.bfloat16)
    return pl.pallas_call(
        functools.partial(gram_kernel, first, ranks),
        out_shape=[half, half, floats(INNER, 2 * PANEL)] + [floats(INNER, columns)] * first,
        in_specs=[HBM] * 4 + [ANY] * (ranks + 1),
        out_specs=[ANY, ANY, VMEM] + [ANY] * first,
        scratch_shapes=[
            vmem(ranks, slots, columns),
            vmem(INNER + slots + SUBLANES, columns),
            vmem(INNER, columns, dtype=jnp.bfloat16),
            vmem(INNER, columns, dtype=jnp.bfloat16),
            flags(ranks),
            flags(3),
        ]
        + table_scratch(*tables[2].shape),
        compiler_params=PARAMS,
        cost_estimate=FREE,
        name="assemble_and_gram",
    )(*tables, *blocks, after)


def update_shapes(first, steps, slots, columns):
    whole = floats(INNER, 2 * PANEL if first else columns)
    return [whole] + [floats(slots, columns)] * len(steps)


def apply_update(first, steps, tables, packed, high, low, slots, *after):
    columns = high.shape[1]
    return pl.pallas_call(
        functools.partial(update_kernel, first, steps),
        out_shape=update_shapes(first, steps, slots, columns),
        in_specs=[HBM] * 4 + [VMEM] + [ANY] * (2 + len(after)),
        out_specs=[ANY] * (1 + len(steps)),
        scratch_shapes=[
            vmem(INNER, INNER),
            vmem(INNER + slots + 2 * SUBLANES, columns),
            vmem(len(steps), slots, columns),
            vmem(INNER, columns, dtype=jnp.bfloat16),
            vmem(INNER, columns, dtype=jnp.bfloat16),
            vmem(INNER, 2 * PANEL),
            flags(2),
            flags(len(steps) + 1),
        ]
        + table_scratch(*tables[2].shape),
        compiler_params=PARAMS,
        cost_estimate=FREE,
        name="apply_update",
    )(*tables, packed, high, low, *after)


def nothing(shapes):
    return pl.pallas_call(idle_kernel, out_shape=shapes, out_specs=[ANY] * len(shapes), name="nothing")()


def settle(value):
    return pl.pallas_call(
        idle_kernel,
        out_shape=floats(SUBLANES, 128),
        in_specs=[ANY],
        out_specs=ANY,
        cost_estimate=pl.CostEstimate(flops=10**11, bytes_accessed=0, transcendentals=0),
        name="settle",
    )(value)


def finish(tables, packed, iterate, inner_result, own_first, own_last, shape):
    slots, columns = own_first.shape
    return pl.pallas_call(
        functools.partial(finish_kernel, tables[1].shape[0]),
        out_shape=[floats(INNER, columns), floats(*shape)],
        in_specs=[HBM] * 4 + [ANY] * 5,
        out_specs=[HBM] * 2,
        scratch_shapes=[
            vmem(INNER, INNER),
            vmem(INNER + slots + 2 * SUBLANES, columns),
            vmem(2, slots, columns),
            vmem(INNER, columns),
            vmem(INNER, 2 * PANEL),
            flags(3),
            flags(3),
        ]
        + table_scratch(*tables[2].shape),
        compiler_params=PARAMS,
        cost_estimate=FREE,
        name="finish",
    )(*tables, packed, iterate, inner_result, own_first, own_last)


def place_blocks(first, owner_group, steps, blocks, shards, ranks):
    return pl.pallas_call(
        functools.partial(place_kernel, first, ranks, steps),
        out_shape=floats(*shards.shape),
        in_specs=[HBM] + [VMEM] * len(blocks) + [HBM],
        out_specs=HBM,
        scratch_shapes=[pltpu.SMEM(owner_group.shape, jnp.int32), flags(), flags(len(steps))],
        input_output_aliases={1 + len(blocks): 0},
        compiler_params=PARAMS,
        cost_estimate=FREE,
        name="place_blocks",
    )(owner_group, *blocks, shards)


def sum_over(block, axis):
    size = lax.axis_size(axis)
    if size & (size - 1) or block.shape[0] % size:
        return lax.psum(block, axis)
    index = lax.axis_index(axis)

    def exchange(piece, bit):
        return lax.ppermute(piece, axis, [(i, i ^ bit) for i in range(size)])

    bits = [1 << shift for shift in range(size.bit_length() - 1)]
    for bit in bits:
        part = block.shape[0] // 2
        mine = jnp.where(index & bit, part, 0)
        away = exchange(lax.dynamic_slice_in_dim(block, part - mine, part, 0), bit)
        block = lax.dynamic_slice_in_dim(block, mine, part, 0) + away
    for bit in reversed(bits):
        part = block.shape[0]
        mine = jnp.where(index & bit, part, 0)
        away = exchange(block, bit)
        whole = jnp.zeros((2 * part, block.shape[1]), block.dtype)
        whole = lax.dynamic_update_slice_in_dim(whole, block, mine, 0)
        block = lax.dynamic_update_slice_in_dim(whole, away, part - mine, 0)
    return block


def on_device(momentum, gradient, live_ranks, owner_group, row_counts, row_offsets):
    ranks = lax.axis_size("fsdp")
    my_rank = lax.axis_index("fsdp")
    _, slots, columns = momentum.shape
    tables = (owner_group, live_ranks, row_counts, row_offsets)
    inner = is_inner(my_rank, ranks)
    last = [2, 1, *range(3, ranks)]
    early = [step for step in last if step != mate(ranks)]

    def pairs(step, inward):
        return [(i, i ^ step) for i in range(ranks) if is_inner(i ^ step if inward else i, ranks)]

    def to_inner(block, step):
        return lax.ppermute(block, "fsdp", pairs(step, True))

    def from_inner(block, step):
        return lax.ppermute(block, "fsdp", pairs(step, False))

    *blends, token = blend(True, tables, momentum, gradient, [])
    first_blocks = [blends[0]] + [to_inner(blends[step], step) for step in range(1, ranks)]
    *blends, token = blend(False, tables, momentum, gradient, [token])
    last_blocks = [blends[0]] + [to_inner(blends[step], step) for step in range(1, ranks)]
    new_momentum = fresh_momentum(tables, momentum, gradient, token)

    high, low, gram_part, iterate = assemble_and_gram(True, tables, first_blocks, new_momentum)
    iterate = from_inner(iterate, mate(ranks))

    def first_update(high, low, gram_part, after):
        return apply_update(True, [0, *early], tables, sum_over(gram_part, "tensor"), high, low, slots, after)

    def first_skip(high, low, gram_part, after):
        return nothing(update_shapes(True, [0, *early], slots, columns))

    packed, own_first, *homes = lax.cond(inner, first_update, first_skip, high, low, gram_part, settle(gram_part))
    packed_there = from_inner(packed, mate(ranks))
    first_home = [from_inner(block, step) for step, block in zip(early, homes)]

    def last_update(after, *blocks):
        high, low, gram_part = assemble_and_gram(False, tables, blocks, after)
        return apply_update(False, [0, *last], tables, sum_over(gram_part, "tensor"), high, low, slots)

    def last_skip(after, *blocks):
        return nothing(update_shapes(False, [0, *last], slots, columns))

    result, own_last, *homes = lax.cond(inner, last_update, last_skip, packed, *last_blocks)
    last_home = [from_inner(block, step) for step, block in zip(last, homes)]

    result, shards = finish(tables, packed_there, iterate, result, own_first, own_last, momentum.shape)
    shards = place_blocks(True, owner_group, early, first_home, shards, ranks)
    for step, block in zip(last, last_home):
        shards = place_blocks(False, owner_group, [step], [block], shards, ranks)
    return (new_momentum, shards, result[None])


def solution(mesh):
    placed = (P(None, "fsdp", "tensor"), P(None, "fsdp", "tensor"), P(), P(), P(), P())
    return jax.shard_map(
        on_device,
        mesh=mesh,
        in_specs=placed,
        out_specs=(P(None, "fsdp", "tensor"), P(None, "fsdp", "tensor"), P("fsdp", None, "tensor")),
        check_vma=False,
    )
```

```python
import functools
import math

import jax
import jax.numpy as jnp
from jax import lax
from jax.experimental import pallas as pl
from jax.experimental.pallas import tpu as pltpu
from jax.sharding import PartitionSpec as P

WIDTH = 7168
INNER = 576
PANEL = INNER // 3
TILE = 256
SUBLANES = 8

MOMENTUM_RATE = 0.95
QUINTIC_FIRST = 3.4445
QUINTIC_SECOND = -4.775
QUINTIC_THIRD = 2.0315
EPSILON = 1e-07
OUT_SCALE = 0.2 * math.sqrt(max(INNER, WIDTH))
FULL = pltpu.CompilerParams(vmem_limit_bytes=60 * 1024 * 1024)
PARAMS = pltpu.CompilerParams(vmem_limit_bytes=24 * 1024 * 1024)
HBM = pl.BlockSpec(memory_space=pltpu.HBM)
ANY = pl.BlockSpec(memory_space=pl.ANY)
VMEM = pl.BlockSpec(memory_space=pltpu.VMEM)


def halves(value):
    high = value.astype(jnp.bfloat16)
    low = (value - high.astype(jnp.float32)).astype(jnp.bfloat16)
    return high, low


def dot(left, right, contract):
    return lax.dot_general(left, right, (contract, ((), ())), preferred_element_type=jnp.float32)


def dot_halves(left, right, contract=((1,), (0,))):
    (left_high, left_low), (right_high, right_low) = left, right
    depth = left_high.shape[1]
    body = depth // TILE * TILE
    if contract == ((1,), (0,)) and 0 < 3 * (depth - body) <= TILE:
        rest_left = jnp.concatenate([left_high[:, body:], left_low[:, body:], left_high[:, body:]], axis=1)
        rest_right = jnp.concatenate([right_low[body:], right_high[body:], right_high[body:]], axis=0)
        left = left_high[:, :body], left_low[:, :body]
        right = right_high[:body], right_low[:body]
        return dot(rest_left, rest_right, contract) + dot_halves(left, right)
    return (
        dot(left_high, right_low, contract) + dot(left_low, right_high, contract)
    ) + dot(left_high, right_high, contract)


def is_inner(rank, ranks):
    low = ranks // 4
    return (rank >= low) & (rank < ranks - low)


def mate(ranks):
    return ranks // 4


def table_scratch(matrices, ranks):
    return [
        pltpu.SMEM((matrices,), jnp.int32),
        pltpu.SMEM((ranks,), jnp.int32),
        pltpu.SMEM((matrices, ranks), jnp.int32),
        pltpu.SMEM((matrices, ranks), jnp.int32),
        pltpu.SemaphoreType.DMA((4,)),
    ]


def fetch_tables(tables, held):
    *places, arrive = held
    copies = [
        pltpu.make_async_copy(table, place, arrive.at[index])
        for index, (table, place) in enumerate(zip(tables, places))
    ]
    for copy in copies:
        copy.start()
    for copy in copies:
        copy.wait()
    return places


def matrix_of(owner_group, rank):
    found = jnp.int32(0)
    for matrix in range(owner_group.shape[0]):
        found = jnp.where(owner_group[matrix] == rank, matrix, found)
    return found


def over_tiles(tiles, body, carry):
    group = next(group for group in (6, 3, 2, 1) if tiles % group == 0)

    def step(index, carry):
        for member in range(group):
            carry = body(index * group + member, carry)
        return carry

    return lax.fori_loop(0, tiles // group, step, carry)


def each_copy(copies, action):
    for condition, source, place, flag in copies:

        @pl.when(condition)
        def _(source=source, place=place, flag=flag):
            getattr(pltpu.make_async_copy(source, place, flag), action)()


def blend_kernel(first, chunks, *refs):
    tables, (momentum, gradient) = refs[:4], refs[4:6]
    ranks = tables[1].shape[0]
    *outs, token, olds, grads, arrive, leave = refs[-ranks - 10 : -5]
    owner_group, live_ranks, row_counts, _ = fetch_tables(tables, refs[-5:])
    rank = lax.axis_index("fsdp")
    slots, columns = outs[0].shape
    size = slots // chunks
    jobs = []
    for step in [*range(1, ranks), 0]:
        target = rank ^ step
        matrix = matrix_of(owner_group, target ^ mate(ranks) if first else target)
        count = row_counts[matrix, rank] * live_ranks[rank]
        for chunk in range(chunks):
            part = pl.ds(chunk * size, size)
            flags = arrive.at[step, chunk, 0], arrive.at[step, chunk, 1]
            incoming = (
                (is_inner(target, ranks), momentum.at[matrix, part], olds.at[step, part], flags[0]),
                (is_inner(target, ranks), gradient.at[matrix, part], grads.at[step, part], flags[1]),
            )
            outgoing = (is_inner(target, ranks), olds.at[step, part], outs[step].at[part], leave.at[step, chunk])
            jobs.append((step, chunk, count, incoming, outgoing))
            each_copy(incoming, "start")
    token[...] = jnp.zeros_like(token)
    for step, chunk, count, incoming, outgoing in jobs:

        @pl.when(incoming[0][0])
        def _(step=step, chunk=chunk, count=count, incoming=incoming, outgoing=outgoing):
            for _, source, place, flag in incoming:
                pltpu.make_async_copy(source, place, flag).wait()
            rows = slice(chunk * size, (chunk + 1) * size)
            grad_now = grads[step, rows, :]
            fresh = MOMENTUM_RATE * olds[step, rows, :] + grad_now
            position = lax.broadcasted_iota(jnp.int32, (size, columns), 0) + chunk * size
            olds[step, rows, :] = jnp.where(position < count, grad_now + MOMENTUM_RATE * fresh, 0.0)
            pltpu.make_async_copy(*outgoing[1:]).start()

    each_copy([job[-1] for job in jobs], "wait")


def fresh_kernel(live_ranks, row_counts, momentum, gradient, _, out, token):
    token[...] = jnp.zeros_like(token)
    rank, matrix = lax.axis_index("fsdp"), pl.program_id(0)
    position = lax.broadcasted_iota(jnp.int32, out.shape, 0)
    keep = position < row_counts[matrix, rank] * live_ranks[rank]
    out[...] = jnp.where(keep, MOMENTUM_RATE * momentum[...] + gradient[...], 0.0)


def gram_kernel(first, ranks, *refs):
    tables, blocks, refs = refs[:4], refs[4 : 4 + ranks], refs[5 + ranks :]
    high_out, low_out, gram = refs[:3]
    landed, padded, high_held, low_held, arrive, leave = refs[-11:-5]
    slots, columns = blocks[0].shape
    rank = lax.axis_index("fsdp")

    @pl.when(is_inner(rank, ranks))
    def _():
        copies = []
        for step in range(ranks):
            copies.append(pltpu.make_async_copy(blocks[step], landed.at[step], arrive.at[step]))
            copies[-1].start()
        owner_group, _, _, row_offsets = fetch_tables(tables, refs[-5:])
        matrix = matrix_of(owner_group, rank ^ mate(ranks) if first else rank)
        padded[...] = jnp.zeros_like(padded)
        sublane = lax.broadcasted_iota(jnp.int32, (SUBLANES, columns), 0)
        for step in range(ranks):
            start = row_offsets[matrix, rank ^ step]
            shift = start % SUBLANES
            base = start - shift
            copies[step].wait()

            def tile(index, before, base=base, shift=shift, step=step):
                moved = pltpu.roll(landed[step, pl.ds(pl.multiple_of(index * SUBLANES, SUBLANES), SUBLANES), :], shift, 0)
                rows = pl.ds(pl.multiple_of(base + index * SUBLANES, SUBLANES), SUBLANES)
                padded[rows, :] = padded[rows, :] + jnp.where(sublane < shift, before, moved)
                return moved

            after = over_tiles(slots // SUBLANES, tile, jnp.zeros((SUBLANES, columns), jnp.float32))
            rows = pl.ds(pl.multiple_of(base + slots, SUBLANES), SUBLANES)
            padded[rows, :] = padded[rows, :] + jnp.where(sublane < shift, after, 0.0)
        high, low = halves(padded[:INNER, :])
        high_held[...] = high
        low_held[...] = low
        outgoing = [
            pltpu.make_async_copy(high_held, high_out, leave.at[0]),
            pltpu.make_async_copy(low_held, low_out, leave.at[1]),
        ]
        if first:
            outgoing.append(pltpu.make_async_copy(padded.at[pl.ds(0, INNER)], refs[3], leave.at[2]))
        for copy in outgoing:
            copy.start()
        for panel in range(3):
            here = slice(panel * PANEL, (panel + 1) * PANEL)
            part = dot_halves((high[panel * PANEL :], low[panel * PANEL :]), (high[here], low[here]), ((1,), (1,)))
            store_panel(gram, panel, part)
        for copy in outgoing:
            copy.wait()


def store_panel(packed, panel, part):
    if panel == 0:
        packed[:, :PANEL] = part
    elif panel == 1:
        packed[: 2 * PANEL, PANEL:] = part
    else:
        packed[2 * PANEL :, PANEL:] = part


def unpack(packed, gram):
    gram[:, :PANEL] = packed[:, :PANEL]
    gram[PANEL:, PANEL : 2 * PANEL] = packed[: 2 * PANEL, PANEL:]
    gram[2 * PANEL :, 2 * PANEL :] = packed[2 * PANEL :, PANEL:]
    gram[:PANEL, PANEL:] = packed[PANEL:, :PANEL].T
    gram[PANEL : 2 * PANEL, 2 * PANEL :] = packed[PANEL : 2 * PANEL, PANEL:].T
    return gram[...]


def symmetric_product(left, right, out):
    for begin in range(0, INNER, TILE):
        end = min(begin + TILE, INNER)
        part = dot_halves(tuple(half[begin:] for half in left), tuple(half[:, begin:end] for half in right))
        out[begin:, begin:end] = part
        if end < INNER:
            out[begin:end, end:] = part[end - begin :].T
    return out[...]


def polynomial(raw, gram):
    diagonal = lax.broadcasted_iota(jnp.int32, raw.shape, 0) == lax.broadcasted_iota(jnp.int32, raw.shape, 1)
    square_total = jnp.sum(jnp.where(diagonal, raw, 0.0))
    norm = jnp.sqrt(jnp.full((1, 1), square_total, jnp.float32)) + EPSILON
    inverse = 1.0 / norm
    first = (raw * inverse) * inverse
    first_halves = halves(first)
    second = symmetric_product(first_halves, first_halves, gram)
    base = QUINTIC_SECOND * first + QUINTIC_THIRD * second + jnp.where(diagonal, QUINTIC_FIRST, 0.0)
    base_halves = halves(base)
    third_halves = halves(symmetric_product(base_halves, first_halves, gram))
    next_gram = symmetric_product(base_halves, third_halves, gram)
    next_halves = halves(next_gram)
    outer = (
        QUINTIC_SECOND * next_gram
        + QUINTIC_THIRD * symmetric_product(next_halves, next_halves, gram)
        + jnp.where(diagonal, QUINTIC_FIRST, 0.0)
    )
    return symmetric_product(halves(outer), base_halves, gram) * (inverse * OUT_SCALE)


def extract(padded, start, count, staged, step):
    _, slots, columns = staged.shape
    sublane = lax.broadcasted_iota(jnp.int32, (SUBLANES, columns), 0)
    shift = start % SUBLANES
    base = start - shift
    back = jnp.where(shift == 0, 0, SUBLANES - shift)

    def window(index):
        rows = pl.ds(pl.multiple_of(base + index * SUBLANES, SUBLANES), SUBLANES)
        return pltpu.roll(padded[rows, :], back, 0)

    def tile(index, here):
        after = window(index + 1)
        moved = jnp.where(sublane < SUBLANES - shift, here, after)
        rows = pl.ds(pl.multiple_of(index * SUBLANES, SUBLANES), SUBLANES)
        staged[step, rows, :] = jnp.where(sublane < count - index * SUBLANES, moved, 0.0)
        return after

    over_tiles(slots // SUBLANES, tile, window(0))


def update_kernel(first, steps, *refs):
    tables, (packed, high, low), refs = refs[:4], refs[4:7], refs[8 if first else 7 :]
    whole, refs = refs[0], refs[1:]
    homes, refs = refs[: len(steps)], refs[len(steps) :]
    gram, padded, staged, high_held, low_held, held, arrive, leave = refs[:8]
    ranks = tables[1].shape[0]
    rank = lax.axis_index("fsdp")
    incoming = [
        pltpu.make_async_copy(high, high_held, arrive.at[0]),
        pltpu.make_async_copy(low, low_held, arrive.at[1]),
    ]
    for copy in incoming:
        copy.start()
    owner_group, live_ranks, row_counts, row_offsets = fetch_tables(tables, refs[8:])
    matrix = matrix_of(owner_group, rank ^ mate(ranks) if first else rank)
    total = polynomial(unpack(packed, gram), gram)
    if first:
        for panel in range(3):
            store_panel(held, panel, total[panel * PANEL :, panel * PANEL : (panel + 1) * PANEL])
        copies = [pltpu.make_async_copy(held, whole, leave.at[len(steps)])]
        copies[0].start()
    for copy in incoming:
        copy.wait()
    padded[:INNER, :] = dot_halves(halves(total), (high_held[...], low_held[...]))
    if not first:
        copies = [pltpu.make_async_copy(padded.at[pl.ds(0, INNER)], whole, leave.at[len(steps)])]
        copies[0].start()
    for index, step in enumerate(steps):
        target = rank ^ step
        extract(padded, row_offsets[matrix, target], row_counts[matrix, target] * live_ranks[target], staged, index)
        copies.append(pltpu.make_async_copy(staged.at[index], homes[index], leave.at[index]))
        copies[-1].start()
    for copy in copies:
        copy.wait()


def finish_kernel(ranks, *refs):
    tables, (packed, iterate, inner_result, own_first, own_last, result, shards), refs = refs[:4], refs[4:11], refs[11:]
    gram, padded, staged, whole, held, arrive, leave = refs[:7]
    rank = lax.axis_index("fsdp")
    owner_group, live_ranks, row_counts, row_offsets = fetch_tables(tables, refs[7:])
    matrix = matrix_of(owner_group, rank)

    def run(jobs):
        copies = [pltpu.make_async_copy(*job) for job in jobs]
        for copy in copies:
            copy.start()
        for copy in copies:
            copy.wait()

    @pl.when(is_inner(rank, ranks))
    def _():
        run(
            [
                (inner_result, whole, arrive.at[0]),
                (own_first, staged.at[0], arrive.at[1]),
                (own_last, staged.at[1], arrive.at[2]),
            ]
        )
        other = matrix_of(owner_group, rank ^ mate(ranks))
        run(
            [
                (whole, result, leave.at[0]),
                (staged.at[0], shards.at[other], leave.at[1]),
                (staged.at[1], shards.at[matrix], leave.at[2]),
            ]
        )

    @pl.when(jnp.logical_not(is_inner(rank, ranks)))
    def _():
        run([(iterate, whole, arrive.at[0]), (packed, held, arrive.at[1])])
        padded[:INNER, :] = dot_halves(halves(unpack(held, gram)), halves(whole[...]))
        extract(padded, row_offsets[matrix, rank], row_counts[matrix, rank] * live_ranks[rank], staged, 0)
        run(
            [
                (padded.at[pl.ds(0, INNER)], result, leave.at[0]),
                (staged.at[0], shards.at[matrix], leave.at[1]),
            ]
        )


def place_kernel(first, ranks, steps, *refs):
    table, blocks, shards = refs[0], refs[1 : 1 + len(steps)], refs[2 + len(steps)]
    owner_group, arrive, leave = refs[3 + len(steps) :]
    rank = lax.axis_index("fsdp")
    fetch = pltpu.make_async_copy(table, owner_group, arrive)
    fetch.start()
    fetch.wait()
    copies = []
    for index, step in enumerate(steps):
        source = rank ^ step
        matrix = matrix_of(owner_group, source ^ mate(ranks) if first else source)
        copies.append((is_inner(source, ranks), blocks[index], shards.at[matrix], leave.at[index]))
    each_copy(copies, "start")
    each_copy(copies, "wait")


def idle_kernel(*refs):
    pass


def floats(*shape):
    return jax.ShapeDtypeStruct(shape, jnp.float32)


def vmem(*shape, dtype=jnp.float32):
    return pltpu.VMEM(shape, dtype)


def flags(*shape):
    return pltpu.SemaphoreType.DMA(shape)


FREE = pl.CostEstimate(flops=0, bytes_accessed=0, transcendentals=0)


def blend(first, tables, momentum, gradient, before):
    _, slots, columns = momentum.shape
    ranks = tables[1].shape[0]
    chunks = 4 if slots % (4 * SUBLANES) == 0 else 1
    return pl.pallas_call(
        functools.partial(blend_kernel, first, chunks),
        out_shape=[floats(slots, columns)] * ranks + [floats(SUBLANES, 128)],
        in_specs=[HBM] * 6 + [ANY] * len(before),
        out_specs=[HBM] * ranks + [VMEM],
        scratch_shapes=[vmem(ranks, slots, columns)] * 2
        + [flags(ranks, chunks, 2), flags(ranks, chunks)]
        + table_scratch(*tables[2].shape),
        compiler_params=FULL,
        cost_estimate=FREE,
        name="blend",
    )(*tables, momentum, gradient, *before)


def fresh_momentum(tables, momentum, gradient, before):
    matrices, slots, columns = momentum.shape
    block = pl.BlockSpec((None, slots, columns), lambda matrix: (matrix, 0, 0))
    return pl.pallas_call(
        fresh_kernel,
        grid=(matrices,),
        out_shape=[floats(*momentum.shape), floats(SUBLANES, 128)],
        in_specs=[pl.BlockSpec(memory_space=pltpu.SMEM)] * 2 + [block] * 2 + [ANY],
        out_specs=[block, pl.BlockSpec((SUBLANES, 128), lambda matrix: (0, 0))],
        compiler_params=FULL,
        cost_estimate=FREE,
        name="fresh_momentum",
    )(*tables[1:3], momentum, gradient, before)


def assemble_and_gram(first, tables, blocks, after):
    slots, columns = blocks[0].shape
    ranks = len(blocks)
    half = jax.ShapeDtypeStruct((INNER, columns), jnp.bfloat16)
    return pl.pallas_call(
        functools.partial(gram_kernel, first, ranks),
        out_shape=[half, half, floats(INNER, 2 * PANEL)] + [floats(INNER, columns)] * first,
        in_specs=[HBM] * 4 + [ANY] * (ranks + 1),
        out_specs=[ANY, ANY, VMEM] + [ANY] * first,
        scratch_shapes=[
            vmem(ranks, slots, columns),
            vmem(INNER + slots + SUBLANES, columns),
            vmem(INNER, columns, dtype=jnp.bfloat16),
            vmem(INNER, columns, dtype=jnp.bfloat16),
            flags(ranks),
            flags(3),
        ]
        + table_scratch(*tables[2].shape),
        compiler_params=PARAMS,
        cost_estimate=FREE,
        name="assemble_and_gram",
    )(*tables, *blocks, after)


def update_shapes(first, steps, slots, columns):
    whole = floats(INNER, 2 * PANEL if first else columns)
    return [whole] + [floats(slots, columns)] * len(steps)


def apply_update(first, steps, tables, packed, high, low, slots, *after):
    columns = high.shape[1]
    return pl.pallas_call(
        functools.partial(update_kernel, first, steps),
        out_shape=update_shapes(first, steps, slots, columns),
        in_specs=[HBM] * 4 + [VMEM] + [ANY] * (2 + len(after)),
        out_specs=[ANY] * (1 + len(steps)),
        scratch_shapes=[
            vmem(INNER, INNER),
            vmem(INNER + slots + 2 * SUBLANES, columns),
            vmem(len(steps), slots, columns),
            vmem(INNER, columns, dtype=jnp.bfloat16),
            vmem(INNER, columns, dtype=jnp.bfloat16),
            vmem(INNER, 2 * PANEL),
            flags(2),
            flags(len(steps) + 1),
        ]
        + table_scratch(*tables[2].shape),
        compiler_params=PARAMS,
        cost_estimate=FREE,
        name="apply_update",
    )(*tables, packed, high, low, *after)


def nothing(shapes):
    return pl.pallas_call(idle_kernel, out_shape=shapes, out_specs=[ANY] * len(shapes), name="nothing")()


def settle(value):
    return pl.pallas_call(
        idle_kernel,
        out_shape=floats(SUBLANES, 128),
        in_specs=[ANY],
        out_specs=ANY,
        cost_estimate=pl.CostEstimate(flops=10**11, bytes_accessed=0, transcendentals=0),
        name="settle",
    )(value)


def finish(tables, packed, iterate, inner_result, own_first, own_last, shape):
    slots, columns = own_first.shape
    return pl.pallas_call(
        functools.partial(finish_kernel, tables[1].shape[0]),
        out_shape=[floats(INNER, columns), floats(*shape)],
        in_specs=[HBM] * 4 + [ANY] * 5,
        out_specs=[HBM] * 2,
        scratch_shapes=[
            vmem(INNER, INNER),
            vmem(INNER + slots + 2 * SUBLANES, columns),
            vmem(2, slots, columns),
            vmem(INNER, columns),
            vmem(INNER, 2 * PANEL),
            flags(3),
            flags(3),
        ]
        + table_scratch(*tables[2].shape),
        compiler_params=PARAMS,
        cost_estimate=FREE,
        name="finish",
    )(*tables, packed, iterate, inner_result, own_first, own_last)


def place_blocks(first, owner_group, steps, blocks, shards, ranks):
    return pl.pallas_call(
        functools.partial(place_kernel, first, ranks, steps),
        out_shape=floats(*shards.shape),
        in_specs=[HBM] + [VMEM] * len(blocks) + [HBM],
        out_specs=HBM,
        scratch_shapes=[pltpu.SMEM(owner_group.shape, jnp.int32), flags(), flags(len(steps))],
        input_output_aliases={1 + len(blocks): 0},
        compiler_params=PARAMS,
        cost_estimate=FREE,
        name="place_blocks",
    )(owner_group, *blocks, shards)


def sum_over(block, axis):
    size = lax.axis_size(axis)
    if size & (size - 1) or block.shape[0] % size:
        return lax.psum(block, axis)
    index = lax.axis_index(axis)

    def exchange(piece, bits):
        return lax.ppermute(piece, axis, [(i, i ^ bits[i & 1]) for i in range(size)])

    def mine(bits, part):
        bit = jnp.where(index & 1, bits[1], bits[0])
        return jnp.where(index & bit, part, 0)

    chips = [1 << shift for shift in range(1, size.bit_length() - 1)]
    stages = [(1, 1), *zip(chips, reversed(chips))]
    for bits in stages:
        part = block.shape[0] // 2
        keep = mine(bits, part)
        away = exchange(lax.dynamic_slice_in_dim(block, part - keep, part, 0), bits)
        block = lax.dynamic_slice_in_dim(block, keep, part, 0) + away
    for bits in reversed(stages):
        part = block.shape[0]
        keep = mine(bits, part)
        away = exchange(block, bits)
        whole = jnp.zeros((2 * part, block.shape[1]), block.dtype)
        whole = lax.dynamic_update_slice_in_dim(whole, block, keep, 0)
        block = lax.dynamic_update_slice_in_dim(whole, away, part - keep, 0)
    return block


def on_device(momentum, gradient, live_ranks, owner_group, row_counts, row_offsets):
    ranks = lax.axis_size("fsdp")
    my_rank = lax.axis_index("fsdp")
    _, slots, columns = momentum.shape
    tables = (owner_group, live_ranks, row_counts, row_offsets)
    inner = is_inner(my_rank, ranks)
    last = [2, 1, *range(3, ranks)]
    early = [step for step in last if step != mate(ranks)]

    def pairs(step, inward):
        return [(i, i ^ step) for i in range(ranks) if is_inner(i ^ step if inward else i, ranks)]

    def to_inner(block, step):
        return lax.ppermute(block, "fsdp", pairs(step, True))

    def from_inner(block, step):
        return lax.ppermute(block, "fsdp", pairs(step, False))

    *blends, token = blend(True, tables, momentum, gradient, [])
    first_blocks = [blends[0]] + [to_inner(blends[step], step) for step in range(1, ranks)]
    *blends, token = blend(False, tables, momentum, gradient, [token])
    last_blocks = [blends[0]] + [to_inner(blends[step], step) for step in range(1, ranks)]
    new_momentum, token = fresh_momentum(tables, momentum, gradient, token)

    high, low, gram_part, iterate = assemble_and_gram(True, tables, first_blocks, token)
    iterate = from_inner(iterate, mate(ranks))

    def first_update(high, low, gram_part, after):
        return apply_update(True, [0, *early], tables, sum_over(gram_part, "tensor"), high, low, slots, after)

    def first_skip(high, low, gram_part, after):
        return nothing(update_shapes(True, [0, *early], slots, columns))

    packed, own_first, *homes = lax.cond(inner, first_update, first_skip, high, low, gram_part, settle(gram_part))
    packed_there = from_inner(packed, mate(ranks))
    first_home = [from_inner(block, step) for step, block in zip(early, homes)]

    def last_update(after, *blocks):
        high, low, gram_part = assemble_and_gram(False, tables, blocks, after)
        return apply_update(False, [0, *last], tables, sum_over(gram_part, "tensor"), high, low, slots)

    def last_skip(after, *blocks):
        return nothing(update_shapes(False, [0, *last], slots, columns))

    result, own_last, *homes = lax.cond(inner, last_update, last_skip, packed, *last_blocks)
    last_home = [from_inner(block, step) for step, block in zip(last, homes)]

    result, shards = finish(tables, packed_there, iterate, result, own_first, own_last, momentum.shape)
    shards = place_blocks(True, owner_group, early, first_home, shards, ranks)
    for step, block in zip(last, last_home):
        shards = place_blocks(False, owner_group, [step], [block], shards, ranks)
    return (new_momentum, shards, result[None])


def solution(mesh):
    placed = (P(None, "fsdp", "tensor"), P(None, "fsdp", "tensor"), P(), P(), P(), P())
    return jax.shard_map(
        on_device,
        mesh=mesh,
        in_specs=placed,
        out_specs=(P(None, "fsdp", "tensor"), P(None, "fsdp", "tensor"), P("fsdp", None, "tensor")),
        check_vma=False,
    )
```

```python
import functools
import math

import jax
import jax.numpy as jnp
from jax import lax
from jax.experimental import pallas as pl
from jax.experimental.pallas import tpu as pltpu
from jax.sharding import PartitionSpec as P

WIDTH = 7168
INNER = 576
PANEL = INNER // 3
TILE = 256
SUBLANES = 8

MOMENTUM_RATE = 0.95
QUINTIC_FIRST = 3.4445
QUINTIC_SECOND = -4.775
QUINTIC_THIRD = 2.0315
EPSILON = 1e-07
OUT_SCALE = 0.2 * math.sqrt(max(INNER, WIDTH))
SMALL = pltpu.CompilerParams(vmem_limit_bytes=1024 * 1024)
FULL = pltpu.CompilerParams(vmem_limit_bytes=60 * 1024 * 1024)
PARAMS = pltpu.CompilerParams(vmem_limit_bytes=24 * 1024 * 1024)
HBM = pl.BlockSpec(memory_space=pltpu.HBM)
ANY = pl.BlockSpec(memory_space=pl.ANY)
VMEM = pl.BlockSpec(memory_space=pltpu.VMEM)


def halves(value):
    high = value.astype(jnp.bfloat16)
    low = (value - high.astype(jnp.float32)).astype(jnp.bfloat16)
    return high, low


def dot(left, right, contract):
    return lax.dot_general(left, right, (contract, ((), ())), preferred_element_type=jnp.float32)


def dot_halves(left, right, contract=((1,), (0,))):
    (left_high, left_low), (right_high, right_low) = left, right
    depth = left_high.shape[1]
    body = depth // TILE * TILE
    if contract == ((1,), (0,)) and 0 < 3 * (depth - body) <= TILE:
        rest_left = jnp.concatenate([left_high[:, body:], left_low[:, body:], left_high[:, body:]], axis=1)
        rest_right = jnp.concatenate([right_low[body:], right_high[body:], right_high[body:]], axis=0)
        left = left_high[:, :body], left_low[:, :body]
        right = right_high[:body], right_low[:body]
        return dot(rest_left, rest_right, contract) + dot_halves(left, right)
    return (
        dot(left_high, right_low, contract) + dot(left_low, right_high, contract)
    ) + dot(left_high, right_high, contract)


def is_inner(rank, ranks):
    low = ranks // 4
    return (rank >= low) & (rank < ranks - low)


def mate(ranks):
    return ranks // 4


def table_scratch(matrices, ranks):
    return [
        pltpu.SMEM((matrices,), jnp.int32),
        pltpu.SMEM((ranks,), jnp.int32),
        pltpu.SMEM((matrices, ranks), jnp.int32),
        pltpu.SMEM((matrices, ranks), jnp.int32),
        pltpu.SemaphoreType.DMA((4,)),
    ]


def fetch_tables(tables, held):
    *places, arrive = held
    copies = [
        pltpu.make_async_copy(table, place, arrive.at[index])
        for index, (table, place) in enumerate(zip(tables, places))
    ]
    for copy in copies:
        copy.start()
    for copy in copies:
        copy.wait()
    return places


def matrix_of(owner_group, rank):
    found = jnp.int32(0)
    for matrix in range(owner_group.shape[0]):
        found = jnp.where(owner_group[matrix] == rank, matrix, found)
    return found


def over_tiles(tiles, body, carry):
    group = next(group for group in (6, 3, 2, 1) if tiles % group == 0)

    def step(index, carry):
        for member in range(group):
            carry = body(index * group + member, carry)
        return carry

    return lax.fori_loop(0, tiles // group, step, carry)


def each_copy(copies, action):
    for condition, source, place, flag in copies:

        @pl.when(condition)
        def _(source=source, place=place, flag=flag):
            getattr(pltpu.make_async_copy(source, place, flag), action)()


def blend_kernel(first, chunks, *refs):
    tables, (momentum, gradient) = refs[:4], refs[4:6]
    ranks = tables[1].shape[0]
    *outs, token, olds, grads, arrive, leave = refs[-ranks - 10 : -5]
    owner_group, live_ranks, row_counts, _ = fetch_tables(tables, refs[-5:])
    rank = lax.axis_index("fsdp")
    slots, columns = outs[0].shape
    size = slots // chunks
    jobs = []
    for step in [*range(1, ranks), 0]:
        target = rank ^ step
        matrix = matrix_of(owner_group, target ^ mate(ranks) if first else target)
        count = row_counts[matrix, rank] * live_ranks[rank]
        for chunk in range(chunks):
            part = pl.ds(chunk * size, size)
            flags = arrive.at[step, chunk, 0], arrive.at[step, chunk, 1]
            incoming = (
                (is_inner(target, ranks), momentum.at[matrix, part], olds.at[step, part], flags[0]),
                (is_inner(target, ranks), gradient.at[matrix, part], grads.at[step, part], flags[1]),
            )
            outgoing = (is_inner(target, ranks), olds.at[step, part], outs[step].at[part], leave.at[step, chunk])
            jobs.append((step, chunk, count, incoming, outgoing))
            each_copy(incoming, "start")
    token[...] = jnp.zeros_like(token)
    for step, chunk, count, incoming, outgoing in jobs:

        @pl.when(incoming[0][0])
        def _(step=step, chunk=chunk, count=count, incoming=incoming, outgoing=outgoing):
            for _, source, place, flag in incoming:
                pltpu.make_async_copy(source, place, flag).wait()
            rows = slice(chunk * size, (chunk + 1) * size)
            grad_now = grads[step, rows, :]
            fresh = MOMENTUM_RATE * olds[step, rows, :] + grad_now
            position = lax.broadcasted_iota(jnp.int32, (size, columns), 0) + chunk * size
            olds[step, rows, :] = jnp.where(position < count, grad_now + MOMENTUM_RATE * fresh, 0.0)
            pltpu.make_async_copy(*outgoing[1:]).start()

    each_copy([job[-1] for job in jobs], "wait")


def fresh_kernel(live_ranks, row_counts, momentum, gradient, _, out, token):
    token[...] = jnp.zeros_like(token)
    rank, matrix = lax.axis_index("fsdp"), pl.program_id(0)
    position = lax.broadcasted_iota(jnp.int32, out.shape, 0)
    keep = position < row_counts[matrix, rank] * live_ranks[rank]
    out[...] = jnp.where(keep, MOMENTUM_RATE * momentum[...] + gradient[...], 0.0)


def gram_kernel(first, ranks, *refs):
    tables, blocks, refs = refs[:4], refs[4 : 4 + ranks], refs[5 + ranks :]
    high_out, low_out, keep, send = refs[:4]
    landed, padded, high_held, low_held, gram, arrive, leave = refs[-12:-5]
    slots, columns = blocks[0].shape
    rank = lax.axis_index("fsdp")

    @pl.when(is_inner(rank, ranks))
    def _():
        copies = []
        for step in range(ranks):
            copies.append(pltpu.make_async_copy(blocks[step], landed.at[step], arrive.at[step]))
            copies[-1].start()
        owner_group, _, _, row_offsets = fetch_tables(tables, refs[-5:])
        matrix = matrix_of(owner_group, rank ^ mate(ranks) if first else rank)
        padded[...] = jnp.zeros_like(padded)
        sublane = lax.broadcasted_iota(jnp.int32, (SUBLANES, columns), 0)
        for step in range(ranks):
            start = row_offsets[matrix, rank ^ step]
            shift = start % SUBLANES
            base = start - shift
            copies[step].wait()

            def tile(index, before, base=base, shift=shift, step=step):
                moved = pltpu.roll(landed[step, pl.ds(pl.multiple_of(index * SUBLANES, SUBLANES), SUBLANES), :], shift, 0)
                rows = pl.ds(pl.multiple_of(base + index * SUBLANES, SUBLANES), SUBLANES)
                padded[rows, :] = padded[rows, :] + jnp.where(sublane < shift, before, moved)
                return moved

            after = over_tiles(slots // SUBLANES, tile, jnp.zeros((SUBLANES, columns), jnp.float32))
            rows = pl.ds(pl.multiple_of(base + slots, SUBLANES), SUBLANES)
            padded[rows, :] = padded[rows, :] + jnp.where(sublane < shift, after, 0.0)
        high, low = halves(padded[:INNER, :])
        high_held[...] = high
        low_held[...] = low
        outgoing = [
            pltpu.make_async_copy(high_held, high_out, leave.at[0]),
            pltpu.make_async_copy(low_held, low_out, leave.at[1]),
        ]
        if first:
            outgoing.append(pltpu.make_async_copy(padded.at[pl.ds(0, INNER)], refs[4], leave.at[2]))
        for copy in outgoing:
            copy.start()
        for panel in range(3):
            here = slice(panel * PANEL, (panel + 1) * PANEL)
            part = dot_halves((high[panel * PANEL :], low[panel * PANEL :]), (high[here], low[here]), ((1,), (1,)))
            store_panel(gram, panel, part)
        mine, other = core_rows()
        keep[...] = gram[mine, :]
        send[...] = gram[other, :]
        for copy in outgoing:
            copy.wait()


def core_rows():
    half = INNER // 2
    first = (lax.axis_index("tensor") & 1) * half
    return tuple(pl.ds(pl.multiple_of(start, SUBLANES), half) for start in (first, half - first))


def store_panel(packed, panel, part):
    if panel == 0:
        packed[:, :PANEL] = part
    elif panel == 1:
        packed[: 2 * PANEL, PANEL:] = part
    else:
        packed[2 * PANEL :, PANEL:] = part


def unpack(packed, gram):
    gram[:, :PANEL] = packed[:, :PANEL]
    gram[PANEL:, PANEL : 2 * PANEL] = packed[: 2 * PANEL, PANEL:]
    gram[2 * PANEL :, 2 * PANEL :] = packed[2 * PANEL :, PANEL:]
    gram[:PANEL, PANEL:] = packed[PANEL:, :PANEL].T
    gram[PANEL : 2 * PANEL, 2 * PANEL :] = packed[PANEL : 2 * PANEL, PANEL:].T
    return gram[...]


def symmetric_product(left, right, out):
    for begin in range(0, INNER, TILE):
        end = min(begin + TILE, INNER)
        part = dot_halves(tuple(half[begin:] for half in left), tuple(half[:, begin:end] for half in right))
        out[begin:, begin:end] = part
        if end < INNER:
            out[begin:end, end:] = part[end - begin :].T
    return out[...]


def polynomial(raw, gram):
    diagonal = lax.broadcasted_iota(jnp.int32, raw.shape, 0) == lax.broadcasted_iota(jnp.int32, raw.shape, 1)
    square_total = jnp.sum(jnp.where(diagonal, raw, 0.0))
    norm = jnp.sqrt(jnp.full((1, 1), square_total, jnp.float32)) + EPSILON
    inverse = 1.0 / norm
    first = (raw * inverse) * inverse
    first_halves = halves(first)
    second = symmetric_product(first_halves, first_halves, gram)
    base = QUINTIC_SECOND * first + QUINTIC_THIRD * second + jnp.where(diagonal, QUINTIC_FIRST, 0.0)
    base_halves = halves(base)
    third_halves = halves(symmetric_product(base_halves, first_halves, gram))
    next_gram = symmetric_product(base_halves, third_halves, gram)
    next_halves = halves(next_gram)
    outer = (
        QUINTIC_SECOND * next_gram
        + QUINTIC_THIRD * symmetric_product(next_halves, next_halves, gram)
        + jnp.where(diagonal, QUINTIC_FIRST, 0.0)
    )
    return symmetric_product(halves(outer), base_halves, gram) * (inverse * OUT_SCALE)


def extract(padded, start, count, staged, step):
    _, slots, columns = staged.shape
    sublane = lax.broadcasted_iota(jnp.int32, (SUBLANES, columns), 0)
    shift = start % SUBLANES
    base = start - shift
    back = jnp.where(shift == 0, 0, SUBLANES - shift)

    def window(index):
        rows = pl.ds(pl.multiple_of(base + index * SUBLANES, SUBLANES), SUBLANES)
        return pltpu.roll(padded[rows, :], back, 0)

    def tile(index, here):
        after = window(index + 1)
        moved = jnp.where(sublane < SUBLANES - shift, here, after)
        rows = pl.ds(pl.multiple_of(index * SUBLANES, SUBLANES), SUBLANES)
        staged[step, rows, :] = jnp.where(sublane < count - index * SUBLANES, moved, 0.0)
        return after

    over_tiles(slots // SUBLANES, tile, window(0))


def update_kernel(first, steps, *refs):
    tables, (keep, away, high, low), refs = refs[:4], refs[4:8], refs[9 if first else 8 :]
    whole, refs = refs[0], refs[1:]
    homes, refs = refs[: len(steps)], refs[len(steps) :]
    gram, padded, staged, high_held, low_held, held, arrive, leave = refs[:8]
    ranks = tables[1].shape[0]
    rank = lax.axis_index("fsdp")

    @pl.when(is_inner(rank, ranks))
    def _():
        incoming = [
            pltpu.make_async_copy(high, high_held, arrive.at[0]),
            pltpu.make_async_copy(low, low_held, arrive.at[1]),
        ]
        for copy in incoming:
            copy.start()
        owner_group, live_ranks, row_counts, row_offsets = fetch_tables(tables, refs[8:])
        matrix = matrix_of(owner_group, rank ^ mate(ranks) if first else rank)
        mine, other = core_rows()
        held[mine, :] = keep[...]
        held[other, :] = away[...]
        total = polynomial(unpack(held, gram), gram)
        copies = []
        if first:
            for panel in range(3):
                store_panel(held, panel, total[panel * PANEL :, panel * PANEL : (panel + 1) * PANEL])
            copies = [pltpu.make_async_copy(held, whole, leave.at[len(steps)])]
            copies[0].start()
        for copy in incoming:
            copy.wait()
        padded[:INNER, :] = dot_halves(halves(total), (high_held[...], low_held[...]))
        if not first:
            copies = [pltpu.make_async_copy(padded.at[pl.ds(0, INNER)], whole, leave.at[len(steps)])]
            copies[0].start()
        for index, step in enumerate(steps):
            target = rank ^ step
            count = row_counts[matrix, target] * live_ranks[target]
            extract(padded, row_offsets[matrix, target], count, staged, index)
            copies.append(pltpu.make_async_copy(staged.at[index], homes[index], leave.at[index]))
            copies[-1].start()
        for copy in copies:
            copy.wait()


def finish_kernel(ranks, *refs):
    tables, (packed, iterate, inner_result, own_first, own_last, result, shards), refs = refs[:4], refs[4:11], refs[11:]
    gram, padded, staged, whole, held, arrive, leave = refs[:7]
    rank = lax.axis_index("fsdp")
    owner_group, live_ranks, row_counts, row_offsets = fetch_tables(tables, refs[7:])
    matrix = matrix_of(owner_group, rank)

    def run(jobs):
        copies = [pltpu.make_async_copy(*job) for job in jobs]
        for copy in copies:
            copy.start()
        for copy in copies:
            copy.wait()

    @pl.when(is_inner(rank, ranks))
    def _():
        run(
            [
                (inner_result, whole, arrive.at[0]),
                (own_first, staged.at[0], arrive.at[1]),
                (own_last, staged.at[1], arrive.at[2]),
            ]
        )
        other = matrix_of(owner_group, rank ^ mate(ranks))
        run(
            [
                (whole, result, leave.at[0]),
                (staged.at[0], shards.at[other], leave.at[1]),
                (staged.at[1], shards.at[matrix], leave.at[2]),
            ]
        )

    @pl.when(jnp.logical_not(is_inner(rank, ranks)))
    def _():
        run([(iterate, whole, arrive.at[0]), (packed, held, arrive.at[1])])
        padded[:INNER, :] = dot_halves(halves(unpack(held, gram)), halves(whole[...]))
        extract(padded, row_offsets[matrix, rank], row_counts[matrix, rank] * live_ranks[rank], staged, 0)
        run(
            [
                (padded.at[pl.ds(0, INNER)], result, leave.at[0]),
                (staged.at[0], shards.at[matrix], leave.at[1]),
            ]
        )


def place_kernel(first, ranks, steps, *refs):
    table, blocks, shards = refs[0], refs[1 : 1 + len(steps)], refs[2 + len(steps)]
    owner_group, arrive, leave = refs[3 + len(steps) :]
    rank = lax.axis_index("fsdp")
    fetch = pltpu.make_async_copy(table, owner_group, arrive)
    fetch.start()
    fetch.wait()
    copies = []
    for index, step in enumerate(steps):
        source = rank ^ step
        matrix = matrix_of(owner_group, source ^ mate(ranks) if first else source)
        copies.append((is_inner(source, ranks), blocks[index], shards.at[matrix], leave.at[index]))
    each_copy(copies, "start")
    each_copy(copies, "wait")


def idle_kernel(*refs):
    pass


def floats(*shape):
    return jax.ShapeDtypeStruct(shape, jnp.float32)


def vmem(*shape, dtype=jnp.float32):
    return pltpu.VMEM(shape, dtype)


def flags(*shape):
    return pltpu.SemaphoreType.DMA(shape)


FREE = pl.CostEstimate(flops=0, bytes_accessed=0, transcendentals=0)


def blend(first, tables, momentum, gradient, before):
    _, slots, columns = momentum.shape
    ranks = tables[1].shape[0]
    chunks = 4 if slots % (4 * SUBLANES) == 0 else 1
    return pl.pallas_call(
        functools.partial(blend_kernel, first, chunks),
        out_shape=[floats(slots, columns)] * ranks + [floats(SUBLANES, 128)],
        in_specs=[HBM] * 6 + [ANY] * len(before),
        out_specs=[HBM] * ranks + [VMEM],
        scratch_shapes=[vmem(ranks, slots, columns)] * 2
        + [flags(ranks, chunks, 2), flags(ranks, chunks)]
        + table_scratch(*tables[2].shape),
        compiler_params=FULL,
        cost_estimate=FREE,
        name="blend",
    )(*tables, momentum, gradient, *before)


def fresh_momentum(tables, momentum, gradient, before):
    matrices, slots, columns = momentum.shape
    block = pl.BlockSpec((None, slots, columns), lambda matrix: (matrix, 0, 0))
    return pl.pallas_call(
        fresh_kernel,
        grid=(matrices,),
        out_shape=[floats(*momentum.shape), floats(SUBLANES, 128)],
        in_specs=[pl.BlockSpec(memory_space=pltpu.SMEM)] * 2 + [block] * 2 + [ANY],
        out_specs=[block, pl.BlockSpec((SUBLANES, 128), lambda matrix: (0, 0))],
        compiler_params=FULL,
        cost_estimate=FREE,
        name="fresh_momentum",
    )(*tables[1:3], momentum, gradient, before)


def assemble_and_gram(first, tables, blocks, after):
    slots, columns = blocks[0].shape
    ranks = len(blocks)
    half = jax.ShapeDtypeStruct((INNER, columns), jnp.bfloat16)
    return pl.pallas_call(
        functools.partial(gram_kernel, first, ranks),
        out_shape=[half, half] + [floats(INNER // 2, 2 * PANEL)] * 2 + [floats(INNER, columns)] * first,
        in_specs=[HBM] * 4 + [ANY] * ranks + [HBM],
        out_specs=[HBM, HBM, VMEM, VMEM] + [ANY] * first,
        scratch_shapes=[
            vmem(ranks, slots, columns),
            vmem(INNER + slots + SUBLANES, columns),
            vmem(INNER, columns, dtype=jnp.bfloat16),
            vmem(INNER, columns, dtype=jnp.bfloat16),
            vmem(INNER, 2 * PANEL),
            flags(ranks),
            flags(3),
        ]
        + table_scratch(*tables[2].shape),
        compiler_params=PARAMS,
        cost_estimate=FREE,
        name="assemble_and_gram",
    )(*tables, *blocks, after)


def update_shapes(first, steps, slots, columns):
    whole = floats(INNER, 2 * PANEL if first else columns)
    return [whole] + [floats(slots, columns)] * len(steps)


def nothing(shapes):
    return pl.pallas_call(
        idle_kernel, out_shape=shapes, out_specs=[ANY] * len(shapes), compiler_params=SMALL, name="nothing"
    )()


def apply_update(first, steps, tables, keep, away, high, low, slots, *after):
    columns = high.shape[1]
    return pl.pallas_call(
        functools.partial(update_kernel, first, steps),
        out_shape=update_shapes(first, steps, slots, columns),
        in_specs=[HBM] * 4 + [VMEM] * 2 + [HBM] * 2 + [ANY] * len(after),
        out_specs=[ANY] * (1 + len(steps)),
        scratch_shapes=[
            vmem(INNER, INNER),
            vmem(INNER + slots + 2 * SUBLANES, columns),
            vmem(len(steps), slots, columns),
            vmem(INNER, columns, dtype=jnp.bfloat16),
            vmem(INNER, columns, dtype=jnp.bfloat16),
            vmem(INNER, 2 * PANEL),
            flags(2),
            flags(len(steps) + 1),
        ]
        + table_scratch(*tables[2].shape),
        compiler_params=PARAMS,
        cost_estimate=FREE,
        name="apply_update",
    )(*tables, keep, away, high, low, *after)


def settle(value):
    return pl.pallas_call(
        idle_kernel,
        out_shape=floats(SUBLANES, 128),
        in_specs=[ANY],
        out_specs=ANY,
        compiler_params=SMALL,
        cost_estimate=pl.CostEstimate(flops=10**11, bytes_accessed=0, transcendentals=0),
        name="settle",
    )(value)


def finish(tables, packed, iterate, inner_result, own_first, own_last, shape):
    slots, columns = own_first.shape
    return pl.pallas_call(
        functools.partial(finish_kernel, tables[1].shape[0]),
        out_shape=[floats(INNER, columns), floats(*shape)],
        in_specs=[HBM] * 4 + [ANY] * 5,
        out_specs=[HBM] * 2,
        scratch_shapes=[
            vmem(INNER, INNER),
            vmem(INNER + slots + 2 * SUBLANES, columns),
            vmem(2, slots, columns),
            vmem(INNER, columns),
            vmem(INNER, 2 * PANEL),
            flags(3),
            flags(3),
        ]
        + table_scratch(*tables[2].shape),
        compiler_params=PARAMS,
        cost_estimate=FREE,
        name="finish",
    )(*tables, packed, iterate, inner_result, own_first, own_last)


def place_blocks(first, owner_group, steps, blocks, shards, ranks):
    return pl.pallas_call(
        functools.partial(place_kernel, first, ranks, steps),
        out_shape=floats(*shards.shape),
        in_specs=[HBM] + [VMEM] * len(blocks) + [HBM],
        out_specs=HBM,
        scratch_shapes=[pltpu.SMEM(owner_group.shape, jnp.int32), flags(), flags(len(steps))],
        input_output_aliases={1 + len(blocks): 0},
        compiler_params=PARAMS,
        cost_estimate=FREE,
        name="place_blocks",
    )(owner_group, *blocks, shards)


def sum_halves(keep, send, axis):
    size = lax.axis_size(axis)

    def exchange(piece, bits):
        return lax.ppermute(piece, axis, [(i, i ^ bits[i & 1]) for i in range(size)])

    chips = [1 << shift for shift in range(1, size.bit_length() - 1)]
    keep = keep + exchange(send, (1, 1))
    for bits in zip(chips, reversed(chips)):
        keep = keep + exchange(keep, bits)
    return keep, exchange(keep, (1, 1))


def on_device(momentum, gradient, live_ranks, owner_group, row_counts, row_offsets):
    ranks = lax.axis_size("fsdp")
    _, slots, columns = momentum.shape
    inner = is_inner(lax.axis_index("fsdp"), ranks)
    tables = (owner_group, live_ranks, row_counts, row_offsets)
    last = [2, 1, *range(3, ranks)]
    early = [step for step in last if step != mate(ranks)]

    def pairs(step, inward):
        return [(i, i ^ step) for i in range(ranks) if is_inner(i ^ step if inward else i, ranks)]

    def to_inner(block, step):
        return lax.ppermute(block, "fsdp", pairs(step, True))

    def from_inner(block, step):
        return lax.ppermute(block, "fsdp", pairs(step, False))

    *blends, token = blend(True, tables, momentum, gradient, [])
    first_blocks = [blends[0]] + [to_inner(blends[step], step) for step in range(1, ranks)]
    *blends, token = blend(False, tables, momentum, gradient, [token])
    last_blocks = [blends[0]] + [to_inner(blends[step], step) for step in range(1, ranks)]
    new_momentum, token = fresh_momentum(tables, momentum, gradient, token)

    high, low, keep, send, iterate = assemble_and_gram(True, tables, first_blocks, token)
    iterate = from_inner(iterate, mate(ranks))

    def first_update(high, low, keep, send, after):
        return apply_update(
            True, [0, *early], tables, *sum_halves(keep, send, "tensor"), high, low, slots, after
        )

    def first_skip(*_):
        return nothing(update_shapes(True, [0, *early], slots, columns))

    packed, own_first, *homes = lax.cond(inner, first_update, first_skip, high, low, keep, send, settle(keep))
    packed_there = from_inner(packed, mate(ranks))
    first_home = [from_inner(block, step) for step, block in zip(early, homes)]

    def last_update(after, *blocks):
        high, low, keep, send = assemble_and_gram(False, tables, blocks, after)
        return apply_update(False, [0, *last], tables, *sum_halves(keep, send, "tensor"), high, low, slots)

    def last_skip(*_):
        return nothing(update_shapes(False, [0, *last], slots, columns))

    result, own_last, *homes = lax.cond(inner, last_update, last_skip, packed, *last_blocks)
    last_home = [from_inner(block, step) for step, block in zip(last, homes)]

    result, shards = finish(tables, packed_there, iterate, result, own_first, own_last, momentum.shape)
    shards = place_blocks(True, owner_group, early, first_home, shards, ranks)
    for step, block in zip(last, last_home):
        shards = place_blocks(False, owner_group, [step], [block], shards, ranks)
    return (new_momentum, shards, result[None])


def solution(mesh):
    placed = (P(None, "fsdp", "tensor"), P(None, "fsdp", "tensor"), P(), P(), P(), P())
    return jax.shard_map(
        on_device,
        mesh=mesh,
        in_specs=placed,
        out_specs=(P(None, "fsdp", "tensor"), P(None, "fsdp", "tensor"), P("fsdp", None, "tensor")),
        check_vma=False,
    )
```

```python
import functools
import math

import jax
import jax.numpy as jnp
from jax import lax
from jax.experimental import pallas as pl
from jax.experimental.pallas import tpu as pltpu
from jax.sharding import PartitionSpec as P

WIDTH = 7168
INNER = 576
PANEL = INNER // 3
TILE = 256
SUBLANES = 8

MOMENTUM_RATE = 0.95
QUINTIC_FIRST = 3.4445
QUINTIC_SECOND = -4.775
QUINTIC_THIRD = 2.0315
EPSILON = 1e-07
OUT_SCALE = 0.2 * math.sqrt(max(INNER, WIDTH))
SMALL = pltpu.CompilerParams(vmem_limit_bytes=1024 * 1024)
FULL = pltpu.CompilerParams(vmem_limit_bytes=60 * 1024 * 1024)
PARAMS = pltpu.CompilerParams(vmem_limit_bytes=24 * 1024 * 1024)
HBM = pl.BlockSpec(memory_space=pltpu.HBM)
ANY = pl.BlockSpec(memory_space=pl.ANY)
VMEM = pl.BlockSpec(memory_space=pltpu.VMEM)


def halves(value):
    high = value.astype(jnp.bfloat16)
    low = (value - high.astype(jnp.float32)).astype(jnp.bfloat16)
    return high, low


def dot(left, right, contract=((1,), (0,))):
    return lax.dot_general(left, right, (contract, ((), ())), preferred_element_type=jnp.float32)


DEPTH = INNER // TILE * TILE
PARTS = [(side, rows) for rows in ((0, DEPTH), (DEPTH, INNER)) if rows[0] < rows[1] for side in (1, 0, 0)]


def passes_left(value):
    high, low = halves(value)
    return jnp.concatenate(
        [part[:, first:last] for first, last in ((0, DEPTH), (DEPTH, INNER)) for part in (high, low, high)], axis=1
    )


def passes_right(value):
    sides = halves(value)
    return jnp.concatenate([sides[side][first:last] for side, (first, last) in PARTS], axis=0)


def is_inner(rank, ranks):
    low = ranks // 4
    return (rank >= low) & (rank < ranks - low)


def mate(ranks):
    return ranks // 4


def table_scratch(matrices, ranks):
    return [
        pltpu.SMEM((matrices,), jnp.int32),
        pltpu.SMEM((ranks,), jnp.int32),
        pltpu.SMEM((matrices, ranks), jnp.int32),
        pltpu.SMEM((matrices, ranks), jnp.int32),
        pltpu.SemaphoreType.DMA((4,)),
    ]


def fetch_tables(tables, held):
    *places, arrive = held
    copies = [
        pltpu.make_async_copy(table, place, arrive.at[index])
        for index, (table, place) in enumerate(zip(tables, places))
    ]
    for copy in copies:
        copy.start()
    for copy in copies:
        copy.wait()
    return places


def matrix_of(owner_group, rank):
    found = jnp.int32(0)
    for matrix in range(owner_group.shape[0]):
        found = jnp.where(owner_group[matrix] == rank, matrix, found)
    return found


def over_tiles(tiles, body, carry):
    group = next(group for group in (6, 3, 2, 1) if tiles % group == 0)

    def step(index, carry):
        for member in range(group):
            carry = body(index * group + member, carry)
        return carry

    return lax.fori_loop(0, tiles // group, step, carry)


def each_copy(copies, action):
    for condition, source, place, flag in copies:

        @pl.when(condition)
        def _(source=source, place=place, flag=flag):
            getattr(pltpu.make_async_copy(source, place, flag), action)()


def blend_kernel(first, chunks, *refs):
    tables, (momentum, gradient) = refs[:4], refs[4:6]
    ranks = tables[1].shape[0]
    *outs, token, olds, grads, arrive, leave = refs[-ranks - 10 : -5]
    owner_group, live_ranks, row_counts, _ = fetch_tables(tables, refs[-5:])
    rank = lax.axis_index("fsdp")
    slots, columns = outs[0].shape
    size = slots // chunks
    jobs = []
    for step in [*range(1, ranks), 0]:
        target = rank ^ step
        matrix = matrix_of(owner_group, target ^ mate(ranks) if first else target)
        count = row_counts[matrix, rank] * live_ranks[rank]
        for chunk in range(chunks):
            part = pl.ds(chunk * size, size)
            flags = arrive.at[step, chunk, 0], arrive.at[step, chunk, 1]
            incoming = (
                (is_inner(target, ranks), momentum.at[matrix, part], olds.at[step, part], flags[0]),
                (is_inner(target, ranks), gradient.at[matrix, part], grads.at[step, part], flags[1]),
            )
            outgoing = (is_inner(target, ranks), olds.at[step, part], outs[step].at[part], leave.at[step, chunk])
            jobs.append((step, chunk, count, incoming, outgoing))
            each_copy(incoming, "start")
    token[...] = jnp.zeros_like(token)
    for step, chunk, count, incoming, outgoing in jobs:

        @pl.when(incoming[0][0])
        def _(step=step, chunk=chunk, count=count, incoming=incoming, outgoing=outgoing):
            for _, source, place, flag in incoming:
                pltpu.make_async_copy(source, place, flag).wait()
            rows = slice(chunk * size, (chunk + 1) * size)
            grad_now = grads[step, rows, :]
            fresh = MOMENTUM_RATE * olds[step, rows, :] + grad_now
            position = lax.broadcasted_iota(jnp.int32, (size, columns), 0) + chunk * size
            olds[step, rows, :] = jnp.where(position < count, grad_now + MOMENTUM_RATE * fresh, 0.0)
            pltpu.make_async_copy(*outgoing[1:]).start()

    each_copy([job[-1] for job in jobs], "wait")


def fresh_kernel(live_ranks, row_counts, momentum, gradient, _, out, token):
    token[...] = jnp.zeros_like(token)
    rank, matrix = lax.axis_index("fsdp"), pl.program_id(0)
    position = lax.broadcasted_iota(jnp.int32, out.shape, 0)
    keep = position < row_counts[matrix, rank] * live_ranks[rank]
    out[...] = jnp.where(keep, MOMENTUM_RATE * momentum[...] + gradient[...], 0.0)


def gram_kernel(first, ranks, *refs):
    tables, blocks, refs = refs[:4], refs[4 : 4 + ranks], refs[(4 if first else 5) + ranks :]
    pair, keep, send = refs[:3]
    landed, padded, high_held, low_held, gram, arrive, leave = refs[-12:-5]
    slots, columns = blocks[0].shape
    rank = lax.axis_index("fsdp")

    @pl.when(is_inner(rank, ranks))
    def _():
        copies = []
        for step in range(ranks):
            copies.append(pltpu.make_async_copy(blocks[step], landed.at[step], arrive.at[step]))
            copies[-1].start()
        owner_group, _, _, row_offsets = fetch_tables(tables, refs[-5:])
        matrix = matrix_of(owner_group, rank ^ mate(ranks) if first else rank)
        padded[...] = jnp.zeros_like(padded)
        sublane = lax.broadcasted_iota(jnp.int32, (SUBLANES, columns), 0)
        for step in range(ranks):
            start = row_offsets[matrix, rank ^ step]
            shift = start % SUBLANES
            base = start - shift
            copies[step].wait()

            def tile(index, before, base=base, shift=shift, step=step):
                moved = pltpu.roll(landed[step, pl.ds(pl.multiple_of(index * SUBLANES, SUBLANES), SUBLANES), :], shift, 0)
                rows = pl.ds(pl.multiple_of(base + index * SUBLANES, SUBLANES), SUBLANES)
                padded[rows, :] = padded[rows, :] + jnp.where(sublane < shift, before, moved)
                return moved

            after = over_tiles(slots // SUBLANES, tile, jnp.zeros((SUBLANES, columns), jnp.float32))
            rows = pl.ds(pl.multiple_of(base + slots, SUBLANES), SUBLANES)
            padded[rows, :] = padded[rows, :] + jnp.where(sublane < shift, after, 0.0)
        high, low = halves(padded[:INNER, :])
        high_held[...] = high
        low_held[...] = low
        outgoing = [
            pltpu.make_async_copy(high_held, pair.at[0], leave.at[0]),
            pltpu.make_async_copy(low_held, pair.at[1], leave.at[1]),
        ]
        if first:
            outgoing.append(pltpu.make_async_copy(padded.at[pl.ds(0, INNER)], refs[3], leave.at[2]))
        for copy in outgoing:
            copy.start()
        left = jnp.concatenate([high, low, high], axis=1)
        right = jnp.concatenate([low, high, high], axis=1)
        for panel in range(3):
            here = slice(panel * PANEL, (panel + 1) * PANEL)
            store_panel(gram, panel, dot(left[panel * PANEL :], right[here], ((1,), (1,))))
        mine, other = core_rows()
        keep[...] = gram[mine, :]
        send[...] = gram[other, :]
        for copy in outgoing:
            copy.wait()


def core_rows():
    half = INNER // 2
    first = (lax.axis_index("tensor") & 1) * half
    return tuple(pl.ds(pl.multiple_of(start, SUBLANES), half) for start in (first, half - first))


def store_panel(packed, panel, part):
    if panel == 0:
        packed[:, :PANEL] = part
    elif panel == 1:
        packed[: 2 * PANEL, PANEL:] = part
    else:
        packed[2 * PANEL :, PANEL:] = part


def unpack(packed, gram):
    gram[:, :PANEL] = packed[:, :PANEL]
    gram[PANEL:, PANEL : 2 * PANEL] = packed[: 2 * PANEL, PANEL:]
    gram[2 * PANEL :, 2 * PANEL :] = packed[2 * PANEL :, PANEL:]
    gram[:PANEL, PANEL:] = packed[PANEL:, :PANEL].T
    gram[PANEL : 2 * PANEL, 2 * PANEL :] = packed[PANEL : 2 * PANEL, PANEL:].T
    return gram[...]


def symmetric_product(left, right, out):
    for begin in range(0, INNER, TILE):
        end = min(begin + TILE, INNER)
        part = dot(left[begin:], right[:, begin:end])
        out[begin:, begin:end] = part
        if end < INNER:
            out[begin:end, end:] = part[end - begin :].T
    return out[...]


def polynomial(raw, gram):
    diagonal = lax.broadcasted_iota(jnp.int32, raw.shape, 0) == lax.broadcasted_iota(jnp.int32, raw.shape, 1)
    square_total = jnp.sum(jnp.where(diagonal, raw, 0.0))
    norm = jnp.sqrt(jnp.full((1, 1), square_total, jnp.float32)) + EPSILON
    inverse = 1.0 / norm
    first = (raw * inverse) * inverse
    first_right = passes_right(first)
    second = symmetric_product(passes_left(first), first_right, gram)
    base = QUINTIC_SECOND * first + QUINTIC_THIRD * second + jnp.where(diagonal, QUINTIC_FIRST, 0.0)
    base_left = passes_left(base)
    third = symmetric_product(base_left, first_right, gram)
    next_gram = symmetric_product(base_left, passes_right(third), gram)
    square = symmetric_product(passes_left(next_gram), passes_right(next_gram), gram)
    outer = QUINTIC_SECOND * next_gram + QUINTIC_THIRD * square + jnp.where(diagonal, QUINTIC_FIRST, 0.0)
    return symmetric_product(passes_left(outer), passes_right(base), gram) * (inverse * OUT_SCALE)


def extract(padded, start, count, staged, step):
    _, slots, columns = staged.shape
    sublane = lax.broadcasted_iota(jnp.int32, (SUBLANES, columns), 0)
    shift = start % SUBLANES
    base = start - shift
    back = jnp.where(shift == 0, 0, SUBLANES - shift)

    def window(index):
        rows = pl.ds(pl.multiple_of(base + index * SUBLANES, SUBLANES), SUBLANES)
        return pltpu.roll(padded[rows, :], back, 0)

    def tile(index, here):
        after = window(index + 1)
        moved = jnp.where(sublane < SUBLANES - shift, here, after)
        rows = pl.ds(pl.multiple_of(index * SUBLANES, SUBLANES), SUBLANES)
        staged[step, rows, :] = jnp.where(sublane < count - index * SUBLANES, moved, 0.0)
        return after

    over_tiles(slots // SUBLANES, tile, window(0))


def update_kernel(first, steps, *refs):
    tables, (keep, away, pair), refs = refs[:4], refs[4:7], refs[8 if first else 7 :]
    whole, refs = refs[0], refs[1:]
    homes, refs = refs[: len(steps)], refs[len(steps) :]
    gram, padded, staged, stacked, held, arrive, leave = refs[:7]
    ranks = tables[1].shape[0]
    rank = lax.axis_index("fsdp")

    @pl.when(is_inner(rank, ranks))
    def _():
        incoming, begin = [], 0
        for index, (side, (first_row, last_row)) in enumerate(PARTS):
            size = last_row - first_row
            source = pair.at[side, pl.ds(first_row, size)]
            incoming.append(pltpu.make_async_copy(source, stacked.at[pl.ds(begin, size)], arrive.at[index]))
            incoming[-1].start()
            begin += size
        owner_group, live_ranks, row_counts, row_offsets = fetch_tables(tables, refs[7:])
        matrix = matrix_of(owner_group, rank ^ mate(ranks) if first else rank)
        mine, other = core_rows()
        held[mine, :] = keep[...]
        held[other, :] = away[...]
        total = polynomial(unpack(held, gram), gram)
        copies = []
        if first:
            for panel in range(3):
                store_panel(held, panel, total[panel * PANEL :, panel * PANEL : (panel + 1) * PANEL])
            copies = [pltpu.make_async_copy(held, whole, leave.at[len(steps)])]
            copies[0].start()
        for copy in incoming:
            copy.wait()
        padded[:INNER, :] = dot(passes_left(total), stacked[...])
        if not first:
            copies = [pltpu.make_async_copy(padded.at[pl.ds(0, INNER)], whole, leave.at[len(steps)])]
            copies[0].start()
        for index, step in enumerate(steps):
            target = rank ^ step
            count = row_counts[matrix, target] * live_ranks[target]
            extract(padded, row_offsets[matrix, target], count, staged, index)
            copies.append(pltpu.make_async_copy(staged.at[index], homes[index], leave.at[index]))
            copies[-1].start()
        for copy in copies:
            copy.wait()


def finish_kernel(ranks, *refs):
    tables, (packed, iterate, inner_result, own_first, own_last), refs = refs[:4], refs[4:9], refs[10:]
    (result, shards), refs = refs[:2], refs[2:]
    gram, padded, staged, whole, held, arrive, leave = refs[:7]
    rank = lax.axis_index("fsdp")
    owner_group, live_ranks, row_counts, row_offsets = fetch_tables(tables, refs[7:])
    matrix = matrix_of(owner_group, rank)

    def run(jobs):
        copies = [pltpu.make_async_copy(*job) for job in jobs]
        for copy in copies:
            copy.start()
        for copy in copies:
            copy.wait()

    @pl.when(is_inner(rank, ranks))
    def _():
        run(
            [
                (inner_result, whole, arrive.at[0]),
                (own_first, staged.at[0], arrive.at[1]),
                (own_last, staged.at[1], arrive.at[2]),
            ]
        )
        other = matrix_of(owner_group, rank ^ mate(ranks))
        run(
            [
                (whole, result, leave.at[0]),
                (staged.at[0], shards.at[other], leave.at[1]),
                (staged.at[1], shards.at[matrix], leave.at[2]),
            ]
        )

    @pl.when(jnp.logical_not(is_inner(rank, ranks)))
    def _():
        run([(iterate, whole, arrive.at[0]), (packed, held, arrive.at[1])])
        padded[:INNER, :] = dot(passes_left(unpack(held, gram)), passes_right(whole[...]))
        extract(padded, row_offsets[matrix, rank], row_counts[matrix, rank] * live_ranks[rank], staged, 0)
        run(
            [
                (padded.at[pl.ds(0, INNER)], result, leave.at[0]),
                (staged.at[0], shards.at[matrix], leave.at[1]),
            ]
        )


def place_kernel(first, ranks, steps, *refs):
    table, blocks, shards = refs[0], refs[1 : 1 + len(steps)], refs[2 + len(steps)]
    owner_group, arrive, leave = refs[3 + len(steps) :]
    rank = lax.axis_index("fsdp")
    fetch = pltpu.make_async_copy(table, owner_group, arrive)
    fetch.start()
    fetch.wait()
    copies = []
    for index, step in enumerate(steps):
        source = rank ^ step
        matrix = matrix_of(owner_group, source ^ mate(ranks) if first else source)
        copies.append((is_inner(source, ranks), blocks[index], shards.at[matrix], leave.at[index]))
    each_copy(copies, "start")
    each_copy(copies, "wait")


def idle_kernel(*refs):
    pass


def floats(*shape):
    return jax.ShapeDtypeStruct(shape, jnp.float32)


def vmem(*shape, dtype=jnp.float32):
    return pltpu.VMEM(shape, dtype)


def flags(*shape):
    return pltpu.SemaphoreType.DMA(shape)


FREE = pl.CostEstimate(flops=0, bytes_accessed=0, transcendentals=0)


def blend(first, tables, momentum, gradient, before):
    _, slots, columns = momentum.shape
    ranks = tables[1].shape[0]
    chunks = 4 if slots % (4 * SUBLANES) == 0 else 1
    return pl.pallas_call(
        functools.partial(blend_kernel, first, chunks),
        out_shape=[floats(slots, columns)] * ranks + [floats(SUBLANES, 128)],
        in_specs=[HBM] * 6 + [ANY] * len(before),
        out_specs=[HBM] * ranks + [VMEM],
        scratch_shapes=[vmem(ranks, slots, columns)] * 2
        + [flags(ranks, chunks, 2), flags(ranks, chunks)]
        + table_scratch(*tables[2].shape),
        compiler_params=FULL,
        cost_estimate=FREE,
        name="blend",
    )(*tables, momentum, gradient, *before)


def fresh_momentum(tables, momentum, gradient, before):
    matrices, slots, columns = momentum.shape
    block = pl.BlockSpec((None, slots, columns), lambda matrix: (matrix, 0, 0))
    return pl.pallas_call(
        fresh_kernel,
        grid=(matrices,),
        out_shape=[floats(*momentum.shape), floats(SUBLANES, 128)],
        in_specs=[pl.BlockSpec(memory_space=pltpu.SMEM)] * 2 + [block] * 2 + [ANY],
        out_specs=[block, pl.BlockSpec((SUBLANES, 128), lambda matrix: (0, 0))],
        compiler_params=FULL,
        cost_estimate=FREE,
        name="fresh_momentum",
    )(*tables[1:3], momentum, gradient, before)


def assemble_and_gram(first, tables, blocks, *after):
    slots, columns = blocks[0].shape
    ranks = len(blocks)
    pair = jax.ShapeDtypeStruct((4, INNER, columns), jnp.bfloat16)
    return pl.pallas_call(
        functools.partial(gram_kernel, first, ranks),
        out_shape=[pair] + [floats(INNER // 2, 2 * PANEL)] * 2 + [floats(INNER, columns)] * first,
        in_specs=[HBM] * 4 + [ANY] * (ranks + len(after)),
        out_specs=[ANY, VMEM, VMEM] + [ANY] * first,
        scratch_shapes=[
            vmem(ranks, slots, columns),
            vmem(INNER + slots + SUBLANES, columns),
            vmem(INNER, columns, dtype=jnp.bfloat16),
            vmem(INNER, columns, dtype=jnp.bfloat16),
            vmem(INNER, 2 * PANEL),
            flags(ranks),
            flags(3),
        ]
        + table_scratch(*tables[2].shape),
        compiler_params=PARAMS,
        cost_estimate=FREE,
        name="assemble_and_gram",
    )(*tables, *blocks, *after)


def update_shapes(first, steps, slots, columns):
    whole = floats(INNER, 2 * PANEL if first else columns)
    return [whole] + [floats(slots, columns)] * len(steps)


def nothing(shapes):
    return pl.pallas_call(
        idle_kernel, out_shape=shapes, out_specs=[ANY] * len(shapes), compiler_params=SMALL, name="nothing"
    )()


def apply_update(first, steps, tables, keep, away, pair, slots, *after):
    columns = pair.shape[2]
    return pl.pallas_call(
        functools.partial(update_kernel, first, steps),
        out_shape=update_shapes(first, steps, slots, columns),
        in_specs=[HBM] * 4 + [VMEM] * 2 + [ANY] * (1 + len(after)),
        out_specs=[ANY] * (1 + len(steps)),
        scratch_shapes=[
            vmem(INNER, INNER),
            vmem(INNER + slots + 2 * SUBLANES, columns),
            vmem(len(steps), slots, columns),
            vmem(3 * INNER, columns, dtype=jnp.bfloat16),
            vmem(INNER, 2 * PANEL),
            flags(len(PARTS)),
            flags(len(steps) + 1),
        ]
        + table_scratch(*tables[2].shape),
        compiler_params=PARAMS,
        cost_estimate=FREE,
        name="apply_update",
    )(*tables, keep, away, pair, *after)


def settle(value):
    return pl.pallas_call(
        idle_kernel,
        out_shape=floats(SUBLANES, 128),
        in_specs=[ANY],
        out_specs=ANY,
        compiler_params=SMALL,
        cost_estimate=pl.CostEstimate(flops=10**11, bytes_accessed=0, transcendentals=0),
        name="settle",
    )(value)


def finish(tables, packed, iterate, inner_result, own_first, own_last, shape, after):
    slots, columns = own_first.shape
    return pl.pallas_call(
        functools.partial(finish_kernel, tables[1].shape[0]),
        out_shape=[floats(INNER, columns), floats(*shape)],
        in_specs=[HBM] * 4 + [ANY] * 6,
        out_specs=[HBM] * 2,
        scratch_shapes=[
            vmem(INNER, INNER),
            vmem(INNER + slots + 2 * SUBLANES, columns),
            vmem(2, slots, columns),
            vmem(INNER, columns),
            vmem(INNER, 2 * PANEL),
            flags(3),
            flags(3),
        ]
        + table_scratch(*tables[2].shape),
        compiler_params=PARAMS,
        cost_estimate=FREE,
        name="finish",
    )(*tables, packed, iterate, inner_result, own_first, own_last, after)


def place_blocks(first, owner_group, steps, blocks, shards, ranks):
    return pl.pallas_call(
        functools.partial(place_kernel, first, ranks, steps),
        out_shape=floats(*shards.shape),
        in_specs=[HBM] + [VMEM] * len(blocks) + [HBM],
        out_specs=HBM,
        scratch_shapes=[pltpu.SMEM(owner_group.shape, jnp.int32), flags(), flags(len(steps))],
        input_output_aliases={1 + len(blocks): 0},
        compiler_params=PARAMS,
        cost_estimate=FREE,
        name="place_blocks",
    )(owner_group, *blocks, shards)


def sum_halves(keep, send, axis):
    size = lax.axis_size(axis)

    def exchange(piece, bits):
        return lax.ppermute(piece, axis, [(i, i ^ bits[i & 1]) for i in range(size)])

    chips = [1 << shift for shift in range(1, size.bit_length() - 1)]
    keep = keep + exchange(send, (1, 1))
    for bits in zip(chips, reversed(chips)):
        keep = keep + exchange(keep, bits)
    return keep, exchange(keep, (1, 1))


def on_device(momentum, gradient, live_ranks, owner_group, row_counts, row_offsets):
    ranks = lax.axis_size("fsdp")
    _, slots, columns = momentum.shape
    inner = is_inner(lax.axis_index("fsdp"), ranks)
    tables = (owner_group, live_ranks, row_counts, row_offsets)
    last = [2, 1, *range(3, ranks)]
    early = [step for step in last if step != mate(ranks)]

    def pairs(step, inward):
        return [(i, i ^ step) for i in range(ranks) if is_inner(i ^ step if inward else i, ranks)]

    def to_inner(block, step):
        return lax.ppermute(block, "fsdp", pairs(step, True))

    def from_inner(block, step):
        return lax.ppermute(block, "fsdp", pairs(step, False))

    *blends, token = blend(True, tables, momentum, gradient, [])
    first_blocks = [blends[0]] + [to_inner(blends[step], step) for step in range(1, ranks)]
    *blends, token = blend(False, tables, momentum, gradient, [token])
    last_blocks = [blends[0]] + [to_inner(blends[step], step) for step in range(1, ranks)]
    new_momentum, token = fresh_momentum(tables, momentum, gradient, token)

    pair, keep, send, iterate = assemble_and_gram(True, tables, first_blocks)
    iterate = from_inner(iterate, mate(ranks))

    def first_update(pair, keep, send, after):
        return apply_update(True, [0, *early], tables, *sum_halves(keep, send, "tensor"), pair, slots, after)

    def first_skip(*_):
        return nothing(update_shapes(True, [0, *early], slots, columns))

    packed, own_first, *homes = lax.cond(inner, first_update, first_skip, pair, keep, send, settle(keep))
    packed_there = from_inner(packed, mate(ranks))
    first_home = [from_inner(block, step) for step, block in zip(early, homes)]

    def last_update(after, *blocks):
        pair, keep, send = assemble_and_gram(False, tables, blocks, after)
        return apply_update(False, [0, *last], tables, *sum_halves(keep, send, "tensor"), pair, slots)

    def last_skip(*_):
        return nothing(update_shapes(False, [0, *last], slots, columns))

    result, own_last, *homes = lax.cond(inner, last_update, last_skip, packed, *last_blocks)
    last_home = [from_inner(block, step) for step, block in zip(last, homes)]

    result, shards = finish(tables, packed_there, iterate, result, own_first, own_last, momentum.shape, token)
    shards = place_blocks(True, owner_group, early, first_home, shards, ranks)
    for step, block in zip(last, last_home):
        shards = place_blocks(False, owner_group, [step], [block], shards, ranks)
    return (new_momentum, shards, result[None])


def solution(mesh):
    placed = (P(None, "fsdp", "tensor"), P(None, "fsdp", "tensor"), P(), P(), P(), P())
    return jax.shard_map(
        on_device,
        mesh=mesh,
        in_specs=placed,
        out_specs=(P(None, "fsdp", "tensor"), P(None, "fsdp", "tensor"), P("fsdp", None, "tensor")),
        check_vma=False,
    )
```

```python
import functools
import math

import jax
import jax.numpy as jnp
from jax import lax
from jax.experimental import pallas as pl
from jax.experimental.pallas import tpu as pltpu
from jax.sharding import PartitionSpec as P

WIDTH = 7168
INNER = 576
PANEL = INNER // 3
TILE = 256
SUBLANES = 8

MOMENTUM_RATE = 0.95
QUINTIC_FIRST = 3.4445
QUINTIC_SECOND = -4.775
QUINTIC_THIRD = 2.0315
EPSILON = 1e-07
OUT_SCALE = 0.2 * math.sqrt(max(INNER, WIDTH))
SMALL = pltpu.CompilerParams(vmem_limit_bytes=1024 * 1024)
FULL = pltpu.CompilerParams(vmem_limit_bytes=60 * 1024 * 1024)
PARAMS = pltpu.CompilerParams(vmem_limit_bytes=24 * 1024 * 1024)
HBM = pl.BlockSpec(memory_space=pltpu.HBM)
ANY = pl.BlockSpec(memory_space=pl.ANY)
VMEM = pl.BlockSpec(memory_space=pltpu.VMEM)


def halves(value):
    high = value.astype(jnp.bfloat16)
    low = (value - high.astype(jnp.float32)).astype(jnp.bfloat16)
    return high, low


def dot(left, right, contract=((1,), (0,))):
    return lax.dot_general(left, right, (contract, ((), ())), preferred_element_type=jnp.float32)


DEPTH = INNER // TILE * TILE
PARTS = [(side, rows) for rows in ((0, DEPTH), (DEPTH, INNER)) if rows[0] < rows[1] for side in (1, 0, 0)]


def passes_left(value):
    high, low = halves(value)
    return jnp.concatenate(
        [part[:, first:last] for first, last in ((0, DEPTH), (DEPTH, INNER)) for part in (high, low, high)], axis=1
    )


def passes_right(value):
    sides = halves(value)
    return jnp.concatenate([sides[side][first:last] for side, (first, last) in PARTS], axis=0)


def is_inner(rank, ranks):
    low = ranks // 4
    return (rank >= low) & (rank < ranks - low)


def mate(ranks):
    return ranks // 4


def table_scratch(matrices, ranks):
    return [
        pltpu.SMEM((matrices,), jnp.int32),
        pltpu.SMEM((ranks,), jnp.int32),
        pltpu.SMEM((matrices, ranks), jnp.int32),
        pltpu.SMEM((matrices, ranks), jnp.int32),
        pltpu.SemaphoreType.DMA((4,)),
    ]


def fetch_tables(tables, held):
    *places, arrive = held
    copies = [
        pltpu.make_async_copy(table, place, arrive.at[index])
        for index, (table, place) in enumerate(zip(tables, places))
    ]
    for copy in copies:
        copy.start()
    for copy in copies:
        copy.wait()
    return places


def matrix_of(owner_group, rank):
    found = jnp.int32(0)
    for matrix in range(owner_group.shape[0]):
        found = jnp.where(owner_group[matrix] == rank, matrix, found)
    return found


def over_tiles(tiles, body, carry):
    group = next(group for group in (6, 3, 2, 1) if tiles % group == 0)

    def step(index, carry):
        for member in range(group):
            carry = body(index * group + member, carry)
        return carry

    return lax.fori_loop(0, tiles // group, step, carry)


def each_copy(copies, action):
    for condition, source, place, flag in copies:

        @pl.when(condition)
        def _(source=source, place=place, flag=flag):
            getattr(pltpu.make_async_copy(source, place, flag), action)()


def blend_kernel(first, chunks, *refs):
    tables, (momentum, gradient) = refs[:4], refs[4:6]
    ranks = tables[1].shape[0]
    *outs, token, olds, grads, arrive, leave = refs[-ranks - 10 : -5]
    owner_group, live_ranks, row_counts, _ = fetch_tables(tables, refs[-5:])
    rank = lax.axis_index("fsdp")
    slots, columns = outs[0].shape
    size = slots // chunks
    jobs = []
    for step in range(1, ranks + 1):
        step = step % ranks
        if first and step == 0:
            continue
        target = rank ^ step
        wanted = is_inner(target, ranks)
        matrix = matrix_of(owner_group, target ^ mate(ranks) if first else target)
        if first and step == mate(ranks):
            matrix = matrix_of(owner_group, jnp.where(wanted, rank, target))
            wanted = rank >= 0
        count = row_counts[matrix, rank] * live_ranks[rank]
        for chunk in range(chunks):
            part = pl.ds(chunk * size, size)
            flags = arrive.at[step, chunk, 0], arrive.at[step, chunk, 1]
            incoming = (
                (wanted, momentum.at[matrix, part], olds.at[step, part], flags[0]),
                (wanted, gradient.at[matrix, part], grads.at[step, part], flags[1]),
            )
            outgoing = (wanted, olds.at[step, part], outs[step].at[part], leave.at[step, chunk])
            jobs.append((step, chunk, count, incoming, outgoing))
            each_copy(incoming, "start")
    token[...] = jnp.zeros_like(token)
    for step, chunk, count, incoming, outgoing in jobs:

        @pl.when(incoming[0][0])
        def _(step=step, chunk=chunk, count=count, incoming=incoming, outgoing=outgoing):
            for _, source, place, flag in incoming:
                pltpu.make_async_copy(source, place, flag).wait()
            rows = slice(chunk * size, (chunk + 1) * size)
            grad_now = grads[step, rows, :]
            fresh = MOMENTUM_RATE * olds[step, rows, :] + grad_now
            position = lax.broadcasted_iota(jnp.int32, (size, columns), 0) + chunk * size
            olds[step, rows, :] = jnp.where(position < count, grad_now + MOMENTUM_RATE * fresh, 0.0)
            pltpu.make_async_copy(*outgoing[1:]).start()

    each_copy([job[-1] for job in jobs], "wait")


def fresh_kernel(live_ranks, row_counts, momentum, gradient, _, out, token):
    token[...] = jnp.zeros_like(token)
    rank, matrix = lax.axis_index("fsdp"), pl.program_id(0)
    position = lax.broadcasted_iota(jnp.int32, out.shape, 0)
    keep = position < row_counts[matrix, rank] * live_ranks[rank]
    out[...] = jnp.where(keep, MOMENTUM_RATE * momentum[...] + gradient[...], 0.0)


def assemble(blocks, landed, padded, arrive, tables, held, first):
    ranks, slots, columns = landed.shape
    copies = []
    for step in range(ranks):
        copies.append(pltpu.make_async_copy(blocks[step], landed.at[step], arrive.at[step]))
        copies[-1].start()
    owner_group, _, _, row_offsets = fetch_tables(tables, held)
    rank = lax.axis_index("fsdp")
    base = jnp.where(is_inner(rank, ranks), rank, rank ^ mate(ranks))
    matrix = matrix_of(owner_group, base ^ mate(ranks) if first else base)
    padded[...] = jnp.zeros_like(padded)
    sublane = lax.broadcasted_iota(jnp.int32, (SUBLANES, columns), 0)
    for step in range(ranks):
        start = row_offsets[matrix, base ^ step]
        shift = start % SUBLANES
        origin = start - shift
        copies[step].wait()

        def tile(index, before, origin=origin, shift=shift, step=step):
            moved = pltpu.roll(landed[step, pl.ds(pl.multiple_of(index * SUBLANES, SUBLANES), SUBLANES), :], shift, 0)
            rows = pl.ds(pl.multiple_of(origin + index * SUBLANES, SUBLANES), SUBLANES)
            padded[rows, :] = padded[rows, :] + jnp.where(sublane < shift, before, moved)
            return moved

        after = over_tiles(slots // SUBLANES, tile, jnp.zeros((SUBLANES, columns), jnp.float32))
        rows = pl.ds(pl.multiple_of(origin + slots, SUBLANES), SUBLANES)
        padded[rows, :] = padded[rows, :] + jnp.where(sublane < shift, after, 0.0)


def outer_kernel(ranks, *refs):
    landed, padded, arrive, leave = refs[-9:-5]

    @pl.when(jnp.logical_not(is_inner(lax.axis_index("fsdp"), ranks)))
    def _():
        assemble(refs[4 : 4 + ranks], landed, padded, arrive, refs[:4], refs[-5:], True)
        copy = pltpu.make_async_copy(padded.at[pl.ds(0, INNER)], refs[4 + ranks], leave.at[0])
        copy.start()
        copy.wait()


def gram_kernel(first, ranks, *refs):
    pair, keep, send = refs[-15:-12]
    landed, padded, high_held, low_held, gram, arrive, leave = refs[-12:-5]

    @pl.when(is_inner(lax.axis_index("fsdp"), ranks))
    def _():
        assemble(refs[4 : 4 + ranks], landed, padded, arrive, refs[:4], refs[-5:], first)
        high, low = halves(padded[:INNER, :])
        high_held[...] = high
        low_held[...] = low
        outgoing = [
            pltpu.make_async_copy(high_held, pair.at[0], leave.at[0]),
            pltpu.make_async_copy(low_held, pair.at[1], leave.at[1]),
        ]
        for copy in outgoing:
            copy.start()
        left = jnp.concatenate([high, low, high], axis=1)
        right = jnp.concatenate([low, high, high], axis=1)
        for panel in range(3):
            here = slice(panel * PANEL, (panel + 1) * PANEL)
            store_panel(gram, panel, dot(left[panel * PANEL :], right[here], ((1,), (1,))))
        mine, other = core_rows()
        keep[...] = gram[mine, :]
        send[...] = gram[other, :]
        for copy in outgoing:
            copy.wait()


def core_rows():
    half = INNER // 2
    first = (lax.axis_index("tensor") & 1) * half
    return tuple(pl.ds(pl.multiple_of(start, SUBLANES), half) for start in (first, half - first))


def store_panel(packed, panel, part):
    if panel == 0:
        packed[:, :PANEL] = part
    elif panel == 1:
        packed[: 2 * PANEL, PANEL:] = part
    else:
        packed[2 * PANEL :, PANEL:] = part


def unpack(packed, gram):
    gram[:, :PANEL] = packed[:, :PANEL]
    gram[PANEL:, PANEL : 2 * PANEL] = packed[: 2 * PANEL, PANEL:]
    gram[2 * PANEL :, 2 * PANEL :] = packed[2 * PANEL :, PANEL:]
    gram[:PANEL, PANEL:] = packed[PANEL:, :PANEL].T
    gram[PANEL : 2 * PANEL, 2 * PANEL :] = packed[PANEL : 2 * PANEL, PANEL:].T
    return gram[...]


def symmetric_product(left, right, out):
    for begin in range(0, INNER, TILE):
        end = min(begin + TILE, INNER)
        part = dot(left[begin:], right[:, begin:end])
        out[begin:, begin:end] = part
        if end < INNER:
            out[begin:end, end:] = part[end - begin :].T
    return out[...]


def polynomial(raw, gram):
    diagonal = lax.broadcasted_iota(jnp.int32, raw.shape, 0) == lax.broadcasted_iota(jnp.int32, raw.shape, 1)
    square_total = jnp.sum(jnp.where(diagonal, raw, 0.0))
    norm = jnp.sqrt(jnp.full((1, 1), square_total, jnp.float32)) + EPSILON
    inverse = 1.0 / norm
    first = (raw * inverse) * inverse
    first_right = passes_right(first)
    second = symmetric_product(passes_left(first), first_right, gram)
    base = QUINTIC_SECOND * first + QUINTIC_THIRD * second + jnp.where(diagonal, QUINTIC_FIRST, 0.0)
    base_left = passes_left(base)
    third = symmetric_product(base_left, first_right, gram)
    next_gram = symmetric_product(base_left, passes_right(third), gram)
    square = symmetric_product(passes_left(next_gram), passes_right(next_gram), gram)
    outer = QUINTIC_SECOND * next_gram + QUINTIC_THIRD * square + jnp.where(diagonal, QUINTIC_FIRST, 0.0)
    return symmetric_product(passes_left(outer), passes_right(base), gram) * (inverse * OUT_SCALE)


def extract(padded, start, count, staged, step):
    _, slots, columns = staged.shape
    sublane = lax.broadcasted_iota(jnp.int32, (SUBLANES, columns), 0)
    shift = start % SUBLANES
    base = start - shift
    back = jnp.where(shift == 0, 0, SUBLANES - shift)

    def window(index):
        rows = pl.ds(pl.multiple_of(base + index * SUBLANES, SUBLANES), SUBLANES)
        return pltpu.roll(padded[rows, :], back, 0)

    def tile(index, here):
        after = window(index + 1)
        moved = jnp.where(sublane < SUBLANES - shift, here, after)
        rows = pl.ds(pl.multiple_of(index * SUBLANES, SUBLANES), SUBLANES)
        staged[step, rows, :] = jnp.where(sublane < count - index * SUBLANES, moved, 0.0)
        return after

    over_tiles(slots // SUBLANES, tile, window(0))


def update_kernel(first, steps, *refs):
    tables, (keep, away, pair), refs = refs[:4], refs[4:7], refs[8 if first else 7 :]
    whole, refs = refs[0], refs[1:]
    homes, refs = refs[: len(steps)], refs[len(steps) :]
    gram, padded, staged, stacked, held, arrive, leave = refs[:7]
    ranks = tables[1].shape[0]
    rank = lax.axis_index("fsdp")

    @pl.when(is_inner(rank, ranks))
    def _():
        incoming, begin = [], 0
        for index, (side, (first_row, last_row)) in enumerate(PARTS):
            size = last_row - first_row
            source = pair.at[side, pl.ds(first_row, size)]
            incoming.append(pltpu.make_async_copy(source, stacked.at[pl.ds(begin, size)], arrive.at[index]))
            incoming[-1].start()
            begin += size
        owner_group, live_ranks, row_counts, row_offsets = fetch_tables(tables, refs[7:])
        matrix = matrix_of(owner_group, rank ^ mate(ranks) if first else rank)
        mine, other = core_rows()
        held[mine, :] = keep[...]
        held[other, :] = away[...]
        total = polynomial(unpack(held, gram), gram)
        copies = []
        if first:
            for panel in range(3):
                store_panel(held, panel, total[panel * PANEL :, panel * PANEL : (panel + 1) * PANEL])
            copies = [pltpu.make_async_copy(held, whole, leave.at[len(steps)])]
            copies[0].start()
        for copy in incoming:
            copy.wait()
        padded[:INNER, :] = dot(passes_left(total), stacked[...])
        if not first:
            copies = [pltpu.make_async_copy(padded.at[pl.ds(0, INNER)], whole, leave.at[len(steps)])]
            copies[0].start()
        for index, step in enumerate(steps):
            target = rank ^ step
            count = row_counts[matrix, target] * live_ranks[target]
            extract(padded, row_offsets[matrix, target], count, staged, index)
            copies.append(pltpu.make_async_copy(staged.at[index], homes[index], leave.at[index]))
            copies[-1].start()
        for copy in copies:
            copy.wait()


def finish_kernel(ranks, *refs):
    tables, (packed, iterate, inner_result, own_first, own_last), refs = refs[:4], refs[4:9], refs[10:]
    (result, shards), refs = refs[:2], refs[2:]
    gram, padded, staged, whole, held, arrive, leave = refs[:7]
    rank = lax.axis_index("fsdp")
    owner_group, live_ranks, row_counts, row_offsets = fetch_tables(tables, refs[7:])
    matrix = matrix_of(owner_group, rank)

    def run(jobs):
        copies = [pltpu.make_async_copy(*job) for job in jobs]
        for copy in copies:
            copy.start()
        for copy in copies:
            copy.wait()

    @pl.when(is_inner(rank, ranks))
    def _():
        run(
            [
                (inner_result, whole, arrive.at[0]),
                (own_first, staged.at[0], arrive.at[1]),
                (own_last, staged.at[1], arrive.at[2]),
            ]
        )
        other = matrix_of(owner_group, rank ^ mate(ranks))
        run(
            [
                (whole, result, leave.at[0]),
                (staged.at[0], shards.at[other], leave.at[1]),
                (staged.at[1], shards.at[matrix], leave.at[2]),
            ]
        )

    @pl.when(jnp.logical_not(is_inner(rank, ranks)))
    def _():
        run([(iterate, whole, arrive.at[0]), (packed, held, arrive.at[1])])
        padded[:INNER, :] = dot(passes_left(unpack(held, gram)), passes_right(whole[...]))
        extract(padded, row_offsets[matrix, rank], row_counts[matrix, rank] * live_ranks[rank], staged, 0)
        run(
            [
                (padded.at[pl.ds(0, INNER)], result, leave.at[0]),
                (staged.at[0], shards.at[matrix], leave.at[1]),
            ]
        )


def place_kernel(first, ranks, steps, *refs):
    table, blocks, shards = refs[0], refs[1 : 1 + len(steps)], refs[2 + len(steps)]
    owner_group, arrive, leave = refs[3 + len(steps) :]
    rank = lax.axis_index("fsdp")
    fetch = pltpu.make_async_copy(table, owner_group, arrive)
    fetch.start()
    fetch.wait()
    copies = []
    for index, step in enumerate(steps):
        source = rank ^ step
        matrix = matrix_of(owner_group, source ^ mate(ranks) if first else source)
        copies.append((is_inner(source, ranks), blocks[index], shards.at[matrix], leave.at[index]))
    each_copy(copies, "start")
    each_copy(copies, "wait")


def idle_kernel(*refs):
    pass


def floats(*shape):
    return jax.ShapeDtypeStruct(shape, jnp.float32)


def vmem(*shape, dtype=jnp.float32):
    return pltpu.VMEM(shape, dtype)


def flags(*shape):
    return pltpu.SemaphoreType.DMA(shape)


FREE = pl.CostEstimate(flops=0, bytes_accessed=0, transcendentals=0)


def blend(first, tables, momentum, gradient, before):
    _, slots, columns = momentum.shape
    ranks = tables[1].shape[0]
    chunks = 4 if slots % (4 * SUBLANES) == 0 else 1
    return pl.pallas_call(
        functools.partial(blend_kernel, first, chunks),
        out_shape=[floats(slots, columns)] * ranks + [floats(SUBLANES, 128)],
        in_specs=[HBM] * 6 + [ANY] * len(before),
        out_specs=[HBM] * ranks + [VMEM],
        scratch_shapes=[vmem(ranks, slots, columns)] * 2
        + [flags(ranks, chunks, 2), flags(ranks, chunks)]
        + table_scratch(*tables[2].shape),
        compiler_params=FULL,
        cost_estimate=FREE,
        name="blend",
    )(*tables, momentum, gradient, *before)


def fresh_momentum(tables, momentum, gradient, before):
    matrices, slots, columns = momentum.shape
    block = pl.BlockSpec((None, slots, columns), lambda matrix: (matrix, 0, 0))
    return pl.pallas_call(
        fresh_kernel,
        grid=(matrices,),
        out_shape=[floats(*momentum.shape), floats(SUBLANES, 128)],
        in_specs=[pl.BlockSpec(memory_space=pltpu.SMEM)] * 2 + [block] * 2 + [ANY],
        out_specs=[block, pl.BlockSpec((SUBLANES, 128), lambda matrix: (0, 0))],
        compiler_params=FULL,
        cost_estimate=FREE,
        name="fresh_momentum",
    )(*tables[1:3], momentum, gradient, before)


def assemble_and_gram(first, tables, blocks, *after):
    slots, columns = blocks[0].shape
    ranks = len(blocks)
    pair = jax.ShapeDtypeStruct((4, INNER, columns), jnp.bfloat16)
    return pl.pallas_call(
        functools.partial(gram_kernel, first, ranks),
        out_shape=[pair] + [floats(INNER // 2, 2 * PANEL)] * 2,
        in_specs=[HBM] * 4 + [ANY] * (ranks + len(after)),
        out_specs=[ANY, VMEM, VMEM],
        scratch_shapes=[
            vmem(ranks, slots, columns),
            vmem(INNER + slots + SUBLANES, columns),
            vmem(INNER, columns, dtype=jnp.bfloat16),
            vmem(INNER, columns, dtype=jnp.bfloat16),
            vmem(INNER, 2 * PANEL),
            flags(ranks),
            flags(2),
        ]
        + table_scratch(*tables[2].shape),
        compiler_params=PARAMS,
        cost_estimate=FREE,
        name="assemble_and_gram",
    )(*tables, *blocks, *after)


def assemble_outer(tables, blocks):
    slots, columns = blocks[0].shape
    ranks = len(blocks)
    return pl.pallas_call(
        functools.partial(outer_kernel, ranks),
        out_shape=floats(INNER, columns),
        in_specs=[HBM] * 4 + [ANY] * ranks,
        out_specs=ANY,
        scratch_shapes=[
            vmem(ranks, slots, columns),
            vmem(INNER + slots + SUBLANES, columns),
            flags(ranks),
            flags(1),
        ]
        + table_scratch(*tables[2].shape),
        compiler_params=PARAMS,
        cost_estimate=FREE,
        name="assemble_outer",
    )(*tables, *blocks)


def update_shapes(first, steps, slots, columns):
    whole = floats(INNER, 2 * PANEL if first else columns)
    return [whole] + [floats(slots, columns)] * len(steps)


def nothing(shapes):
    return pl.pallas_call(
        idle_kernel, out_shape=shapes, out_specs=[ANY] * len(shapes), compiler_params=SMALL, name="nothing"
    )()


def apply_update(first, steps, tables, keep, away, pair, slots, *after):
    columns = pair.shape[2]
    return pl.pallas_call(
        functools.partial(update_kernel, first, steps),
        out_shape=update_shapes(first, steps, slots, columns),
        in_specs=[HBM] * 4 + [VMEM] * 2 + [ANY] * (1 + len(after)),
        out_specs=[ANY] * (1 + len(steps)),
        scratch_shapes=[
            vmem(INNER, INNER),
            vmem(INNER + slots + 2 * SUBLANES, columns),
            vmem(len(steps), slots, columns),
            vmem(3 * INNER, columns, dtype=jnp.bfloat16),
            vmem(INNER, 2 * PANEL),
            flags(len(PARTS)),
            flags(len(steps) + 1),
        ]
        + table_scratch(*tables[2].shape),
        compiler_params=PARAMS,
        cost_estimate=FREE,
        name="apply_update",
    )(*tables, keep, away, pair, *after)


def touch(value, flops=0):
    return pl.pallas_call(
        idle_kernel,
        out_shape=floats(SUBLANES, 128),
        in_specs=[ANY],
        out_specs=ANY,
        compiler_params=SMALL,
        cost_estimate=pl.CostEstimate(flops=flops, bytes_accessed=0, transcendentals=0),
        name="touch",
    )(value)


def finish(tables, packed, iterate, inner_result, own_first, own_last, shape, after):
    slots, columns = own_first.shape
    return pl.pallas_call(
        functools.partial(finish_kernel, tables[1].shape[0]),
        out_shape=[floats(INNER, columns), floats(*shape)],
        in_specs=[HBM] * 4 + [ANY] * 6,
        out_specs=[HBM] * 2,
        scratch_shapes=[
            vmem(INNER, INNER),
            vmem(INNER + slots + 2 * SUBLANES, columns),
            vmem(2, slots, columns),
            vmem(INNER, columns),
            vmem(INNER, 2 * PANEL),
            flags(3),
            flags(3),
        ]
        + table_scratch(*tables[2].shape),
        compiler_params=PARAMS,
        cost_estimate=FREE,
        name="finish",
    )(*tables, packed, iterate, inner_result, own_first, own_last, after)


def place_blocks(first, owner_group, steps, blocks, shards, ranks):
    return pl.pallas_call(
        functools.partial(place_kernel, first, ranks, steps),
        out_shape=floats(*shards.shape),
        in_specs=[HBM] + [VMEM] * len(blocks) + [HBM],
        out_specs=HBM,
        scratch_shapes=[pltpu.SMEM(owner_group.shape, jnp.int32), flags(), flags(len(steps))],
        input_output_aliases={1 + len(blocks): 0},
        compiler_params=PARAMS,
        cost_estimate=FREE,
        name="place_blocks",
    )(owner_group, *blocks, shards)


def sum_halves(keep, send, axis):
    size = lax.axis_size(axis)

    def exchange(piece, bits):
        return lax.ppermute(piece, axis, [(i, i ^ bits[i & 1]) for i in range(size)])

    chips = [1 << shift for shift in range(1, size.bit_length() - 1)]
    keep = keep + exchange(send, (1, 1))
    for bits in zip(chips, reversed(chips)):
        keep = keep + exchange(keep, bits)
    return keep, exchange(keep, (1, 1))


def on_device(momentum, gradient, live_ranks, owner_group, row_counts, row_offsets):
    ranks = lax.axis_size("fsdp")
    _, slots, columns = momentum.shape
    inner = is_inner(lax.axis_index("fsdp"), ranks)
    tables = (owner_group, live_ranks, row_counts, row_offsets)
    last = [2, 1, *range(3, ranks)]
    early = [step for step in last if step != mate(ranks)]

    def pairs(step, inward):
        return [(i, i ^ step) for i in range(ranks) if is_inner(i ^ step if inward else i, ranks)]

    def to_inner(block, step):
        return lax.ppermute(block, "fsdp", pairs(step, True))

    def from_inner(block, step):
        return lax.ppermute(block, "fsdp", pairs(step, False))

    near = mate(ranks)
    far = [step for step in last if step != near]
    *blends, token = blend(True, tables, momentum, gradient, [])
    own = blends[near]
    swapped = lax.ppermute(own, "fsdp", [(i, i ^ near) for i in range(ranks)])
    arrived = {step: to_inner(blends[step], step) for step in far}
    *blends, token = blend(False, tables, momentum, gradient, [token, touch(swapped)])
    last_blocks = [blends[0]] + [to_inner(blends[step], step) for step in range(1, ranks)]
    new_momentum, token = fresh_momentum(tables, momentum, gradient, token)
    handed = {step: from_inner(arrived[step], near) for step in far}

    def ordered(base, opposite, others):
        return [{0: base, near: opposite, **others}[step] for step in range(ranks)]

    first_blocks = ordered(own, swapped, arrived)
    pair, keep, send = assemble_and_gram(True, tables, first_blocks, *[handed[step] for step in far[1:]])

    def first_update(pair, keep, send, after):
        return apply_update(True, [0, *early], tables, *sum_halves(keep, send, "tensor"), pair, slots, after)

    def first_skip(*_):
        return nothing(update_shapes(True, [0, *early], slots, columns))

    packed, own_first, *homes = lax.cond(inner, first_update, first_skip, pair, keep, send, touch(keep, 10**11))
    packed_there = from_inner(packed, near)
    iterate = assemble_outer(tables, ordered(swapped, own, handed))
    first_home = [from_inner(block, step) for step, block in zip(early, homes)]

    def last_update(after, *blocks):
        pair, keep, send = assemble_and_gram(False, tables, blocks, after)
        return apply_update(False, [0, *last], tables, *sum_halves(keep, send, "tensor"), pair, slots)

    def last_skip(*_):
        return nothing(update_shapes(False, [0, *last], slots, columns))

    result, own_last, *homes = lax.cond(inner, last_update, last_skip, iterate, *last_blocks)
    last_home = [from_inner(block, step) for step, block in zip(last, homes)]

    result, shards = finish(tables, packed_there, iterate, result, own_first, own_last, momentum.shape, token)
    shards = place_blocks(True, owner_group, early, first_home, shards, ranks)
    for step, block in zip(last, last_home):
        shards = place_blocks(False, owner_group, [step], [block], shards, ranks)
    return (new_momentum, shards, result[None])


def solution(mesh):
    placed = (P(None, "fsdp", "tensor"), P(None, "fsdp", "tensor"), P(), P(), P(), P())
    return jax.shard_map(
        on_device,
        mesh=mesh,
        in_specs=placed,
        out_specs=(P(None, "fsdp", "tensor"), P(None, "fsdp", "tensor"), P("fsdp", None, "tensor")),
        check_vma=False,
    )
```

```python
import functools
import math

import jax
import jax.numpy as jnp
from jax import lax
from jax.experimental import pallas as pl
from jax.experimental.pallas import tpu as pltpu
from jax.sharding import PartitionSpec as P

WIDTH = 7168
INNER = 576
PANEL = INNER // 3
TILE = 256
SUBLANES = 8

MOMENTUM_RATE = 0.95
QUINTIC_FIRST = 3.4445
QUINTIC_SECOND = -4.775
QUINTIC_THIRD = 2.0315
EPSILON = 1e-07
OUT_SCALE = 0.2 * math.sqrt(max(INNER, WIDTH))
SMALL = pltpu.CompilerParams(vmem_limit_bytes=1024 * 1024)
FULL = pltpu.CompilerParams(vmem_limit_bytes=60 * 1024 * 1024)
PARAMS = pltpu.CompilerParams(vmem_limit_bytes=24 * 1024 * 1024)
HBM = pl.BlockSpec(memory_space=pltpu.HBM)
ANY = pl.BlockSpec(memory_space=pl.ANY)
VMEM = pl.BlockSpec(memory_space=pltpu.VMEM)


def halves(value):
    high = value.astype(jnp.bfloat16)
    low = (value - high.astype(jnp.float32)).astype(jnp.bfloat16)
    return high, low


def dot(left, right, contract=((1,), (0,))):
    return lax.dot_general(left, right, (contract, ((), ())), preferred_element_type=jnp.float32)


DEPTH = INNER // TILE * TILE
PARTS = [(side, rows) for rows in ((0, DEPTH), (DEPTH, INNER)) if rows[0] < rows[1] for side in (1, 0, 0)]


def passes_left(value):
    high, low = halves(value)
    return jnp.concatenate(
        [part[:, first:last] for first, last in ((0, DEPTH), (DEPTH, INNER)) for part in (high, low, high)], axis=1
    )


def passes_right(value):
    sides = halves(value)
    return jnp.concatenate([sides[side][first:last] for side, (first, last) in PARTS], axis=0)


def is_inner(rank, ranks):
    low = ranks // 4
    return (rank >= low) & (rank < ranks - low)


def mate(ranks):
    return ranks // 4


def table_scratch(matrices, ranks):
    return [
        pltpu.SMEM((matrices,), jnp.int32),
        pltpu.SMEM((ranks,), jnp.int32),
        pltpu.SMEM((matrices, ranks), jnp.int32),
        pltpu.SMEM((matrices, ranks), jnp.int32),
        pltpu.SemaphoreType.DMA((4,)),
    ]


def fetch_tables(tables, held):
    *places, arrive = held
    copies = [
        pltpu.make_async_copy(table, place, arrive.at[index])
        for index, (table, place) in enumerate(zip(tables, places))
    ]
    for copy in copies:
        copy.start()
    for copy in copies:
        copy.wait()
    return places


def matrix_of(owner_group, rank):
    found = jnp.int32(0)
    for matrix in range(owner_group.shape[0]):
        found = jnp.where(owner_group[matrix] == rank, matrix, found)
    return found


def over_tiles(tiles, body, carry):
    group = next(group for group in (6, 3, 2, 1) if tiles % group == 0)

    def step(index, carry):
        for member in range(group):
            carry = body(index * group + member, carry)
        return carry

    return lax.fori_loop(0, tiles // group, step, carry)


def each_copy(copies, action):
    for condition, source, place, flag in copies:

        @pl.when(condition)
        def _(source=source, place=place, flag=flag):
            getattr(pltpu.make_async_copy(source, place, flag), action)()


def blend_kernel(first, chunks, *refs):
    tables, (momentum, gradient) = refs[:4], refs[4:6]
    ranks = tables[1].shape[0]
    *outs, token, olds, grads, arrive, leave = refs[-ranks - 10 : -5]
    owner_group, live_ranks, row_counts, _ = fetch_tables(tables, refs[-5:])
    rank = lax.axis_index("fsdp")
    slots, columns = outs[0].shape
    size = slots // chunks
    jobs = []
    for step in range(1, ranks + 1):
        step = step % ranks
        if first and step == 0:
            continue
        target = rank ^ step
        wanted = is_inner(target, ranks)
        matrix = matrix_of(owner_group, target ^ mate(ranks) if first else target)
        if first and step == mate(ranks):
            matrix = matrix_of(owner_group, jnp.where(wanted, rank, target))
            wanted = rank >= 0
        count = row_counts[matrix, rank] * live_ranks[rank]
        for chunk in range(chunks):
            part = pl.ds(chunk * size, size)
            flags = arrive.at[step, chunk, 0], arrive.at[step, chunk, 1]
            incoming = (
                (wanted, momentum.at[matrix, part], olds.at[step, part], flags[0]),
                (wanted, gradient.at[matrix, part], grads.at[step, part], flags[1]),
            )
            outgoing = (wanted, olds.at[step, part], outs[step].at[part], leave.at[step, chunk])
            jobs.append((step, chunk, count, incoming, outgoing))
            each_copy(incoming, "start")
    token[...] = jnp.zeros_like(token)
    for step, chunk, count, incoming, outgoing in jobs:

        @pl.when(incoming[0][0])
        def _(step=step, chunk=chunk, count=count, incoming=incoming, outgoing=outgoing):
            for _, source, place, flag in incoming:
                pltpu.make_async_copy(source, place, flag).wait()
            rows = slice(chunk * size, (chunk + 1) * size)
            grad_now = grads[step, rows, :]
            fresh = MOMENTUM_RATE * olds[step, rows, :] + grad_now
            position = lax.broadcasted_iota(jnp.int32, (size, columns), 0) + chunk * size
            olds[step, rows, :] = jnp.where(position < count, grad_now + MOMENTUM_RATE * fresh, 0.0)
            pltpu.make_async_copy(*outgoing[1:]).start()

    each_copy([job[-1] for job in jobs], "wait")


def fresh_kernel(live_ranks, row_counts, momentum, gradient, _, out, token):
    token[...] = jnp.zeros_like(token)
    rank, matrix = lax.axis_index("fsdp"), pl.program_id(0)
    position = lax.broadcasted_iota(jnp.int32, out.shape, 0)
    keep = position < row_counts[matrix, rank] * live_ranks[rank]
    out[...] = jnp.where(keep, MOMENTUM_RATE * momentum[...] + gradient[...], 0.0)


def assemble(blocks, landed, padded, arrive, tables, held, first):
    ranks, slots, columns = landed.shape
    copies = []
    for step in range(ranks):
        copies.append(pltpu.make_async_copy(blocks[step], landed.at[step], arrive.at[step]))
        copies[-1].start()
    owner_group, _, _, row_offsets = fetch_tables(tables, held)
    rank = lax.axis_index("fsdp")
    base = jnp.where(is_inner(rank, ranks), rank, rank ^ mate(ranks))
    matrix = matrix_of(owner_group, base ^ mate(ranks) if first else base)
    padded[...] = jnp.zeros_like(padded)
    sublane = lax.broadcasted_iota(jnp.int32, (SUBLANES, columns), 0)
    for step in range(ranks):
        start = row_offsets[matrix, base ^ step]
        shift = start % SUBLANES
        origin = start - shift
        copies[step].wait()

        def tile(index, before, origin=origin, shift=shift, step=step):
            moved = pltpu.roll(landed[step, pl.ds(pl.multiple_of(index * SUBLANES, SUBLANES), SUBLANES), :], shift, 0)
            rows = pl.ds(pl.multiple_of(origin + index * SUBLANES, SUBLANES), SUBLANES)
            padded[rows, :] = padded[rows, :] + jnp.where(sublane < shift, before, moved)
            return moved

        after = over_tiles(slots // SUBLANES, tile, jnp.zeros((SUBLANES, columns), jnp.float32))
        rows = pl.ds(pl.multiple_of(origin + slots, SUBLANES), SUBLANES)
        padded[rows, :] = padded[rows, :] + jnp.where(sublane < shift, after, 0.0)


def outer_kernel(ranks, *refs):
    landed, padded, arrive, leave = refs[-9:-5]

    @pl.when(jnp.logical_not(is_inner(lax.axis_index("fsdp"), ranks)))
    def _():
        assemble(refs[4 : 4 + ranks], landed, padded, arrive, refs[:4], refs[-5:], True)
        copy = pltpu.make_async_copy(padded.at[pl.ds(0, INNER)], refs[4 + ranks], leave.at[0])
        copy.start()
        copy.wait()


def gram_kernel(first, ranks, *refs):
    pair, keep, send = refs[-15:-12]
    landed, padded, high_held, low_held, gram, arrive, leave = refs[-12:-5]

    @pl.when(is_inner(lax.axis_index("fsdp"), ranks))
    def _():
        assemble(refs[4 : 4 + ranks], landed, padded, arrive, refs[:4], refs[-5:], first)
        high, low = halves(padded[:INNER, :])
        high_held[...] = high
        low_held[...] = low
        outgoing = [
            pltpu.make_async_copy(high_held, pair.at[0], leave.at[0]),
            pltpu.make_async_copy(low_held, pair.at[1], leave.at[1]),
        ]
        for copy in outgoing:
            copy.start()
        left = jnp.concatenate([high, low, high], axis=1)
        right = jnp.concatenate([low, high, high], axis=1)
        for panel in range(3):
            here = slice(panel * PANEL, (panel + 1) * PANEL)
            store_panel(gram, panel, dot(left[panel * PANEL :], right[here], ((1,), (1,))))
        mine, other = core_rows()
        keep[...] = gram[mine, :]
        send[...] = gram[other, :]
        for copy in outgoing:
            copy.wait()


def core_rows():
    half = INNER // 2
    first = (lax.axis_index("tensor") & 1) * half
    return tuple(pl.ds(pl.multiple_of(start, SUBLANES), half) for start in (first, half - first))


def store_panel(packed, panel, part):
    if panel == 0:
        packed[:, :PANEL] = part
    elif panel == 1:
        packed[: 2 * PANEL, PANEL:] = part
    else:
        packed[2 * PANEL :, PANEL:] = part


def unpack(packed, gram):
    gram[:, :PANEL] = packed[:, :PANEL]
    gram[PANEL:, PANEL : 2 * PANEL] = packed[: 2 * PANEL, PANEL:]
    gram[2 * PANEL :, 2 * PANEL :] = packed[2 * PANEL :, PANEL:]
    gram[:PANEL, PANEL:] = packed[PANEL:, :PANEL].T
    gram[PANEL : 2 * PANEL, 2 * PANEL :] = packed[PANEL : 2 * PANEL, PANEL:].T
    return gram[...]


def symmetric_product(left, right, out):
    for begin in range(0, INNER, TILE):
        end = min(begin + TILE, INNER)
        part = dot(left[begin:], right[:, begin:end])
        out[begin:, begin:end] = part
        if end < INNER:
            out[begin:end, end:] = part[end - begin :].T
    return out[...]


def polynomial(raw, gram):
    diagonal = lax.broadcasted_iota(jnp.int32, raw.shape, 0) == lax.broadcasted_iota(jnp.int32, raw.shape, 1)
    square_total = jnp.sum(jnp.where(diagonal, raw, 0.0))
    norm = jnp.sqrt(jnp.full((1, 1), square_total, jnp.float32)) + EPSILON
    inverse = 1.0 / norm
    first = (raw * inverse) * inverse
    first_right = passes_right(first)
    second = symmetric_product(passes_left(first), first_right, gram)
    base = QUINTIC_SECOND * first + QUINTIC_THIRD * second + jnp.where(diagonal, QUINTIC_FIRST, 0.0)
    base_left = passes_left(base)
    third = symmetric_product(base_left, first_right, gram)
    next_gram = symmetric_product(base_left, passes_right(third), gram)
    square = symmetric_product(passes_left(next_gram), passes_right(next_gram), gram)
    outer = QUINTIC_SECOND * next_gram + QUINTIC_THIRD * square + jnp.where(diagonal, QUINTIC_FIRST, 0.0)
    return symmetric_product(passes_left(outer), passes_right(base), gram) * (inverse * OUT_SCALE)


def extract(padded, start, count, staged, step):
    _, slots, columns = staged.shape
    sublane = lax.broadcasted_iota(jnp.int32, (SUBLANES, columns), 0)
    shift = start % SUBLANES
    base = start - shift
    back = jnp.where(shift == 0, 0, SUBLANES - shift)

    def window(index):
        rows = pl.ds(pl.multiple_of(base + index * SUBLANES, SUBLANES), SUBLANES)
        return pltpu.roll(padded[rows, :], back, 0)

    def tile(index, here):
        after = window(index + 1)
        moved = jnp.where(sublane < SUBLANES - shift, here, after)
        rows = pl.ds(pl.multiple_of(index * SUBLANES, SUBLANES), SUBLANES)
        staged[step, rows, :] = jnp.where(sublane < count - index * SUBLANES, moved, 0.0)
        return after

    over_tiles(slots // SUBLANES, tile, window(0))


def update_kernel(first, steps, *refs):
    tables, (keep, away, pair), refs = refs[:4], refs[4:7], refs[8 if first else 7 :]
    whole, refs = refs[0], refs[1:]
    homes, refs = refs[: len(steps)], refs[len(steps) :]
    gram, padded, staged, stacked, held, arrive, leave = refs[:7]
    ranks = tables[1].shape[0]
    rank = lax.axis_index("fsdp")

    @pl.when(is_inner(rank, ranks))
    def _():
        incoming, begin = [], 0
        for index, (side, (first_row, last_row)) in enumerate(PARTS):
            size = last_row - first_row
            source = pair.at[side, pl.ds(first_row, size)]
            incoming.append(pltpu.make_async_copy(source, stacked.at[pl.ds(begin, size)], arrive.at[index]))
            incoming[-1].start()
            begin += size
        owner_group, live_ranks, row_counts, row_offsets = fetch_tables(tables, refs[7:])
        matrix = matrix_of(owner_group, rank ^ mate(ranks) if first else rank)
        mine, other = core_rows()
        held[mine, :] = keep[...]
        held[other, :] = away[...]
        total = polynomial(unpack(held, gram), gram)
        copies = []
        if first:
            for panel in range(3):
                store_panel(held, panel, total[panel * PANEL :, panel * PANEL : (panel + 1) * PANEL])
            copies = [pltpu.make_async_copy(held, whole, leave.at[len(steps)])]
            copies[0].start()
        for copy in incoming:
            copy.wait()
        padded[:INNER, :] = dot(passes_left(total), stacked[...])
        if not first:
            copies = [pltpu.make_async_copy(padded.at[pl.ds(0, INNER)], whole, leave.at[len(steps)])]
            copies[0].start()
        for index, step in enumerate(steps):
            target = rank ^ step
            count = row_counts[matrix, target] * live_ranks[target]
            extract(padded, row_offsets[matrix, target], count, staged, index)
            copies.append(pltpu.make_async_copy(staged.at[index], homes[index], leave.at[index]))
            copies[-1].start()
        for copy in copies:
            copy.wait()


def finish_kernel(ranks, *refs):
    tables, (packed, iterate, inner_result, own_first, own_last), refs = refs[:4], refs[4:9], refs[10:]
    (result, shards), refs = refs[:2], refs[2:]
    gram, padded, staged, whole, held, arrive, leave = refs[:7]
    rank = lax.axis_index("fsdp")
    owner_group, live_ranks, row_counts, row_offsets = fetch_tables(tables, refs[7:])
    matrix = matrix_of(owner_group, rank)

    def run(jobs):
        copies = [pltpu.make_async_copy(*job) for job in jobs]
        for copy in copies:
            copy.start()
        for copy in copies:
            copy.wait()

    @pl.when(is_inner(rank, ranks))
    def _():
        run(
            [
                (inner_result, whole, arrive.at[0]),
                (own_first, staged.at[0], arrive.at[1]),
                (own_last, staged.at[1], arrive.at[2]),
            ]
        )
        other = matrix_of(owner_group, rank ^ mate(ranks))
        run(
            [
                (whole, result, leave.at[0]),
                (staged.at[0], shards.at[other], leave.at[1]),
                (staged.at[1], shards.at[matrix], leave.at[2]),
            ]
        )

    @pl.when(jnp.logical_not(is_inner(rank, ranks)))
    def _():
        run([(iterate, whole, arrive.at[0]), (packed, held, arrive.at[1])])
        padded[:INNER, :] = dot(passes_left(unpack(held, gram)), passes_right(whole[...]))
        extract(padded, row_offsets[matrix, rank], row_counts[matrix, rank] * live_ranks[rank], staged, 0)
        run(
            [
                (padded.at[pl.ds(0, INNER)], result, leave.at[0]),
                (staged.at[0], shards.at[matrix], leave.at[1]),
            ]
        )


def place_kernel(first, ranks, steps, *refs):
    table, blocks, shards = refs[0], refs[1 : 1 + len(steps)], refs[2 + len(steps)]
    owner_group, arrive, leave = refs[3 + len(steps) :]
    rank = lax.axis_index("fsdp")
    fetch = pltpu.make_async_copy(table, owner_group, arrive)
    fetch.start()
    fetch.wait()
    copies = []
    for index, step in enumerate(steps):
        source = rank ^ step
        matrix = matrix_of(owner_group, source ^ mate(ranks) if first else source)
        copies.append((is_inner(source, ranks), blocks[index], shards.at[matrix], leave.at[index]))
    each_copy(copies, "start")
    each_copy(copies, "wait")


def idle_kernel(*refs):
    pass


def floats(*shape):
    return jax.ShapeDtypeStruct(shape, jnp.float32)


def vmem(*shape, dtype=jnp.float32):
    return pltpu.VMEM(shape, dtype)


def flags(*shape):
    return pltpu.SemaphoreType.DMA(shape)


FREE = pl.CostEstimate(flops=0, bytes_accessed=0, transcendentals=0)


def blend(first, tables, momentum, gradient, before):
    _, slots, columns = momentum.shape
    ranks = tables[1].shape[0]
    chunks = 2 if slots % (2 * SUBLANES) == 0 else 1
    return pl.pallas_call(
        functools.partial(blend_kernel, first, chunks),
        out_shape=[floats(slots, columns)] * ranks + [floats(SUBLANES, 128)],
        in_specs=[HBM] * 6 + [ANY] * len(before),
        out_specs=[HBM] * ranks + [VMEM],
        scratch_shapes=[vmem(ranks, slots, columns)] * 2
        + [flags(ranks, chunks, 2), flags(ranks, chunks)]
        + table_scratch(*tables[2].shape),
        compiler_params=FULL,
        cost_estimate=FREE,
        name="blend",
    )(*tables, momentum, gradient, *before)


def fresh_momentum(tables, momentum, gradient, before):
    matrices, slots, columns = momentum.shape
    block = pl.BlockSpec((None, slots, columns), lambda matrix: (matrix, 0, 0))
    return pl.pallas_call(
        fresh_kernel,
        grid=(matrices,),
        out_shape=[floats(*momentum.shape), floats(SUBLANES, 128)],
        in_specs=[pl.BlockSpec(memory_space=pltpu.SMEM)] * 2 + [block] * 2 + [ANY],
        out_specs=[block, pl.BlockSpec((SUBLANES, 128), lambda matrix: (0, 0))],
        compiler_params=FULL,
        cost_estimate=FREE,
        name="fresh_momentum",
    )(*tables[1:3], momentum, gradient, before)


def assemble_and_gram(first, tables, blocks, *after):
    slots, columns = blocks[0].shape
    ranks = len(blocks)
    pair = jax.ShapeDtypeStruct((4, INNER, columns), jnp.bfloat16)
    return pl.pallas_call(
        functools.partial(gram_kernel, first, ranks),
        out_shape=[pair] + [floats(INNER // 2, 2 * PANEL)] * 2,
        in_specs=[HBM] * 4 + [ANY] * (ranks + len(after)),
        out_specs=[ANY, VMEM, VMEM],
        scratch_shapes=[
            vmem(ranks, slots, columns),
            vmem(INNER + slots + SUBLANES, columns),
            vmem(INNER, columns, dtype=jnp.bfloat16),
            vmem(INNER, columns, dtype=jnp.bfloat16),
            vmem(INNER, 2 * PANEL),
            flags(ranks),
            flags(2),
        ]
        + table_scratch(*tables[2].shape),
        compiler_params=PARAMS,
        cost_estimate=FREE,
        name="assemble_and_gram",
    )(*tables, *blocks, *after)


def assemble_outer(tables, blocks):
    slots, columns = blocks[0].shape
    ranks = len(blocks)
    return pl.pallas_call(
        functools.partial(outer_kernel, ranks),
        out_shape=floats(INNER, columns),
        in_specs=[HBM] * 4 + [ANY] * ranks,
        out_specs=ANY,
        scratch_shapes=[
            vmem(ranks, slots, columns),
            vmem(INNER + slots + SUBLANES, columns),
            flags(ranks),
            flags(1),
        ]
        + table_scratch(*tables[2].shape),
        compiler_params=PARAMS,
        cost_estimate=FREE,
        name="assemble_outer",
    )(*tables, *blocks)


def update_shapes(first, steps, slots, columns):
    whole = floats(INNER, 2 * PANEL if first else columns)
    return [whole] + [floats(slots, columns)] * len(steps)


def nothing(shapes):
    return pl.pallas_call(
        idle_kernel, out_shape=shapes, out_specs=[ANY] * len(shapes), compiler_params=SMALL, name="nothing"
    )()


def apply_update(first, steps, tables, keep, away, pair, slots, *after):
    columns = pair.shape[2]
    return pl.pallas_call(
        functools.partial(update_kernel, first, steps),
        out_shape=update_shapes(first, steps, slots, columns),
        in_specs=[HBM] * 4 + [VMEM] * 2 + [ANY] * (1 + len(after)),
        out_specs=[ANY] * (1 + len(steps)),
        scratch_shapes=[
            vmem(INNER, INNER),
            vmem(INNER + slots + 2 * SUBLANES, columns),
            vmem(len(steps), slots, columns),
            vmem(3 * INNER, columns, dtype=jnp.bfloat16),
            vmem(INNER, 2 * PANEL),
            flags(len(PARTS)),
            flags(len(steps) + 1),
        ]
        + table_scratch(*tables[2].shape),
        compiler_params=PARAMS,
        cost_estimate=FREE,
        name="apply_update",
    )(*tables, keep, away, pair, *after)


def touch(value, flops=0):
    return pl.pallas_call(
        idle_kernel,
        out_shape=floats(SUBLANES, 128),
        in_specs=[ANY],
        out_specs=ANY,
        compiler_params=SMALL,
        cost_estimate=pl.CostEstimate(flops=flops, bytes_accessed=0, transcendentals=0),
        name="touch",
    )(value)


def finish(tables, packed, iterate, inner_result, own_first, own_last, shape, after):
    slots, columns = own_first.shape
    return pl.pallas_call(
        functools.partial(finish_kernel, tables[1].shape[0]),
        out_shape=[floats(INNER, columns), floats(*shape)],
        in_specs=[HBM] * 4 + [ANY] * 6,
        out_specs=[HBM] * 2,
        scratch_shapes=[
            vmem(INNER, INNER),
            vmem(INNER + slots + 2 * SUBLANES, columns),
            vmem(2, slots, columns),
            vmem(INNER, columns),
            vmem(INNER, 2 * PANEL),
            flags(3),
            flags(3),
        ]
        + table_scratch(*tables[2].shape),
        compiler_params=PARAMS,
        cost_estimate=FREE,
        name="finish",
    )(*tables, packed, iterate, inner_result, own_first, own_last, after)


def place_blocks(first, owner_group, steps, blocks, shards, ranks):
    return pl.pallas_call(
        functools.partial(place_kernel, first, ranks, steps),
        out_shape=floats(*shards.shape),
        in_specs=[HBM] + [VMEM] * len(blocks) + [HBM],
        out_specs=HBM,
        scratch_shapes=[pltpu.SMEM(owner_group.shape, jnp.int32), flags(), flags(len(steps))],
        input_output_aliases={1 + len(blocks): 0},
        compiler_params=PARAMS,
        cost_estimate=FREE,
        name="place_blocks",
    )(owner_group, *blocks, shards)


def sum_halves(keep, send, axis, streams):
    size = lax.axis_size(axis)

    def exchange(piece, bits):
        return lax.ppermute(piece, axis, [(i, i ^ bits[i & 1]) for i in range(size)])

    chips = [1 << shift for shift in range(1, size.bit_length() - 1)]
    keep = keep + exchange(send, (1, 1))
    pieces = jnp.split(keep, streams, axis=0)
    for bits in zip(chips, reversed(chips)):
        pieces = [piece + exchange(piece, bits[:: 1 - 2 * index]) for index, piece in enumerate(pieces)]
    keep = jnp.concatenate(pieces, axis=0)
    return keep, exchange(keep, (1, 1))


def on_device(momentum, gradient, live_ranks, owner_group, row_counts, row_offsets):
    ranks = lax.axis_size("fsdp")
    _, slots, columns = momentum.shape
    inner = is_inner(lax.axis_index("fsdp"), ranks)
    tables = (owner_group, live_ranks, row_counts, row_offsets)
    last = [2, 1, *range(3, ranks)]
    early = [step for step in last if step != mate(ranks)]

    def pairs(step, inward):
        return [(i, i ^ step) for i in range(ranks) if is_inner(i ^ step if inward else i, ranks)]

    def to_inner(block, step):
        return lax.ppermute(block, "fsdp", pairs(step, True))

    def from_inner(block, step):
        return lax.ppermute(block, "fsdp", pairs(step, False))

    near = mate(ranks)
    far = [step for step in last if step != near]
    *blends, token = blend(True, tables, momentum, gradient, [])
    own = blends[near]
    swapped = lax.ppermute(own, "fsdp", [(i, i ^ near) for i in range(ranks)])
    arrived = {step: to_inner(blends[step], step) for step in far}
    *blends, token = blend(False, tables, momentum, gradient, [token, touch(swapped)])
    last_blocks = [blends[0]] + [to_inner(blends[step], step) for step in range(1, ranks)]
    new_momentum, token = fresh_momentum(tables, momentum, gradient, token)
    handed = {step: from_inner(arrived[step], near) for step in far}

    def ordered(base, opposite, others):
        return [{0: base, near: opposite, **others}[step] for step in range(ranks)]

    first_blocks = ordered(own, swapped, arrived)
    pair, keep, send = assemble_and_gram(True, tables, first_blocks, *[handed[step] for step in far[1:]])

    def first_update(pair, keep, send, after):
        return apply_update(True, [0, *early], tables, *sum_halves(keep, send, "tensor", 1), pair, slots, after)

    def first_skip(*_):
        return nothing(update_shapes(True, [0, *early], slots, columns))

    packed, own_first, *homes = lax.cond(inner, first_update, first_skip, pair, keep, send, touch(keep, 10**11))
    packed_there = from_inner(packed, near)
    iterate = assemble_outer(tables, ordered(swapped, own, handed))
    first_home = [from_inner(block, step) for step, block in zip(early, homes)]

    def last_update(after, *blocks):
        pair, keep, send = assemble_and_gram(False, tables, blocks, after)
        return apply_update(False, [0, *last], tables, *sum_halves(keep, send, "tensor", 2), pair, slots)

    def last_skip(*_):
        return nothing(update_shapes(False, [0, *last], slots, columns))

    result, own_last, *homes = lax.cond(inner, last_update, last_skip, iterate, *last_blocks)
    last_home = [from_inner(block, step) for step, block in zip(last, homes)]

    result, shards = finish(tables, packed_there, iterate, result, own_first, own_last, momentum.shape, token)
    shards = place_blocks(True, owner_group, early, first_home, shards, ranks)
    for step, block in zip(last, last_home):
        shards = place_blocks(False, owner_group, [step], [block], shards, ranks)
    return (new_momentum, shards, result[None])


def solution(mesh):
    placed = (P(None, "fsdp", "tensor"), P(None, "fsdp", "tensor"), P(), P(), P(), P())
    return jax.shard_map(
        on_device,
        mesh=mesh,
        in_specs=placed,
        out_specs=(P(None, "fsdp", "tensor"), P(None, "fsdp", "tensor"), P("fsdp", None, "tensor")),
        check_vma=False,
    )
```

```python
import functools
import math

import jax
import jax.numpy as jnp
from jax import lax
from jax.experimental import pallas as pl
from jax.experimental.pallas import tpu as pltpu
from jax.sharding import PartitionSpec as P

WIDTH = 7168
INNER = 576
PANEL = INNER // 3
TILE = 256
SUBLANES = 8

MOMENTUM_RATE = 0.95
QUINTIC_FIRST = 3.4445
QUINTIC_SECOND = -4.775
QUINTIC_THIRD = 2.0315
EPSILON = 1e-07
OUT_SCALE = 0.2 * math.sqrt(max(INNER, WIDTH))
SMALL = pltpu.CompilerParams(vmem_limit_bytes=1024 * 1024)
FULL = pltpu.CompilerParams(vmem_limit_bytes=60 * 1024 * 1024)
PARAMS = pltpu.CompilerParams(vmem_limit_bytes=24 * 1024 * 1024)
HBM = pl.BlockSpec(memory_space=pltpu.HBM)
ANY = pl.BlockSpec(memory_space=pl.ANY)
VMEM = pl.BlockSpec(memory_space=pltpu.VMEM)


def halves(value):
    high = value.astype(jnp.bfloat16)
    low = (value - high.astype(jnp.float32)).astype(jnp.bfloat16)
    return high, low


def dot(left, right, contract=((1,), (0,))):
    return lax.dot_general(left, right, (contract, ((), ())), preferred_element_type=jnp.float32)


DEPTH = INNER // TILE * TILE
PARTS = [(side, rows) for rows in ((0, DEPTH), (DEPTH, INNER)) if rows[0] < rows[1] for side in (1, 0, 0)]


def passes_left(value):
    high, low = halves(value)
    return jnp.concatenate(
        [part[:, first:last] for first, last in ((0, DEPTH), (DEPTH, INNER)) for part in (high, low, high)], axis=1
    )


def passes_right(value):
    sides = halves(value)
    return jnp.concatenate([sides[side][first:last] for side, (first, last) in PARTS], axis=0)


def is_inner(rank, ranks):
    low = ranks // 4
    return (rank >= low) & (rank < ranks - low)


def mate(ranks):
    return ranks // 4


def table_scratch(matrices, ranks):
    return [
        pltpu.SMEM((matrices,), jnp.int32),
        pltpu.SMEM((ranks,), jnp.int32),
        pltpu.SMEM((matrices, ranks), jnp.int32),
        pltpu.SMEM((matrices, ranks), jnp.int32),
        pltpu.SemaphoreType.DMA((4,)),
    ]


def fetch_tables(tables, held):
    *places, arrive = held
    copies = [
        pltpu.make_async_copy(table, place, arrive.at[index])
        for index, (table, place) in enumerate(zip(tables, places))
    ]
    for copy in copies:
        copy.start()
    for copy in copies:
        copy.wait()
    return places


def matrix_of(owner_group, rank):
    found = jnp.int32(0)
    for matrix in range(owner_group.shape[0]):
        found = jnp.where(owner_group[matrix] == rank, matrix, found)
    return found


def over_tiles(tiles, body, carry):
    group = next(group for group in (6, 3, 2, 1) if tiles % group == 0)

    def step(index, carry):
        for member in range(group):
            carry = body(index * group + member, carry)
        return carry

    return lax.fori_loop(0, tiles // group, step, carry)


def each_copy(copies, action):
    for condition, source, place, flag in copies:

        @pl.when(condition)
        def _(source=source, place=place, flag=flag):
            getattr(pltpu.make_async_copy(source, place, flag), action)()


def blend_kernel(first, chunks, *refs):
    tables, (momentum, gradient) = refs[:4], refs[4:6]
    ranks = tables[1].shape[0]
    *outs, token, olds, grads, arrive, leave = refs[-ranks - 10 + first : -5]
    owner_group, live_ranks, row_counts, _ = fetch_tables(tables, refs[-5:])
    rank = lax.axis_index("fsdp")
    slots, columns = outs[0].shape
    size = slots // chunks
    jobs = []
    for step in range(1, ranks + 1):
        step = step % ranks
        if first and step == 0:
            continue
        target = rank ^ step
        wanted = is_inner(target, ranks)
        matrix = matrix_of(owner_group, target ^ mate(ranks) if first else target)
        if first and step == mate(ranks):
            matrix = matrix_of(owner_group, jnp.where(wanted, rank, target))
            wanted = rank >= 0
        count = row_counts[matrix, rank] * live_ranks[rank]
        for chunk in range(chunks):
            part = pl.ds(chunk * size, size)
            flags = arrive.at[step, chunk, 0], arrive.at[step, chunk, 1]
            incoming = (
                (wanted, momentum.at[matrix, part], olds.at[step, part], flags[0]),
                (wanted, gradient.at[matrix, part], grads.at[step, part], flags[1]),
            )
            outgoing = (wanted, olds.at[step, part], outs[step - first].at[part], leave.at[step, chunk])
            jobs.append((step, chunk, count, incoming, outgoing))
            each_copy(incoming, "start")
    token[...] = jnp.zeros_like(token)
    for step, chunk, count, incoming, outgoing in jobs:

        @pl.when(incoming[0][0])
        def _(step=step, chunk=chunk, count=count, incoming=incoming, outgoing=outgoing):
            for _, source, place, flag in incoming:
                pltpu.make_async_copy(source, place, flag).wait()
            rows = slice(chunk * size, (chunk + 1) * size)
            grad_now = grads[step, rows, :]
            fresh = MOMENTUM_RATE * olds[step, rows, :] + grad_now
            position = lax.broadcasted_iota(jnp.int32, (size, columns), 0) + chunk * size
            olds[step, rows, :] = jnp.where(position < count, grad_now + MOMENTUM_RATE * fresh, 0.0)
            pltpu.make_async_copy(*outgoing[1:]).start()

    each_copy([job[-1] for job in jobs], "wait")


def fresh_kernel(live_ranks, row_counts, momentum, gradient, _, out, token):
    token[...] = jnp.zeros_like(token)
    rank, matrix = lax.axis_index("fsdp"), pl.program_id(0)
    position = lax.broadcasted_iota(jnp.int32, out.shape, 0)
    keep = position < row_counts[matrix, rank] * live_ranks[rank]
    out[...] = jnp.where(keep, MOMENTUM_RATE * momentum[...] + gradient[...], 0.0)


def assemble(blocks, landed, padded, arrive, tables, held, first):
    ranks, slots, columns = landed.shape
    copies = []
    for step in range(ranks):
        copies.append(pltpu.make_async_copy(blocks[step], landed.at[step], arrive.at[step]))
        copies[-1].start()
    owner_group, _, _, row_offsets = fetch_tables(tables, held)
    rank = lax.axis_index("fsdp")
    base = jnp.where(is_inner(rank, ranks), rank, rank ^ mate(ranks))
    matrix = matrix_of(owner_group, base ^ mate(ranks) if first else base)
    padded[...] = jnp.zeros_like(padded)
    sublane = lax.broadcasted_iota(jnp.int32, (SUBLANES, columns), 0)
    for step in range(ranks):
        start = row_offsets[matrix, base ^ step]
        shift = start % SUBLANES
        origin = start - shift
        copies[step].wait()

        def tile(index, before, origin=origin, shift=shift, step=step):
            moved = pltpu.roll(landed[step, pl.ds(pl.multiple_of(index * SUBLANES, SUBLANES), SUBLANES), :], shift, 0)
            rows = pl.ds(pl.multiple_of(origin + index * SUBLANES, SUBLANES), SUBLANES)
            padded[rows, :] = padded[rows, :] + jnp.where(sublane < shift, before, moved)
            return moved

        after = over_tiles(slots // SUBLANES, tile, jnp.zeros((SUBLANES, columns), jnp.float32))
        rows = pl.ds(pl.multiple_of(origin + slots, SUBLANES), SUBLANES)
        padded[rows, :] = padded[rows, :] + jnp.where(sublane < shift, after, 0.0)


def outer_kernel(ranks, *refs):
    landed, padded, arrive, leave = refs[-9:-5]

    @pl.when(jnp.logical_not(is_inner(lax.axis_index("fsdp"), ranks)))
    def _():
        assemble(refs[4 : 4 + ranks], landed, padded, arrive, refs[:4], refs[-5:], True)
        copy = pltpu.make_async_copy(padded.at[pl.ds(0, INNER)], refs[4 + ranks], leave.at[0])
        copy.start()
        copy.wait()


def gram_kernel(first, ranks, *refs):
    pair, keep, send = refs[-15:-12]
    landed, padded, high_held, low_held, gram, arrive, leave = refs[-12:-5]

    @pl.when(is_inner(lax.axis_index("fsdp"), ranks))
    def _():
        assemble(refs[4 : 4 + ranks], landed, padded, arrive, refs[:4], refs[-5:], first)
        high, low = halves(padded[:INNER, :])
        high_held[...] = high
        low_held[...] = low
        outgoing = [
            pltpu.make_async_copy(high_held, pair.at[0], leave.at[0]),
            pltpu.make_async_copy(low_held, pair.at[1], leave.at[1]),
        ]
        for copy in outgoing:
            copy.start()
        left = jnp.concatenate([high, low, high], axis=1)
        right = jnp.concatenate([low, high, high], axis=1)
        for panel in range(3):
            here = slice(panel * PANEL, (panel + 1) * PANEL)
            store_panel(gram, panel, dot(left[panel * PANEL :], right[here], ((1,), (1,))))
        mine, other = core_rows()
        keep[...] = gram[mine, :]
        send[...] = gram[other, :]
        for copy in outgoing:
            copy.wait()


def core_rows():
    half = INNER // 2
    first = (lax.axis_index("tensor") & 1) * half
    return tuple(pl.ds(pl.multiple_of(start, SUBLANES), half) for start in (first, half - first))


def store_panel(packed, panel, part):
    if panel == 0:
        packed[:, :PANEL] = part
    elif panel == 1:
        packed[: 2 * PANEL, PANEL:] = part
    else:
        packed[2 * PANEL :, PANEL:] = part


def unpack(packed, gram):
    gram[:, :PANEL] = packed[:, :PANEL]
    gram[PANEL:, PANEL : 2 * PANEL] = packed[: 2 * PANEL, PANEL:]
    gram[2 * PANEL :, 2 * PANEL :] = packed[2 * PANEL :, PANEL:]
    gram[:PANEL, PANEL:] = packed[PANEL:, :PANEL].T
    gram[PANEL : 2 * PANEL, 2 * PANEL :] = packed[PANEL : 2 * PANEL, PANEL:].T
    return gram[...]


def symmetric_product(left, right, out):
    for begin in range(0, INNER, TILE):
        end = min(begin + TILE, INNER)
        part = dot(left[begin:], right[:, begin:end])
        out[begin:, begin:end] = part
        if end < INNER:
            out[begin:end, end:] = part[end - begin :].T
    return out[...]


def polynomial(raw, gram):
    diagonal = lax.broadcasted_iota(jnp.int32, raw.shape, 0) == lax.broadcasted_iota(jnp.int32, raw.shape, 1)
    square_total = jnp.sum(jnp.where(diagonal, raw, 0.0))
    norm = jnp.sqrt(jnp.full((1, 1), square_total, jnp.float32)) + EPSILON
    inverse = 1.0 / norm
    first = (raw * inverse) * inverse
    first_right = passes_right(first)
    second = symmetric_product(passes_left(first), first_right, gram)
    base = QUINTIC_SECOND * first + QUINTIC_THIRD * second + jnp.where(diagonal, QUINTIC_FIRST, 0.0)
    base_left = passes_left(base)
    third = symmetric_product(base_left, first_right, gram)
    next_gram = symmetric_product(base_left, passes_right(third), gram)
    square = symmetric_product(passes_left(next_gram), passes_right(next_gram), gram)
    outer = QUINTIC_SECOND * next_gram + QUINTIC_THIRD * square + jnp.where(diagonal, QUINTIC_FIRST, 0.0)
    return symmetric_product(passes_left(outer), passes_right(base), gram) * (inverse * OUT_SCALE)


def extract(padded, start, count, staged, step):
    _, slots, columns = staged.shape
    sublane = lax.broadcasted_iota(jnp.int32, (SUBLANES, columns), 0)
    shift = start % SUBLANES
    base = start - shift
    back = jnp.where(shift == 0, 0, SUBLANES - shift)

    def window(index):
        rows = pl.ds(pl.multiple_of(base + index * SUBLANES, SUBLANES), SUBLANES)
        return pltpu.roll(padded[rows, :], back, 0)

    def tile(index, here):
        after = window(index + 1)
        moved = jnp.where(sublane < SUBLANES - shift, here, after)
        rows = pl.ds(pl.multiple_of(index * SUBLANES, SUBLANES), SUBLANES)
        staged[step, rows, :] = jnp.where(sublane < count - index * SUBLANES, moved, 0.0)
        return after

    over_tiles(slots // SUBLANES, tile, window(0))


def stack_copies(pair, stacked, arrive):
    copies, begin = [], 0
    for index, (side, (first_row, last_row)) in enumerate(PARTS):
        size = last_row - first_row
        source = pair.at[side, pl.ds(first_row, size)]
        copies.append(pltpu.make_async_copy(source, stacked.at[pl.ds(begin, size)], arrive.at[index]))
        begin += size
    return copies


def update_kernel(first, steps, *refs):
    tables, (keep, away, pair), refs = refs[:4], refs[4:7], refs[8 if first else 7 :]
    whole, refs = refs[0], refs[1:]
    homes, refs = refs[: len(steps)], refs[len(steps) :]
    gram, padded, staged, stacked, held, arrive, leave = refs[:7]
    ranks = tables[1].shape[0]
    rank = lax.axis_index("fsdp")

    @pl.when(is_inner(rank, ranks))
    def _():
        incoming = stack_copies(pair, stacked, arrive)
        for copy in incoming:
            copy.start()
        owner_group, live_ranks, row_counts, row_offsets = fetch_tables(tables, refs[7:])
        matrix = matrix_of(owner_group, rank ^ mate(ranks) if first else rank)
        mine, other = core_rows()
        held[mine, :] = keep[...]
        held[other, :] = away[...]
        total = polynomial(unpack(held, gram), gram)
        for panel in range(3):
            store_panel(held, panel, total[panel * PANEL :, panel * PANEL : (panel + 1) * PANEL])
        copies = [pltpu.make_async_copy(held, whole, leave.at[len(steps)])]
        copies[0].start()
        for copy in incoming:
            copy.wait()
        padded[:INNER, :] = dot(passes_left(total), stacked[...])
        for index, step in enumerate(steps):
            target = rank ^ step
            count = row_counts[matrix, target] * live_ranks[target]
            extract(padded, row_offsets[matrix, target], count, staged, index)
            copies.append(pltpu.make_async_copy(staged.at[index], homes[index], leave.at[index]))
            copies[-1].start()
        for copy in copies:
            copy.wait()


def finish_kernel(ranks, *refs):
    tables, (first_there, iterate, first_packed, first_pair, last_packed, last_pair) = refs[:4], refs[4:10]
    (result, shards, gram, padded, staged, whole, stacked, held, arrive, leave), refs = refs[11:21], refs[21:]
    rank = lax.axis_index("fsdp")
    owner_group, live_ranks, row_counts, row_offsets = fetch_tables(tables, refs)

    def run(copies):
        for copy in copies:
            copy.start()
        for copy in copies:
            copy.wait()

    def own_block(matrix, index):
        extract(padded, row_offsets[matrix, rank], row_counts[matrix, rank] * live_ranks[rank], staged, index)
        return pltpu.make_async_copy(staged.at[index], shards.at[matrix], leave.at[index])

    def to_result():
        return pltpu.make_async_copy(padded.at[pl.ds(0, INNER)], result, leave.at[2])

    @pl.when(is_inner(rank, ranks))
    def _():
        for index, (packed, pair) in enumerate(((last_packed, last_pair), (first_packed, first_pair))):
            run([pltpu.make_async_copy(packed, held, leave.at[2]), *stack_copies(pair, stacked, arrive)])
            padded[:INNER, :] = dot(passes_left(unpack(held, gram)), stacked[...])
            matrix = matrix_of(owner_group, rank ^ (index * mate(ranks)))
            run([own_block(matrix, index)] + [to_result()] * (index == 0))

    @pl.when(jnp.logical_not(is_inner(rank, ranks)))
    def _():
        run(
            [
                pltpu.make_async_copy(iterate, whole, leave.at[0]),
                pltpu.make_async_copy(first_there, held, leave.at[2]),
            ]
        )
        padded[:INNER, :] = dot(passes_left(unpack(held, gram)), passes_right(whole[...]))
        run([own_block(matrix_of(owner_group, rank), 0), to_result()])


def place_kernel(first, ranks, steps, *refs):
    table, blocks, shards = refs[0], refs[1 : 1 + len(steps)], refs[2 + len(steps)]
    owner_group, arrive, leave = refs[3 + len(steps) :]
    rank = lax.axis_index("fsdp")
    fetch = pltpu.make_async_copy(table, owner_group, arrive)
    fetch.start()
    fetch.wait()
    copies = []
    for index, step in enumerate(steps):
        source = rank ^ step
        matrix = matrix_of(owner_group, source ^ mate(ranks) if first else source)
        copies.append((is_inner(source, ranks), blocks[index], shards.at[matrix], leave.at[index]))
    each_copy(copies, "start")
    each_copy(copies, "wait")


def idle_kernel(*refs):
    pass


def floats(*shape):
    return jax.ShapeDtypeStruct(shape, jnp.float32)


def vmem(*shape, dtype=jnp.float32):
    return pltpu.VMEM(shape, dtype)


def flags(*shape):
    return pltpu.SemaphoreType.DMA(shape)


FREE = pl.CostEstimate(flops=0, bytes_accessed=0, transcendentals=0)


def blend(first, tables, momentum, gradient, before):
    _, slots, columns = momentum.shape
    ranks = tables[1].shape[0]
    chunks = 2 if slots % (2 * SUBLANES) == 0 else 1
    return pl.pallas_call(
        functools.partial(blend_kernel, first, chunks),
        out_shape=[floats(slots, columns)] * (ranks - first) + [floats(SUBLANES, 128)],
        in_specs=[HBM] * 6 + [ANY] * len(before),
        out_specs=[ANY] * (ranks - first) + [VMEM],
        scratch_shapes=[vmem(ranks, slots, columns)] * 2
        + [flags(ranks, chunks, 2), flags(ranks, chunks)]
        + table_scratch(*tables[2].shape),
        compiler_params=FULL,
        cost_estimate=FREE,
        name="blend",
    )(*tables, momentum, gradient, *before)


def fresh_momentum(tables, momentum, gradient, before):
    matrices, slots, columns = momentum.shape
    block = pl.BlockSpec((None, slots, columns), lambda matrix: (matrix, 0, 0))
    return pl.pallas_call(
        fresh_kernel,
        grid=(matrices,),
        out_shape=[floats(*momentum.shape), floats(SUBLANES, 128)],
        in_specs=[pl.BlockSpec(memory_space=pltpu.SMEM)] * 2 + [block] * 2 + [ANY],
        out_specs=[block, pl.BlockSpec((SUBLANES, 128), lambda matrix: (0, 0))],
        compiler_params=FULL,
        cost_estimate=FREE,
        name="fresh_momentum",
    )(*tables[1:3], momentum, gradient, before)


def assemble_and_gram(first, tables, blocks, *after):
    slots, columns = blocks[0].shape
    ranks = len(blocks)
    pair = jax.ShapeDtypeStruct((4, INNER, columns), jnp.bfloat16)
    return pl.pallas_call(
        functools.partial(gram_kernel, first, ranks),
        out_shape=[pair] + [floats(INNER // 2, 2 * PANEL)] * 2,
        in_specs=[HBM] * 4 + [ANY] * (ranks + len(after)),
        out_specs=[ANY, VMEM, VMEM],
        scratch_shapes=[
            vmem(ranks, slots, columns),
            vmem(INNER + slots + SUBLANES, columns),
            vmem(INNER, columns, dtype=jnp.bfloat16),
            vmem(INNER, columns, dtype=jnp.bfloat16),
            vmem(INNER, 2 * PANEL),
            flags(ranks),
            flags(2),
        ]
        + table_scratch(*tables[2].shape),
        compiler_params=PARAMS,
        cost_estimate=FREE,
        name="assemble_and_gram",
    )(*tables, *blocks, *after)


def assemble_outer(tables, blocks):
    slots, columns = blocks[0].shape
    ranks = len(blocks)
    return pl.pallas_call(
        functools.partial(outer_kernel, ranks),
        out_shape=floats(INNER, columns),
        in_specs=[HBM] * 4 + [ANY] * ranks,
        out_specs=ANY,
        scratch_shapes=[
            vmem(ranks, slots, columns),
            vmem(INNER + slots + SUBLANES, columns),
            flags(ranks),
            flags(1),
        ]
        + table_scratch(*tables[2].shape),
        compiler_params=PARAMS,
        cost_estimate=FREE,
        name="assemble_outer",
    )(*tables, *blocks)


def update_shapes(steps, slots, columns):
    return [floats(INNER, 2 * PANEL)] + [floats(slots, columns)] * len(steps)


def nothing(shapes):
    return pl.pallas_call(
        idle_kernel, out_shape=shapes, out_specs=[ANY] * len(shapes), compiler_params=SMALL, name="nothing"
    )()


def apply_update(first, steps, tables, keep, away, pair, slots, *after):
    columns = pair.shape[2]
    return pl.pallas_call(
        functools.partial(update_kernel, first, steps),
        out_shape=update_shapes(steps, slots, columns),
        in_specs=[HBM] * 4 + [VMEM] * 2 + [ANY] * (1 + len(after)),
        out_specs=[ANY] * (1 + len(steps)),
        scratch_shapes=[
            vmem(INNER, INNER),
            vmem(INNER + slots + 2 * SUBLANES, columns),
            vmem(len(steps), slots, columns),
            vmem(3 * INNER, columns, dtype=jnp.bfloat16),
            vmem(INNER, 2 * PANEL),
            flags(len(PARTS)),
            flags(len(steps) + 1),
        ]
        + table_scratch(*tables[2].shape),
        compiler_params=PARAMS,
        cost_estimate=FREE,
        name="apply_update",
    )(*tables, keep, away, pair, *after)


def touch(value, flops=0):
    return pl.pallas_call(
        idle_kernel,
        out_shape=floats(SUBLANES, 128),
        in_specs=[ANY],
        out_specs=ANY,
        compiler_params=SMALL,
        cost_estimate=pl.CostEstimate(flops=flops, bytes_accessed=0, transcendentals=0),
        name="touch",
    )(value)


def finish(tables, first_there, iterate, first_packed, first_pair, last_packed, last_pair, shape, after):
    _, slots, columns = shape
    return pl.pallas_call(
        functools.partial(finish_kernel, tables[1].shape[0]),
        out_shape=[floats(INNER, columns), floats(*shape)],
        in_specs=[HBM] * 4 + [ANY] * 7,
        out_specs=[HBM] * 2,
        scratch_shapes=[
            vmem(INNER, INNER),
            vmem(INNER + slots + 2 * SUBLANES, columns),
            vmem(2, slots, columns),
            vmem(INNER, columns),
            vmem(3 * INNER, columns, dtype=jnp.bfloat16),
            vmem(INNER, 2 * PANEL),
            flags(len(PARTS)),
            flags(3),
        ]
        + table_scratch(*tables[2].shape),
        compiler_params=PARAMS,
        cost_estimate=FREE,
        name="finish",
    )(*tables, first_there, iterate, first_packed, first_pair, last_packed, last_pair, after)


def place_blocks(first, owner_group, steps, blocks, shards, ranks):
    return pl.pallas_call(
        functools.partial(place_kernel, first, ranks, steps),
        out_shape=floats(*shards.shape),
        in_specs=[HBM] + [VMEM] * len(blocks) + [HBM],
        out_specs=HBM,
        scratch_shapes=[pltpu.SMEM(owner_group.shape, jnp.int32), flags(), flags(len(steps))],
        input_output_aliases={1 + len(blocks): 0},
        compiler_params=PARAMS,
        cost_estimate=FREE,
        name="place_blocks",
    )(owner_group, *blocks, shards)


def sum_halves(keep, send, axis, streams):
    size = lax.axis_size(axis)

    def exchange(piece, bits):
        return lax.ppermute(piece, axis, [(i, i ^ bits[i & 1]) for i in range(size)])

    chips = [1 << shift for shift in range(1, size.bit_length() - 1)]
    keep = keep + exchange(send, (1, 1))
    pieces = jnp.split(keep, streams, axis=0)
    for bits in zip(chips, reversed(chips)):
        pieces = [piece + exchange(piece, bits[:: 1 - 2 * index]) for index, piece in enumerate(pieces)]
    keep = jnp.concatenate(pieces, axis=0)
    return keep, exchange(keep, (1, 1))


def on_device(momentum, gradient, live_ranks, owner_group, row_counts, row_offsets):
    ranks = lax.axis_size("fsdp")
    _, slots, columns = momentum.shape
    inner = is_inner(lax.axis_index("fsdp"), ranks)
    tables = (owner_group, live_ranks, row_counts, row_offsets)
    last = [2, 1, *range(3, ranks)]
    early = [step for step in last if step != mate(ranks)]

    def pairs(step, inward):
        return [(i, i ^ step) for i in range(ranks) if is_inner(i ^ step if inward else i, ranks)]

    def to_inner(block, step):
        return lax.ppermute(block, "fsdp", pairs(step, True))

    def from_inner(block, step):
        return lax.ppermute(block, "fsdp", pairs(step, False))

    near = mate(ranks)
    far = [step for step in last if step != near]
    *blends, token = blend(True, tables, momentum, gradient, [])
    own = blends[near - 1]
    swapped = lax.ppermute(own, "fsdp", [(i, i ^ near) for i in range(ranks)])
    arrived = {step: to_inner(blends[step - 1], step) for step in far}
    *blends, token = blend(False, tables, momentum, gradient, [token, touch(swapped)])
    last_blocks = [blends[0]] + [to_inner(blends[step], step) for step in range(1, ranks)]
    new_momentum, token = fresh_momentum(tables, momentum, gradient, token)
    handed = {step: from_inner(arrived[step], near) for step in far}

    def ordered(base, opposite, others):
        return [{0: base, near: opposite, **others}[step] for step in range(ranks)]

    first_blocks = ordered(own, swapped, arrived)
    pair, keep, send = assemble_and_gram(True, tables, first_blocks, *[handed[step] for step in far[1:]])

    def first_update(pair, keep, send, after):
        return apply_update(True, early, tables, *sum_halves(keep, send, "tensor", 1), pair, slots, after)

    def first_skip(*_):
        return nothing(update_shapes(early, slots, columns))

    packed, *homes = lax.cond(inner, first_update, first_skip, pair, keep, send, touch(keep, 10**11))
    packed_there = from_inner(packed, near)
    iterate = assemble_outer(tables, ordered(swapped, own, handed))
    first_home = [from_inner(block, step) for step, block in zip(early, homes)]

    def last_update(after, *blocks):
        pair, keep, send = assemble_and_gram(False, tables, blocks, after)
        return (pair, *apply_update(False, last, tables, *sum_halves(keep, send, "tensor", 2), pair, slots))

    def last_skip(*_):
        return tuple(nothing([jax.ShapeDtypeStruct(pair.shape, pair.dtype), *update_shapes(last, slots, columns)]))

    last_pair, last_packed, *homes = lax.cond(inner, last_update, last_skip, iterate, *last_blocks)
    last_home = [from_inner(block, step) for step, block in zip(last, homes)]

    result, shards = finish(
        tables, packed_there, iterate, packed, pair, last_packed, last_pair, momentum.shape, token
    )
    shards = place_blocks(True, owner_group, early, first_home, shards, ranks)
    for step, block in zip(last, last_home):
        shards = place_blocks(False, owner_group, [step], [block], shards, ranks)
    return (new_momentum, shards, result[None])


def solution(mesh):
    placed = (P(None, "fsdp", "tensor"), P(None, "fsdp", "tensor"), P(), P(), P(), P())
    return jax.shard_map(
        on_device,
        mesh=mesh,
        in_specs=placed,
        out_specs=(P(None, "fsdp", "tensor"), P(None, "fsdp", "tensor"), P("fsdp", None, "tensor")),
        check_vma=False,
    )
```

```python
import functools
import math

import jax
import jax.numpy as jnp
from jax import lax
from jax.experimental import pallas as pl
from jax.experimental.pallas import tpu as pltpu
from jax.sharding import PartitionSpec as P

WIDTH = 7168
INNER = 576
PANEL = INNER // 3
TILE = 256
SUBLANES = 8

MOMENTUM_RATE = 0.95
QUINTIC_FIRST = 3.4445
QUINTIC_SECOND = -4.775
QUINTIC_THIRD = 2.0315
EPSILON = 1e-07
OUT_SCALE = 0.2 * math.sqrt(max(INNER, WIDTH))
SMALL = pltpu.CompilerParams(vmem_limit_bytes=1024 * 1024)
FULL = pltpu.CompilerParams(vmem_limit_bytes=60 * 1024 * 1024)
PARAMS = pltpu.CompilerParams(vmem_limit_bytes=24 * 1024 * 1024)
HBM = pl.BlockSpec(memory_space=pltpu.HBM)
ANY = pl.BlockSpec(memory_space=pl.ANY)
VMEM = pl.BlockSpec(memory_space=pltpu.VMEM)


def halves(value):
    high = value.astype(jnp.bfloat16)
    low = (value - high.astype(jnp.float32)).astype(jnp.bfloat16)
    return high, low


def dot(left, right, contract=((1,), (0,))):
    return lax.dot_general(left, right, (contract, ((), ())), preferred_element_type=jnp.float32)


DEPTH = INNER // TILE * TILE
PARTS = [(side, rows) for rows in ((0, DEPTH), (DEPTH, INNER)) if rows[0] < rows[1] for side in (1, 0, 0)]


def passes_left(value):
    high, low = halves(value)
    return jnp.concatenate(
        [part[:, first:last] for first, last in ((0, DEPTH), (DEPTH, INNER)) for part in (high, low, high)], axis=1
    )


def passes_right(value):
    sides = halves(value)
    return jnp.concatenate([sides[side][first:last] for side, (first, last) in PARTS], axis=0)


def is_inner(rank, ranks):
    low = ranks // 4
    return (rank >= low) & (rank < ranks - low)


def mate(ranks):
    return ranks // 4


def table_scratch(matrices, ranks):
    return [
        pltpu.SMEM((matrices,), jnp.int32),
        pltpu.SMEM((ranks,), jnp.int32),
        pltpu.SMEM((matrices, ranks), jnp.int32),
        pltpu.SMEM((matrices, ranks), jnp.int32),
        pltpu.SemaphoreType.DMA((4,)),
    ]


def table_jobs(tables, held):
    *places, arrive = held
    copies = [
        pltpu.make_async_copy(table, place, arrive.at[index])
        for index, (table, place) in enumerate(zip(tables, places))
    ]
    return copies, places


def fetch_tables(tables, held):
    copies, places = table_jobs(tables, held)
    for copy in copies:
        copy.start()
    for copy in copies:
        copy.wait()
    return places


def matrix_of(owner_group, rank):
    found = jnp.int32(0)
    for matrix in range(owner_group.shape[0]):
        found = jnp.where(owner_group[matrix] == rank, matrix, found)
    return found


def over_tiles(tiles, body, carry):
    group = next(group for group in (6, 3, 2, 1) if tiles % group == 0)

    def step(index, carry):
        for member in range(group):
            carry = body(index * group + member, carry)
        return carry

    return lax.fori_loop(0, tiles // group, step, carry)


def each_copy(copies, action):
    for condition, source, place, flag in copies:

        @pl.when(condition)
        def _(source=source, place=place, flag=flag):
            getattr(pltpu.make_async_copy(source, place, flag), action)()


def blend_kernel(first, chunks, *refs):
    tables, (momentum, gradient) = refs[:4], refs[4:6]
    ranks = tables[1].shape[0]
    *outs, token, olds, grads, arrive, leave = refs[-ranks - 10 + first : -5]
    owner_group, live_ranks, row_counts, _ = fetch_tables(tables, refs[-5:])
    rank = lax.axis_index("fsdp")
    slots, columns = outs[0].shape
    size = slots // chunks
    jobs = []
    for step in range(1, ranks + 1):
        step = step % ranks
        if first and step == 0:
            continue
        target = rank ^ step
        wanted = is_inner(target, ranks)
        matrix = matrix_of(owner_group, target ^ mate(ranks) if first else target)
        if first and step == mate(ranks):
            matrix = matrix_of(owner_group, jnp.where(wanted, rank, target))
            wanted = rank >= 0
        count = row_counts[matrix, rank] * live_ranks[rank]
        for chunk in range(chunks):
            part = pl.ds(chunk * size, size)
            flags = arrive.at[step, chunk, 0], arrive.at[step, chunk, 1]
            incoming = (
                (wanted, momentum.at[matrix, part], olds.at[step, part], flags[0]),
                (wanted, gradient.at[matrix, part], grads.at[step, part], flags[1]),
            )
            outgoing = (wanted, olds.at[step, part], outs[step - first].at[part], leave.at[step, chunk])
            jobs.append((step, chunk, count, incoming, outgoing))
            each_copy(incoming, "start")
    token[...] = jnp.zeros_like(token)
    for step, chunk, count, incoming, outgoing in jobs:

        @pl.when(incoming[0][0])
        def _(step=step, chunk=chunk, count=count, incoming=incoming, outgoing=outgoing):
            for _, source, place, flag in incoming:
                pltpu.make_async_copy(source, place, flag).wait()
            rows = slice(chunk * size, (chunk + 1) * size)
            grad_now = grads[step, rows, :]
            fresh = MOMENTUM_RATE * olds[step, rows, :] + grad_now
            position = lax.broadcasted_iota(jnp.int32, (size, columns), 0) + chunk * size
            olds[step, rows, :] = jnp.where(position < count, grad_now + MOMENTUM_RATE * fresh, 0.0)
            pltpu.make_async_copy(*outgoing[1:]).start()

    each_copy([job[-1] for job in jobs], "wait")


def fresh_kernel(live_ranks, row_counts, momentum, gradient, _, out, token):
    token[...] = jnp.zeros_like(token)
    rank, matrix = lax.axis_index("fsdp"), pl.program_id(0)
    position = lax.broadcasted_iota(jnp.int32, out.shape, 0)
    keep = position < row_counts[matrix, rank] * live_ranks[rank]
    out[...] = jnp.where(keep, MOMENTUM_RATE * momentum[...] + gradient[...], 0.0)


def assemble(blocks, landed, padded, arrive, tables, held, first):
    ranks, slots, columns = landed.shape
    copies = []
    for step in range(ranks):
        copies.append(pltpu.make_async_copy(blocks[step], landed.at[step], arrive.at[step]))
        copies[-1].start()
    owner_group, _, _, row_offsets = fetch_tables(tables, held)
    rank = lax.axis_index("fsdp")
    base = jnp.where(is_inner(rank, ranks), rank, rank ^ mate(ranks))
    matrix = matrix_of(owner_group, base ^ mate(ranks) if first else base)
    padded[...] = jnp.zeros_like(padded)
    sublane = lax.broadcasted_iota(jnp.int32, (SUBLANES, columns), 0)
    for step in range(ranks):
        start = row_offsets[matrix, base ^ step]
        shift = start % SUBLANES
        origin = start - shift
        copies[step].wait()

        def tile(index, before, origin=origin, shift=shift, step=step):
            moved = pltpu.roll(landed[step, pl.ds(pl.multiple_of(index * SUBLANES, SUBLANES), SUBLANES), :], shift, 0)
            rows = pl.ds(pl.multiple_of(origin + index * SUBLANES, SUBLANES), SUBLANES)
            padded[rows, :] = padded[rows, :] + jnp.where(sublane < shift, before, moved)
            return moved

        after = over_tiles(slots // SUBLANES, tile, jnp.zeros((SUBLANES, columns), jnp.float32))
        rows = pl.ds(pl.multiple_of(origin + slots, SUBLANES), SUBLANES)
        padded[rows, :] = padded[rows, :] + jnp.where(sublane < shift, after, 0.0)


def gram_kernel(inner, first, ranks, *refs):
    pair, keep, send = refs[-15:-12]
    landed, padded, high_held, low_held, gram, arrive, leave = refs[-12:-5]

    @pl.when(is_inner(lax.axis_index("fsdp"), ranks) == inner)
    def _():
        assemble(refs[4 : 4 + ranks], landed, padded, arrive, refs[:4], refs[-5:], first)
        high, low = halves(padded[:INNER, :])
        high_held[...] = high
        low_held[...] = low
        outgoing = [
            pltpu.make_async_copy(high_held, pair.at[0], leave.at[0]),
            pltpu.make_async_copy(low_held, pair.at[1], leave.at[1]),
        ]
        for copy in outgoing:
            copy.start()
        left = jnp.concatenate([high, low, high], axis=1)
        right = jnp.concatenate([low, high, high], axis=1)
        for panel in range(3):
            here = slice(panel * PANEL, (panel + 1) * PANEL)
            store_panel(gram, panel, dot(left[panel * PANEL :], right[here], ((1,), (1,))))
        mine, other = core_rows()
        keep[...] = gram[mine, :]
        send[...] = gram[other, :]
        for copy in outgoing:
            copy.wait()


def core_rows():
    half = INNER // 2
    first = (lax.axis_index("tensor") & 1) * half
    return tuple(pl.ds(pl.multiple_of(start, SUBLANES), half) for start in (first, half - first))


def store_panel(packed, panel, part):
    if panel == 0:
        packed[:, :PANEL] = part
    elif panel == 1:
        packed[: 2 * PANEL, PANEL:] = part
    else:
        packed[2 * PANEL :, PANEL:] = part


def unpack(packed, gram):
    gram[:, :PANEL] = packed[:, :PANEL]
    gram[PANEL:, PANEL : 2 * PANEL] = packed[: 2 * PANEL, PANEL:]
    gram[2 * PANEL :, 2 * PANEL :] = packed[2 * PANEL :, PANEL:]
    gram[:PANEL, PANEL:] = packed[PANEL:, :PANEL].T
    gram[PANEL : 2 * PANEL, 2 * PANEL :] = packed[PANEL : 2 * PANEL, PANEL:].T
    return gram[...]


def symmetric_product(left, right, out):
    for begin in range(0, INNER, TILE):
        end = min(begin + TILE, INNER)
        part = dot(left[begin:], right[:, begin:end])
        out[begin:, begin:end] = part
        if end < INNER:
            out[begin:end, end:] = part[end - begin :].T
    return out[...]


def polynomial(raw, gram):
    diagonal = lax.broadcasted_iota(jnp.int32, raw.shape, 0) == lax.broadcasted_iota(jnp.int32, raw.shape, 1)
    square_total = jnp.sum(jnp.where(diagonal, raw, 0.0))
    norm = jnp.sqrt(jnp.full((1, 1), square_total, jnp.float32)) + EPSILON
    inverse = 1.0 / norm
    first = (raw * inverse) * inverse
    first_right = passes_right(first)
    second = symmetric_product(passes_left(first), first_right, gram)
    base = QUINTIC_SECOND * first + QUINTIC_THIRD * second + jnp.where(diagonal, QUINTIC_FIRST, 0.0)
    base_left = passes_left(base)
    third = symmetric_product(base_left, first_right, gram)
    next_gram = symmetric_product(base_left, passes_right(third), gram)
    square = symmetric_product(passes_left(next_gram), passes_right(next_gram), gram)
    outer = QUINTIC_SECOND * next_gram + QUINTIC_THIRD * square + jnp.where(diagonal, QUINTIC_FIRST, 0.0)
    return symmetric_product(passes_left(outer), passes_right(base), gram) * (inverse * OUT_SCALE)


def extract(padded, start, count, staged, step):
    _, slots, columns = staged.shape
    sublane = lax.broadcasted_iota(jnp.int32, (SUBLANES, columns), 0)
    shift = start % SUBLANES
    base = start - shift
    back = jnp.where(shift == 0, 0, SUBLANES - shift)

    def window(index):
        rows = pl.ds(pl.multiple_of(base + index * SUBLANES, SUBLANES), SUBLANES)
        return pltpu.roll(padded[rows, :], back, 0)

    def tile(index, here):
        after = window(index + 1)
        moved = jnp.where(sublane < SUBLANES - shift, here, after)
        rows = pl.ds(pl.multiple_of(index * SUBLANES, SUBLANES), SUBLANES)
        staged[step, rows, :] = jnp.where(sublane < count - index * SUBLANES, moved, 0.0)
        return after

    over_tiles(slots // SUBLANES, tile, window(0))


def stack_copies(pair, stacked, arrive):
    copies, begin = [], 0
    for index, (side, (first_row, last_row)) in enumerate(PARTS):
        size = last_row - first_row
        source = pair.at[side, pl.ds(first_row, size)]
        copies.append(pltpu.make_async_copy(source, stacked.at[pl.ds(begin, size)], arrive.at[index]))
        begin += size
    return copies


def update_kernel(first, steps, *refs):
    tables, (keep, away, pair) = refs[:4], refs[4:7]
    gram, padded, staged, stacked, held, arrive, leave = refs[-12:-5]
    whole, *homes = refs[-13 - len(steps) : -12]
    ranks = tables[1].shape[0]
    rank = lax.axis_index("fsdp")
    incoming = stack_copies(pair, stacked, arrive) if steps else []
    for copy in incoming:
        copy.start()
    table_copies, places = table_jobs(tables, refs[-5:])
    for copy in table_copies:
        copy.start()
    mine, other = core_rows()
    held[mine, :] = keep[...]
    held[other, :] = away[...]
    total = polynomial(unpack(held, gram), gram)
    for panel in range(3):
        store_panel(held, panel, total[panel * PANEL :, panel * PANEL : (panel + 1) * PANEL])
    copies = [pltpu.make_async_copy(held, whole, leave.at[len(steps)])]
    copies[0].start()
    for copy in [*incoming, *table_copies]:
        copy.wait()
    if steps:
        padded[:INNER, :] = dot(passes_left(total), stacked[...])
    owner_group, live_ranks, row_counts, row_offsets = places
    matrix = matrix_of(owner_group, rank ^ mate(ranks) if first else rank)
    for index, step in enumerate(steps):
        target = rank ^ step
        count = row_counts[matrix, target] * live_ranks[target]
        extract(padded, row_offsets[matrix, target], count, staged, index)
        copies.append(pltpu.make_async_copy(staged.at[index], homes[index], leave.at[index]))
        copies[-1].start()
    for copy in copies:
        copy.wait()


def finish_kernel(ranks, *refs):
    tables, sources = refs[:4], refs[4:10]
    (result, shards, gram, padded, staged, stacked, held, arrive, leave), refs = refs[11:20], refs[20:]
    rank = lax.axis_index("fsdp")
    owner_group, live_ranks, row_counts, row_offsets = fetch_tables(tables, refs)

    def run(copies):
        for copy in copies:
            copy.start()
        for copy in copies:
            copy.wait()

    def make(packed, pair, matrix, index, is_result):
        run([pltpu.make_async_copy(packed, held, leave.at[2]), *stack_copies(pair, stacked, arrive)])
        padded[:INNER, :] = dot(passes_left(unpack(held, gram)), stacked[...])
        extract(padded, row_offsets[matrix, rank], row_counts[matrix, rank] * live_ranks[rank], staged, index)
        copies = [pltpu.make_async_copy(staged.at[index], shards.at[matrix], leave.at[index])]
        if is_result:
            copies.append(pltpu.make_async_copy(padded.at[pl.ds(0, INNER)], result, leave.at[2]))
        run(copies)

    own = matrix_of(owner_group, rank)

    @pl.when(is_inner(rank, ranks))
    def _():
        make(*sources[2:4], own, 0, True)
        make(*sources[:2], matrix_of(owner_group, rank ^ mate(ranks)), 1, False)

    @pl.when(jnp.logical_not(is_inner(rank, ranks)))
    def _():
        make(*sources[4:], own, 0, True)


def place_kernel(first, ranks, steps, *refs):
    table, blocks, shards = refs[0], refs[1 : 1 + len(steps)], refs[2 + len(steps)]
    owner_group, arrive, leave = refs[3 + len(steps) :]
    rank = lax.axis_index("fsdp")
    fetch = pltpu.make_async_copy(table, owner_group, arrive)
    fetch.start()
    fetch.wait()
    copies = []
    for index, step in enumerate(steps):
        source = rank ^ step
        matrix = matrix_of(owner_group, source ^ mate(ranks) if first else source)
        copies.append((is_inner(source, ranks), blocks[index], shards.at[matrix], leave.at[index]))
    each_copy(copies, "start")
    each_copy(copies, "wait")


def idle_kernel(*refs):
    pass


def floats(*shape):
    return jax.ShapeDtypeStruct(shape, jnp.float32)


def vmem(*shape, dtype=jnp.float32):
    return pltpu.VMEM(shape, dtype)


def flags(*shape):
    return pltpu.SemaphoreType.DMA(shape)


FREE = pl.CostEstimate(flops=0, bytes_accessed=0, transcendentals=0)


def blend(first, tables, momentum, gradient, before):
    _, slots, columns = momentum.shape
    ranks = tables[1].shape[0]
    chunks = 2 if slots % (2 * SUBLANES) == 0 else 1
    return pl.pallas_call(
        functools.partial(blend_kernel, first, chunks),
        out_shape=[floats(slots, columns)] * (ranks - first) + [floats(SUBLANES, 128)],
        in_specs=[HBM] * 6 + [ANY] * len(before),
        out_specs=[ANY] * (ranks - first) + [VMEM],
        scratch_shapes=[vmem(ranks, slots, columns)] * 2
        + [flags(ranks, chunks, 2), flags(ranks, chunks)]
        + table_scratch(*tables[2].shape),
        compiler_params=FULL,
        cost_estimate=FREE,
        name="blend",
    )(*tables, momentum, gradient, *before)


def fresh_momentum(tables, momentum, gradient, before):
    matrices, slots, columns = momentum.shape
    block = pl.BlockSpec((None, slots, columns), lambda matrix: (matrix, 0, 0))
    return pl.pallas_call(
        fresh_kernel,
        grid=(matrices,),
        out_shape=[floats(*momentum.shape), floats(SUBLANES, 128)],
        in_specs=[pl.BlockSpec(memory_space=pltpu.SMEM)] * 2 + [block] * 2 + [ANY],
        out_specs=[block, pl.BlockSpec((SUBLANES, 128), lambda matrix: (0, 0))],
        compiler_params=FULL,
        cost_estimate=FREE,
        name="fresh_momentum",
    )(*tables[1:3], momentum, gradient, before)


def assemble_and_gram(inner, first, tables, blocks, *after):
    slots, columns = blocks[0].shape
    ranks = len(blocks)
    pair = jax.ShapeDtypeStruct((4, INNER, columns), jnp.bfloat16)
    return pl.pallas_call(
        functools.partial(gram_kernel, inner, first, ranks),
        out_shape=[pair] + [floats(INNER // 2, 2 * PANEL)] * 2,
        in_specs=[HBM] * 4 + [ANY] * (ranks + len(after)),
        out_specs=[ANY, VMEM, VMEM],
        scratch_shapes=[
            vmem(ranks, slots, columns),
            vmem(INNER + slots + SUBLANES, columns),
            vmem(INNER, columns, dtype=jnp.bfloat16),
            vmem(INNER, columns, dtype=jnp.bfloat16),
            vmem(INNER, 2 * PANEL),
            flags(ranks),
            flags(2),
        ]
        + table_scratch(*tables[2].shape),
        compiler_params=PARAMS,
        cost_estimate=FREE,
        name="assemble_and_gram",
    )(*tables, *blocks, *after)


def update_shapes(steps, slots, columns):
    return [floats(INNER, 2 * PANEL)] + [floats(slots, columns)] * len(steps)


def nothing(shapes):
    return pl.pallas_call(
        idle_kernel, out_shape=shapes, out_specs=[ANY] * len(shapes), compiler_params=SMALL, name="nothing"
    )()


def apply_update(first, steps, tables, keep, away, pair, slots, *after):
    columns = pair.shape[2]
    return pl.pallas_call(
        functools.partial(update_kernel, first, steps),
        out_shape=update_shapes(steps, slots, columns),
        in_specs=[HBM] * 4 + [VMEM] * 2 + [ANY] * (1 + len(after)),
        out_specs=[ANY] * (1 + len(steps)),
        scratch_shapes=[
            vmem(INNER, INNER),
            vmem(INNER + slots + 2 * SUBLANES, columns),
            vmem(max(len(steps), 1), slots, columns),
            vmem(3 * INNER, columns, dtype=jnp.bfloat16),
            vmem(INNER, 2 * PANEL),
            flags(len(PARTS)),
            flags(len(steps) + 1),
        ]
        + table_scratch(*tables[2].shape),
        compiler_params=PARAMS,
        cost_estimate=FREE,
        name="apply_update",
    )(*tables, keep, away, pair, *after)


def touch(value, flops=0):
    return pl.pallas_call(
        idle_kernel,
        out_shape=floats(SUBLANES, 128),
        in_specs=[ANY],
        out_specs=ANY,
        compiler_params=SMALL,
        cost_estimate=pl.CostEstimate(flops=flops, bytes_accessed=0, transcendentals=0),
        name="touch",
    )(value)


def finish(tables, sources, shape, after):
    _, slots, columns = shape
    return pl.pallas_call(
        functools.partial(finish_kernel, tables[1].shape[0]),
        out_shape=[floats(INNER, columns), floats(*shape)],
        in_specs=[HBM] * 4 + [ANY] * 7,
        out_specs=[HBM] * 2,
        scratch_shapes=[
            vmem(INNER, INNER),
            vmem(INNER + slots + 2 * SUBLANES, columns),
            vmem(2, slots, columns),
            vmem(3 * INNER, columns, dtype=jnp.bfloat16),
            vmem(INNER, 2 * PANEL),
            flags(len(PARTS)),
            flags(3),
        ]
        + table_scratch(*tables[2].shape),
        compiler_params=PARAMS,
        cost_estimate=FREE,
        name="finish",
    )(*tables, *sources, after)


def place_blocks(first, owner_group, steps, blocks, shards, ranks):
    return pl.pallas_call(
        functools.partial(place_kernel, first, ranks, steps),
        out_shape=floats(*shards.shape),
        in_specs=[HBM] + [VMEM] * len(blocks) + [HBM],
        out_specs=HBM,
        scratch_shapes=[pltpu.SMEM(owner_group.shape, jnp.int32), flags(), flags(len(steps))],
        input_output_aliases={1 + len(blocks): 0},
        compiler_params=PARAMS,
        cost_estimate=FREE,
        name="place_blocks",
    )(owner_group, *blocks, shards)


def sum_halves(keep, send, axis, streams):
    size = lax.axis_size(axis)

    def exchange(piece, bits):
        return lax.ppermute(piece, axis, [(i, i ^ bits[i & 1]) for i in range(size)])

    chips = [1 << shift for shift in range(1, size.bit_length() - 1)]
    keep = keep + exchange(send, (1, 1))
    pieces = jnp.split(keep, streams, axis=0)
    for bits in zip(chips, reversed(chips)):
        pieces = [piece + exchange(piece, bits[:: 1 - 2 * index]) for index, piece in enumerate(pieces)]
    keep = jnp.concatenate(pieces, axis=0)
    return keep, exchange(keep, (1, 1))


def on_device(momentum, gradient, live_ranks, owner_group, row_counts, row_offsets):
    ranks = lax.axis_size("fsdp")
    _, slots, columns = momentum.shape
    inner = is_inner(lax.axis_index("fsdp"), ranks)
    tables = (owner_group, live_ranks, row_counts, row_offsets)
    last = [2, 1, *range(3, ranks)]
    early = [step for step in last if step != mate(ranks)]

    def pairs(step, inward):
        return [(i, i ^ step) for i in range(ranks) if is_inner(i ^ step if inward else i, ranks)]

    def to_inner(block, step):
        return lax.ppermute(block, "fsdp", pairs(step, True))

    def from_inner(block, step):
        return lax.ppermute(block, "fsdp", pairs(step, False))

    near = mate(ranks)
    far = [step for step in last if step != near]
    *blends, token = blend(True, tables, momentum, gradient, [])
    own = blends[near - 1]
    swapped = lax.ppermute(own, "fsdp", [(i, i ^ near) for i in range(ranks)])
    arrived = {step: to_inner(blends[step - 1], step) for step in far}
    *blends, token = blend(False, tables, momentum, gradient, [token, touch(swapped)])
    last_blocks = [blends[0]] + [to_inner(blends[step], step) for step in range(1, ranks)]
    new_momentum, token = fresh_momentum(tables, momentum, gradient, token)
    handed = {step: from_inner(arrived[step], near) for step in far}

    def ordered(base, opposite, others):
        return [{0: base, near: opposite, **others}[step] for step in range(ranks)]

    first_blocks = ordered(own, swapped, arrived)
    pair, keep, send = assemble_and_gram(True, True, tables, first_blocks, *[handed[step] for step in far[1:]])

    def first_update(pair, keep, send, after):
        return apply_update(True, early, tables, *sum_halves(keep, send, "tensor", 1), pair, slots, after)

    def first_skip(*_):
        return nothing(update_shapes(early, slots, columns))

    packed, *homes = lax.cond(inner, first_update, first_skip, pair, keep, send, touch(keep, 10**11))
    first_home = [from_inner(block, step) for step, block in zip(early, homes)]
    pair_shape = jax.ShapeDtypeStruct(pair.shape, pair.dtype)

    def outer_update(*blocks):
        pair, keep, send = assemble_and_gram(False, True, tables, blocks)
        return (pair, *apply_update(True, [], tables, *sum_halves(keep, send, "tensor", 1), pair, slots, keep))

    def outer_skip(*_):
        return tuple(nothing([pair_shape, *update_shapes([], slots, columns)]))

    outer_pair, outer_packed = lax.cond(inner, outer_skip, outer_update, *ordered(swapped, own, handed))

    def last_update(after, *blocks):
        pair, keep, send = assemble_and_gram(True, False, tables, blocks, after)
        return (pair, *apply_update(False, last, tables, *sum_halves(keep, send, "tensor", 2), pair, slots))

    def last_skip(*_):
        return tuple(nothing([pair_shape, *update_shapes(last, slots, columns)]))

    last_pair, last_packed, *homes = lax.cond(inner, last_update, last_skip, outer_packed, *last_blocks)
    last_home = [from_inner(block, step) for step, block in zip(last, homes)]

    sources = [packed, pair, last_packed, last_pair, outer_packed, outer_pair]
    result, shards = finish(tables, sources, momentum.shape, token)
    shards = place_blocks(True, owner_group, early, first_home, shards, ranks)
    for step, block in zip(last, last_home):
        shards = place_blocks(False, owner_group, [step], [block], shards, ranks)
    return (new_momentum, shards, result[None])


def solution(mesh):
    placed = (P(None, "fsdp", "tensor"), P(None, "fsdp", "tensor"), P(), P(), P(), P())
    return jax.shard_map(
        on_device,
        mesh=mesh,
        in_specs=placed,
        out_specs=(P(None, "fsdp", "tensor"), P(None, "fsdp", "tensor"), P("fsdp", None, "tensor")),
        check_vma=False,
    )
```

```python
import functools
import math

import jax
import jax.numpy as jnp
from jax import lax
from jax.experimental import pallas as pl
from jax.experimental.pallas import tpu as pltpu
from jax.sharding import PartitionSpec as P

WIDTH = 7168
INNER = 576
PANEL = INNER // 3
TILE = 256
SUBLANES = 8

MOMENTUM_RATE = 0.95
QUINTIC_FIRST = 3.4445
QUINTIC_SECOND = -4.775
QUINTIC_THIRD = 2.0315
EPSILON = 1e-07
OUT_SCALE = 0.2 * math.sqrt(max(INNER, WIDTH))
SMALL = pltpu.CompilerParams(vmem_limit_bytes=1024 * 1024)
FULL = pltpu.CompilerParams(vmem_limit_bytes=60 * 1024 * 1024)
PARAMS = pltpu.CompilerParams(vmem_limit_bytes=24 * 1024 * 1024)
HBM = pl.BlockSpec(memory_space=pltpu.HBM)
ANY = pl.BlockSpec(memory_space=pl.ANY)
VMEM = pl.BlockSpec(memory_space=pltpu.VMEM)


def halves(value):
    high = value.astype(jnp.bfloat16)
    low = (value - high.astype(jnp.float32)).astype(jnp.bfloat16)
    return high, low


def dot(left, right, contract=((1,), (0,))):
    return lax.dot_general(left, right, (contract, ((), ())), preferred_element_type=jnp.float32)


DEPTH = INNER // TILE * TILE
PARTS = [(side, rows) for rows in ((0, DEPTH), (DEPTH, INNER)) if rows[0] < rows[1] for side in (1, 0, 0)]


def passes_left(value):
    high, low = halves(value)
    return jnp.concatenate(
        [part[:, first:last] for first, last in ((0, DEPTH), (DEPTH, INNER)) for part in (high, low, high)], axis=1
    )


def passes_right(value):
    sides = halves(value)
    return jnp.concatenate([sides[side][first:last] for side, (first, last) in PARTS], axis=0)


def is_inner(rank, ranks):
    low = ranks // 4
    return (rank >= low) & (rank < ranks - low)


def mate(ranks):
    return ranks // 4


def table_scratch(matrices, ranks):
    return [
        pltpu.SMEM((matrices,), jnp.int32),
        pltpu.SMEM((ranks,), jnp.int32),
        pltpu.SMEM((matrices, ranks), jnp.int32),
        pltpu.SMEM((matrices, ranks), jnp.int32),
        pltpu.SemaphoreType.DMA((4,)),
    ]


def table_jobs(tables, held):
    *places, arrive = held
    copies = [
        pltpu.make_async_copy(table, place, arrive.at[index])
        for index, (table, place) in enumerate(zip(tables, places))
    ]
    return copies, places


def fetch_tables(tables, held):
    copies, places = table_jobs(tables, held)
    for copy in copies:
        copy.start()
    for copy in copies:
        copy.wait()
    return places


def matrix_of(owner_group, rank):
    found = jnp.int32(0)
    for matrix in range(owner_group.shape[0]):
        found = jnp.where(owner_group[matrix] == rank, matrix, found)
    return found


def over_tiles(tiles, body, carry):
    group = next(group for group in (6, 3, 2, 1) if tiles % group == 0)

    def step(index, carry):
        for member in range(group):
            carry = body(index * group + member, carry)
        return carry

    return lax.fori_loop(0, tiles // group, step, carry)


def each_copy(copies, action):
    for condition, source, place, flag in copies:

        @pl.when(condition)
        def _(source=source, place=place, flag=flag):
            getattr(pltpu.make_async_copy(source, place, flag), action)()


def blend_kernel(first, chunks, *refs):
    tables, (momentum, gradient) = refs[:4], refs[4:6]
    ranks = tables[1].shape[0]
    *outs, token, olds, grads, arrive, leave = refs[-ranks - 10 + first : -5]
    owner_group, live_ranks, row_counts, _ = fetch_tables(tables, refs[-5:])
    rank = lax.axis_index("fsdp")
    slots, columns = outs[0].shape
    size = slots // chunks
    jobs = []
    for step in range(1, ranks + 1):
        step = step % ranks
        if first and step == 0:
            continue
        target = rank ^ step
        wanted = is_inner(target, ranks)
        matrix = matrix_of(owner_group, target ^ mate(ranks) if first else target)
        if first and step == mate(ranks):
            matrix = matrix_of(owner_group, jnp.where(wanted, rank, target))
            wanted = rank >= 0
        count = row_counts[matrix, rank] * live_ranks[rank]
        for chunk in range(chunks):
            part = pl.ds(chunk * size, size)
            flags = arrive.at[step, chunk, 0], arrive.at[step, chunk, 1]
            incoming = (
                (wanted, momentum.at[matrix, part], olds.at[step, part], flags[0]),
                (wanted, gradient.at[matrix, part], grads.at[step, part], flags[1]),
            )
            outgoing = (wanted, olds.at[step, part], outs[step - first].at[part], leave.at[step, chunk])
            jobs.append((step, chunk, count, incoming, outgoing))
            each_copy(incoming, "start")
    token[...] = jnp.zeros_like(token)
    for step, chunk, count, incoming, outgoing in jobs:

        @pl.when(incoming[0][0])
        def _(step=step, chunk=chunk, count=count, incoming=incoming, outgoing=outgoing):
            for _, source, place, flag in incoming:
                pltpu.make_async_copy(source, place, flag).wait()
            sublane = lax.broadcasted_iota(jnp.int32, (SUBLANES, columns), 0)

            def tile(index, carry):
                first_row = chunk * size + index * SUBLANES
                rows = pl.ds(pl.multiple_of(first_row, SUBLANES), SUBLANES)
                grad_now = grads[step, rows, :]
                fresh = MOMENTUM_RATE * olds[step, rows, :] + grad_now
                olds[step, rows, :] = jnp.where(sublane < count - first_row, grad_now + MOMENTUM_RATE * fresh, 0.0)
                return carry

            over_tiles(size // SUBLANES, tile, 0)
            pltpu.make_async_copy(*outgoing[1:]).start()

    each_copy([job[-1] for job in jobs], "wait")


def fresh_kernel(live_ranks, row_counts, momentum, gradient, _, out, token):
    token[...] = jnp.zeros_like(token)
    rank, matrix = lax.axis_index("fsdp"), pl.program_id(0)
    slots, columns = out.shape
    count = row_counts[matrix, rank] * live_ranks[rank]
    sublane = lax.broadcasted_iota(jnp.int32, (SUBLANES, columns), 0)

    def tile(index, carry):
        rows = pl.ds(pl.multiple_of(index * SUBLANES, SUBLANES), SUBLANES)
        fresh = MOMENTUM_RATE * momentum[rows, :] + gradient[rows, :]
        out[rows, :] = jnp.where(sublane < count - index * SUBLANES, fresh, 0.0)
        return carry

    over_tiles(slots // SUBLANES, tile, 0)


def assemble(blocks, landed, padded, arrive, tables, held, first):
    ranks, slots, columns = landed.shape
    copies = []
    for step in range(ranks):
        copies.append(pltpu.make_async_copy(blocks[step], landed.at[step], arrive.at[step]))
        copies[-1].start()
    owner_group, _, _, row_offsets = fetch_tables(tables, held)
    rank = lax.axis_index("fsdp")
    base = jnp.where(is_inner(rank, ranks), rank, rank ^ mate(ranks))
    matrix = matrix_of(owner_group, base ^ mate(ranks) if first else base)
    padded[...] = jnp.zeros_like(padded)
    sublane = lax.broadcasted_iota(jnp.int32, (SUBLANES, columns), 0)
    for step in range(ranks):
        start = row_offsets[matrix, base ^ step]
        shift = start % SUBLANES
        origin = start - shift
        copies[step].wait()

        def tile(index, before, origin=origin, shift=shift, step=step):
            moved = pltpu.roll(landed[step, pl.ds(pl.multiple_of(index * SUBLANES, SUBLANES), SUBLANES), :], shift, 0)
            rows = pl.ds(pl.multiple_of(origin + index * SUBLANES, SUBLANES), SUBLANES)
            padded[rows, :] = padded[rows, :] + jnp.where(sublane < shift, before, moved)
            return moved

        after = over_tiles(slots // SUBLANES, tile, jnp.zeros((SUBLANES, columns), jnp.float32))
        rows = pl.ds(pl.multiple_of(origin + slots, SUBLANES), SUBLANES)
        padded[rows, :] = padded[rows, :] + jnp.where(sublane < shift, after, 0.0)


def gram_kernel(inner, first, ranks, *refs):
    pair, keep, send = refs[-15:-12]
    landed, padded, high_held, low_held, gram, arrive, leave = refs[-12:-5]

    @pl.when(is_inner(lax.axis_index("fsdp"), ranks) == inner)
    def _():
        assemble(refs[4 : 4 + ranks], landed, padded, arrive, refs[:4], refs[-5:], first)
        high, low = halves(padded[:INNER, :])
        high_held[...] = high
        low_held[...] = low
        outgoing = [
            pltpu.make_async_copy(high_held, pair.at[0], leave.at[0]),
            pltpu.make_async_copy(low_held, pair.at[1], leave.at[1]),
        ]
        for copy in outgoing:
            copy.start()
        left = jnp.concatenate([high, low, high], axis=1)
        right = jnp.concatenate([low, high, high], axis=1)
        for panel in range(3):
            here = slice(panel * PANEL, (panel + 1) * PANEL)
            store_panel(gram, panel, dot(left[panel * PANEL :], right[here], ((1,), (1,))))
        mine, other = core_rows()
        keep[...] = gram[mine, :]
        send[...] = gram[other, :]
        for copy in outgoing:
            copy.wait()


def core_rows():
    half = INNER // 2
    first = (lax.axis_index("tensor") & 1) * half
    return tuple(pl.ds(pl.multiple_of(start, SUBLANES), half) for start in (first, half - first))


def store_panel(packed, panel, part):
    if panel == 0:
        packed[:, :PANEL] = part
    elif panel == 1:
        packed[: 2 * PANEL, PANEL:] = part
    else:
        packed[2 * PANEL :, PANEL:] = part


def unpack(packed, gram):
    gram[:, :PANEL] = packed[:, :PANEL]
    gram[PANEL:, PANEL : 2 * PANEL] = packed[: 2 * PANEL, PANEL:]
    gram[2 * PANEL :, 2 * PANEL :] = packed[2 * PANEL :, PANEL:]
    gram[:PANEL, PANEL:] = packed[PANEL:, :PANEL].T
    gram[PANEL : 2 * PANEL, 2 * PANEL :] = packed[PANEL : 2 * PANEL, PANEL:].T
    return gram[...]


def symmetric_product(left, right, out):
    for begin in range(0, INNER, TILE):
        end = min(begin + TILE, INNER)
        part = dot(left[begin:], right[:, begin:end])
        out[begin:, begin:end] = part
        if end < INNER:
            out[begin:end, end:] = part[end - begin :].T
    return out[...]


def polynomial(raw, gram):
    diagonal = lax.broadcasted_iota(jnp.int32, raw.shape, 0) == lax.broadcasted_iota(jnp.int32, raw.shape, 1)
    square_total = jnp.sum(jnp.where(diagonal, raw, 0.0))
    norm = jnp.sqrt(jnp.full((1, 1), square_total, jnp.float32)) + EPSILON
    inverse = 1.0 / norm
    first = (raw * inverse) * inverse
    first_right = passes_right(first)
    second = symmetric_product(passes_left(first), first_right, gram)
    base = QUINTIC_SECOND * first + QUINTIC_THIRD * second + jnp.where(diagonal, QUINTIC_FIRST, 0.0)
    base_left = passes_left(base)
    third = symmetric_product(base_left, first_right, gram)
    next_gram = symmetric_product(base_left, passes_right(third), gram)
    square = symmetric_product(passes_left(next_gram), passes_right(next_gram), gram)
    outer = QUINTIC_SECOND * next_gram + QUINTIC_THIRD * square + jnp.where(diagonal, QUINTIC_FIRST, 0.0)
    return symmetric_product(passes_left(outer), passes_right(base), gram) * (inverse * OUT_SCALE)


def extract(padded, start, count, staged, step):
    _, slots, columns = staged.shape
    sublane = lax.broadcasted_iota(jnp.int32, (SUBLANES, columns), 0)
    shift = start % SUBLANES
    base = start - shift
    back = jnp.where(shift == 0, 0, SUBLANES - shift)

    def window(index):
        rows = pl.ds(pl.multiple_of(base + index * SUBLANES, SUBLANES), SUBLANES)
        return pltpu.roll(padded[rows, :], back, 0)

    def tile(index, here):
        after = window(index + 1)
        moved = jnp.where(sublane < SUBLANES - shift, here, after)
        rows = pl.ds(pl.multiple_of(index * SUBLANES, SUBLANES), SUBLANES)
        staged[step, rows, :] = jnp.where(sublane < count - index * SUBLANES, moved, 0.0)
        return after

    over_tiles(slots // SUBLANES, tile, window(0))


def stack_jobs(pair, stacked, arrive):
    jobs, begin = [], 0
    for index, (side, (first_row, last_row)) in enumerate(PARTS):
        size = last_row - first_row
        source = pair.at[side, pl.ds(first_row, size)]
        jobs.append((source, stacked.at[pl.ds(begin, size)], arrive.at[index]))
        begin += size
    return jobs


def update_kernel(first, steps, *refs):
    tables, (keep, away, pair) = refs[:4], refs[4:7]
    gram, padded, staged, stacked, held, arrive, leave = refs[-12:-5]
    whole, *homes = refs[-13 - len(steps) : -12]
    ranks = tables[1].shape[0]
    rank = lax.axis_index("fsdp")
    incoming = [pltpu.make_async_copy(*job) for job in stack_jobs(pair, stacked, arrive)] if steps else []
    for copy in incoming:
        copy.start()
    table_copies, places = table_jobs(tables, refs[-5:])
    for copy in table_copies:
        copy.start()
    mine, other = core_rows()
    held[mine, :] = keep[...]
    held[other, :] = away[...]
    total = polynomial(unpack(held, gram), gram)
    for panel in range(3):
        store_panel(held, panel, total[panel * PANEL :, panel * PANEL : (panel + 1) * PANEL])
    copies = [pltpu.make_async_copy(held, whole, leave.at[len(steps)])]
    copies[0].start()
    for copy in [*incoming, *table_copies]:
        copy.wait()
    if steps:
        padded[:INNER, :] = dot(passes_left(total), stacked[...])
    owner_group, live_ranks, row_counts, row_offsets = places
    matrix = matrix_of(owner_group, rank ^ mate(ranks) if first else rank)
    for index, step in enumerate(steps):
        target = rank ^ step
        count = row_counts[matrix, target] * live_ranks[target]
        extract(padded, row_offsets[matrix, target], count, staged, index)
        copies.append(pltpu.make_async_copy(staged.at[index], homes[index], leave.at[index]))
        copies[-1].start()
    for copy in copies:
        copy.wait()


def finish_kernel(ranks, *refs):
    tables, sources = refs[:4], refs[4:10]
    (result, shards, gram, padded, staged, stacked, held, arrive, leave), refs = refs[11:20], refs[20:]
    rank = lax.axis_index("fsdp")
    owner_group, live_ranks, row_counts, row_offsets = fetch_tables(tables, refs)

    inner = is_inner(rank, ranks)
    outer = jnp.logical_not(inner)

    def make(index, carry):
        wanted = [jnp.logical_and(inner, index == 1), jnp.logical_and(inner, index == 0), outer]
        incoming = []
        for condition, packed, pair in zip(wanted, sources[::2], sources[1::2]):
            incoming.append((condition, packed, held, leave.at[2]))
            incoming += [(condition, *job) for job in stack_jobs(pair, stacked, arrive)]
        each_copy(incoming, "start")
        each_copy(incoming, "wait")
        padded[:INNER, :] = dot(passes_left(unpack(held, gram)), stacked[...])
        matrix = matrix_of(owner_group, rank ^ (index * mate(ranks)))
        extract(padded, row_offsets[matrix, rank], row_counts[matrix, rank] * live_ranks[rank], staged, 0)
        outgoing = [
            (index >= 0, staged.at[0], shards.at[matrix], leave.at[0]),
            (index == 0, padded.at[pl.ds(0, INNER)], result, leave.at[1]),
        ]
        each_copy(outgoing, "start")
        each_copy(outgoing, "wait")
        return carry

    lax.fori_loop(0, jnp.where(inner, 2, 1), make, 0)


def place_kernel(first, ranks, steps, *refs):
    table, blocks, shards = refs[0], refs[1 : 1 + len(steps)], refs[2 + len(steps)]
    owner_group, arrive, leave = refs[3 + len(steps) :]
    rank = lax.axis_index("fsdp")
    fetch = pltpu.make_async_copy(table, owner_group, arrive)
    fetch.start()
    fetch.wait()
    copies = []
    for index, step in enumerate(steps):
        source = rank ^ step
        matrix = matrix_of(owner_group, source ^ mate(ranks) if first else source)
        copies.append((is_inner(source, ranks), blocks[index], shards.at[matrix], leave.at[index]))
    each_copy(copies, "start")
    each_copy(copies, "wait")


def idle_kernel(*refs):
    pass


def floats(*shape):
    return jax.ShapeDtypeStruct(shape, jnp.float32)


def vmem(*shape, dtype=jnp.float32):
    return pltpu.VMEM(shape, dtype)


def flags(*shape):
    return pltpu.SemaphoreType.DMA(shape)


FREE = pl.CostEstimate(flops=0, bytes_accessed=0, transcendentals=0)


def blend(first, tables, momentum, gradient, before):
    _, slots, columns = momentum.shape
    ranks = tables[1].shape[0]
    chunks = 2 if slots % (2 * SUBLANES) == 0 else 1
    return pl.pallas_call(
        functools.partial(blend_kernel, first, chunks),
        out_shape=[floats(slots, columns)] * (ranks - first) + [floats(SUBLANES, 128)],
        in_specs=[HBM] * 6 + [ANY] * len(before),
        out_specs=[ANY] * (ranks - first) + [VMEM],
        scratch_shapes=[vmem(ranks, slots, columns)] * 2
        + [flags(ranks, chunks, 2), flags(ranks, chunks)]
        + table_scratch(*tables[2].shape),
        compiler_params=FULL,
        cost_estimate=FREE,
        name="blend",
    )(*tables, momentum, gradient, *before)


def fresh_momentum(tables, momentum, gradient, before):
    matrices, slots, columns = momentum.shape
    block = pl.BlockSpec((None, slots, columns), lambda matrix: (matrix, 0, 0))
    return pl.pallas_call(
        fresh_kernel,
        grid=(matrices,),
        out_shape=[floats(*momentum.shape), floats(SUBLANES, 128)],
        in_specs=[pl.BlockSpec(memory_space=pltpu.SMEM)] * 2 + [block] * 2 + [ANY],
        out_specs=[block, pl.BlockSpec((SUBLANES, 128), lambda matrix: (0, 0))],
        compiler_params=FULL,
        cost_estimate=FREE,
        name="fresh_momentum",
    )(*tables[1:3], momentum, gradient, before)


def assemble_and_gram(inner, first, tables, blocks, *after):
    slots, columns = blocks[0].shape
    ranks = len(blocks)
    pair = jax.ShapeDtypeStruct((4, INNER, columns), jnp.bfloat16)
    return pl.pallas_call(
        functools.partial(gram_kernel, inner, first, ranks),
        out_shape=[pair] + [floats(INNER // 2, 2 * PANEL)] * 2,
        in_specs=[HBM] * 4 + [ANY] * (ranks + len(after)),
        out_specs=[ANY, VMEM, VMEM],
        scratch_shapes=[
            vmem(ranks, slots, columns),
            vmem(INNER + slots + SUBLANES, columns),
            vmem(INNER, columns, dtype=jnp.bfloat16),
            vmem(INNER, columns, dtype=jnp.bfloat16),
            vmem(INNER, 2 * PANEL),
            flags(ranks),
            flags(2),
        ]
        + table_scratch(*tables[2].shape),
        compiler_params=PARAMS,
        cost_estimate=FREE,
        name="assemble_and_gram",
    )(*tables, *blocks, *after)


def update_shapes(steps, slots, columns):
    return [floats(INNER, 2 * PANEL)] + [floats(slots, columns)] * len(steps)


def nothing(shapes):
    return pl.pallas_call(
        idle_kernel, out_shape=shapes, out_specs=[ANY] * len(shapes), compiler_params=SMALL, name="nothing"
    )()


def apply_update(first, steps, tables, keep, away, pair, slots, *after):
    columns = pair.shape[2]
    return pl.pallas_call(
        functools.partial(update_kernel, first, steps),
        out_shape=update_shapes(steps, slots, columns),
        in_specs=[HBM] * 4 + [VMEM] * 2 + [ANY] * (1 + len(after)),
        out_specs=[ANY] * (1 + len(steps)),
        scratch_shapes=[
            vmem(INNER, INNER),
            vmem(INNER + slots + 2 * SUBLANES, columns),
            vmem(max(len(steps), 1), slots, columns),
            vmem(3 * INNER, columns, dtype=jnp.bfloat16),
            vmem(INNER, 2 * PANEL),
            flags(len(PARTS)),
            flags(len(steps) + 1),
        ]
        + table_scratch(*tables[2].shape),
        compiler_params=PARAMS,
        cost_estimate=FREE,
        name="apply_update",
    )(*tables, keep, away, pair, *after)


def touch(value, flops=0):
    return pl.pallas_call(
        idle_kernel,
        out_shape=floats(SUBLANES, 128),
        in_specs=[ANY],
        out_specs=ANY,
        compiler_params=SMALL,
        cost_estimate=pl.CostEstimate(flops=flops, bytes_accessed=0, transcendentals=0),
        name="touch",
    )(value)


def finish(tables, sources, shape, after):
    _, slots, columns = shape
    return pl.pallas_call(
        functools.partial(finish_kernel, tables[1].shape[0]),
        out_shape=[floats(INNER, columns), floats(*shape)],
        in_specs=[HBM] * 4 + [ANY] * 7,
        out_specs=[HBM] * 2,
        scratch_shapes=[
            vmem(INNER, INNER),
            vmem(INNER + slots + 2 * SUBLANES, columns),
            vmem(2, slots, columns),
            vmem(3 * INNER, columns, dtype=jnp.bfloat16),
            vmem(INNER, 2 * PANEL),
            flags(len(PARTS)),
            flags(3),
        ]
        + table_scratch(*tables[2].shape),
        compiler_params=PARAMS,
        cost_estimate=FREE,
        name="finish",
    )(*tables, *sources, after)


def place_blocks(first, owner_group, steps, blocks, shards, ranks):
    return pl.pallas_call(
        functools.partial(place_kernel, first, ranks, steps),
        out_shape=floats(*shards.shape),
        in_specs=[HBM] + [VMEM] * len(blocks) + [HBM],
        out_specs=HBM,
        scratch_shapes=[pltpu.SMEM(owner_group.shape, jnp.int32), flags(), flags(len(steps))],
        input_output_aliases={1 + len(blocks): 0},
        compiler_params=PARAMS,
        cost_estimate=FREE,
        name="place_blocks",
    )(owner_group, *blocks, shards)


def sum_halves(keep, send, axis, streams):
    size = lax.axis_size(axis)

    def exchange(piece, bits):
        return lax.ppermute(piece, axis, [(i, i ^ bits[i & 1]) for i in range(size)])

    chips = [1 << shift for shift in range(1, size.bit_length() - 1)]
    keep = keep + exchange(send, (1, 1))
    pieces = jnp.split(keep, streams, axis=0)
    for bits in zip(chips, reversed(chips)):
        pieces = [piece + exchange(piece, bits[:: 1 - 2 * index]) for index, piece in enumerate(pieces)]
    keep = jnp.concatenate(pieces, axis=0)
    return keep, exchange(keep, (1, 1))


def on_device(momentum, gradient, live_ranks, owner_group, row_counts, row_offsets):
    ranks = lax.axis_size("fsdp")
    _, slots, columns = momentum.shape
    inner = is_inner(lax.axis_index("fsdp"), ranks)
    tables = (owner_group, live_ranks, row_counts, row_offsets)
    last = [2, 1, *range(3, ranks)]
    early = [step for step in last if step != mate(ranks)]

    def pairs(step, inward):
        return [(i, i ^ step) for i in range(ranks) if is_inner(i ^ step if inward else i, ranks)]

    def to_inner(block, step):
        return lax.ppermute(block, "fsdp", pairs(step, True))

    def from_inner(block, step):
        return lax.ppermute(block, "fsdp", pairs(step, False))

    near = mate(ranks)
    far = [step for step in last if step != near]
    *blends, token = blend(True, tables, momentum, gradient, [])
    own = blends[near - 1]
    swapped = lax.ppermute(own, "fsdp", [(i, i ^ near) for i in range(ranks)])
    arrived = {step: to_inner(blends[step - 1], step) for step in far}
    *blends, token = blend(False, tables, momentum, gradient, [token, touch(swapped)])
    last_blocks = [blends[0]] + [to_inner(blends[step], step) for step in range(1, ranks)]
    new_momentum, token = fresh_momentum(tables, momentum, gradient, token)
    handed = {step: from_inner(arrived[step], near) for step in far}

    def ordered(base, opposite, others):
        return [{0: base, near: opposite, **others}[step] for step in range(ranks)]

    first_blocks = ordered(own, swapped, arrived)
    pair, keep, send = assemble_and_gram(True, True, tables, first_blocks, *[handed[step] for step in far[1:]])

    def first_update(pair, keep, send, after):
        return apply_update(True, early, tables, *sum_halves(keep, send, "tensor", 1), pair, slots, after)

    def first_skip(*_):
        return nothing(update_shapes(early, slots, columns))

    packed, *homes = lax.cond(inner, first_update, first_skip, pair, keep, send, touch(keep, 10**11))
    first_home = [from_inner(block, step) for step, block in zip(early, homes)]
    pair_shape = jax.ShapeDtypeStruct(pair.shape, pair.dtype)

    def outer_update(*blocks):
        pair, keep, send = assemble_and_gram(False, True, tables, blocks)
        return (pair, *apply_update(True, [], tables, *sum_halves(keep, send, "tensor", 1), pair, slots, keep))

    def outer_skip(*_):
        return tuple(nothing([pair_shape, *update_shapes([], slots, columns)]))

    outer_pair, outer_packed = lax.cond(inner, outer_skip, outer_update, *ordered(swapped, own, handed))

    def last_update(after, *blocks):
        pair, keep, send = assemble_and_gram(True, False, tables, blocks, after)
        return (pair, *apply_update(False, last, tables, *sum_halves(keep, send, "tensor", 2), pair, slots))

    def last_skip(*_):
        return tuple(nothing([pair_shape, *update_shapes(last, slots, columns)]))

    last_pair, last_packed, *homes = lax.cond(inner, last_update, last_skip, outer_packed, *last_blocks)
    last_home = [from_inner(block, step) for step, block in zip(last, homes)]

    sources = [packed, pair, last_packed, last_pair, outer_packed, outer_pair]
    result, shards = finish(tables, sources, momentum.shape, token)
    shards = place_blocks(True, owner_group, early, first_home, shards, ranks)
    for step, block in zip(last, last_home):
        shards = place_blocks(False, owner_group, [step], [block], shards, ranks)
    return (new_momentum, shards, result[None])


def solution(mesh):
    placed = (P(None, "fsdp", "tensor"), P(None, "fsdp", "tensor"), P(), P(), P(), P())
    return jax.shard_map(
        on_device,
        mesh=mesh,
        in_specs=placed,
        out_specs=(P(None, "fsdp", "tensor"), P(None, "fsdp", "tensor"), P("fsdp", None, "tensor")),
        check_vma=False,
    )
```

```python
import functools
import math

import jax
import jax.numpy as jnp
from jax import lax
from jax.experimental import pallas as pl
from jax.experimental.pallas import tpu as pltpu
from jax.sharding import PartitionSpec as P

WIDTH = 7168
INNER = 576
PANEL = INNER // 3
TILE = 256
SUBLANES = 8

MOMENTUM_RATE = 0.95
QUINTIC_FIRST = 3.4445
QUINTIC_SECOND = -4.775
QUINTIC_THIRD = 2.0315
EPSILON = 1e-07
OUT_SCALE = 0.2 * math.sqrt(max(INNER, WIDTH))
SMALL = pltpu.CompilerParams(vmem_limit_bytes=1024 * 1024)
FULL = pltpu.CompilerParams(vmem_limit_bytes=60 * 1024 * 1024)
PARAMS = pltpu.CompilerParams(vmem_limit_bytes=24 * 1024 * 1024)
HBM = pl.BlockSpec(memory_space=pltpu.HBM)
ANY = pl.BlockSpec(memory_space=pl.ANY)
VMEM = pl.BlockSpec(memory_space=pltpu.VMEM)


def halves(value):
    high = value.astype(jnp.bfloat16)
    low = (value - high.astype(jnp.float32)).astype(jnp.bfloat16)
    return high, low


def dot(left, right, contract=((1,), (0,))):
    return lax.dot_general(left, right, (contract, ((), ())), preferred_element_type=jnp.float32)


DEPTH = INNER // TILE * TILE
PARTS = [(side, rows) for rows in ((0, DEPTH), (DEPTH, INNER)) if rows[0] < rows[1] for side in (1, 0, 0)]


def passes_left(value):
    high, low = halves(value)
    return jnp.concatenate(
        [part[:, first:last] for first, last in ((0, DEPTH), (DEPTH, INNER)) for part in (high, low, high)], axis=1
    )


def passes_right(value):
    sides = halves(value)
    return jnp.concatenate([sides[side][first:last] for side, (first, last) in PARTS], axis=0)


def is_inner(rank, ranks):
    low = ranks // 4
    return (rank >= low) & (rank < ranks - low)


def mate(ranks):
    return ranks // 4


def table_scratch(matrices, ranks):
    return [
        pltpu.SMEM((matrices,), jnp.int32),
        pltpu.SMEM((ranks,), jnp.int32),
        pltpu.SMEM((matrices, ranks), jnp.int32),
        pltpu.SMEM((matrices, ranks), jnp.int32),
        pltpu.SemaphoreType.DMA((4,)),
    ]


def table_jobs(tables, held):
    *places, arrive = held
    copies = [
        pltpu.make_async_copy(table, place, arrive.at[index])
        for index, (table, place) in enumerate(zip(tables, places))
    ]
    return copies, places


def fetch_tables(tables, held):
    copies, places = table_jobs(tables, held)
    for copy in copies:
        copy.start()
    for copy in copies:
        copy.wait()
    return places


def matrix_of(owner_group, rank):
    found = jnp.int32(0)
    for matrix in range(owner_group.shape[0]):
        found = jnp.where(owner_group[matrix] == rank, matrix, found)
    return found


def over_tiles(tiles, body, carry):
    group = next(group for group in (6, 3, 2, 1) if tiles % group == 0)

    def step(index, carry):
        for member in range(group):
            carry = body(index * group + member, carry)
        return carry

    return lax.fori_loop(0, tiles // group, step, carry)


def each_copy(copies, action):
    for condition, source, place, flag in copies:

        @pl.when(condition)
        def _(source=source, place=place, flag=flag):
            getattr(pltpu.make_async_copy(source, place, flag), action)()


def step_pairs(ranks):
    outer = [step for step in range(1, ranks) if is_inner(step, ranks)]
    inner = [step for step in range(1, ranks) if is_inner(mate(ranks) ^ step, ranks)]
    return list(zip(outer, [*inner, 0]))


def blend_kernel(first, steps, chunks, *refs):
    tables, (momentum, gradient) = refs[:4], refs[4:6]
    ranks = tables[1].shape[0]
    *outs, token, olds, grads, arrive, leave = refs[-len(steps) - 10 : -5]
    owner_group, live_ranks, row_counts, _ = fetch_tables(tables, refs[-5:])
    rank = lax.axis_index("fsdp")
    slots, columns = outs[0].shape
    size = slots // chunks
    jobs = []
    for step, (outer, inner) in enumerate(steps):
        target = rank ^ jnp.where(is_inner(rank, ranks), inner, outer)
        wanted = rank >= 0
        matrix = matrix_of(owner_group, target ^ mate(ranks) if first else target)
        count = row_counts[matrix, rank] * live_ranks[rank]
        for chunk in range(chunks):
            part = pl.ds(chunk * size, size)
            flags = arrive.at[step, chunk, 0], arrive.at[step, chunk, 1]
            incoming = (
                (wanted, momentum.at[matrix, part], olds.at[step, part], flags[0]),
                (wanted, gradient.at[matrix, part], grads.at[step, part], flags[1]),
            )
            outgoing = (wanted, olds.at[step, part], outs[step].at[part], leave.at[step, chunk])
            jobs.append((step, chunk, count, incoming, outgoing))
            each_copy(incoming, "start")
    token[...] = jnp.zeros_like(token)
    for step, chunk, count, incoming, outgoing in jobs:

        @pl.when(incoming[0][0])
        def _(step=step, chunk=chunk, count=count, incoming=incoming, outgoing=outgoing):
            for _, source, place, flag in incoming:
                pltpu.make_async_copy(source, place, flag).wait()
            sublane = lax.broadcasted_iota(jnp.int32, (SUBLANES, columns), 0)

            def tile(index, carry):
                first_row = chunk * size + index * SUBLANES
                rows = pl.ds(pl.multiple_of(first_row, SUBLANES), SUBLANES)
                grad_now = grads[step, rows, :]
                fresh = MOMENTUM_RATE * olds[step, rows, :] + grad_now
                olds[step, rows, :] = jnp.where(sublane < count - first_row, grad_now + MOMENTUM_RATE * fresh, 0.0)
                return carry

            over_tiles(size // SUBLANES, tile, 0)
            pltpu.make_async_copy(*outgoing[1:]).start()

    each_copy([job[-1] for job in jobs], "wait")


def fresh_kernel(live_ranks, row_counts, momentum, gradient, _, out, token):
    token[...] = jnp.zeros_like(token)
    rank, matrix = lax.axis_index("fsdp"), pl.program_id(0)
    slots, columns = out.shape
    count = row_counts[matrix, rank] * live_ranks[rank]
    sublane = lax.broadcasted_iota(jnp.int32, (SUBLANES, columns), 0)

    def tile(index, carry):
        rows = pl.ds(pl.multiple_of(index * SUBLANES, SUBLANES), SUBLANES)
        fresh = MOMENTUM_RATE * momentum[rows, :] + gradient[rows, :]
        out[rows, :] = jnp.where(sublane < count - index * SUBLANES, fresh, 0.0)
        return carry

    over_tiles(slots // SUBLANES, tile, 0)


def assemble(blocks, landed, padded, arrive, tables, held, first):
    ranks, slots, columns = landed.shape
    copies = []
    for step in range(ranks):
        copies.append(pltpu.make_async_copy(blocks[step], landed.at[step], arrive.at[step]))
        copies[-1].start()
    owner_group, _, _, row_offsets = fetch_tables(tables, held)
    rank = lax.axis_index("fsdp")
    base = jnp.where(is_inner(rank, ranks), rank, rank ^ mate(ranks))
    matrix = matrix_of(owner_group, base ^ mate(ranks) if first else base)
    padded[...] = jnp.zeros_like(padded)
    sublane = lax.broadcasted_iota(jnp.int32, (SUBLANES, columns), 0)
    for step in range(ranks):
        start = row_offsets[matrix, base ^ step]
        shift = start % SUBLANES
        origin = start - shift
        copies[step].wait()

        def tile(index, before, origin=origin, shift=shift, step=step):
            moved = pltpu.roll(landed[step, pl.ds(pl.multiple_of(index * SUBLANES, SUBLANES), SUBLANES), :], shift, 0)
            rows = pl.ds(pl.multiple_of(origin + index * SUBLANES, SUBLANES), SUBLANES)
            padded[rows, :] = padded[rows, :] + jnp.where(sublane < shift, before, moved)
            return moved

        after = over_tiles(slots // SUBLANES, tile, jnp.zeros((SUBLANES, columns), jnp.float32))
        rows = pl.ds(pl.multiple_of(origin + slots, SUBLANES), SUBLANES)
        padded[rows, :] = padded[rows, :] + jnp.where(sublane < shift, after, 0.0)


def gram_kernel(inner, first, ranks, *refs):
    pair, keep, send = refs[-15:-12]
    landed, padded, high_held, low_held, gram, arrive, leave = refs[-12:-5]

    @pl.when(is_inner(lax.axis_index("fsdp"), ranks) == inner)
    def _():
        assemble(refs[4 : 4 + ranks], landed, padded, arrive, refs[:4], refs[-5:], first)
        high, low = halves(padded[:INNER, :])
        high_held[...] = high
        low_held[...] = low
        outgoing = [
            pltpu.make_async_copy(high_held, pair.at[0], leave.at[0]),
            pltpu.make_async_copy(low_held, pair.at[1], leave.at[1]),
        ]
        for copy in outgoing:
            copy.start()
        left = jnp.concatenate([high, low, high], axis=1)
        right = jnp.concatenate([low, high, high], axis=1)
        for panel in range(3):
            here = slice(panel * PANEL, (panel + 1) * PANEL)
            store_panel(gram, panel, dot(left[panel * PANEL :], right[here], ((1,), (1,))))
        mine, other = core_rows()
        keep[...] = gram[mine, :]
        send[...] = gram[other, :]
        for copy in outgoing:
            copy.wait()


def core_rows():
    half = INNER // 2
    first = (lax.axis_index("tensor") & 1) * half
    return tuple(pl.ds(pl.multiple_of(start, SUBLANES), half) for start in (first, half - first))


def store_panel(packed, panel, part):
    if panel == 0:
        packed[:, :PANEL] = part
    elif panel == 1:
        packed[: 2 * PANEL, PANEL:] = part
    else:
        packed[2 * PANEL :, PANEL:] = part


def unpack(packed, gram):
    gram[:, :PANEL] = packed[:, :PANEL]
    gram[PANEL:, PANEL : 2 * PANEL] = packed[: 2 * PANEL, PANEL:]
    gram[2 * PANEL :, 2 * PANEL :] = packed[2 * PANEL :, PANEL:]
    gram[:PANEL, PANEL:] = packed[PANEL:, :PANEL].T
    gram[PANEL : 2 * PANEL, 2 * PANEL :] = packed[PANEL : 2 * PANEL, PANEL:].T
    return gram[...]


def symmetric_product(left, right, out):
    for begin in range(0, INNER, TILE):
        end = min(begin + TILE, INNER)
        part = dot(left[begin:], right[:, begin:end])
        out[begin:, begin:end] = part
        if end < INNER:
            out[begin:end, end:] = part[end - begin :].T
    return out[...]


def polynomial(raw, gram):
    diagonal = lax.broadcasted_iota(jnp.int32, raw.shape, 0) == lax.broadcasted_iota(jnp.int32, raw.shape, 1)
    square_total = jnp.sum(jnp.where(diagonal, raw, 0.0))
    norm = jnp.sqrt(jnp.full((1, 1), square_total, jnp.float32)) + EPSILON
    inverse = 1.0 / norm
    first = (raw * inverse) * inverse
    first_right = passes_right(first)
    second = symmetric_product(passes_left(first), first_right, gram)
    base = QUINTIC_SECOND * first + QUINTIC_THIRD * second + jnp.where(diagonal, QUINTIC_FIRST, 0.0)
    base_left = passes_left(base)
    third = symmetric_product(base_left, first_right, gram)
    next_gram = symmetric_product(base_left, passes_right(third), gram)
    square = symmetric_product(passes_left(next_gram), passes_right(next_gram), gram)
    outer = QUINTIC_SECOND * next_gram + QUINTIC_THIRD * square + jnp.where(diagonal, QUINTIC_FIRST, 0.0)
    return symmetric_product(passes_left(outer), passes_right(base), gram) * (inverse * OUT_SCALE)


def extract(padded, start, count, staged, step):
    _, slots, columns = staged.shape
    sublane = lax.broadcasted_iota(jnp.int32, (SUBLANES, columns), 0)
    shift = start % SUBLANES
    base = start - shift
    back = jnp.where(shift == 0, 0, SUBLANES - shift)

    def window(index):
        rows = pl.ds(pl.multiple_of(base + index * SUBLANES, SUBLANES), SUBLANES)
        return pltpu.roll(padded[rows, :], back, 0)

    def tile(index, here):
        after = window(index + 1)
        moved = jnp.where(sublane < SUBLANES - shift, here, after)
        rows = pl.ds(pl.multiple_of(index * SUBLANES, SUBLANES), SUBLANES)
        staged[step, rows, :] = jnp.where(sublane < count - index * SUBLANES, moved, 0.0)
        return after

    over_tiles(slots // SUBLANES, tile, window(0))


def stack_jobs(pair, stacked, arrive):
    jobs, begin = [], 0
    for index, (side, (first_row, last_row)) in enumerate(PARTS):
        size = last_row - first_row
        source = pair.at[side, pl.ds(first_row, size)]
        jobs.append((source, stacked.at[pl.ds(begin, size)], arrive.at[index]))
        begin += size
    return jobs


def update_kernel(first, steps, *refs):
    tables, (keep, away, pair) = refs[:4], refs[4:7]
    gram, padded, staged, stacked, held, arrive, leave = refs[-12:-5]
    whole, *homes = refs[-13 - len(steps) : -12]
    ranks = tables[1].shape[0]
    rank = lax.axis_index("fsdp")
    incoming = [pltpu.make_async_copy(*job) for job in stack_jobs(pair, stacked, arrive)] if steps else []
    for copy in incoming:
        copy.start()
    table_copies, places = table_jobs(tables, refs[-5:])
    for copy in table_copies:
        copy.start()
    mine, other = core_rows()
    held[mine, :] = keep[...]
    held[other, :] = away[...]
    total = polynomial(unpack(held, gram), gram)
    for panel in range(3):
        store_panel(held, panel, total[panel * PANEL :, panel * PANEL : (panel + 1) * PANEL])
    copies = [pltpu.make_async_copy(held, whole, leave.at[len(steps)])]
    copies[0].start()
    for copy in [*incoming, *table_copies]:
        copy.wait()
    if steps:
        padded[:INNER, :] = dot(passes_left(total), stacked[...])
    owner_group, live_ranks, row_counts, row_offsets = places
    matrix = matrix_of(owner_group, rank ^ mate(ranks) if first else rank)
    for index, step in enumerate(steps):
        target = rank ^ step
        count = row_counts[matrix, target] * live_ranks[target]
        extract(padded, row_offsets[matrix, target], count, staged, index)
        copies.append(pltpu.make_async_copy(staged.at[index], homes[index], leave.at[index]))
        copies[-1].start()
    for copy in copies:
        copy.wait()


def finish_kernel(ranks, *refs):
    tables, sources = refs[:4], refs[4:10]
    (result, shards, gram, padded, staged, stacked, held, arrive, leave), refs = refs[11:20], refs[20:]
    rank = lax.axis_index("fsdp")
    owner_group, live_ranks, row_counts, row_offsets = fetch_tables(tables, refs)

    inner = is_inner(rank, ranks)
    outer = jnp.logical_not(inner)

    def make(index, carry):
        wanted = [jnp.logical_and(inner, index == 1), jnp.logical_and(inner, index == 0), outer]
        incoming = []
        for condition, packed, pair in zip(wanted, sources[::2], sources[1::2]):
            incoming.append((condition, packed, held, leave.at[2]))
            incoming += [(condition, *job) for job in stack_jobs(pair, stacked, arrive)]
        each_copy(incoming, "start")
        each_copy(incoming, "wait")
        padded[:INNER, :] = dot(passes_left(unpack(held, gram)), stacked[...])
        matrix = matrix_of(owner_group, rank ^ (index * mate(ranks)))
        extract(padded, row_offsets[matrix, rank], row_counts[matrix, rank] * live_ranks[rank], staged, 0)
        outgoing = [
            (index >= 0, staged.at[0], shards.at[matrix], leave.at[0]),
            (index == 0, padded.at[pl.ds(0, INNER)], result, leave.at[1]),
        ]
        each_copy(outgoing, "start")
        each_copy(outgoing, "wait")
        return carry

    lax.fori_loop(0, jnp.where(inner, 2, 1), make, 0)


def place_kernel(first, ranks, steps, *refs):
    table, blocks, shards = refs[0], refs[1 : 1 + len(steps)], refs[2 + len(steps)]
    owner_group, arrive, leave = refs[3 + len(steps) :]
    rank = lax.axis_index("fsdp")
    fetch = pltpu.make_async_copy(table, owner_group, arrive)
    fetch.start()
    fetch.wait()
    copies = []
    for index, step in enumerate(steps):
        source = rank ^ step
        matrix = matrix_of(owner_group, source ^ mate(ranks) if first else source)
        copies.append((is_inner(source, ranks), blocks[index], shards.at[matrix], leave.at[index]))
    each_copy(copies, "start")
    each_copy(copies, "wait")


def idle_kernel(*refs):
    pass


def floats(*shape):
    return jax.ShapeDtypeStruct(shape, jnp.float32)


def vmem(*shape, dtype=jnp.float32):
    return pltpu.VMEM(shape, dtype)


def flags(*shape):
    return pltpu.SemaphoreType.DMA(shape)


FREE = pl.CostEstimate(flops=0, bytes_accessed=0, transcendentals=0)


def blend(first, steps, tables, momentum, gradient, before):
    _, slots, columns = momentum.shape
    chunks = 2 if slots % (2 * SUBLANES) == 0 else 1
    return pl.pallas_call(
        functools.partial(blend_kernel, first, steps, chunks),
        out_shape=[floats(slots, columns)] * len(steps) + [floats(SUBLANES, 128)],
        in_specs=[HBM] * 6 + [ANY] * len(before),
        out_specs=[ANY] * len(steps) + [VMEM],
        scratch_shapes=[vmem(len(steps), slots, columns)] * 2
        + [flags(len(steps), chunks, 2), flags(len(steps), chunks)]
        + table_scratch(*tables[2].shape),
        compiler_params=FULL,
        cost_estimate=FREE,
        name="blend",
    )(*tables, momentum, gradient, *before)


def fresh_momentum(tables, momentum, gradient, before):
    matrices, slots, columns = momentum.shape
    block = pl.BlockSpec((None, slots, columns), lambda matrix: (matrix, 0, 0))
    return pl.pallas_call(
        fresh_kernel,
        grid=(matrices,),
        out_shape=[floats(*momentum.shape), floats(SUBLANES, 128)],
        in_specs=[pl.BlockSpec(memory_space=pltpu.SMEM)] * 2 + [block] * 2 + [ANY],
        out_specs=[block, pl.BlockSpec((SUBLANES, 128), lambda matrix: (0, 0))],
        compiler_params=FULL,
        cost_estimate=FREE,
        name="fresh_momentum",
    )(*tables[1:3], momentum, gradient, before)


def assemble_and_gram(inner, first, tables, blocks, *after):
    slots, columns = blocks[0].shape
    ranks = len(blocks)
    pair = jax.ShapeDtypeStruct((4, INNER, columns), jnp.bfloat16)
    return pl.pallas_call(
        functools.partial(gram_kernel, inner, first, ranks),
        out_shape=[pair] + [floats(INNER // 2, 2 * PANEL)] * 2,
        in_specs=[HBM] * 4 + [ANY] * (ranks + len(after)),
        out_specs=[ANY, VMEM, VMEM],
        scratch_shapes=[
            vmem(ranks, slots, columns),
            vmem(INNER + slots + SUBLANES, columns),
            vmem(INNER, columns, dtype=jnp.bfloat16),
            vmem(INNER, columns, dtype=jnp.bfloat16),
            vmem(INNER, 2 * PANEL),
            flags(ranks),
            flags(2),
        ]
        + table_scratch(*tables[2].shape),
        compiler_params=PARAMS,
        cost_estimate=FREE,
        name="assemble_and_gram",
    )(*tables, *blocks, *after)


def update_shapes(steps, slots, columns):
    return [floats(INNER, 2 * PANEL)] + [floats(slots, columns)] * len(steps)


def nothing(shapes):
    return pl.pallas_call(
        idle_kernel, out_shape=shapes, out_specs=[ANY] * len(shapes), compiler_params=SMALL, name="nothing"
    )()


def apply_update(first, steps, tables, keep, away, pair, slots, *after):
    columns = pair.shape[2]
    return pl.pallas_call(
        functools.partial(update_kernel, first, steps),
        out_shape=update_shapes(steps, slots, columns),
        in_specs=[HBM] * 4 + [VMEM] * 2 + [ANY] * (1 + len(after)),
        out_specs=[ANY] * (1 + len(steps)),
        scratch_shapes=[
            vmem(INNER, INNER),
            vmem(INNER + slots + 2 * SUBLANES, columns),
            vmem(max(len(steps), 1), slots, columns),
            vmem(3 * INNER, columns, dtype=jnp.bfloat16),
            vmem(INNER, 2 * PANEL),
            flags(len(PARTS)),
            flags(len(steps) + 1),
        ]
        + table_scratch(*tables[2].shape),
        compiler_params=PARAMS,
        cost_estimate=FREE,
        name="apply_update",
    )(*tables, keep, away, pair, *after)


def touch(value, flops=0):
    return pl.pallas_call(
        idle_kernel,
        out_shape=floats(SUBLANES, 128),
        in_specs=[ANY],
        out_specs=ANY,
        compiler_params=SMALL,
        cost_estimate=pl.CostEstimate(flops=flops, bytes_accessed=0, transcendentals=0),
        name="touch",
    )(value)


def finish(tables, sources, shape, after):
    _, slots, columns = shape
    return pl.pallas_call(
        functools.partial(finish_kernel, tables[1].shape[0]),
        out_shape=[floats(INNER, columns), floats(*shape)],
        in_specs=[HBM] * 4 + [ANY] * 7,
        out_specs=[HBM] * 2,
        scratch_shapes=[
            vmem(INNER, INNER),
            vmem(INNER + slots + 2 * SUBLANES, columns),
            vmem(2, slots, columns),
            vmem(3 * INNER, columns, dtype=jnp.bfloat16),
            vmem(INNER, 2 * PANEL),
            flags(len(PARTS)),
            flags(3),
        ]
        + table_scratch(*tables[2].shape),
        compiler_params=PARAMS,
        cost_estimate=FREE,
        name="finish",
    )(*tables, *sources, after)


def place_blocks(first, owner_group, steps, blocks, shards, ranks):
    return pl.pallas_call(
        functools.partial(place_kernel, first, ranks, steps),
        out_shape=floats(*shards.shape),
        in_specs=[HBM] + [VMEM] * len(blocks) + [HBM],
        out_specs=HBM,
        scratch_shapes=[pltpu.SMEM(owner_group.shape, jnp.int32), flags(), flags(len(steps))],
        input_output_aliases={1 + len(blocks): 0},
        compiler_params=PARAMS,
        cost_estimate=FREE,
        name="place_blocks",
    )(owner_group, *blocks, shards)


def sum_halves(keep, send, axis, streams):
    size = lax.axis_size(axis)

    def exchange(piece, bits):
        return lax.ppermute(piece, axis, [(i, i ^ bits[i & 1]) for i in range(size)])

    chips = [1 << shift for shift in range(1, size.bit_length() - 1)]
    keep = keep + exchange(send, (1, 1))
    pieces = jnp.split(keep, streams, axis=0)
    for bits in zip(chips, reversed(chips)):
        pieces = [piece + exchange(piece, bits[:: 1 - 2 * index]) for index, piece in enumerate(pieces)]
    keep = jnp.concatenate(pieces, axis=0)
    return keep, exchange(keep, (1, 1))


def on_device(momentum, gradient, live_ranks, owner_group, row_counts, row_offsets):
    ranks = lax.axis_size("fsdp")
    _, slots, columns = momentum.shape
    inner = is_inner(lax.axis_index("fsdp"), ranks)
    tables = (owner_group, live_ranks, row_counts, row_offsets)
    last = [2, 1, *range(3, ranks)]
    early = [step for step in last if step != mate(ranks)]

    def passes(step, from_inside):
        return [(i, i ^ step) for i in range(ranks) if is_inner(i, ranks) == from_inside]

    def permute(block, pairs):
        return lax.ppermute(block, "fsdp", pairs)

    def from_inner(block, step):
        return permute(block, passes(step, True))

    near = mate(ranks)
    steps = step_pairs(ranks)
    arrived, last_arrived = {}, {}
    *heads, token = blend(True, steps[:-1], tables, momentum, gradient, [])
    for (outer_step, inner_step), block in zip(steps, heads):
        arrived[outer_step] = permute(block, passes(outer_step, False))
        arrived[inner_step] = from_inner(block, inner_step)
    own, token = blend(True, steps[-1:], tables, momentum, gradient, [token])
    swapped = permute(own, passes(steps[-1][0], False) + passes(near, True))
    arrived[steps[-1][0]] = swapped
    *blends, token = blend(False, steps, tables, momentum, gradient, [token, touch(arrived[near])])
    for (outer_step, inner_step), block in zip(steps, blends):
        last_arrived[outer_step] = permute(block, passes(outer_step, False))
        if inner_step:
            last_arrived[inner_step] = from_inner(block, inner_step)
    last_blocks = [blends[-1]] + [last_arrived[step] for step in range(1, ranks)]
    far = [step for step in last if step != near]
    new_momentum, token = fresh_momentum(tables, momentum, gradient, token)
    handed = {step: from_inner(arrived[step], near) for step in far}

    def ordered(base, opposite, others):
        return [{0: base, near: opposite, **others}[step] for step in range(ranks)]

    first_blocks = ordered(own, arrived[near], arrived)
    pair, keep, send = assemble_and_gram(True, True, tables, first_blocks, *[handed[step] for step in far[1:]])

    def first_update(pair, keep, send, after):
        return apply_update(True, early, tables, *sum_halves(keep, send, "tensor", 1), pair, slots, after)

    def first_skip(*_):
        return nothing(update_shapes(early, slots, columns))

    packed, *homes = lax.cond(inner, first_update, first_skip, pair, keep, send, touch(keep, 10**11))
    first_home = [from_inner(block, step) for step, block in zip(early, homes)]
    pair_shape = jax.ShapeDtypeStruct(pair.shape, pair.dtype)

    def outer_update(*blocks):
        pair, keep, send = assemble_and_gram(False, True, tables, blocks)
        return (pair, *apply_update(True, [], tables, *sum_halves(keep, send, "tensor", 1), pair, slots, keep))

    def outer_skip(*_):
        return tuple(nothing([pair_shape, *update_shapes([], slots, columns)]))

    outer_pair, outer_packed = lax.cond(inner, outer_skip, outer_update, *ordered(swapped, heads[0], handed))

    def last_update(after, *blocks):
        pair, keep, send = assemble_and_gram(True, False, tables, blocks, after)
        return (pair, *apply_update(False, last, tables, *sum_halves(keep, send, "tensor", 2), pair, slots))

    def last_skip(*_):
        return tuple(nothing([pair_shape, *update_shapes(last, slots, columns)]))

    last_pair, last_packed, *homes = lax.cond(inner, last_update, last_skip, outer_packed, *last_blocks)
    last_home = [from_inner(block, step) for step, block in zip(last, homes)]

    sources = [packed, pair, last_packed, last_pair, outer_packed, outer_pair]
    result, shards = finish(tables, sources, momentum.shape, token)
    shards = place_blocks(True, owner_group, early, first_home, shards, ranks)
    for step, block in zip(last, last_home):
        shards = place_blocks(False, owner_group, [step], [block], shards, ranks)
    return (new_momentum, shards, result[None])


def solution(mesh):
    placed = (P(None, "fsdp", "tensor"), P(None, "fsdp", "tensor"), P(), P(), P(), P())
    return jax.shard_map(
        on_device,
        mesh=mesh,
        in_specs=placed,
        out_specs=(P(None, "fsdp", "tensor"), P(None, "fsdp", "tensor"), P("fsdp", None, "tensor")),
        check_vma=False,
    )
```

```python
import functools
import math

import jax
import jax.numpy as jnp
from jax import lax
from jax.experimental import pallas as pl
from jax.experimental.pallas import tpu as pltpu
from jax.sharding import PartitionSpec as P

WIDTH = 7168
INNER = 576
PANEL = INNER // 3
TILE = 256
SUBLANES = 8

MOMENTUM_RATE = 0.95
QUINTIC_FIRST = 3.4445
QUINTIC_SECOND = -4.775
QUINTIC_THIRD = 2.0315
EPSILON = 1e-07
OUT_SCALE = 0.2 * math.sqrt(max(INNER, WIDTH))
SMALL = pltpu.CompilerParams(vmem_limit_bytes=1024 * 1024)
FULL = pltpu.CompilerParams(vmem_limit_bytes=60 * 1024 * 1024)
PARAMS = pltpu.CompilerParams(vmem_limit_bytes=24 * 1024 * 1024)
HBM = pl.BlockSpec(memory_space=pltpu.HBM)
ANY = pl.BlockSpec(memory_space=pl.ANY)
VMEM = pl.BlockSpec(memory_space=pltpu.VMEM)


def halves(value):
    high = value.astype(jnp.bfloat16)
    low = (value - high.astype(jnp.float32)).astype(jnp.bfloat16)
    return high, low


def dot(left, right, contract=((1,), (0,))):
    return lax.dot_general(left, right, (contract, ((), ())), preferred_element_type=jnp.float32)


DEPTH = INNER // TILE * TILE
PARTS = [(side, rows) for rows in ((0, DEPTH), (DEPTH, INNER)) if rows[0] < rows[1] for side in (1, 0, 0)]


def passes_left(value):
    high, low = halves(value)
    return jnp.concatenate(
        [part[:, first:last] for first, last in ((0, DEPTH), (DEPTH, INNER)) for part in (high, low, high)], axis=1
    )


def passes_right(value):
    sides = halves(value)
    return jnp.concatenate([sides[side][first:last] for side, (first, last) in PARTS], axis=0)


def is_inner(rank, ranks):
    low = ranks // 4
    return (rank >= low) & (rank < ranks - low)


def mate(ranks):
    return ranks // 4


def table_scratch(matrices, ranks):
    return [
        pltpu.SMEM((matrices,), jnp.int32),
        pltpu.SMEM((ranks,), jnp.int32),
        pltpu.SMEM((matrices, ranks), jnp.int32),
        pltpu.SMEM((matrices, ranks), jnp.int32),
        pltpu.SemaphoreType.DMA((4,)),
    ]


def table_jobs(tables, held):
    *places, arrive = held
    copies = [
        pltpu.make_async_copy(table, place, arrive.at[index])
        for index, (table, place) in enumerate(zip(tables, places))
    ]
    return copies, places


def fetch_tables(tables, held):
    copies, places = table_jobs(tables, held)
    for copy in copies:
        copy.start()
    for copy in copies:
        copy.wait()
    return places


def matrix_of(owner_group, rank):
    found = jnp.int32(0)
    for matrix in range(owner_group.shape[0]):
        found = jnp.where(owner_group[matrix] == rank, matrix, found)
    return found


def over_tiles(tiles, body, carry):
    group = next(group for group in (6, 3, 2, 1) if tiles % group == 0)

    def step(index, carry):
        for member in range(group):
            carry = body(index * group + member, carry)
        return carry

    return lax.fori_loop(0, tiles // group, step, carry)


def each_copy(copies, action):
    for condition, source, place, flag in copies:

        @pl.when(condition)
        def _(source=source, place=place, flag=flag):
            getattr(pltpu.make_async_copy(source, place, flag), action)()


def blend_kernel(first, chunks, *refs):
    tables, (momentum, gradient) = refs[:4], refs[4:6]
    ranks = tables[1].shape[0]
    *outs, token, olds, grads, arrive, leave = refs[-ranks - 10 + first : -5]
    owner_group, live_ranks, row_counts, _ = fetch_tables(tables, refs[-5:])
    rank = lax.axis_index("fsdp")
    slots, columns = outs[0].shape
    size = slots // chunks
    jobs = []
    for step in range(1, ranks + 1):
        step = step % ranks
        if first and step == 0:
            continue
        target = rank ^ step
        wanted = is_inner(target, ranks)
        matrix = matrix_of(owner_group, target ^ mate(ranks) if first else target)
        if first and step == mate(ranks):
            matrix = matrix_of(owner_group, jnp.where(wanted, rank, target))
            wanted = rank >= 0
        count = row_counts[matrix, rank] * live_ranks[rank]
        for chunk in range(chunks):
            part = pl.ds(chunk * size, size)
            flags = arrive.at[step, chunk, 0], arrive.at[step, chunk, 1]
            incoming = (
                (wanted, momentum.at[matrix, part], olds.at[step, part], flags[0]),
                (wanted, gradient.at[matrix, part], grads.at[step, part], flags[1]),
            )
            outgoing = (wanted, olds.at[step, part], outs[step - first].at[part], leave.at[step, chunk])
            jobs.append((step, chunk, count, incoming, outgoing))
            each_copy(incoming, "start")
    token[...] = jnp.zeros_like(token)
    for step, chunk, count, incoming, outgoing in jobs:

        @pl.when(incoming[0][0])
        def _(step=step, chunk=chunk, count=count, incoming=incoming, outgoing=outgoing):
            for _, source, place, flag in incoming:
                pltpu.make_async_copy(source, place, flag).wait()
            sublane = lax.broadcasted_iota(jnp.int32, (SUBLANES, columns), 0)

            def tile(index, carry):
                first_row = chunk * size + index * SUBLANES
                rows = pl.ds(pl.multiple_of(first_row, SUBLANES), SUBLANES)
                grad_now = grads[step, rows, :]
                fresh = MOMENTUM_RATE * olds[step, rows, :] + grad_now
                olds[step, rows, :] = jnp.where(sublane < count - first_row, grad_now + MOMENTUM_RATE * fresh, 0.0)
                return carry

            over_tiles(size // SUBLANES, tile, 0)
            pltpu.make_async_copy(*outgoing[1:]).start()

    each_copy([job[-1] for job in jobs], "wait")


def fresh_kernel(live_ranks, row_counts, momentum, gradient, _, out, token):
    token[...] = jnp.zeros_like(token)
    rank, matrix = lax.axis_index("fsdp"), pl.program_id(0)
    slots, columns = out.shape
    count = row_counts[matrix, rank] * live_ranks[rank]
    sublane = lax.broadcasted_iota(jnp.int32, (SUBLANES, columns), 0)

    def tile(index, carry):
        rows = pl.ds(pl.multiple_of(index * SUBLANES, SUBLANES), SUBLANES)
        fresh = MOMENTUM_RATE * momentum[rows, :] + gradient[rows, :]
        out[rows, :] = jnp.where(sublane < count - index * SUBLANES, fresh, 0.0)
        return carry

    over_tiles(slots // SUBLANES, tile, 0)


def assemble(blocks, landed, padded, arrive, tables, held, first):
    ranks, slots, columns = landed.shape
    copies = []
    for step in range(ranks):
        copies.append(pltpu.make_async_copy(blocks[step], landed.at[step], arrive.at[step]))
        copies[-1].start()
    owner_group, _, _, row_offsets = fetch_tables(tables, held)
    rank = lax.axis_index("fsdp")
    base = jnp.where(is_inner(rank, ranks), rank, rank ^ mate(ranks))
    matrix = matrix_of(owner_group, base ^ mate(ranks) if first else base)
    padded[...] = jnp.zeros_like(padded)
    sublane = lax.broadcasted_iota(jnp.int32, (SUBLANES, columns), 0)
    for step in range(ranks):
        start = row_offsets[matrix, base ^ step]
        shift = start % SUBLANES
        origin = start - shift
        copies[step].wait()

        def tile(index, before, origin=origin, shift=shift, step=step):
            moved = pltpu.roll(landed[step, pl.ds(pl.multiple_of(index * SUBLANES, SUBLANES), SUBLANES), :], shift, 0)
            rows = pl.ds(pl.multiple_of(origin + index * SUBLANES, SUBLANES), SUBLANES)
            padded[rows, :] = padded[rows, :] + jnp.where(sublane < shift, before, moved)
            return moved

        after = over_tiles(slots // SUBLANES, tile, jnp.zeros((SUBLANES, columns), jnp.float32))
        rows = pl.ds(pl.multiple_of(origin + slots, SUBLANES), SUBLANES)
        padded[rows, :] = padded[rows, :] + jnp.where(sublane < shift, after, 0.0)


def gram_kernel(inner, first, ranks, *refs):
    pair, keep, send = refs[-15:-12]
    landed, padded, high_held, low_held, gram, arrive, leave = refs[-12:-5]

    @pl.when(is_inner(lax.axis_index("fsdp"), ranks) == inner)
    def _():
        assemble(refs[4 : 4 + ranks], landed, padded, arrive, refs[:4], refs[-5:], first)
        high, low = halves(padded[:INNER, :])
        high_held[...] = high
        low_held[...] = low
        outgoing = [
            pltpu.make_async_copy(high_held, pair.at[0], leave.at[0]),
            pltpu.make_async_copy(low_held, pair.at[1], leave.at[1]),
        ]
        for copy in outgoing:
            copy.start()
        left = jnp.concatenate([high, low, high], axis=1)
        right = jnp.concatenate([low, high, high], axis=1)
        for panel in range(3):
            here = slice(panel * PANEL, (panel + 1) * PANEL)
            store_panel(gram, panel, dot(left[panel * PANEL :], right[here], ((1,), (1,))))
        mine, other = core_rows()
        keep[...] = gram[mine, :]
        send[...] = gram[other, :]
        for copy in outgoing:
            copy.wait()


def core_rows():
    half = INNER // 2
    first = (lax.axis_index("tensor") & 1) * half
    return tuple(pl.ds(pl.multiple_of(start, SUBLANES), half) for start in (first, half - first))


def store_panel(packed, panel, part):
    if panel == 0:
        packed[:, :PANEL] = part
    elif panel == 1:
        packed[: 2 * PANEL, PANEL:] = part
    else:
        packed[2 * PANEL :, PANEL:] = part


def unpack(packed, gram):
    gram[:, :PANEL] = packed[:, :PANEL]
    gram[PANEL:, PANEL : 2 * PANEL] = packed[: 2 * PANEL, PANEL:]
    gram[2 * PANEL :, 2 * PANEL :] = packed[2 * PANEL :, PANEL:]
    gram[:PANEL, PANEL:] = packed[PANEL:, :PANEL].T
    gram[PANEL : 2 * PANEL, 2 * PANEL :] = packed[PANEL : 2 * PANEL, PANEL:].T
    return gram[...]


def symmetric_product(left, right, out):
    for begin in range(0, INNER, TILE):
        end = min(begin + TILE, INNER)
        part = dot(left[begin:], right[:, begin:end])
        out[begin:, begin:end] = part
        if end < INNER:
            out[begin:end, end:] = part[end - begin :].T
    return out[...]


def polynomial(raw, gram):
    diagonal = lax.broadcasted_iota(jnp.int32, raw.shape, 0) == lax.broadcasted_iota(jnp.int32, raw.shape, 1)
    square_total = jnp.sum(jnp.where(diagonal, raw, 0.0))
    norm = jnp.sqrt(jnp.full((1, 1), square_total, jnp.float32)) + EPSILON
    inverse = 1.0 / norm
    first = (raw * inverse) * inverse
    first_right = passes_right(first)
    second = symmetric_product(passes_left(first), first_right, gram)
    base = QUINTIC_SECOND * first + QUINTIC_THIRD * second + jnp.where(diagonal, QUINTIC_FIRST, 0.0)
    base_left = passes_left(base)
    third = symmetric_product(base_left, first_right, gram)
    next_gram = symmetric_product(base_left, passes_right(third), gram)
    square = symmetric_product(passes_left(next_gram), passes_right(next_gram), gram)
    outer = QUINTIC_SECOND * next_gram + QUINTIC_THIRD * square + jnp.where(diagonal, QUINTIC_FIRST, 0.0)
    return symmetric_product(passes_left(outer), passes_right(base), gram) * (inverse * OUT_SCALE)


def extract(padded, start, count, staged, step):
    _, slots, columns = staged.shape
    sublane = lax.broadcasted_iota(jnp.int32, (SUBLANES, columns), 0)
    shift = start % SUBLANES
    base = start - shift
    back = jnp.where(shift == 0, 0, SUBLANES - shift)

    def window(index):
        rows = pl.ds(pl.multiple_of(base + index * SUBLANES, SUBLANES), SUBLANES)
        return pltpu.roll(padded[rows, :], back, 0)

    def tile(index, here):
        after = window(index + 1)
        moved = jnp.where(sublane < SUBLANES - shift, here, after)
        rows = pl.ds(pl.multiple_of(index * SUBLANES, SUBLANES), SUBLANES)
        staged[step, rows, :] = jnp.where(sublane < count - index * SUBLANES, moved, 0.0)
        return after

    over_tiles(slots // SUBLANES, tile, window(0))


def stack_jobs(pair, stacked, arrive):
    jobs, begin = [], 0
    for index, (side, (first_row, last_row)) in enumerate(PARTS):
        size = last_row - first_row
        source = pair.at[side, pl.ds(first_row, size)]
        jobs.append((source, stacked.at[pl.ds(begin, size)], arrive.at[index]))
        begin += size
    return jobs


def update_kernel(first, steps, *refs):
    tables, (keep, away, pair) = refs[:4], refs[4:7]
    gram, padded, staged, stacked, held, arrive, leave = refs[-12:-5]
    whole, *homes = refs[-13 - len(steps) : -12]
    ranks = tables[1].shape[0]
    rank = lax.axis_index("fsdp")
    incoming = [pltpu.make_async_copy(*job) for job in stack_jobs(pair, stacked, arrive)] if steps else []
    for copy in incoming:
        copy.start()
    table_copies, places = table_jobs(tables, refs[-5:])
    for copy in table_copies:
        copy.start()
    mine, other = core_rows()
    held[mine, :] = keep[...]
    held[other, :] = away[...]
    total = polynomial(unpack(held, gram), gram)
    for panel in range(3):
        store_panel(held, panel, total[panel * PANEL :, panel * PANEL : (panel + 1) * PANEL])
    copies = [pltpu.make_async_copy(held, whole, leave.at[len(steps)])]
    copies[0].start()
    for copy in [*incoming, *table_copies]:
        copy.wait()
    if steps:
        padded[:INNER, :] = dot(passes_left(total), stacked[...])
    owner_group, live_ranks, row_counts, row_offsets = places
    matrix = matrix_of(owner_group, rank ^ mate(ranks) if first else rank)
    for index, step in enumerate(steps):
        target = rank ^ step
        count = row_counts[matrix, target] * live_ranks[target]
        extract(padded, row_offsets[matrix, target], count, staged, index)
        copies.append(pltpu.make_async_copy(staged.at[index], homes[index], leave.at[index]))
        copies[-1].start()
    for copy in copies:
        copy.wait()


def finish_kernel(ranks, *refs):
    tables, sources = refs[:4], refs[4:10]
    (result, shards, gram, padded, staged, stacked, held, arrive, leave), refs = refs[11:20], refs[20:]
    rank = lax.axis_index("fsdp")
    owner_group, live_ranks, row_counts, row_offsets = fetch_tables(tables, refs)

    inner = is_inner(rank, ranks)
    outer = jnp.logical_not(inner)

    def make(index, carry):
        wanted = [jnp.logical_and(inner, index == 1), jnp.logical_and(inner, index == 0), outer]
        incoming = []
        for condition, packed, pair in zip(wanted, sources[::2], sources[1::2]):
            incoming.append((condition, packed, held, leave.at[2]))
            incoming += [(condition, *job) for job in stack_jobs(pair, stacked, arrive)]
        each_copy(incoming, "start")
        each_copy(incoming, "wait")
        padded[:INNER, :] = dot(passes_left(unpack(held, gram)), stacked[...])
        matrix = matrix_of(owner_group, rank ^ (index * mate(ranks)))
        extract(padded, row_offsets[matrix, rank], row_counts[matrix, rank] * live_ranks[rank], staged, 0)
        outgoing = [
            (index >= 0, staged.at[0], shards.at[matrix], leave.at[0]),
            (index == 0, padded.at[pl.ds(0, INNER)], result, leave.at[1]),
        ]
        each_copy(outgoing, "start")
        each_copy(outgoing, "wait")
        return carry

    lax.fori_loop(0, jnp.where(inner, 2, 1), make, 0)


def place_kernel(first, ranks, steps, *refs):
    table, blocks, shards = refs[0], refs[1 : 1 + len(steps)], refs[2 + len(steps)]
    owner_group, arrive, leave = refs[3 + len(steps) :]
    rank = lax.axis_index("fsdp")
    fetch = pltpu.make_async_copy(table, owner_group, arrive)
    fetch.start()
    fetch.wait()
    copies = []
    for index, step in enumerate(steps):
        source = rank ^ step
        matrix = matrix_of(owner_group, source ^ mate(ranks) if first else source)
        copies.append((is_inner(source, ranks), blocks[index], shards.at[matrix], leave.at[index]))
    each_copy(copies, "start")
    each_copy(copies, "wait")


def idle_kernel(*refs):
    pass


def floats(*shape):
    return jax.ShapeDtypeStruct(shape, jnp.float32)


def vmem(*shape, dtype=jnp.float32):
    return pltpu.VMEM(shape, dtype)


def flags(*shape):
    return pltpu.SemaphoreType.DMA(shape)


FREE = pl.CostEstimate(flops=0, bytes_accessed=0, transcendentals=0)


def blend(first, tables, momentum, gradient, before):
    _, slots, columns = momentum.shape
    ranks = tables[1].shape[0]
    chunks = 2 if slots % (2 * SUBLANES) == 0 else 1
    return pl.pallas_call(
        functools.partial(blend_kernel, first, chunks),
        out_shape=[floats(slots, columns)] * (ranks - first) + [floats(SUBLANES, 128)],
        in_specs=[HBM] * 6 + [ANY] * len(before),
        out_specs=[ANY] * (ranks - first) + [VMEM],
        scratch_shapes=[vmem(ranks, slots, columns)] * 2
        + [flags(ranks, chunks, 2), flags(ranks, chunks)]
        + table_scratch(*tables[2].shape),
        compiler_params=FULL,
        cost_estimate=FREE,
        name="blend",
    )(*tables, momentum, gradient, *before)


def fresh_momentum(tables, momentum, gradient, before):
    matrices, slots, columns = momentum.shape
    block = pl.BlockSpec((None, slots, columns), lambda matrix: (matrix, 0, 0))
    return pl.pallas_call(
        fresh_kernel,
        grid=(matrices,),
        out_shape=[floats(*momentum.shape), floats(SUBLANES, 128)],
        in_specs=[pl.BlockSpec(memory_space=pltpu.SMEM)] * 2 + [block] * 2 + [ANY],
        out_specs=[block, pl.BlockSpec((SUBLANES, 128), lambda matrix: (0, 0))],
        compiler_params=FULL,
        cost_estimate=FREE,
        name="fresh_momentum",
    )(*tables[1:3], momentum, gradient, before)


def assemble_and_gram(inner, first, tables, blocks, *after):
    slots, columns = blocks[0].shape
    ranks = len(blocks)
    pair = jax.ShapeDtypeStruct((4, INNER, columns), jnp.bfloat16)
    return pl.pallas_call(
        functools.partial(gram_kernel, inner, first, ranks),
        out_shape=[pair] + [floats(INNER // 2, 2 * PANEL)] * 2,
        in_specs=[HBM] * 4 + [ANY] * (ranks + len(after)),
        out_specs=[ANY, VMEM, VMEM],
        scratch_shapes=[
            vmem(ranks, slots, columns),
            vmem(INNER + slots + SUBLANES, columns),
            vmem(INNER, columns, dtype=jnp.bfloat16),
            vmem(INNER, columns, dtype=jnp.bfloat16),
            vmem(INNER, 2 * PANEL),
            flags(ranks),
            flags(2),
        ]
        + table_scratch(*tables[2].shape),
        compiler_params=PARAMS,
        cost_estimate=FREE,
        name="assemble_and_gram",
    )(*tables, *blocks, *after)


def update_shapes(steps, slots, columns):
    return [floats(INNER, 2 * PANEL)] + [floats(slots, columns)] * len(steps)


def nothing(shapes):
    return pl.pallas_call(
        idle_kernel, out_shape=shapes, out_specs=[ANY] * len(shapes), compiler_params=SMALL, name="nothing"
    )()


def apply_update(first, steps, tables, keep, away, pair, slots, *after):
    columns = pair.shape[2]
    return pl.pallas_call(
        functools.partial(update_kernel, first, steps),
        out_shape=update_shapes(steps, slots, columns),
        in_specs=[HBM] * 4 + [VMEM] * 2 + [ANY] * (1 + len(after)),
        out_specs=[ANY] * (1 + len(steps)),
        scratch_shapes=[
            vmem(INNER, INNER),
            vmem(INNER + slots + 2 * SUBLANES, columns),
            vmem(max(len(steps), 1), slots, columns),
            vmem(3 * INNER, columns, dtype=jnp.bfloat16),
            vmem(INNER, 2 * PANEL),
            flags(len(PARTS)),
            flags(len(steps) + 1),
        ]
        + table_scratch(*tables[2].shape),
        compiler_params=PARAMS,
        cost_estimate=FREE,
        name="apply_update",
    )(*tables, keep, away, pair, *after)


def touch(value, flops=0):
    return pl.pallas_call(
        idle_kernel,
        out_shape=floats(SUBLANES, 128),
        in_specs=[ANY],
        out_specs=ANY,
        compiler_params=SMALL,
        cost_estimate=pl.CostEstimate(flops=flops, bytes_accessed=0, transcendentals=0),
        name="touch",
    )(value)


def finish(tables, sources, shape, after):
    _, slots, columns = shape
    return pl.pallas_call(
        functools.partial(finish_kernel, tables[1].shape[0]),
        out_shape=[floats(INNER, columns), floats(*shape)],
        in_specs=[HBM] * 4 + [ANY] * 7,
        out_specs=[HBM] * 2,
        scratch_shapes=[
            vmem(INNER, INNER),
            vmem(INNER + slots + 2 * SUBLANES, columns),
            vmem(2, slots, columns),
            vmem(3 * INNER, columns, dtype=jnp.bfloat16),
            vmem(INNER, 2 * PANEL),
            flags(len(PARTS)),
            flags(3),
        ]
        + table_scratch(*tables[2].shape),
        compiler_params=PARAMS,
        cost_estimate=FREE,
        name="finish",
    )(*tables, *sources, after)


def place_blocks(first, owner_group, steps, blocks, shards, ranks):
    return pl.pallas_call(
        functools.partial(place_kernel, first, ranks, steps),
        out_shape=floats(*shards.shape),
        in_specs=[HBM] + [VMEM] * len(blocks) + [HBM],
        out_specs=HBM,
        scratch_shapes=[pltpu.SMEM(owner_group.shape, jnp.int32), flags(), flags(len(steps))],
        input_output_aliases={1 + len(blocks): 0},
        compiler_params=PARAMS,
        cost_estimate=FREE,
        name="place_blocks",
    )(owner_group, *blocks, shards)


def sum_halves(keep, send, axis, streams):
    size = lax.axis_size(axis)

    def exchange(piece, bits):
        return lax.ppermute(piece, axis, [(i, i ^ bits[i & 1]) for i in range(size)])

    chips = [1 << shift for shift in range(1, size.bit_length() - 1)]
    keep = keep + exchange(send, (1, 1))
    pieces = jnp.split(keep, streams, axis=0)
    for bits in zip(chips, reversed(chips)):
        pieces = [piece + exchange(piece, bits[:: 1 - 2 * index]) for index, piece in enumerate(pieces)]
    keep = jnp.concatenate(pieces, axis=0)
    return keep, exchange(keep, (1, 1))


def on_device(momentum, gradient, live_ranks, owner_group, row_counts, row_offsets):
    ranks = lax.axis_size("fsdp")
    _, slots, columns = momentum.shape
    inner = is_inner(lax.axis_index("fsdp"), ranks)
    tables = (owner_group, live_ranks, row_counts, row_offsets)
    last = [2, 1, *range(3, ranks)]
    early = [step for step in last if step != mate(ranks)]

    def pairs(step, inward):
        return [(i, i ^ step) for i in range(ranks) if is_inner(i ^ step if inward else i, ranks)]

    def to_inner(block, step):
        return lax.ppermute(block, "fsdp", pairs(step, True))

    def from_inner(block, step):
        return lax.ppermute(block, "fsdp", pairs(step, False))

    near = mate(ranks)
    far = [step for step in last if step != near]
    *blends, token = blend(True, tables, momentum, gradient, [])
    own = blends[near - 1]
    swapped = lax.ppermute(own, "fsdp", [(i, i ^ near) for i in range(ranks)])
    arrived = {step: to_inner(blends[step - 1], step) for step in far}
    *blends, token = blend(False, tables, momentum, gradient, [token, touch(swapped)])
    last_blocks = [blends[0]] + [to_inner(blends[step], step) for step in range(1, ranks)]
    new_momentum, token = fresh_momentum(tables, momentum, gradient, token)
    handed = {step: from_inner(arrived[step], near) for step in far}

    def ordered(base, opposite, others):
        return [{0: base, near: opposite, **others}[step] for step in range(ranks)]

    first_blocks = ordered(own, swapped, arrived)
    pair, keep, send = assemble_and_gram(True, True, tables, first_blocks, *[handed[step] for step in far[1:]])

    def first_update(pair, keep, send, after):
        return apply_update(True, early, tables, *sum_halves(keep, send, "tensor", 1), pair, slots, after)

    def first_skip(*_):
        return nothing(update_shapes(early, slots, columns))

    packed, *homes = lax.cond(inner, first_update, first_skip, pair, keep, send, touch(keep, 10**11))
    first_home = [from_inner(block, step) for step, block in zip(early, homes)]
    pair_shape = jax.ShapeDtypeStruct(pair.shape, pair.dtype)

    def outer_update(*blocks):
        pair, keep, send = assemble_and_gram(False, True, tables, blocks)
        return (pair, *apply_update(True, [], tables, *sum_halves(keep, send, "tensor", 1), pair, slots, keep))

    def outer_skip(*_):
        return tuple(nothing([pair_shape, *update_shapes([], slots, columns)]))

    outer_pair, outer_packed = lax.cond(inner, outer_skip, outer_update, *ordered(swapped, own, handed))

    def last_update(after, *blocks):
        pair, keep, send = assemble_and_gram(True, False, tables, blocks, after)
        return (pair, *apply_update(False, last, tables, *sum_halves(keep, send, "tensor", 2), pair, slots))

    def last_skip(*_):
        return tuple(nothing([pair_shape, *update_shapes(last, slots, columns)]))

    last_pair, last_packed, *homes = lax.cond(inner, last_update, last_skip, outer_packed, *last_blocks)
    last_home = [from_inner(block, step) for step, block in zip(last, homes)]

    sources = [packed, pair, last_packed, last_pair, outer_packed, outer_pair]
    result, shards = finish(tables, sources, momentum.shape, token)
    shards = place_blocks(True, owner_group, early, first_home, shards, ranks)
    shards = place_blocks(False, owner_group, last[:1], last_home[:1], shards, ranks)
    shards = place_blocks(False, owner_group, last[1:], last_home[1:], shards, ranks)
    return (new_momentum, shards, result[None])


def solution(mesh):
    placed = (P(None, "fsdp", "tensor"), P(None, "fsdp", "tensor"), P(), P(), P(), P())
    return jax.shard_map(
        on_device,
        mesh=mesh,
        in_specs=placed,
        out_specs=(P(None, "fsdp", "tensor"), P(None, "fsdp", "tensor"), P("fsdp", None, "tensor")),
        check_vma=False,
    )
```

```python
import functools
import math

import jax
import jax.numpy as jnp
from jax import lax
from jax.experimental import pallas as pl
from jax.experimental.pallas import tpu as pltpu
from jax.sharding import PartitionSpec as P

WIDTH = 7168
INNER = 576
PANEL = INNER // 3
TILE = 256
SUBLANES = 8

MOMENTUM_RATE = 0.95
QUINTIC_FIRST = 3.4445
QUINTIC_SECOND = -4.775
QUINTIC_THIRD = 2.0315
EPSILON = 1e-07
OUT_SCALE = 0.2 * math.sqrt(max(INNER, WIDTH))
SMALL = pltpu.CompilerParams(vmem_limit_bytes=1024 * 1024)
FULL = pltpu.CompilerParams(vmem_limit_bytes=60 * 1024 * 1024)
PARAMS = pltpu.CompilerParams(vmem_limit_bytes=24 * 1024 * 1024)
HBM = pl.BlockSpec(memory_space=pltpu.HBM)
ANY = pl.BlockSpec(memory_space=pl.ANY)
VMEM = pl.BlockSpec(memory_space=pltpu.VMEM)


def halves(value):
    high = value.astype(jnp.bfloat16)
    low = (value - high.astype(jnp.float32)).astype(jnp.bfloat16)
    return high, low


def dot(left, right, contract=((1,), (0,))):
    return lax.dot_general(left, right, (contract, ((), ())), preferred_element_type=jnp.float32)


DEPTH = INNER // TILE * TILE
PARTS = [(side, rows) for rows in ((0, DEPTH), (DEPTH, INNER)) if rows[0] < rows[1] for side in (1, 0, 0)]


def passes_left(value):
    high, low = halves(value)
    return jnp.concatenate(
        [part[:, first:last] for first, last in ((0, DEPTH), (DEPTH, INNER)) for part in (high, low, high)], axis=1
    )


def passes_right(value):
    sides = halves(value)
    return jnp.concatenate([sides[side][first:last] for side, (first, last) in PARTS], axis=0)


def is_inner(rank, ranks):
    low = ranks // 4
    return (rank >= low) & (rank < ranks - low)


def mate(ranks):
    return ranks // 4


def table_scratch(matrices, ranks):
    return [
        pltpu.SMEM((matrices,), jnp.int32),
        pltpu.SMEM((ranks,), jnp.int32),
        pltpu.SMEM((matrices, ranks), jnp.int32),
        pltpu.SMEM((matrices, ranks), jnp.int32),
        pltpu.SemaphoreType.DMA((4,)),
    ]


def table_jobs(tables, held):
    *places, arrive = held
    copies = [
        pltpu.make_async_copy(table, place, arrive.at[index])
        for index, (table, place) in enumerate(zip(tables, places))
    ]
    return copies, places


def fetch_tables(tables, held):
    copies, places = table_jobs(tables, held)
    for copy in copies:
        copy.start()
    for copy in copies:
        copy.wait()
    return places


def matrix_of(owner_group, rank):
    found = jnp.int32(0)
    for matrix in range(owner_group.shape[0]):
        found = jnp.where(owner_group[matrix] == rank, matrix, found)
    return found


def over_tiles(tiles, body, carry):
    group = next(group for group in (6, 3, 2, 1) if tiles % group == 0)

    def step(index, carry):
        for member in range(group):
            carry = body(index * group + member, carry)
        return carry

    return lax.fori_loop(0, tiles // group, step, carry)


def each_copy(copies, action):
    for condition, source, place, flag in copies:

        @pl.when(condition)
        def _(source=source, place=place, flag=flag):
            getattr(pltpu.make_async_copy(source, place, flag), action)()


def blend_kernel(first, chunks, *refs):
    tables, (momentum, gradient) = refs[:4], refs[4:6]
    ranks = tables[1].shape[0]
    *outs, token, olds, grads, arrive, leave = refs[-ranks - 10 + first : -5]
    owner_group, live_ranks, row_counts, _ = fetch_tables(tables, refs[-5:])
    rank = lax.axis_index("fsdp")
    slots, columns = outs[0].shape
    size = slots // chunks
    jobs = []
    for step in range(1, ranks + 1):
        step = step % ranks
        if first and step == 0:
            continue
        target = rank ^ step
        wanted = is_inner(target, ranks)
        matrix = matrix_of(owner_group, target ^ mate(ranks) if first else target)
        if first and step == mate(ranks):
            matrix = matrix_of(owner_group, jnp.where(wanted, rank, target))
            wanted = rank >= 0
        count = row_counts[matrix, rank] * live_ranks[rank]
        for chunk in range(chunks):
            part = pl.ds(chunk * size, size)
            flags = arrive.at[step, chunk, 0], arrive.at[step, chunk, 1]
            incoming = (
                (wanted, momentum.at[matrix, part], olds.at[step, part], flags[0]),
                (wanted, gradient.at[matrix, part], grads.at[step, part], flags[1]),
            )
            outgoing = (wanted, olds.at[step, part], outs[step - first].at[part], leave.at[step, chunk])
            jobs.append((step, chunk, count, incoming, outgoing))
            each_copy(incoming, "start")
    token[...] = jnp.zeros_like(token)
    for step, chunk, count, incoming, outgoing in jobs:

        @pl.when(incoming[0][0])
        def _(step=step, chunk=chunk, count=count, incoming=incoming, outgoing=outgoing):
            for _, source, place, flag in incoming:
                pltpu.make_async_copy(source, place, flag).wait()
            sublane = lax.broadcasted_iota(jnp.int32, (SUBLANES, columns), 0)

            def tile(index, carry):
                first_row = chunk * size + index * SUBLANES
                rows = pl.ds(pl.multiple_of(first_row, SUBLANES), SUBLANES)
                grad_now = grads[step, rows, :]
                fresh = MOMENTUM_RATE * olds[step, rows, :] + grad_now
                olds[step, rows, :] = jnp.where(sublane < count - first_row, grad_now + MOMENTUM_RATE * fresh, 0.0)
                return carry

            over_tiles(size // SUBLANES, tile, 0)
            pltpu.make_async_copy(*outgoing[1:]).start()

    each_copy([job[-1] for job in jobs], "wait")


def fresh_kernel(live_ranks, row_counts, momentum, gradient, _, out, token):
    token[...] = jnp.zeros_like(token)
    rank, matrix = lax.axis_index("fsdp"), pl.program_id(0)
    slots, columns = out.shape
    count = row_counts[matrix, rank] * live_ranks[rank]
    sublane = lax.broadcasted_iota(jnp.int32, (SUBLANES, columns), 0)

    def tile(index, carry):
        rows = pl.ds(pl.multiple_of(index * SUBLANES, SUBLANES), SUBLANES)
        fresh = MOMENTUM_RATE * momentum[rows, :] + gradient[rows, :]
        out[rows, :] = jnp.where(sublane < count - index * SUBLANES, fresh, 0.0)
        return carry

    over_tiles(slots // SUBLANES, tile, 0)


def assemble(blocks, landed, padded, arrive, tables, held, first):
    ranks, slots, columns = landed.shape
    copies = []
    for step in range(ranks):
        copies.append(pltpu.make_async_copy(blocks[step], landed.at[step], arrive.at[step]))
        copies[-1].start()
    owner_group, _, _, row_offsets = fetch_tables(tables, held)
    rank = lax.axis_index("fsdp")
    base = jnp.where(is_inner(rank, ranks), rank, rank ^ mate(ranks))
    matrix = matrix_of(owner_group, base ^ mate(ranks) if first else base)
    padded[...] = jnp.zeros_like(padded)
    sublane = lax.broadcasted_iota(jnp.int32, (SUBLANES, columns), 0)
    for step in range(ranks):
        start = row_offsets[matrix, base ^ step]
        shift = start % SUBLANES
        origin = start - shift
        copies[step].wait()

        def tile(index, before, origin=origin, shift=shift, step=step):
            moved = pltpu.roll(landed[step, pl.ds(pl.multiple_of(index * SUBLANES, SUBLANES), SUBLANES), :], shift, 0)
            rows = pl.ds(pl.multiple_of(origin + index * SUBLANES, SUBLANES), SUBLANES)
            padded[rows, :] = padded[rows, :] + jnp.where(sublane < shift, before, moved)
            return moved

        after = over_tiles(slots // SUBLANES, tile, jnp.zeros((SUBLANES, columns), jnp.float32))
        rows = pl.ds(pl.multiple_of(origin + slots, SUBLANES), SUBLANES)
        padded[rows, :] = padded[rows, :] + jnp.where(sublane < shift, after, 0.0)


def gram_kernel(inner, first, ranks, *refs):
    pair, keep, send = refs[-15:-12]
    landed, padded, high_held, low_held, gram, arrive, leave = refs[-12:-5]

    @pl.when(is_inner(lax.axis_index("fsdp"), ranks) == inner)
    def _():
        assemble(refs[4 : 4 + ranks], landed, padded, arrive, refs[:4], refs[-5:], first)
        high, low = halves(padded[:INNER, :])
        high_held[...] = high
        low_held[...] = low
        outgoing = [
            pltpu.make_async_copy(high_held, pair.at[0], leave.at[0]),
            pltpu.make_async_copy(low_held, pair.at[1], leave.at[1]),
        ]
        for copy in outgoing:
            copy.start()
        left = jnp.concatenate([high, low, high], axis=1)
        right = jnp.concatenate([low, high, high], axis=1)
        for panel in range(3):
            here = slice(panel * PANEL, (panel + 1) * PANEL)
            store_panel(gram, panel, dot(left[panel * PANEL :], right[here], ((1,), (1,))))
        mine, other = core_rows()
        keep[...] = gram[mine, :]
        send[...] = gram[other, :]
        for copy in outgoing:
            copy.wait()


def core_rows():
    half = INNER // 2
    first = (lax.axis_index("tensor") & 1) * half
    return tuple(pl.ds(pl.multiple_of(start, SUBLANES), half) for start in (first, half - first))


def store_panel(packed, panel, part):
    if panel == 0:
        packed[:, :PANEL] = part
    elif panel == 1:
        packed[: 2 * PANEL, PANEL:] = part
    else:
        packed[2 * PANEL :, PANEL:] = part


def unpack(packed, gram):
    gram[:, :PANEL] = packed[:, :PANEL]
    gram[PANEL:, PANEL : 2 * PANEL] = packed[: 2 * PANEL, PANEL:]
    gram[2 * PANEL :, 2 * PANEL :] = packed[2 * PANEL :, PANEL:]
    gram[:PANEL, PANEL:] = packed[PANEL:, :PANEL].T
    gram[PANEL : 2 * PANEL, 2 * PANEL :] = packed[PANEL : 2 * PANEL, PANEL:].T
    return gram[...]


def symmetric_product(left, right, out):
    for begin in range(0, INNER, TILE):
        end = min(begin + TILE, INNER)
        part = dot(left[begin:], right[:, begin:end])
        out[begin:, begin:end] = part
        if end < INNER:
            out[begin:end, end:] = part[end - begin :].T
    return out[...]


def polynomial(raw, gram):
    diagonal = lax.broadcasted_iota(jnp.int32, raw.shape, 0) == lax.broadcasted_iota(jnp.int32, raw.shape, 1)
    square_total = jnp.sum(jnp.where(diagonal, raw, 0.0))
    norm = jnp.sqrt(jnp.full((1, 1), square_total, jnp.float32)) + EPSILON
    inverse = 1.0 / norm
    first = (raw * inverse) * inverse
    first_right = passes_right(first)
    second = symmetric_product(passes_left(first), first_right, gram)
    base = QUINTIC_SECOND * first + QUINTIC_THIRD * second + jnp.where(diagonal, QUINTIC_FIRST, 0.0)
    base_left = passes_left(base)
    third = symmetric_product(base_left, first_right, gram)
    next_gram = symmetric_product(base_left, passes_right(third), gram)
    square = symmetric_product(passes_left(next_gram), passes_right(next_gram), gram)
    outer = QUINTIC_SECOND * next_gram + QUINTIC_THIRD * square + jnp.where(diagonal, QUINTIC_FIRST, 0.0)
    return symmetric_product(passes_left(outer), passes_right(base), gram) * (inverse * OUT_SCALE)


def extract(padded, start, count, staged, step):
    _, slots, columns = staged.shape
    sublane = lax.broadcasted_iota(jnp.int32, (SUBLANES, columns), 0)
    shift = start % SUBLANES
    base = start - shift
    back = jnp.where(shift == 0, 0, SUBLANES - shift)

    def window(index):
        rows = pl.ds(pl.multiple_of(base + index * SUBLANES, SUBLANES), SUBLANES)
        return pltpu.roll(padded[rows, :], back, 0)

    def tile(index, here):
        after = window(index + 1)
        moved = jnp.where(sublane < SUBLANES - shift, here, after)
        rows = pl.ds(pl.multiple_of(index * SUBLANES, SUBLANES), SUBLANES)
        staged[step, rows, :] = jnp.where(sublane < count - index * SUBLANES, moved, 0.0)
        return after

    over_tiles(slots // SUBLANES, tile, window(0))


def stack_jobs(pair, stacked, arrive):
    jobs, begin = [], 0
    for index, (side, (first_row, last_row)) in enumerate(PARTS):
        size = last_row - first_row
        source = pair.at[side, pl.ds(first_row, size)]
        jobs.append((source, stacked.at[pl.ds(begin, size)], arrive.at[index]))
        begin += size
    return jobs


def update_kernel(first, steps, *refs):
    tables, (keep, away, pair) = refs[:4], refs[4:7]
    gram, padded, staged, stacked, held, arrive, leave = refs[-12:-5]
    whole, *homes = refs[-13 - len(steps) : -12]
    ranks = tables[1].shape[0]
    rank = lax.axis_index("fsdp")
    incoming = [pltpu.make_async_copy(*job) for job in stack_jobs(pair, stacked, arrive)] if steps else []
    for copy in incoming:
        copy.start()
    table_copies, places = table_jobs(tables, refs[-5:])
    for copy in table_copies:
        copy.start()
    mine, other = core_rows()
    held[mine, :] = keep[...]
    held[other, :] = away[...]
    total = polynomial(unpack(held, gram), gram)
    for panel in range(3):
        store_panel(held, panel, total[panel * PANEL :, panel * PANEL : (panel + 1) * PANEL])
    copies = [pltpu.make_async_copy(held, whole, leave.at[len(steps)])]
    copies[0].start()
    for copy in [*incoming, *table_copies]:
        copy.wait()
    if steps:
        padded[:INNER, :] = dot(passes_left(total), stacked[...])
    owner_group, live_ranks, row_counts, row_offsets = places
    matrix = matrix_of(owner_group, rank ^ mate(ranks) if first else rank)
    for index, step in enumerate(steps):
        target = rank ^ step
        count = row_counts[matrix, target] * live_ranks[target]
        extract(padded, row_offsets[matrix, target], count, staged, index)
        copies.append(pltpu.make_async_copy(staged.at[index], homes[index], leave.at[index]))
        copies[-1].start()
    for copy in copies:
        copy.wait()


def finish_kernel(ranks, *refs):
    tables, sources = refs[:4], refs[4:10]
    (result, shards, gram, padded, staged, stacked, held, arrive, leave), refs = refs[11:20], refs[20:]
    rank = lax.axis_index("fsdp")
    owner_group, live_ranks, row_counts, row_offsets = fetch_tables(tables, refs)

    inner = is_inner(rank, ranks)
    outer = jnp.logical_not(inner)

    def make(index, carry):
        wanted = [jnp.logical_and(inner, index == 1), jnp.logical_and(inner, index == 0), outer]
        incoming = []
        for condition, packed, pair in zip(wanted, sources[::2], sources[1::2]):
            incoming.append((condition, packed, held, leave.at[2]))
            incoming += [(condition, *job) for job in stack_jobs(pair, stacked, arrive)]
        each_copy(incoming, "start")
        each_copy(incoming, "wait")
        padded[:INNER, :] = dot(passes_left(unpack(held, gram)), stacked[...])
        matrix = matrix_of(owner_group, rank ^ (index * mate(ranks)))
        extract(padded, row_offsets[matrix, rank], row_counts[matrix, rank] * live_ranks[rank], staged, 0)
        outgoing = [
            (index >= 0, staged.at[0], shards.at[matrix], leave.at[0]),
            (index == 0, padded.at[pl.ds(0, INNER)], result, leave.at[1]),
        ]
        each_copy(outgoing, "start")
        each_copy(outgoing, "wait")
        return carry

    lax.fori_loop(0, jnp.where(inner, 2, 1), make, 0)


def place_kernel(first, ranks, steps, *refs):
    table, blocks, shards = refs[0], refs[1 : 1 + len(steps)], refs[2 + len(steps)]
    owner_group, arrive, leave = refs[3 + len(steps) :]
    rank = lax.axis_index("fsdp")
    fetch = pltpu.make_async_copy(table, owner_group, arrive)
    fetch.start()
    fetch.wait()
    copies = []
    for index, step in enumerate(steps):
        source = rank ^ step
        matrix = matrix_of(owner_group, source ^ mate(ranks) if first else source)
        copies.append((is_inner(source, ranks), blocks[index], shards.at[matrix], leave.at[index]))
    each_copy(copies, "start")
    each_copy(copies, "wait")


def idle_kernel(*refs):
    pass


def floats(*shape):
    return jax.ShapeDtypeStruct(shape, jnp.float32)


def vmem(*shape, dtype=jnp.float32):
    return pltpu.VMEM(shape, dtype)


def flags(*shape):
    return pltpu.SemaphoreType.DMA(shape)


FREE = pl.CostEstimate(flops=0, bytes_accessed=0, transcendentals=0)


def blend(first, tables, momentum, gradient, before):
    _, slots, columns = momentum.shape
    ranks = tables[1].shape[0]
    chunks = 1
    return pl.pallas_call(
        functools.partial(blend_kernel, first, chunks),
        out_shape=[floats(slots, columns)] * (ranks - first) + [floats(SUBLANES, 128)],
        in_specs=[HBM] * 6 + [ANY] * len(before),
        out_specs=[ANY] * (ranks - first) + [VMEM],
        scratch_shapes=[vmem(ranks, slots, columns)] * 2
        + [flags(ranks, chunks, 2), flags(ranks, chunks)]
        + table_scratch(*tables[2].shape),
        compiler_params=FULL,
        cost_estimate=FREE,
        name="blend",
    )(*tables, momentum, gradient, *before)


def fresh_momentum(tables, momentum, gradient, before):
    matrices, slots, columns = momentum.shape
    block = pl.BlockSpec((None, slots, columns), lambda matrix: (matrix, 0, 0))
    return pl.pallas_call(
        fresh_kernel,
        grid=(matrices,),
        out_shape=[floats(*momentum.shape), floats(SUBLANES, 128)],
        in_specs=[pl.BlockSpec(memory_space=pltpu.SMEM)] * 2 + [block] * 2 + [ANY],
        out_specs=[block, pl.BlockSpec((SUBLANES, 128), lambda matrix: (0, 0))],
        compiler_params=FULL,
        cost_estimate=FREE,
        name="fresh_momentum",
    )(*tables[1:3], momentum, gradient, before)


def assemble_and_gram(inner, first, tables, blocks, *after):
    slots, columns = blocks[0].shape
    ranks = len(blocks)
    pair = jax.ShapeDtypeStruct((4, INNER, columns), jnp.bfloat16)
    return pl.pallas_call(
        functools.partial(gram_kernel, inner, first, ranks),
        out_shape=[pair] + [floats(INNER // 2, 2 * PANEL)] * 2,
        in_specs=[HBM] * 4 + [ANY] * (ranks + len(after)),
        out_specs=[ANY, VMEM, VMEM],
        scratch_shapes=[
            vmem(ranks, slots, columns),
            vmem(INNER + slots + SUBLANES, columns),
            vmem(INNER, columns, dtype=jnp.bfloat16),
            vmem(INNER, columns, dtype=jnp.bfloat16),
            vmem(INNER, 2 * PANEL),
            flags(ranks),
            flags(2),
        ]
        + table_scratch(*tables[2].shape),
        compiler_params=PARAMS,
        cost_estimate=FREE,
        name="assemble_and_gram",
    )(*tables, *blocks, *after)


def update_shapes(steps, slots, columns):
    return [floats(INNER, 2 * PANEL)] + [floats(slots, columns)] * len(steps)


def nothing(shapes):
    return pl.pallas_call(
        idle_kernel, out_shape=shapes, out_specs=[ANY] * len(shapes), compiler_params=SMALL, name="nothing"
    )()


def apply_update(first, steps, tables, keep, away, pair, slots, *after):
    columns = pair.shape[2]
    return pl.pallas_call(
        functools.partial(update_kernel, first, steps),
        out_shape=update_shapes(steps, slots, columns),
        in_specs=[HBM] * 4 + [VMEM] * 2 + [ANY] * (1 + len(after)),
        out_specs=[ANY] * (1 + len(steps)),
        scratch_shapes=[
            vmem(INNER, INNER),
            vmem(INNER + slots + 2 * SUBLANES, columns),
            vmem(max(len(steps), 1), slots, columns),
            vmem(3 * INNER, columns, dtype=jnp.bfloat16),
            vmem(INNER, 2 * PANEL),
            flags(len(PARTS)),
            flags(len(steps) + 1),
        ]
        + table_scratch(*tables[2].shape),
        compiler_params=PARAMS,
        cost_estimate=FREE,
        name="apply_update",
    )(*tables, keep, away, pair, *after)


def touch(value, flops=0):
    return pl.pallas_call(
        idle_kernel,
        out_shape=floats(SUBLANES, 128),
        in_specs=[ANY],
        out_specs=ANY,
        compiler_params=SMALL,
        cost_estimate=pl.CostEstimate(flops=flops, bytes_accessed=0, transcendentals=0),
        name="touch",
    )(value)


def finish(tables, sources, shape, after):
    _, slots, columns = shape
    return pl.pallas_call(
        functools.partial(finish_kernel, tables[1].shape[0]),
        out_shape=[floats(INNER, columns), floats(*shape)],
        in_specs=[HBM] * 4 + [ANY] * 7,
        out_specs=[HBM] * 2,
        scratch_shapes=[
            vmem(INNER, INNER),
            vmem(INNER + slots + 2 * SUBLANES, columns),
            vmem(2, slots, columns),
            vmem(3 * INNER, columns, dtype=jnp.bfloat16),
            vmem(INNER, 2 * PANEL),
            flags(len(PARTS)),
            flags(3),
        ]
        + table_scratch(*tables[2].shape),
        compiler_params=PARAMS,
        cost_estimate=FREE,
        name="finish",
    )(*tables, *sources, after)


def place_blocks(first, owner_group, steps, blocks, shards, ranks):
    return pl.pallas_call(
        functools.partial(place_kernel, first, ranks, steps),
        out_shape=floats(*shards.shape),
        in_specs=[HBM] + [VMEM] * len(blocks) + [HBM],
        out_specs=HBM,
        scratch_shapes=[pltpu.SMEM(owner_group.shape, jnp.int32), flags(), flags(len(steps))],
        input_output_aliases={1 + len(blocks): 0},
        compiler_params=PARAMS,
        cost_estimate=FREE,
        name="place_blocks",
    )(owner_group, *blocks, shards)


def sum_halves(keep, send, axis, streams):
    size = lax.axis_size(axis)

    def exchange(piece, bits):
        return lax.ppermute(piece, axis, [(i, i ^ bits[i & 1]) for i in range(size)])

    chips = [1 << shift for shift in range(1, size.bit_length() - 1)]
    keep = keep + exchange(send, (1, 1))
    pieces = jnp.split(keep, streams, axis=0)
    for bits in zip(chips, reversed(chips)):
        pieces = [piece + exchange(piece, bits[:: 1 - 2 * index]) for index, piece in enumerate(pieces)]
    keep = jnp.concatenate(pieces, axis=0)
    return keep, exchange(keep, (1, 1))


def on_device(momentum, gradient, live_ranks, owner_group, row_counts, row_offsets):
    ranks = lax.axis_size("fsdp")
    _, slots, columns = momentum.shape
    inner = is_inner(lax.axis_index("fsdp"), ranks)
    tables = (owner_group, live_ranks, row_counts, row_offsets)
    last = [2, 1, *range(3, ranks)]
    early = [step for step in last if step != mate(ranks)]

    def pairs(step, inward):
        return [(i, i ^ step) for i in range(ranks) if is_inner(i ^ step if inward else i, ranks)]

    def to_inner(block, step):
        return lax.ppermute(block, "fsdp", pairs(step, True))

    def from_inner(block, step):
        return lax.ppermute(block, "fsdp", pairs(step, False))

    near = mate(ranks)
    far = [step for step in last if step != near]
    *blends, token = blend(True, tables, momentum, gradient, [])
    own = blends[near - 1]
    swapped = lax.ppermute(own, "fsdp", [(i, i ^ near) for i in range(ranks)])
    arrived = {step: to_inner(blends[step - 1], step) for step in far}
    *blends, token = blend(False, tables, momentum, gradient, [token, touch(swapped)])
    last_blocks = [blends[0]] + [to_inner(blends[step], step) for step in range(1, ranks)]
    new_momentum, token = fresh_momentum(tables, momentum, gradient, token)
    handed = {step: from_inner(arrived[step], near) for step in far}

    def ordered(base, opposite, others):
        return [{0: base, near: opposite, **others}[step] for step in range(ranks)]

    first_blocks = ordered(own, swapped, arrived)
    pair, keep, send = assemble_and_gram(True, True, tables, first_blocks, *[handed[step] for step in far[1:]])

    def first_update(pair, keep, send, after):
        return apply_update(True, early, tables, *sum_halves(keep, send, "tensor", 1), pair, slots, after)

    def first_skip(*_):
        return nothing(update_shapes(early, slots, columns))

    packed, *homes = lax.cond(inner, first_update, first_skip, pair, keep, send, touch(keep, 10**11))
    first_home = [from_inner(block, step) for step, block in zip(early, homes)]
    pair_shape = jax.ShapeDtypeStruct(pair.shape, pair.dtype)

    def outer_update(*blocks):
        pair, keep, send = assemble_and_gram(False, True, tables, blocks)
        return (pair, *apply_update(True, [], tables, *sum_halves(keep, send, "tensor", 1), pair, slots, keep))

    def outer_skip(*_):
        return tuple(nothing([pair_shape, *update_shapes([], slots, columns)]))

    outer_pair, outer_packed = lax.cond(inner, outer_skip, outer_update, *ordered(swapped, own, handed))

    def last_update(after, *blocks):
        pair, keep, send = assemble_and_gram(True, False, tables, blocks, after)
        return (pair, *apply_update(False, last, tables, *sum_halves(keep, send, "tensor", 2), pair, slots))

    def last_skip(*_):
        return tuple(nothing([pair_shape, *update_shapes(last, slots, columns)]))

    last_pair, last_packed, *homes = lax.cond(inner, last_update, last_skip, outer_packed, *last_blocks)
    last_home = [from_inner(block, step) for step, block in zip(last, homes)]

    sources = [packed, pair, last_packed, last_pair, outer_packed, outer_pair]
    result, shards = finish(tables, sources, momentum.shape, token)
    shards = place_blocks(True, owner_group, early, first_home, shards, ranks)
    for step, block in sorted(zip(last, last_home), key=lambda home: (home[0] == near, last.index(home[0]))):
        shards = place_blocks(False, owner_group, [step], [block], shards, ranks)
    return (new_momentum, shards, result[None])


def solution(mesh):
    placed = (P(None, "fsdp", "tensor"), P(None, "fsdp", "tensor"), P(), P(), P(), P())
    return jax.shard_map(
        on_device,
        mesh=mesh,
        in_specs=placed,
        out_specs=(P(None, "fsdp", "tensor"), P(None, "fsdp", "tensor"), P("fsdp", None, "tensor")),
        check_vma=False,
    )
```

```python
import functools
import math

import jax
import jax.numpy as jnp
from jax import lax
from jax.experimental import pallas as pl
from jax.experimental.pallas import tpu as pltpu
from jax.sharding import PartitionSpec as P

WIDTH = 7168
INNER = 576
PANEL = INNER // 3
TILE = 256
SUBLANES = 8

MOMENTUM_RATE = 0.95
QUINTIC_FIRST = 3.4445
QUINTIC_SECOND = -4.775
QUINTIC_THIRD = 2.0315
EPSILON = 1e-07
OUT_SCALE = 0.2 * math.sqrt(max(INNER, WIDTH))
SMALL = pltpu.CompilerParams(vmem_limit_bytes=1024 * 1024)
FULL = pltpu.CompilerParams(vmem_limit_bytes=60 * 1024 * 1024)
PARAMS = pltpu.CompilerParams(vmem_limit_bytes=24 * 1024 * 1024)
HBM = pl.BlockSpec(memory_space=pltpu.HBM)
ANY = pl.BlockSpec(memory_space=pl.ANY)
VMEM = pl.BlockSpec(memory_space=pltpu.VMEM)


def halves(value):
    high = value.astype(jnp.bfloat16)
    low = (value - high.astype(jnp.float32)).astype(jnp.bfloat16)
    return high, low


def dot(left, right, contract=((1,), (0,))):
    return lax.dot_general(left, right, (contract, ((), ())), preferred_element_type=jnp.float32)


DEPTH = INNER // TILE * TILE
PARTS = [(side, rows) for rows in ((0, DEPTH), (DEPTH, INNER)) if rows[0] < rows[1] for side in (1, 0, 0)]


def passes_left(value):
    high, low = halves(value)
    return jnp.concatenate(
        [part[:, first:last] for first, last in ((0, DEPTH), (DEPTH, INNER)) for part in (high, low, high)], axis=1
    )


def passes_right(value):
    sides = halves(value)
    return jnp.concatenate([sides[side][first:last] for side, (first, last) in PARTS], axis=0)


def is_inner(rank, ranks):
    low = ranks // 4
    return (rank >= low) & (rank < ranks - low)


def mate(ranks):
    return ranks // 4


def table_scratch(matrices, ranks):
    return [
        pltpu.SMEM((matrices,), jnp.int32),
        pltpu.SMEM((ranks,), jnp.int32),
        pltpu.SMEM((matrices, ranks), jnp.int32),
        pltpu.SMEM((matrices, ranks), jnp.int32),
        pltpu.SemaphoreType.DMA((4,)),
    ]


def table_jobs(tables, held):
    *places, arrive = held
    copies = [
        pltpu.make_async_copy(table, place, arrive.at[index])
        for index, (table, place) in enumerate(zip(tables, places))
    ]
    return copies, places


def fetch_tables(tables, held):
    copies, places = table_jobs(tables, held)
    for copy in copies:
        copy.start()
    for copy in copies:
        copy.wait()
    return places


def matrix_of(owner_group, rank):
    found = jnp.int32(0)
    for matrix in range(owner_group.shape[0]):
        found = jnp.where(owner_group[matrix] == rank, matrix, found)
    return found


def over_tiles(tiles, body, carry):
    group = next(group for group in (6, 3, 2, 1) if tiles % group == 0)

    def step(index, carry):
        for member in range(group):
            carry = body(index * group + member, carry)
        return carry

    return lax.fori_loop(0, tiles // group, step, carry)


def each_copy(copies, action):
    for condition, source, place, flag in copies:

        @pl.when(condition)
        def _(source=source, place=place, flag=flag):
            getattr(pltpu.make_async_copy(source, place, flag), action)()


def blend_kernel(first, chunks, *refs):
    tables, (momentum, gradient) = refs[:4], refs[4:6]
    ranks = tables[1].shape[0]
    *outs, token, olds, grads, arrive, leave = refs[-ranks - 10 + first : -5]
    owner_group, live_ranks, row_counts, _ = fetch_tables(tables, refs[-5:])
    rank = lax.axis_index("fsdp")
    slots, columns = outs[0].shape
    size = slots // chunks
    jobs = []
    for step in range(1, ranks + 1):
        step = step % ranks
        if first and step == 0:
            continue
        target = rank ^ step
        wanted = is_inner(target, ranks)
        matrix = matrix_of(owner_group, target ^ mate(ranks) if first else target)
        if first and step == mate(ranks):
            matrix = matrix_of(owner_group, jnp.where(wanted, rank, target))
            wanted = rank >= 0
        count = row_counts[matrix, rank] * live_ranks[rank]
        for chunk in range(chunks):
            part = pl.ds(chunk * size, size)
            flags = arrive.at[step, chunk, 0], arrive.at[step, chunk, 1]
            incoming = (
                (wanted, momentum.at[matrix, part], olds.at[step, part], flags[0]),
                (wanted, gradient.at[matrix, part], grads.at[step, part], flags[1]),
            )
            outgoing = (wanted, olds.at[step, part], outs[step - first].at[part], leave.at[step, chunk])
            jobs.append((step, chunk, count, incoming, outgoing))
            each_copy(incoming, "start")
    token[...] = jnp.zeros_like(token)
    for step, chunk, count, incoming, outgoing in jobs:

        @pl.when(incoming[0][0])
        def _(step=step, chunk=chunk, count=count, incoming=incoming, outgoing=outgoing):
            for _, source, place, flag in incoming:
                pltpu.make_async_copy(source, place, flag).wait()
            sublane = lax.broadcasted_iota(jnp.int32, (SUBLANES, columns), 0)

            def tile(index, carry):
                first_row = chunk * size + index * SUBLANES
                rows = pl.ds(pl.multiple_of(first_row, SUBLANES), SUBLANES)
                grad_now = grads[step, rows, :]
                fresh = MOMENTUM_RATE * olds[step, rows, :] + grad_now
                olds[step, rows, :] = jnp.where(sublane < count - first_row, grad_now + MOMENTUM_RATE * fresh, 0.0)
                return carry

            over_tiles(size // SUBLANES, tile, 0)
            pltpu.make_async_copy(*outgoing[1:]).start()

    each_copy([job[-1] for job in jobs], "wait")


def fresh_kernel(live_ranks, row_counts, momentum, gradient, _, out, token):
    token[...] = jnp.zeros_like(token)
    rank, matrix = lax.axis_index("fsdp"), pl.program_id(0)
    slots, columns = out.shape
    count = row_counts[matrix, rank] * live_ranks[rank]
    sublane = lax.broadcasted_iota(jnp.int32, (SUBLANES, columns), 0)

    def tile(index, carry):
        rows = pl.ds(pl.multiple_of(index * SUBLANES, SUBLANES), SUBLANES)
        fresh = MOMENTUM_RATE * momentum[rows, :] + gradient[rows, :]
        out[rows, :] = jnp.where(sublane < count - index * SUBLANES, fresh, 0.0)
        return carry

    over_tiles(slots // SUBLANES, tile, 0)


def assemble(blocks, landed, padded, arrive, tables, held, first):
    ranks, slots, columns = landed.shape
    copies = []
    for step in range(ranks):
        copies.append(pltpu.make_async_copy(blocks[step], landed.at[step], arrive.at[step]))
        copies[-1].start()
    table_copies, (owner_group, _, _, row_offsets) = table_jobs(tables, held)
    for copy in table_copies:
        copy.start()
    padded[...] = jnp.zeros_like(padded)
    for copy in table_copies:
        copy.wait()
    rank = lax.axis_index("fsdp")
    base = jnp.where(is_inner(rank, ranks), rank, rank ^ mate(ranks))
    matrix = matrix_of(owner_group, base ^ mate(ranks) if first else base)
    sublane = lax.broadcasted_iota(jnp.int32, (SUBLANES, columns), 0)
    for step in range(ranks):
        start = row_offsets[matrix, base ^ step]
        shift = start % SUBLANES
        origin = start - shift
        copies[step].wait()

        def tile(index, before, origin=origin, shift=shift, step=step):
            moved = pltpu.roll(landed[step, pl.ds(pl.multiple_of(index * SUBLANES, SUBLANES), SUBLANES), :], shift, 0)
            rows = pl.ds(pl.multiple_of(origin + index * SUBLANES, SUBLANES), SUBLANES)
            padded[rows, :] = padded[rows, :] + jnp.where(sublane < shift, before, moved)
            return moved

        after = over_tiles(slots // SUBLANES, tile, jnp.zeros((SUBLANES, columns), jnp.float32))
        rows = pl.ds(pl.multiple_of(origin + slots, SUBLANES), SUBLANES)
        padded[rows, :] = padded[rows, :] + jnp.where(sublane < shift, after, 0.0)


def gram_kernel(inner, first, ranks, *refs):
    pair, keep, send = refs[-15:-12]
    landed, padded, high_held, low_held, gram, arrive, leave = refs[-12:-5]

    @pl.when(is_inner(lax.axis_index("fsdp"), ranks) == inner)
    def _():
        assemble(refs[4 : 4 + ranks], landed, padded, arrive, refs[:4], refs[-5:], first)
        high, low = halves(padded[:INNER, :])
        high_held[...] = high
        low_held[...] = low
        outgoing = [
            pltpu.make_async_copy(high_held, pair.at[0], leave.at[0]),
            pltpu.make_async_copy(low_held, pair.at[1], leave.at[1]),
        ]
        for copy in outgoing:
            copy.start()
        left = jnp.concatenate([high, low, high], axis=1)
        right = jnp.concatenate([low, high, high], axis=1)
        for panel in range(3):
            here = slice(panel * PANEL, (panel + 1) * PANEL)
            store_panel(gram, panel, dot(left[panel * PANEL :], right[here], ((1,), (1,))))
        mine, other = core_rows()
        keep[...] = gram[mine, :]
        send[...] = gram[other, :]
        for copy in outgoing:
            copy.wait()


def core_rows():
    half = INNER // 2
    first = (lax.axis_index("tensor") & 1) * half
    return tuple(pl.ds(pl.multiple_of(start, SUBLANES), half) for start in (first, half - first))


def store_panel(packed, panel, part):
    if panel == 0:
        packed[:, :PANEL] = part
    elif panel == 1:
        packed[: 2 * PANEL, PANEL:] = part
    else:
        packed[2 * PANEL :, PANEL:] = part


def unpack(packed, gram):
    gram[:, :PANEL] = packed[:, :PANEL]
    gram[PANEL:, PANEL : 2 * PANEL] = packed[: 2 * PANEL, PANEL:]
    gram[2 * PANEL :, 2 * PANEL :] = packed[2 * PANEL :, PANEL:]
    gram[:PANEL, PANEL:] = packed[PANEL:, :PANEL].T
    gram[PANEL : 2 * PANEL, 2 * PANEL :] = packed[PANEL : 2 * PANEL, PANEL:].T
    return gram[...]


def symmetric_product(left, right, out):
    for begin in range(0, INNER, TILE):
        end = min(begin + TILE, INNER)
        part = dot(left[begin:], right[:, begin:end])
        out[begin:, begin:end] = part
        if end < INNER:
            out[begin:end, end:] = part[end - begin :].T
    return out[...]


def polynomial(raw, gram):
    diagonal = lax.broadcasted_iota(jnp.int32, raw.shape, 0) == lax.broadcasted_iota(jnp.int32, raw.shape, 1)
    square_total = jnp.sum(jnp.where(diagonal, raw, 0.0))
    norm = jnp.sqrt(jnp.full((1, 1), square_total, jnp.float32)) + EPSILON
    inverse = 1.0 / norm
    first = (raw * inverse) * inverse
    first_right = passes_right(first)
    second = symmetric_product(passes_left(first), first_right, gram)
    base = QUINTIC_SECOND * first + QUINTIC_THIRD * second + jnp.where(diagonal, QUINTIC_FIRST, 0.0)
    base_left = passes_left(base)
    third = symmetric_product(base_left, first_right, gram)
    next_gram = symmetric_product(base_left, passes_right(third), gram)
    square = symmetric_product(passes_left(next_gram), passes_right(next_gram), gram)
    outer = QUINTIC_SECOND * next_gram + QUINTIC_THIRD * square + jnp.where(diagonal, QUINTIC_FIRST, 0.0)
    return symmetric_product(passes_left(outer), passes_right(base), gram) * (inverse * OUT_SCALE)


def extract(padded, start, count, staged, step):
    _, slots, columns = staged.shape
    sublane = lax.broadcasted_iota(jnp.int32, (SUBLANES, columns), 0)
    shift = start % SUBLANES
    base = start - shift
    back = jnp.where(shift == 0, 0, SUBLANES - shift)

    def window(index):
        rows = pl.ds(pl.multiple_of(base + index * SUBLANES, SUBLANES), SUBLANES)
        return pltpu.roll(padded[rows, :], back, 0)

    def tile(index, here):
        after = window(index + 1)
        moved = jnp.where(sublane < SUBLANES - shift, here, after)
        rows = pl.ds(pl.multiple_of(index * SUBLANES, SUBLANES), SUBLANES)
        staged[step, rows, :] = jnp.where(sublane < count - index * SUBLANES, moved, 0.0)
        return after

    over_tiles(slots // SUBLANES, tile, window(0))


def stack_jobs(pair, stacked, arrive):
    jobs, begin = [], 0
    for index, (side, (first_row, last_row)) in enumerate(PARTS):
        size = last_row - first_row
        source = pair.at[side, pl.ds(first_row, size)]
        jobs.append((source, stacked.at[pl.ds(begin, size)], arrive.at[index]))
        begin += size
    return jobs


def update_kernel(first, steps, *refs):
    tables, (keep, away, pair) = refs[:4], refs[4:7]
    gram, padded, staged, stacked, held, arrive, leave = refs[-12:-5]
    whole, *homes = refs[-13 - len(steps) : -12]
    ranks = tables[1].shape[0]
    rank = lax.axis_index("fsdp")
    incoming = [pltpu.make_async_copy(*job) for job in stack_jobs(pair, stacked, arrive)] if steps else []
    for copy in incoming:
        copy.start()
    table_copies, places = table_jobs(tables, refs[-5:])
    for copy in table_copies:
        copy.start()
    mine, other = core_rows()
    held[mine, :] = keep[...]
    held[other, :] = away[...]
    total = polynomial(unpack(held, gram), gram)
    for panel in range(3):
        store_panel(held, panel, total[panel * PANEL :, panel * PANEL : (panel + 1) * PANEL])
    copies = [pltpu.make_async_copy(held, whole, leave.at[len(steps)])]
    copies[0].start()
    for copy in [*incoming, *table_copies]:
        copy.wait()
    if steps:
        padded[:INNER, :] = dot(passes_left(total), stacked[...])
    owner_group, live_ranks, row_counts, row_offsets = places
    matrix = matrix_of(owner_group, rank ^ mate(ranks) if first else rank)
    for index, step in enumerate(steps):
        target = rank ^ step
        count = row_counts[matrix, target] * live_ranks[target]
        extract(padded, row_offsets[matrix, target], count, staged, index)
        copies.append(pltpu.make_async_copy(staged.at[index], homes[index], leave.at[index]))
        copies[-1].start()
    for copy in copies:
        copy.wait()


def finish_kernel(ranks, *refs):
    tables, sources = refs[:4], refs[4:10]
    (result, shards, gram, padded, staged, stacked, held, arrive, leave), refs = refs[11:20], refs[20:]
    rank = lax.axis_index("fsdp")
    owner_group, live_ranks, row_counts, row_offsets = fetch_tables(tables, refs)

    inner = is_inner(rank, ranks)
    outer = jnp.logical_not(inner)

    def make(index, carry):
        wanted = [jnp.logical_and(inner, index == 1), jnp.logical_and(inner, index == 0), outer]
        incoming = []
        for condition, packed, pair in zip(wanted, sources[::2], sources[1::2]):
            incoming.append((condition, packed, held, leave.at[2]))
            incoming += [(condition, *job) for job in stack_jobs(pair, stacked, arrive)]
        each_copy(incoming, "start")
        each_copy(incoming, "wait")
        padded[:INNER, :] = dot(passes_left(unpack(held, gram)), stacked[...])
        matrix = matrix_of(owner_group, rank ^ (index * mate(ranks)))
        extract(padded, row_offsets[matrix, rank], row_counts[matrix, rank] * live_ranks[rank], staged, 0)
        outgoing = [
            (index >= 0, staged.at[0], shards.at[matrix], leave.at[0]),
            (index == 0, padded.at[pl.ds(0, INNER)], result, leave.at[1]),
        ]
        each_copy(outgoing, "start")
        each_copy(outgoing, "wait")
        return carry

    lax.fori_loop(0, jnp.where(inner, 2, 1), make, 0)


def place_kernel(first, ranks, steps, *refs):
    table, blocks, shards = refs[0], refs[1 : 1 + len(steps)], refs[2 + len(steps)]
    owner_group, arrive, leave = refs[3 + len(steps) :]
    rank = lax.axis_index("fsdp")
    fetch = pltpu.make_async_copy(table, owner_group, arrive)
    fetch.start()
    fetch.wait()
    copies = []
    for index, step in enumerate(steps):
        source = rank ^ step
        matrix = matrix_of(owner_group, source ^ mate(ranks) if first else source)
        copies.append((is_inner(source, ranks), blocks[index], shards.at[matrix], leave.at[index]))
    each_copy(copies, "start")
    each_copy(copies, "wait")


def idle_kernel(*refs):
    pass


def floats(*shape):
    return jax.ShapeDtypeStruct(shape, jnp.float32)


def vmem(*shape, dtype=jnp.float32):
    return pltpu.VMEM(shape, dtype)


def flags(*shape):
    return pltpu.SemaphoreType.DMA(shape)


FREE = pl.CostEstimate(flops=0, bytes_accessed=0, transcendentals=0)


def blend(first, tables, momentum, gradient, before):
    _, slots, columns = momentum.shape
    ranks = tables[1].shape[0]
    chunks = 2 if slots % (2 * SUBLANES) == 0 else 1
    return pl.pallas_call(
        functools.partial(blend_kernel, first, chunks),
        out_shape=[floats(slots, columns)] * (ranks - first) + [floats(SUBLANES, 128)],
        in_specs=[HBM] * 6 + [ANY] * len(before),
        out_specs=[ANY] * (ranks - first) + [VMEM],
        scratch_shapes=[vmem(ranks, slots, columns)] * 2
        + [flags(ranks, chunks, 2), flags(ranks, chunks)]
        + table_scratch(*tables[2].shape),
        compiler_params=FULL,
        cost_estimate=FREE,
        name="blend",
    )(*tables, momentum, gradient, *before)


def fresh_momentum(tables, momentum, gradient, before):
    matrices, slots, columns = momentum.shape
    block = pl.BlockSpec((None, slots, columns), lambda matrix: (matrix, 0, 0))
    return pl.pallas_call(
        fresh_kernel,
        grid=(matrices,),
        out_shape=[floats(*momentum.shape), floats(SUBLANES, 128)],
        in_specs=[pl.BlockSpec(memory_space=pltpu.SMEM)] * 2 + [block] * 2 + [ANY],
        out_specs=[block, pl.BlockSpec((SUBLANES, 128), lambda matrix: (0, 0))],
        compiler_params=FULL,
        cost_estimate=FREE,
        name="fresh_momentum",
    )(*tables[1:3], momentum, gradient, before)


def assemble_and_gram(inner, first, tables, blocks, *after):
    slots, columns = blocks[0].shape
    ranks = len(blocks)
    pair = jax.ShapeDtypeStruct((4, INNER, columns), jnp.bfloat16)
    return pl.pallas_call(
        functools.partial(gram_kernel, inner, first, ranks),
        out_shape=[pair] + [floats(INNER // 2, 2 * PANEL)] * 2,
        in_specs=[HBM] * 4 + [ANY] * (ranks + len(after)),
        out_specs=[ANY, VMEM, VMEM],
        scratch_shapes=[
            vmem(ranks, slots, columns),
            vmem(INNER + slots + SUBLANES, columns),
            vmem(INNER, columns, dtype=jnp.bfloat16),
            vmem(INNER, columns, dtype=jnp.bfloat16),
            vmem(INNER, 2 * PANEL),
            flags(ranks),
            flags(2),
        ]
        + table_scratch(*tables[2].shape),
        compiler_params=PARAMS,
        cost_estimate=FREE,
        name="assemble_and_gram",
    )(*tables, *blocks, *after)


def update_shapes(steps, slots, columns):
    return [floats(INNER, 2 * PANEL)] + [floats(slots, columns)] * len(steps)


def nothing(shapes):
    return pl.pallas_call(
        idle_kernel, out_shape=shapes, out_specs=[ANY] * len(shapes), compiler_params=SMALL, name="nothing"
    )()


def apply_update(first, steps, tables, keep, away, pair, slots, *after):
    columns = pair.shape[2]
    return pl.pallas_call(
        functools.partial(update_kernel, first, steps),
        out_shape=update_shapes(steps, slots, columns),
        in_specs=[HBM] * 4 + [VMEM] * 2 + [ANY] * (1 + len(after)),
        out_specs=[ANY] * (1 + len(steps)),
        scratch_shapes=[
            vmem(INNER, INNER),
            vmem(INNER + slots + 2 * SUBLANES, columns),
            vmem(max(len(steps), 1), slots, columns),
            vmem(3 * INNER, columns, dtype=jnp.bfloat16),
            vmem(INNER, 2 * PANEL),
            flags(len(PARTS)),
            flags(len(steps) + 1),
        ]
        + table_scratch(*tables[2].shape),
        compiler_params=PARAMS,
        cost_estimate=FREE,
        name="apply_update",
    )(*tables, keep, away, pair, *after)


def touch(*values, flops=0):
    return pl.pallas_call(
        idle_kernel,
        out_shape=floats(SUBLANES, 128),
        in_specs=[ANY] * len(values),
        out_specs=ANY,
        compiler_params=SMALL,
        cost_estimate=pl.CostEstimate(flops=flops, bytes_accessed=0, transcendentals=0),
        name="touch",
    )(*values)


def finish(tables, sources, shape, after):
    _, slots, columns = shape
    return pl.pallas_call(
        functools.partial(finish_kernel, tables[1].shape[0]),
        out_shape=[floats(INNER, columns), floats(*shape)],
        in_specs=[HBM] * 4 + [ANY] * 7,
        out_specs=[HBM] * 2,
        scratch_shapes=[
            vmem(INNER, INNER),
            vmem(INNER + slots + 2 * SUBLANES, columns),
            vmem(2, slots, columns),
            vmem(3 * INNER, columns, dtype=jnp.bfloat16),
            vmem(INNER, 2 * PANEL),
            flags(len(PARTS)),
            flags(3),
        ]
        + table_scratch(*tables[2].shape),
        compiler_params=PARAMS,
        cost_estimate=FREE,
        name="finish",
    )(*tables, *sources, after)


def place_blocks(first, owner_group, steps, blocks, shards, ranks):
    return pl.pallas_call(
        functools.partial(place_kernel, first, ranks, steps),
        out_shape=floats(*shards.shape),
        in_specs=[HBM] + [VMEM] * len(blocks) + [HBM],
        out_specs=HBM,
        scratch_shapes=[pltpu.SMEM(owner_group.shape, jnp.int32), flags(), flags(len(steps))],
        input_output_aliases={1 + len(blocks): 0},
        compiler_params=PARAMS,
        cost_estimate=FREE,
        name="place_blocks",
    )(owner_group, *blocks, shards)


def sum_halves(keep, send, axis, streams):
    size = lax.axis_size(axis)

    def exchange(piece, bits):
        return lax.ppermute(piece, axis, [(i, i ^ bits[i & 1]) for i in range(size)])

    chips = [1 << shift for shift in range(1, size.bit_length() - 1)]
    keep = keep + exchange(send, (1, 1))
    pieces = jnp.split(keep, streams, axis=0)
    for bits in zip(chips, reversed(chips)):
        pieces = [piece + exchange(piece, bits[:: 1 - 2 * index]) for index, piece in enumerate(pieces)]
    keep = jnp.concatenate(pieces, axis=0)
    return keep, exchange(keep, (1, 1))


def on_device(momentum, gradient, live_ranks, owner_group, row_counts, row_offsets):
    ranks = lax.axis_size("fsdp")
    _, slots, columns = momentum.shape
    inner = is_inner(lax.axis_index("fsdp"), ranks)
    tables = (owner_group, live_ranks, row_counts, row_offsets)
    last = [2, 1, *range(3, ranks)]
    early = [step for step in last if step != mate(ranks)]

    def pairs(step, inward):
        return [(i, i ^ step) for i in range(ranks) if is_inner(i ^ step if inward else i, ranks)]

    def to_inner(block, step):
        return lax.ppermute(block, "fsdp", pairs(step, True))

    def from_inner(block, step):
        return lax.ppermute(block, "fsdp", pairs(step, False))

    near = mate(ranks)
    far = [step for step in last if step != near]
    *blends, token = blend(True, tables, momentum, gradient, [])
    own = blends[near - 1]
    swapped = lax.ppermute(own, "fsdp", [(i, i ^ near) for i in range(ranks)])
    arrived = {step: to_inner(blends[step - 1], step) for step in far}
    *blends, token = blend(False, tables, momentum, gradient, [token, touch(swapped)])
    last_blocks = [blends[0]] + [to_inner(blends[step], step) for step in range(1, ranks)]
    new_momentum, token = fresh_momentum(tables, momentum, gradient, token)
    handed = {step: from_inner(arrived[step], near) for step in far}

    def ordered(base, opposite, others):
        return [{0: base, near: opposite, **others}[step] for step in range(ranks)]

    first_blocks = ordered(own, swapped, arrived)
    pair, keep, send = assemble_and_gram(True, True, tables, first_blocks, *[handed[step] for step in far[1:]])

    def first_update(pair, keep, send, after):
        return apply_update(True, early, tables, *sum_halves(keep, send, "tensor", 1), pair, slots, after)

    def first_skip(*_):
        return nothing(update_shapes(early, slots, columns))

    packed, *homes = lax.cond(inner, first_update, first_skip, pair, keep, send, touch(keep, send, flops=10**11))
    first_home = [from_inner(block, step) for step, block in zip(early, homes)]
    pair_shape = jax.ShapeDtypeStruct(pair.shape, pair.dtype)

    def outer_update(*blocks):
        pair, keep, send = assemble_and_gram(False, True, tables, blocks)
        return (pair, *apply_update(True, [], tables, *sum_halves(keep, send, "tensor", 1), pair, slots, keep))

    def outer_skip(*_):
        return tuple(nothing([pair_shape, *update_shapes([], slots, columns)]))

    outer_pair, outer_packed = lax.cond(inner, outer_skip, outer_update, *ordered(swapped, own, handed))

    def last_update(after, *blocks):
        pair, keep, send = assemble_and_gram(True, False, tables, blocks, after)
        return (pair, *apply_update(False, last, tables, *sum_halves(keep, send, "tensor", 2), pair, slots))

    def last_skip(*_):
        return tuple(nothing([pair_shape, *update_shapes(last, slots, columns)]))

    last_pair, last_packed, *homes = lax.cond(inner, last_update, last_skip, outer_packed, *last_blocks)
    last_home = [from_inner(block, step) for step, block in zip(last, homes)]

    sources = [packed, pair, last_packed, last_pair, outer_packed, outer_pair]
    result, shards = finish(tables, sources, momentum.shape, token)
    shards = place_blocks(True, owner_group, early, first_home, shards, ranks)
    for step, block in sorted(zip(last, last_home), key=lambda home: (home[0] == near, last.index(home[0]))):
        shards = place_blocks(False, owner_group, [step], [block], shards, ranks)
    return (new_momentum, shards, result[None])


def solution(mesh):
    placed = (P(None, "fsdp", "tensor"), P(None, "fsdp", "tensor"), P(), P(), P(), P())
    return jax.shard_map(
        on_device,
        mesh=mesh,
        in_specs=placed,
        out_specs=(P(None, "fsdp", "tensor"), P(None, "fsdp", "tensor"), P("fsdp", None, "tensor")),
        check_vma=False,
    )
```
